32 devices in a mesh: fs: 4 (over y, core), nodes: 8 (over z, x).
Axes of the slice: x: 2, y: 2, z: 4, core: 2. Of those that a mesh axis runs over, the one named last changes fastest.
Arguments:
- edge_latent: bfloat16 [16, 12288, 256], P('fs', 'nodes'), may hold values from -6 to 6
- node_latent: bfloat16 [16, 2048, 256], P('fs', 'nodes'), may hold values from -6 to 6
- edge_cot: bfloat16 [16, 12288, 256], P('fs', 'nodes'), may hold values from -6 to 6
- node_cot: bfloat16 [16, 2048, 256], P('fs', 'nodes'), may hold values from -6 to 6
- five_flag: int32 [2048], P('nodes'), may hold values 0 or 1
- senders: int32 [12288], P('nodes'), may hold values from 0 to 287, as said below
- send_rows: int32 [16, 16], P('nodes'), may hold values from 0 to 255, as said below
- kernels: float32 [1792, 256], P('fs')
- kernel_first: float32 [1792, 256], P('fs')
- kernel_second: float32 [1792, 256], P('fs')
- vectors: float32 [6, 256], replicated
- vector_first: float32 [6, 256], replicated
- vector_second: float32 [6, 256], replicated
- statistics: float32 [4, 256, 256], replicated, as said below
- bases: float32 [4, 256, 256], replicated
Outputs:
- edge_output: bfloat16 [16, 12288, 256], P('fs', 'nodes')
- node_output: bfloat16 [16, 2048, 256], P('fs', 'nodes')
- edge_grad: bfloat16 [16, 12288, 256], P('fs', 'nodes')
- node_grad: bfloat16 [16, 2048, 256], P('fs', 'nodes')
- kernel_new: float32 [1792, 256], P('fs')
- kernel_first_new: float32 [1792, 256], P('fs')
- kernel_second_new: float32 [1792, 256], P('fs')
- vector_new: float32 [6, 256], replicated
- vector_first_new: float32 [6, 256], replicated
- vector_second_new: float32 [6, 256], replicated
- statistics_new: float32 [4, 256, 256], replicated
- bases_new: float32 [4, 256, 256], replicated
- weights_half: bfloat16 [1792, 256], replicated
The draws below stay inside these ranges and needn't reach their ends.
Inputs may be any that keep to these rules, and one draw needn't show every extreme that they name: `senders`: entries below 16 occur only on devices with a lower neighbour, entries from 272 on only on devices with an upper neighbour. `send_rows`: each row lists distinct nodes of its device; row 2 * d goes to device d - 1, row 2 * d + 1 to device d + 1. `statistics`: each matrix is symmetric.
All inputs are finite; a program needn't handle non-finite values. No bound on the sum of `five_flag` on one device may be relied on, other than what follows from the above.
Results may differ from the reference program's by a relative error of at most 0.0075.
Values may be sent and summed in bfloat16 or wider, within the bound.
A program may use at most 192 MiB of HBM per device.

```python
import math
import jax
import jax.numpy as jnp
from jax import lax

D = 256
NB = 256
HALO = 16
DEG = 6
STEP = 5
SAMPLES = 16
NODES = 2048
EDGES = 12288
ROWS = 1792
N_NODES = 8


def edge_scale():
    return 2.0 * math.sqrt(SAMPLES * EDGES)


def node_scale():
    return 2.0 * math.sqrt(SAMPLES * NODES)


def row_scales():
    rows_index = jnp.arange(ROWS)
    return jnp.where(rows_index < 4 * D, edge_scale(), node_scale()).astype(jnp.float32)


def vector_scales():
    return jnp.array([edge_scale(), edge_scale(), edge_scale(), node_scale(), node_scale(), node_scale()], jnp.float32)


def draw_senders(key, part):
    key = jax.random.fold_in(key, 11)
    key_one, key_two, key_three = jax.random.split(key, 3)
    global_node = jnp.arange(NODES, dtype=jnp.int32)
    owner_dev = global_node // NB
    local_node = global_node % NB
    offsets = jax.random.randint(key_one, (NODES, DEG), -12, 13, dtype=jnp.int32)
    local_pick = jnp.clip(local_node[:, None] + offsets, 0, NB - 1) + HALO
    shift_low = jax.random.randint(key_two, (N_NODES,), 0, HALO, dtype=jnp.int32)
    shift_high = jax.random.randint(key_three, (N_NODES,), 0, HALO, dtype=jnp.int32)
    from_low = (local_node + shift_low[owner_dev]) % HALO
    from_high = HALO + NB + (local_node - (NB - HALO) + shift_high[owner_dev]) % HALO
    use_low = (local_node < HALO) & (owner_dev > 0)
    use_high = (local_node >= NB - HALO) & (owner_dev < N_NODES - 1)
    first_slot = jnp.where(use_low, from_low, jnp.where(use_high, from_high, local_pick[:, 0]))
    picked = local_pick.at[:, 0].set(first_slot)
    return picked.reshape(EDGES).astype(jnp.int32)


def draw_send_rows(key, part):
    key = jax.random.fold_in(key, 12)
    bits = jax.random.randint(key, (N_NODES, 2, HALO), 0, 2, dtype=jnp.int32)
    place = jnp.arange(HALO, dtype=jnp.int32)
    lower_list = jnp.where(place[None, :] == 0, 0, 2 * place[None, :] + bits[:, 0])
    upper_list = jnp.where(place[None, :] == HALO - 1, NB - 1, NB - 2 * HALO + 2 * place[None, :] + bits[:, 1])
    return jnp.stack([lower_list, upper_list], 1).reshape(2 * N_NODES, HALO).astype(jnp.int32)


def draw_kernels(key, part):
    key = jax.random.fold_in(key, 13)
    rows_index = jnp.arange(ROWS)
    fan = jnp.where(rows_index < 3 * D, 3 * D, jnp.where(rows_index < 4 * D, D, jnp.where(rows_index < 6 * D, 2 * D, D))).astype(jnp.float32)
    base = jax.random.normal(key, (ROWS, D), jnp.float32)
    return base / jnp.sqrt(fan)[:, None]


def draw_kernel_first(key, part):
    key = jax.random.fold_in(key, 14)
    base = jax.random.normal(key, (ROWS, D), jnp.float32)
    return base * row_scales()[:, None]


def draw_kernel_second(key, part):
    key = jax.random.fold_in(key, 15)
    factor = jnp.exp(jax.random.uniform(key, (ROWS, D), jnp.float32, 0.0, 1.3862944))
    scale_rows = row_scales()
    return factor * (scale_rows * scale_rows)[:, None]


def draw_vectors(key, part):
    key = jax.random.fold_in(key, 16)
    base = jax.random.normal(key, (6, D), jnp.float32)
    spread = jnp.array([0.5, 0.25, 0.3, 0.5, 0.25, 0.3], jnp.float32)
    centre = jnp.array([0.0, 1.0, 0.0, 0.0, 1.0, 0.0], jnp.float32)
    return centre[:, None] + spread[:, None] * jnp.clip(base, -2.0, 2.0)


def draw_vector_first(key, part):
    key = jax.random.fold_in(key, 17)
    base = jax.random.normal(key, (6, D), jnp.float32)
    return base * vector_scales()[:, None]


def draw_vector_second(key, part):
    key = jax.random.fold_in(key, 18)
    factor = jnp.exp(jax.random.uniform(key, (6, D), jnp.float32, 0.0, 1.3862944))
    scale_rows = vector_scales()
    return factor * (scale_rows * scale_rows)[:, None]


def draw_statistics(key, part):
    key = jax.random.fold_in(key, 19)
    key_one, key_two = jax.random.split(key)
    counts = jnp.array([3 * D, D, 2 * D, D], jnp.float32)
    grads_each = jnp.array([edge_scale(), edge_scale(), node_scale(), node_scale()], jnp.float32)
    level = counts * grads_each * grads_each
    diagonal = jnp.exp(jax.random.uniform(key_one, (4, D), jnp.float32, 0.0, 1.3862944)) * level[:, None]
    raw = jax.random.normal(key_two, (4, D, D), jnp.float32)
    symmetric = (raw + jnp.swapaxes(raw, 1, 2)) * (0.01 * 0.70710678) * level[:, None, None]
    identity = jnp.eye(D, dtype=jnp.float32)[None]
    return symmetric * (1.0 - identity) + identity * diagonal[:, :, None]


def draw_bases(key, part):
    key = jax.random.fold_in(key, 20)
    raw = jax.random.normal(key, (4, D, D), jnp.float32)
    return jnp.eye(D, dtype=jnp.float32)[None] + raw * (0.25 / math.sqrt(D))


def touch_ends(result, key, least, largest):
    longest = result.shape.index(max(result.shape))
    spots = []
    for shift in (0, 1):
        where = [jax.random.randint(jax.random.fold_in(key, axis), (), 0, length) for axis, length in enumerate(result.shape)]
        where[longest] = (where[longest] + shift) % result.shape[longest]
        spots.append(tuple(where))
    return result.at[spots[0]].set(least).at[spots[1]].set(largest)


def levels(stream_key, extent, cuts, smallest, high):
    def one(dim, blocks):
        draws = jax.random.uniform(jax.random.fold_in(jax.random.fold_in(stream_key, 6), dim), (blocks,), jnp.float32, smallest / len(cuts), high / len(cuts))
        return jnp.repeat(jnp.exp(draws), extent[dim] // blocks).reshape((-1,) + (1,) * (len(extent) - dim - 1))

    level = one(*cuts[0])
    for cut in cuts[1:]:
        level = level * one(*cut)
    return level


def normal_values(key, shape, width, reach, pieces=(), held_as=jnp.bfloat16):
    result = width * jax.random.normal(key, shape, jnp.float32)
    if pieces:
        result = result * levels(key, shape, pieces, -0.22, 0.18)
    return jnp.clip(result, -reach, reach).astype(held_as)


def setup_inputs(seed: int = 0) -> dict:
    splits = jax.random.split(jax.random.key(seed), 16)
    return {
        "edge_latent": normal_values(splits[0], (SAMPLES, EDGES, D), 1.0, 6.0, ((0, 4), (1, 8))),
        "node_latent": normal_values(splits[1], (SAMPLES, NODES, D), 1.0, 6.0, ((0, 4), (1, 8))),
        "edge_cot": normal_values(splits[2], (SAMPLES, EDGES, D), 1.0, 6.0, ((0, 4), (1, 8))),
        "node_cot": normal_values(splits[3], (SAMPLES, NODES, D), 1.0, 6.0, ((0, 4), (1, 8))),
        "five_flag": touch_ends((jax.random.randint(splits[4], (NODES,), 0, 16) < 1).astype(jnp.int32), jax.random.fold_in(splits[4], 1), 0, 1),
        "senders": draw_senders(jax.random.fold_in(splits[15], 71), 0),
        "send_rows": draw_send_rows(jax.random.fold_in(splits[15], 71), 0),
        "kernels": draw_kernels(jax.random.fold_in(splits[15], 71), 0),
        "kernel_first": draw_kernel_first(jax.random.fold_in(splits[15], 71), 0),
        "kernel_second": draw_kernel_second(jax.random.fold_in(splits[15], 71), 0),
        "vectors": draw_vectors(jax.random.fold_in(splits[15], 71), 0),
        "vector_first": draw_vector_first(jax.random.fold_in(splits[15], 71), 0),
        "vector_second": draw_vector_second(jax.random.fold_in(splits[15], 71), 0),
        "statistics": draw_statistics(jax.random.fold_in(splits[15], 71), 0),
        "bases": draw_bases(jax.random.fold_in(splits[15], 71), 0),
    }


NORM_EPS = 1e-05
BETA_ONE = 0.5
BETA_TWO = 0.5
RATE_MATRIX = 0.05
RATE_VECTOR = 0.2
DECAY_RATE = 0.01
ADAM_EPS = 1e-08
HIGH = lax.Precision.HIGHEST

@jax.custom_vjp
def low(v):
    return lax.optimization_barrier(v.astype(jnp.bfloat16)).astype(jnp.float32)

@jax.custom_vjp
def low_back(v):
    return v

def low_keep(v):
    return (low(v), None)

def low_pass(kept, grad):
    return (grad,)

def back_keep(v):
    return (v, None)

def back_low(kept, grad):
    return (low(grad),)
low.defvjp(low_keep, low_pass)
low_back.defvjp(back_keep, back_low)

def norm_rows(values, gain, shift):
    centre = values - lax.optimization_barrier(jnp.mean(values, -1, keepdims=True))
    spread = lax.optimization_barrier(jnp.mean(centre * centre, -1, keepdims=True))
    return centre * lax.rsqrt(spread + NORM_EPS) * gain + shift

def layer(edge_in, node_in, first_edge, second_edge, first_node, second_node, vector_set, sender_node, live):
    sent = node_in[sender_node]
    received = jnp.repeat(node_in, DEG, axis=0)
    joined = jnp.concatenate([edge_in, sent, received], -1)
    pre_edge = low_back(jnp.dot(joined, first_edge, precision=HIGH) + vector_set[0])
    act_edge = low(jax.nn.silu(pre_edge))
    out_edge = low_back(jnp.dot(act_edge, second_edge, precision=HIGH))
    update = norm_rows(out_edge, vector_set[1], vector_set[2]) * live
    edge_new = edge_in + update
    gathered = lax.optimization_barrier(jnp.sum(update.reshape(NODES, DEG, -1), 1))
    joined_node = jnp.concatenate([node_in, low(gathered)], -1)
    pre_node = low_back(jnp.dot(joined_node, first_node, precision=HIGH) + vector_set[3])
    act_node = low(jax.nn.silu(pre_node))
    out_node = low_back(jnp.dot(act_node, second_node, precision=HIGH))
    node_new = node_in + norm_rows(out_node, vector_set[4], vector_set[5])
    return (edge_new, node_new)

def reference(edge_latent, node_latent, edge_cot, node_cot, five_flag, senders, send_rows, kernels, kernel_first, kernel_second, vectors, vector_first, vector_second, statistics, bases):
    edge_ids = jnp.arange(EDGES, dtype=jnp.int32)
    owner_dev = edge_ids // (NB * DEG)
    to_lower = send_rows[0::2]
    to_upper = send_rows[1::2]
    lower_dev = jnp.clip(owner_dev - 1, 0, N_NODES - 1)
    upper_dev = jnp.clip(owner_dev + 1, 0, N_NODES - 1)
    from_lower = lower_dev * NB + to_upper[lower_dev, jnp.clip(senders, 0, HALO - 1)]
    from_own = owner_dev * NB + jnp.clip(senders - HALO, 0, NB - 1)
    from_upper = upper_dev * NB + to_lower[upper_dev, jnp.clip(senders - HALO - NB, 0, HALO - 1)]
    sender_node = jnp.where(senders < HALO, from_lower, jnp.where(senders < HALO + NB, from_own, from_upper)).astype(jnp.int32)
    slot_index = edge_ids % DEG
    live = (slot_index < DEG - five_flag[edge_ids // DEG]).astype(jnp.float32)[:, None]
    weights_full = kernels.astype(jnp.bfloat16).astype(jnp.float32)
    first_edge = weights_full[:3 * D]
    second_edge = weights_full[3 * D:4 * D]
    first_node = weights_full[4 * D:6 * D]
    second_node = weights_full[6 * D:]

    def one_sample(running, sample_items):
        edge_half, node_half, edge_back, node_back = sample_items

        def wrapped(edge_in, node_in, weight_one, weight_two, weight_three, weight_four, vector_set):
            return layer(edge_in, node_in, weight_one, weight_two, weight_three, weight_four, vector_set, sender_node, live)
        outputs, pullback = jax.vjp(wrapped, edge_half.astype(jnp.float32), node_half.astype(jnp.float32), first_edge, second_edge, first_node, second_node, vectors)
        grads_all = pullback((edge_back.astype(jnp.float32), node_back.astype(jnp.float32)))
        running = tuple((total + piece for total, piece in zip(running, grads_all[2:])))
        return (running, (outputs[0].astype(jnp.bfloat16), outputs[1].astype(jnp.bfloat16), grads_all[0].astype(jnp.bfloat16), grads_all[1].astype(jnp.bfloat16)))
    start_sums = (jnp.zeros_like(first_edge), jnp.zeros_like(second_edge), jnp.zeros_like(first_node), jnp.zeros_like(second_node), jnp.zeros_like(vectors))
    sums, stacked = lax.scan(one_sample, start_sums, (edge_latent, node_latent, edge_cot, node_cot))
    edge_output, node_output, edge_grad, node_grad = stacked
    correct = 1.0 - BETA_ONE ** STEP
    correct_two = 1.0 - BETA_TWO ** STEP
    bounds = [0, 3 * D, 4 * D, 6 * D, 7 * D]
    new_rows, first_rows, second_rows, stat_list, basis_list = ([], [], [], [], [])
    for block in range(4):
        lower_row = bounds[block]
        upper_row = bounds[block + 1]
        grad_block = sums[block]
        basis = bases[block]
        rotated = jnp.dot(grad_block, basis, precision=HIGH)
        first_new = BETA_ONE * kernel_first[lower_row:upper_row] + (1.0 - BETA_ONE) * rotated
        second_new = BETA_TWO * kernel_second[lower_row:upper_row] + (1.0 - BETA_TWO) * rotated * rotated
        scaled_step = first_new / correct / (jnp.sqrt(second_new / correct_two) + ADAM_EPS)
        master = kernels[lower_row:upper_row]
        new_rows.append(master - RATE_MATRIX * (jnp.dot(scaled_step, basis.T, precision=HIGH) + DECAY_RATE * master))
        first_rows.append(first_new)
        second_rows.append(second_new)
        stat_new = BETA_TWO * statistics[block] + (1.0 - BETA_TWO) * jnp.dot(grad_block.T, grad_block, precision=HIGH)
        projected = jnp.dot(stat_new, basis, precision=HIGH)
        gram = jnp.dot(projected.T, projected, precision=HIGH)
        factor = jnp.linalg.cholesky(gram)
        basis_list.append(jax.scipy.linalg.solve_triangular(factor, projected.T, lower=True).T)
        stat_list.append(stat_new)
    grad_vectors = sums[4]
    vector_first_new = BETA_ONE * vector_first + (1.0 - BETA_ONE) * grad_vectors
    vector_second_new = BETA_TWO * vector_second + (1.0 - BETA_TWO) * grad_vectors * grad_vectors
    vector_new = vectors - RATE_VECTOR * (vector_first_new / correct) / (jnp.sqrt(vector_second_new / correct_two) + ADAM_EPS)
    kernel_new = jnp.concatenate(new_rows, 0)
    return (edge_output, node_output, edge_grad, node_grad, kernel_new, jnp.concatenate(first_rows, 0), jnp.concatenate(second_rows, 0), vector_new, vector_first_new, vector_second_new, jnp.stack(stat_list), jnp.stack(basis_list), kernel_new.astype(jnp.bfloat16))
```

```python
from functools import partial

import jax
import jax.numpy as jnp
from jax import lax
from jax.experimental import pallas as pl
from jax.experimental.pallas import tpu as pltpu
from jax.sharding import PartitionSpec as P

STEP = 5

NORM_EPS = 1e-05
BETA_ONE = 0.5
BETA_TWO = 0.5
RATE_MATRIX = 0.05
RATE_VECTOR = 0.2
DECAY_RATE = 0.01
ADAM_EPS = 1e-08
HIGH = lax.Precision.HIGHEST
F32 = jnp.float32
BF16 = jnp.bfloat16
LANES = 128
VMEM_LIMIT = 56 * 1024 * 1024


def dot_nn(left, right):
    return lax.dot_general(left, right, (((1,), (0,)), ((), ())), preferred_element_type=F32)


def dot_nt(left, right):
    return lax.dot_general(left, right, (((1,), (1,)), ((), ())), preferred_element_type=F32)


def dot_tn(left, right):
    return lax.dot_general(left, right, (((0,), (0,)), ((), ())), preferred_element_type=F32)


def split(value):
    high = value.astype(BF16)
    return high, (value - high.astype(F32)).astype(BF16)


def iota(shape, dim):
    return lax.broadcasted_iota(jnp.int32, shape, dim)


def ones_where(mask):
    return jnp.where(mask, 1.0, 0.0).astype(BF16)


def fold_rows(value):
    rows, width = value.shape
    return jnp.sum(value.reshape(rows // 8, 8, width), 0)


def aligned(index, step):
    return pl.ds(pl.multiple_of(index * step, step), step)


class Sizes:
    def __init__(self, samples, nodes, slots, halo, width):
        self.samples, self.nodes, self.slots = samples, nodes, slots
        self.halo, self.width = halo, width
        self.edges = nodes * slots
        self.fwd_nodes, self.bwd_nodes = 64, 128
        self.fwd_rows = self.fwd_nodes * slots
        self.bwd_rows = self.bwd_nodes * slots
        self.fwd_chunks = nodes // self.fwd_nodes
        self.bwd_chunks = nodes // self.bwd_nodes


def main_scratch(z):
    rows, width = z.samples * z.edges, z.width
    per_node = z.samples * z.nodes
    per_halo = z.samples * 2 * z.halo
    return dict(
        edge_v=pltpu.VMEM((rows, width), BF16),
        cot_v=pltpu.VMEM((rows, width), BF16),
        eout_v=pltpu.VMEM((rows, width), BF16),
        egrad_v=pltpu.VMEM((rows, width), BF16),
        act_v=pltpu.VMEM((rows, width), BF16),
        slope_v=pltpu.VMEM((rows, width), F32),
        norm_v=pltpu.VMEM((rows, width), BF16),
        inv_v=pltpu.VMEM((rows, LANES), F32),
        own_v=pltpu.VMEM((z.edges, z.nodes), BF16),
        own_t=pltpu.VMEM((z.nodes, z.edges), BF16),
        halo_t=pltpu.VMEM((2 * z.halo, z.edges), BF16),
        sel_v=pltpu.VMEM((z.edges, 2 * LANES), BF16),
        rep_v=pltpu.VMEM((z.bwd_rows, 2 * LANES), BF16),
        rep_t=pltpu.VMEM((LANES, z.bwd_rows), BF16),
        live_v=pltpu.VMEM((z.edges, LANES), F32),
        half_v=pltpu.VMEM((7 * width, width), BF16),
        pown_v=pltpu.VMEM((z.samples * 2 * z.nodes, width), BF16),
        psel_v=pltpu.VMEM((z.samples * z.fwd_chunks * 2 * LANES, width), BF16),
        gath_v=pltpu.VMEM((per_node, width), BF16),
        drep_v=pltpu.VMEM((z.samples * z.bwd_chunks * 2 * LANES, width), BF16),
        recv_v=pltpu.VMEM((per_node, width), F32),
        aown_v=pltpu.VMEM((per_node, width), F32),
        ahalo_v=pltpu.VMEM((per_halo, width), F32),
        table_v=pltpu.VMEM((per_halo, width), BF16),
        gmat_v=pltpu.VMEM((7 * width, width), F32),
        vsum_v=pltpu.VMEM((6 * 8, width), F32),
        edge_sem=pltpu.SemaphoreType.DMA((z.samples,)),
        cot_sem=pltpu.SemaphoreType.DMA((z.samples,)),
        eout_sem=pltpu.SemaphoreType.DMA((z.samples,)),
        egrad_sem=pltpu.SemaphoreType.DMA((z.samples,)),
    )


def build_selectors(z, m, five_ref, send_ref):
    halo, nodes, slots = z.halo, z.nodes, z.slots
    lane = iota((LANES, LANES), 1)
    row = iota((LANES, LANES), 0)
    for g in range(z.edges // LANES):
        rows = slice(g * LANES, (g + 1) * LANES)
        line = jnp.broadcast_to(send_ref[:, rows].astype(F32), (LANES, LANES))
        column = line.T.astype(jnp.int32)
        for h in range(nodes // LANES):
            m.own_v[rows, h * LANES : (h + 1) * LANES] = ones_where(column == lane + (halo + h * LANES))
        place = jnp.where(column < halo, column, jnp.where(column >= halo + nodes, column - nodes, -1))
        in_halo = (place == (lane & (2 * halo - 1))) & (lane < 4 * halo)
        first = slots * (lane & (z.fwd_nodes - 1))
        local = row + (g * LANES) % z.fwd_rows
        m.sel_v[rows, 0:LANES] = ones_where((first <= local) & (local < first + slots))
        m.sel_v[rows, LANES : 2 * LANES] = ones_where(in_halo)
    senders = jnp.broadcast_to(send_ref[...], (8, z.edges))
    for i in range(nodes // 16):
        node = iota((16, z.edges), 0) + (halo + i * 16)
        m.own_t[i * 16 : (i + 1) * 16, :] = ones_where(jnp.broadcast_to(senders[0:1], (16, z.edges)) == node)
    wide = jnp.broadcast_to(senders[0:1], (2 * halo, z.edges))
    node = iota((2 * halo, z.edges), 0)
    node = jnp.where(node < halo, node, node + nodes)
    m.halo_t[...] = ones_where(wide == node)
    first = slots * (iota((z.bwd_rows, 2 * LANES), 1) & (LANES - 1))
    local = iota((z.bwd_rows, 2 * LANES), 0)
    rep = ones_where((first <= local) & (local < first + slots))
    m.rep_v[...] = rep
    first = slots * iota((LANES, z.bwd_rows), 0)
    local = iota((LANES, z.bwd_rows), 1)
    m.rep_t[...] = ones_where((first <= local) & (local < first + slots))
    local = iota((z.bwd_rows, LANES), 0).astype(F32)
    slot = local - slots * jnp.floor((local + 0.5) * (1.0 / slots))
    for h in range(nodes // LANES):
        five = jnp.broadcast_to(five_ref[:, h * LANES : (h + 1) * LANES].astype(F32), (LANES, LANES)).T
        spread = dot_nn(rep[:, :LANES], five.astype(BF16))
        m.live_v[h * z.bwd_rows : (h + 1) * z.bwd_rows, :] = jnp.where(slot < slots - spread, 1.0, 0.0)


def both(column):
    return jnp.concatenate([column, column], 1)


def row_mean(value):
    return jnp.sum(value, -1, keepdims=True) * (1.0 / value.shape[-1])


def centred(value):
    centre = value - row_mean(value)
    return centre, lax.rsqrt(row_mean(centre * centre) + NORM_EPS)


def act_and_slope(half):
    turn = jnp.tanh(half)
    above = 1.0 + turn
    act = half * above
    return act, above + act * (1.0 - turn)


def main_kernel(
    z, names, edge_ref, cot_ref, node_ref, ncot_ref, five_ref, send_ref, weight_ref, halo_ref, vec_ref,
    eout_ref, egrad_ref, nout_ref, ntot_ref, border_ref, grad_ref, gvec_ref, *scratch,
):
    m = type("Held", (), {})()
    for name, ref in zip(names, scratch, strict=True):
        setattr(m, name, ref)
    width, nodes, edges, samples, halo = z.width, z.nodes, z.edges, z.samples, z.halo
    two_halo = 2 * halo

    def sample_copy(source, target, sem, s):
        rows = aligned(s, edges)
        return pltpu.make_async_copy(source.at[rows], target.at[rows], sem.at[s])

    for s in range(samples):
        sample_copy(edge_ref, m.edge_v, m.edge_sem, s).start()
    for s in range(samples):
        sample_copy(cot_ref, m.cot_v, m.cot_sem, s).start()

    build_selectors(z, m, five_ref, send_ref)
    m.half_v[...] = weight_ref[...] * jnp.asarray(0.5, BF16)
    m.gmat_v[...] = jnp.zeros_like(m.gmat_v)
    m.vsum_v[...] = jnp.zeros_like(m.vsum_v)
    m.aown_v[...] = jnp.zeros_like(m.aown_v)
    m.ahalo_v[...] = jnp.zeros_like(m.ahalo_v)
    for s in range(samples):
        for side in range(2):
            m.table_v[s * two_halo + side * halo : s * two_halo + (side + 1) * halo, :] = halo_ref[
                side, s * halo : (s + 1) * halo, :
            ]

    send_half = m.half_v[width : 2 * width, :]
    recv_half = m.half_v[2 * width : 3 * width, :]
    bias_edge, gain_edge, shift_edge = vec_ref[0:1, :] * 0.5, vec_ref[1:2, :], vec_ref[2:3, :]
    bias_node, gain_node, shift_node = vec_ref[3:4, :] * 0.5, vec_ref[4:5, :], vec_ref[5:6, :]

    for s in range(samples):
        node = node_ref[s * nodes : (s + 1) * nodes, :]
        high, low = split(dot_nn(node, send_half))
        m.pown_v[s * 2 * nodes : (s * 2 + 1) * nodes, :] = high
        m.pown_v[(s * 2 + 1) * nodes : (s * 2 + 2) * nodes, :] = low
        high, low = split(dot_nn(node, recv_half) + bias_edge)
        out_high, out_low = split(dot_nn(m.table_v[s * two_halo : (s + 1) * two_halo, :], send_half))
        zero = jnp.zeros((2 * LANES - 2 * z.fwd_nodes - 2 * two_halo, width), BF16)
        for c in range(z.fwd_chunks):
            own = slice(c * z.fwd_nodes, (c + 1) * z.fwd_nodes)
            base = (s * z.fwd_chunks + c) * 2 * LANES
            m.psel_v[base : base + 2 * LANES, :] = jnp.concatenate(
                [high[own], low[own], out_high, out_low, zero], 0
            )

    def forward(i, carry):
        s, c = i // z.fwd_chunks, i % z.fwd_chunks
        rows, local = aligned(i, z.fwd_rows), aligned(c, z.fwd_rows)

        @pl.when(c == 0)
        def _():
            sample_copy(edge_ref, m.edge_v, m.edge_sem, s).wait()

        edge = m.edge_v[rows, :]
        own = m.own_v[local, :]
        left = jnp.concatenate([edge, own, own, m.sel_v[local, :]], 1)
        right = jnp.concatenate(
            [m.half_v[0:width, :], m.pown_v[aligned(s, 2 * nodes), :], m.psel_v[aligned(i, 2 * LANES), :]], 0
        )
        act, slope = act_and_slope(dot_nn(left, right))
        act = act.astype(BF16)
        m.act_v[rows, :] = act
        m.slope_v[rows, :] = slope
        centre, inv = centred(dot_nn(act, weight_ref[3 * width : 4 * width, :]))
        live = m.live_v[local, :]
        inv = inv * live
        m.inv_v[rows, :] = inv
        normed = centre * both(inv)
        m.norm_v[rows, :] = normed.astype(BF16)
        update = normed * gain_edge + both(live) * shift_edge
        m.eout_v[rows, :] = (edge.astype(F32) + update).astype(BF16)
        gathered = dot_nn(m.rep_t[0 : z.fwd_nodes, 0 : z.fwd_rows], update.astype(BF16))
        m.gath_v[aligned(i, z.fwd_nodes), :] = gathered.astype(BF16)

        @pl.when(c == z.fwd_chunks - 1)
        def _():
            sample_copy(m.eout_v, eout_ref, m.eout_sem, s).start()

        return carry

    lax.fori_loop(0, samples * z.fwd_chunks, forward, 0)

    def node_part(i, carry):
        rows = aligned(i, 2 * nodes)
        node, gath = node_ref[rows, :], m.gath_v[rows, :]
        joined = jnp.concatenate([node, gath], 1)
        act, slope = act_and_slope(dot_nn(joined, m.half_v[4 * width : 6 * width, :]) + bias_node)
        act = act.astype(BF16)
        centre, inv = centred(dot_nn(act, weight_ref[6 * width : 7 * width, :]))
        normed = centre * inv
        nout_ref[rows, :] = (node.astype(F32) + normed * gain_node + shift_node).astype(BF16)
        back = ncot_ref[rows, :].astype(F32)
        back_normed = back * normed
        scaled, scaled_normed = back * gain_node, back_normed * gain_node
        d_out = (inv * (scaled - row_mean(scaled) - normed * row_mean(scaled_normed))).astype(BF16)
        m.gmat_v[6 * width : 7 * width, :] += dot_tn(act, d_out)
        m.vsum_v[32:40, :] += fold_rows(back_normed)
        m.vsum_v[40:48, :] += fold_rows(back)
        d_pre = dot_nt(d_out, m.half_v[6 * width : 7 * width, :]) * slope
        d_pre = d_pre.astype(BF16)
        m.vsum_v[24:32, :] += fold_rows(d_pre.astype(F32))
        m.gmat_v[4 * width : 6 * width, :] += dot_tn(joined, d_pre)
        d_joined = dot_nt(d_pre, weight_ref[4 * width : 6 * width, :])
        ntot_ref[rows, :] = back + d_joined[:, :width]
        high, low = split(d_joined[:, width:])
        for k in range(2):
            for c in range(z.bwd_chunks):
                own = slice(k * nodes + c * z.bwd_nodes, k * nodes + (c + 1) * z.bwd_nodes)
                m.drep_v[aligned((i * 2 + k) * z.bwd_chunks + c, 2 * LANES), :] = jnp.concatenate(
                    [high[own], low[own]], 0
                )
        return carry

    lax.fori_loop(0, samples // 2, node_part, 0)

    def backward(i, carry):
        s, c = i // z.bwd_chunks, i % z.bwd_chunks
        rows, local = aligned(i, z.bwd_rows), aligned(c, z.bwd_rows)

        @pl.when(c == 0)
        def _():
            sample_copy(cot_ref, m.cot_v, m.cot_sem, s).wait()

        cot = m.cot_v[rows, :].astype(F32)
        d_update = (cot + dot_nn(m.rep_v[...], m.drep_v[aligned(i, 2 * LANES), :])) * both(m.live_v[local, :])
        normed = m.norm_v[rows, :].astype(F32)
        d_normed = d_update * normed
        m.vsum_v[8:16, :] += fold_rows(d_normed)
        m.vsum_v[16:24, :] += fold_rows(d_update)
        scaled, scaled_normed = d_update * gain_edge, d_normed * gain_edge
        d_out = both(m.inv_v[rows, :]) * (scaled - row_mean(scaled) - normed * row_mean(scaled_normed))
        d_out = d_out.astype(BF16)
        d_pre = dot_nt(d_out, m.half_v[3 * width : 4 * width, :]) * m.slope_v[rows, :]
        d_pre = d_pre.astype(BF16)
        m.gmat_v[3 * width : 4 * width, :] += dot_tn(m.act_v[rows, :], d_out)
        m.gmat_v[0:width, :] += dot_tn(m.edge_v[rows, :], d_pre)
        m.recv_v[aligned(i, z.bwd_nodes), :] = dot_nn(m.rep_t[...], d_pre)
        m.aown_v[aligned(s, nodes), :] += dot_nn(m.own_t[:, local], d_pre)
        m.ahalo_v[aligned(s, two_halo), :] += dot_nn(m.halo_t[:, local], d_pre)
        m.egrad_v[rows, :] = (cot + dot_nt(d_pre, weight_ref[0:width, :])).astype(BF16)

        @pl.when(c == z.bwd_chunks - 1)
        def _():
            sample_copy(m.egrad_v, egrad_ref, m.egrad_sem, s).start()

        return carry

    lax.fori_loop(0, samples * z.bwd_chunks, backward, 0)

    send_full = weight_ref[width : 2 * width, :]
    recv_full = weight_ref[2 * width : 3 * width, :]
    out_high, out_low = split(m.ahalo_v[...])
    border_ref[...] = (dot_nt(out_high, send_full) + dot_nt(out_low, send_full)).astype(BF16)
    table = m.table_v[...]
    grad_send = dot_tn(table, out_high) + dot_tn(table, out_low)
    grad_recv = jnp.zeros((width, width), F32)
    for s in range(samples):
        rows = slice(s * nodes, (s + 1) * nodes)
        recv = m.recv_v[rows, :]
        m.vsum_v[0:8, :] += fold_rows(recv)
        recv_high, recv_low = split(recv)
        own_high, own_low = split(m.aown_v[rows, :])
        node = node_ref[rows, :]
        grad_recv += dot_tn(node, recv_high) + dot_tn(node, recv_low)
        grad_send += dot_tn(node, own_high) + dot_tn(node, own_low)
        ntot_ref[rows, :] += (
            dot_nt(recv_high, recv_full) + dot_nt(recv_low, recv_full)
            + dot_nt(own_high, send_full) + dot_nt(own_low, send_full)
        )
    grad_ref[0:width, :] = m.gmat_v[0:width, :].astype(BF16)
    grad_ref[width : 2 * width, :] = grad_send.astype(BF16)
    grad_ref[2 * width : 3 * width, :] = grad_recv.astype(BF16)
    grad_ref[3 * width :, :] = m.gmat_v[3 * width :, :].astype(BF16)
    for k in range(6):
        gvec_ref[k : k + 1, :] = jnp.sum(m.vsum_v[k * 8 : (k + 1) * 8, :], 0, keepdims=True)
    gvec_ref[6:8, :] = jnp.zeros((2, width), F32)
    for s in range(samples):
        sample_copy(m.eout_v, eout_ref, m.eout_sem, s).wait()
        sample_copy(m.egrad_v, egrad_ref, m.egrad_sem, s).wait()


def main_call(z, edge, cot, node, ncot, five, senders, weights, halo, vectors):
    scratch = main_scratch(z)
    rows, per_node, width = z.samples * z.edges, z.samples * z.nodes, z.width
    whole = pl.BlockSpec(memory_space=pltpu.VMEM)
    anywhere = pl.BlockSpec(memory_space=pl.ANY)
    return pl.pallas_call(
        partial(main_kernel, z, tuple(scratch)),
        out_shape=(
            jax.ShapeDtypeStruct((rows, width), BF16),
            jax.ShapeDtypeStruct((rows, width), BF16),
            jax.ShapeDtypeStruct((per_node, width), BF16),
            jax.ShapeDtypeStruct((per_node, width), F32),
            jax.ShapeDtypeStruct((z.samples * 2 * z.halo, width), BF16),
            jax.ShapeDtypeStruct((7 * width, width), BF16),
            jax.ShapeDtypeStruct((8, width), F32),
        ),
        in_specs=[anywhere] * 2 + [whole] * 7,
        out_specs=(anywhere, anywhere, whole, whole, whole, whole, whole),
        scratch_shapes=list(scratch.values()),
        compiler_params=pltpu.CompilerParams(vmem_limit_bytes=VMEM_LIMIT),
        name="edge_node_round",
    )(edge, cot, node, ncot, five, senders, weights, halo, vectors)


def dot_exact(left, right, dims):
    return lax.dot_general(left, right, (dims, ((), ())), precision=HIGH, preferred_element_type=F32)


BLOCK = 32
COUNT = 4


def factor_block(packed):
    sub = iota((8, LANES), 0)
    lane = iota((8, LANES), 1)
    tiles = BLOCK // 8
    group = lane & (LANES - BLOCK)
    parts = [packed[8 * r : 8 * r + 8, :] for r in range(tiles)]
    columns = [
        [jnp.take_along_axis(parts[r], group + l, axis=1) if r >= l // 8 else None for r in range(tiles)]
        for l in range(BLOCK)
    ]
    inverse = [jnp.where((lane & (BLOCK - 1)) == sub + 8 * r, 1.0, 0.0) for r in range(tiles)]

    def line(tile, s):
        return jnp.broadcast_to(tile[s : s + 1, :], (8, LANES))

    for j in range(BLOCK):
        rj, sj = j // 8, j % 8
        scale = lax.rsqrt(line(columns[j][rj], sj))
        below = [None if r < rj else columns[j][r] * scale for r in range(tiles)]
        below[rj] = jnp.where(sub > sj, below[rj], 0.0)
        for l in range(j + 1, BLOCK):
            weight = line(below[l // 8], l % 8)
            for r in range(l // 8, tiles):
                columns[l][r] = columns[l][r] - below[r] * weight
        row = line(inverse[rj], sj) * scale
        inverse[rj] = jnp.where(sub == sj, row, inverse[rj] - below[rj] * row)
        for r in range(rj + 1, tiles):
            inverse[r] = inverse[r] - below[r] * row
    return jnp.concatenate(inverse, 0)


def orthogonalize(work_v, width):
    per_half = LANES // BLOCK
    group = iota((BLOCK, LANES), 1) // BLOCK
    for b in range(width // BLOCK):
        half = b // per_half
        first = b * BLOCK
        rows = slice(first, first + BLOCK)
        lanes = slice(half * LANES, (half + 1) * LANES)
        place = [(b + k) % COUNT for k in range(COUNT)]
        packed = work_v[0, rows, lanes]
        for k in range(1, COUNT):
            packed = jnp.where(group == place[k], work_v[k, rows, lanes], packed)
        inverse = factor_block(packed)
        spread = jnp.concatenate([jnp.where(group == place[k], inverse, 0.0) for k in range(COUNT)], 0)
        start = (first + BLOCK) // LANES * LANES
        stack = jnp.concatenate([work_v[(g - b) % COUNT, rows, start:] for g in range(COUNT)], 0)
        solved = dot_exact(spread, stack, ((1,), (0,)))
        for k in range(COUNT):
            work_v[k, rows, width:] = solved[k * BLOCK : (k + 1) * BLOCK, width - start :]
        edges = [first + BLOCK, min(first + 2 * BLOCK, width), width]
        for low, high in zip(edges[:-1], edges[1:], strict=True):
            if low >= high:
                continue
            column = iota((high - low, LANES), 1) // BLOCK
            for k in range(COUNT):
                turned = dot_exact(work_v[k, low:high, lanes], spread, ((1,), (1,)))
                turned = jnp.where(column == k, turned, 0.0)
                work_v[k, low:high, start:] -= dot_exact(turned, solved, ((1,), (0,)))


def matrix_of(row, width):
    return sum((row >= bound * width).astype(jnp.int32) for bound in (3, 4, 6))


def update_kernel(
    grad_ref, gvec_ref, kern_ref, kfirst_ref, ksecond_ref, vec_ref, vfirst_ref, vsecond_ref, stat_ref, bases_ref,
    kern_out, kfirst_out, ksecond_out, half_out, vec_out, vfirst_out, vsecond_out, stat_out, bases_out, work_v,
):
    width = stat_ref.shape[-1]
    shard = kern_ref.shape[0]
    correct = 1.0 - BETA_ONE**STEP
    correct_two = 1.0 - BETA_TWO**STEP
    bounds = [0, 3 * width, 4 * width, 6 * width, 7 * width]
    half = LANES // BLOCK
    for k in range(COUNT):
        rows = grad_ref[bounds[k] : bounds[k + 1], :]
        stat = BETA_TWO * stat_ref[k] + (1.0 - BETA_TWO) * dot_tn(rows, rows)
        stat_out[k] = stat
        turned = dot_exact(bases_ref[k], stat, ((0,), (0,)))
        order = [h * half + (g - k) % half for h in range(width // LANES) for g in range(half)]
        moved = jnp.concatenate([turned[i * BLOCK : (i + 1) * BLOCK, :] for i in order], 0)
        work_v[k, :, 0:width] = dot_exact(turned, moved, ((1,), (1,)))
        work_v[k, :, width:] = turned

    first_row = lax.axis_index("fs") * shard
    grad = grad_ref[pl.ds(pl.multiple_of(first_row, 64), shard), :].astype(F32)
    one = matrix_of(first_row, width)
    two = matrix_of(first_row + shard - 1, width)
    in_two = matrix_of(first_row + iota((shard, width), 0), width) != one
    basis_one, basis_two = bases_ref[one], bases_ref[two]
    rotated = jnp.where(
        in_two, dot_exact(grad, basis_two, ((1,), (0,))), dot_exact(grad, basis_one, ((1,), (0,)))
    )
    first_new = BETA_ONE * kfirst_ref[...] + (1.0 - BETA_ONE) * rotated
    second_new = BETA_TWO * ksecond_ref[...] + (1.0 - BETA_TWO) * rotated * rotated
    kfirst_out[...] = first_new
    ksecond_out[...] = second_new
    step = first_new / correct / (jnp.sqrt(second_new / correct_two) + ADAM_EPS)
    turned = jnp.where(in_two, dot_exact(step, basis_two, ((1,), (1,))), dot_exact(step, basis_one, ((1,), (1,))))
    kern = kern_ref[...]
    kern_new = kern - RATE_MATRIX * (turned + DECAY_RATE * kern)
    kern_out[...] = kern_new
    half_out[...] = kern_new.astype(BF16)
    gvec = gvec_ref[0:6, :]
    first_new = BETA_ONE * vfirst_ref[...] + (1.0 - BETA_ONE) * gvec
    second_new = BETA_TWO * vsecond_ref[...] + (1.0 - BETA_TWO) * gvec * gvec
    vfirst_out[...] = first_new
    vsecond_out[...] = second_new
    vec_out[...] = vec_ref[...] - RATE_VECTOR * (first_new / correct) / (jnp.sqrt(second_new / correct_two) + ADAM_EPS)

    orthogonalize(work_v, width)
    for k in range(COUNT):
        bases_out[k] = work_v[k, :, width:].T


def update_call(grad, gvec, kern, kfirst, ksecond, vec, vfirst, vsecond, stat, bases):
    shard, width = kern.shape
    whole = pl.BlockSpec(memory_space=pltpu.VMEM)
    rows = jax.ShapeDtypeStruct((shard, width), F32)
    six = jax.ShapeDtypeStruct(vec.shape, F32)
    square = jax.ShapeDtypeStruct(stat.shape, F32)
    return pl.pallas_call(
        update_kernel,
        out_shape=(rows, rows, rows, jax.ShapeDtypeStruct((shard, width), BF16), six, six, six, square, square),
        in_specs=[whole] * 10,
        out_specs=(whole,) * 9,
        scratch_shapes=[pltpu.VMEM((COUNT, width, 2 * width), F32)],
        compiler_params=pltpu.CompilerParams(vmem_limit_bytes=VMEM_LIMIT),
        name="update",
    )(grad, gvec, kern, kfirst, ksecond, vec, vfirst, vsecond, stat, bases)


def exchange(low_part, high_part):
    count = lax.axis_size("nodes")
    up = [(i, i + 1) for i in range(count - 1)]
    down = [(i + 1, i) for i in range(count - 1)]
    return lax.ppermute(high_part, "nodes", up), lax.ppermute(low_part, "nodes", down)


def on_device(
    edge_latent, node_latent, edge_cot, node_cot, five_flag, senders, send_rows, kernels, kernel_first, kernel_second,
    vectors, vector_first, vector_second, statistics, bases,
):
    samples, nodes, width = node_latent.shape
    slots = senders.shape[0] // nodes
    halo = send_rows.shape[1]
    z = Sizes(samples, nodes, slots, halo, width)
    weights = lax.all_gather(kernels.astype(BF16), "fs", axis=0, tiled=True)
    packed = jnp.take(node_latent, send_rows.reshape(-1), axis=1).reshape(samples, 2, halo, width)
    below, above = exchange(packed[:, 0], packed[:, 1])
    around = jnp.stack([below.reshape(samples * halo, width), above.reshape(samples * halo, width)])
    edge_out, edge_grad, node_out, node_total, border, grad, gvec = main_call(
        z,
        edge_latent.reshape(-1, width),
        edge_cot.reshape(-1, width),
        node_latent.reshape(-1, width),
        node_cot.reshape(-1, width),
        five_flag.reshape(1, -1),
        senders.reshape(1, -1),
        weights,
        around,
        vectors,
    )
    border = border.reshape(samples, 2, halo, width)
    below, above = exchange(border[:, 0], border[:, 1])
    node_total = node_total.reshape(samples, nodes, width)
    node_total = node_total.at[:, send_rows[0]].add(below.astype(F32))
    node_total = node_total.at[:, send_rows[1]].add(above.astype(F32))
    grad = lax.psum(grad, ("nodes", "fs"))
    gvec = lax.psum(gvec, ("nodes", "fs"))
    kernel_new, first_new, second_new, half, vec_new, vfirst_new, vsecond_new, stat_new, bases_new = update_call(
        grad, gvec, kernels, kernel_first, kernel_second, vectors, vector_first, vector_second, statistics, bases
    )
    weights_half = lax.all_gather(half, "fs", axis=0, tiled=True)
    return (
        edge_out.reshape(edge_latent.shape),
        node_out.reshape(node_latent.shape),
        edge_grad.reshape(edge_latent.shape),
        node_total.astype(BF16),
        kernel_new, first_new, second_new, vec_new, vfirst_new, vsecond_new, stat_new, bases_new, weights_half,
    )


def solution(mesh):
    in_specs = (
        P("fs", "nodes", None),
        P("fs", "nodes", None),
        P("fs", "nodes", None),
        P("fs", "nodes", None),
        P("nodes"),
        P("nodes"),
        P("nodes", None),
        P("fs", None),
        P("fs", None),
        P("fs", None),
        P(),
        P(),
        P(),
        P(),
        P(),
    )
    out_specs = (
        P("fs", "nodes", None),
        P("fs", "nodes", None),
        P("fs", "nodes", None),
        P("fs", "nodes", None),
        P("fs", None),
        P("fs", None),
        P("fs", None),
        P(),
        P(),
        P(),
        P(),
        P(),
        P(),
    )
    return jax.shard_map(
        on_device, mesh=mesh, in_specs=in_specs, out_specs=out_specs, check_vma=False
    )
```

```python
from functools import partial

import jax
import jax.numpy as jnp
from jax import lax
from jax.experimental import pallas as pl
from jax.experimental.pallas import tpu as pltpu
from jax.sharding import PartitionSpec as P

STEP = 5

NORM_EPS = 1e-05
BETA_ONE = 0.5
BETA_TWO = 0.5
RATE_MATRIX = 0.05
RATE_VECTOR = 0.2
DECAY_RATE = 0.01
ADAM_EPS = 1e-08
HIGH = lax.Precision.HIGHEST
F32 = jnp.float32
BF16 = jnp.bfloat16
LANES = 128
VMEM_LIMIT = 56 * 1024 * 1024


def dot_nn(left, right):
    return lax.dot_general(left, right, (((1,), (0,)), ((), ())), preferred_element_type=F32)


def dot_nt(left, right):
    return lax.dot_general(left, right, (((1,), (1,)), ((), ())), preferred_element_type=F32)


def dot_tn(left, right):
    return lax.dot_general(left, right, (((0,), (0,)), ((), ())), preferred_element_type=F32)


def split(value):
    high = value.astype(BF16)
    return high, (value - high.astype(F32)).astype(BF16)


def iota(shape, dim):
    return lax.broadcasted_iota(jnp.int32, shape, dim)


def ones_where(mask):
    return jnp.where(mask, 1.0, 0.0).astype(BF16)


def fold_rows(value):
    rows, width = value.shape
    return jnp.sum(value.reshape(rows // 8, 8, width), 0)


def aligned(index, step):
    return pl.ds(pl.multiple_of(index * step, step), step)


class Sizes:
    def __init__(self, samples, nodes, slots, halo, width):
        self.samples, self.nodes, self.slots = samples, nodes, slots
        self.halo, self.width = halo, width
        self.edges = nodes * slots
        self.fwd_nodes, self.bwd_nodes = 64, 128
        self.fwd_rows = self.fwd_nodes * slots
        self.bwd_rows = self.bwd_nodes * slots
        self.fwd_chunks = nodes // self.fwd_nodes
        self.bwd_chunks = nodes // self.bwd_nodes


def main_scratch(z):
    rows, width = z.samples * z.edges, z.width
    per_node = z.samples * z.nodes
    per_halo = z.samples * 2 * z.halo
    return dict(
        edge_v=pltpu.VMEM((rows, width), BF16),
        cot_v=pltpu.VMEM((rows, width), BF16),
        eout_v=pltpu.VMEM((rows, width), BF16),
        egrad_v=pltpu.VMEM((rows, width), BF16),
        act_v=pltpu.VMEM((rows, width), BF16),
        slope_v=pltpu.VMEM((rows, width), F32),
        norm_v=pltpu.VMEM((rows, width), BF16),
        inv_v=pltpu.VMEM((rows, LANES), F32),
        own_v=pltpu.VMEM((z.edges, z.nodes), BF16),
        own_t=pltpu.VMEM((z.nodes, z.edges), BF16),
        halo_t=pltpu.VMEM((2 * z.halo, z.edges), BF16),
        sel_v=pltpu.VMEM((z.edges, 2 * LANES), BF16),
        rep_v=pltpu.VMEM((z.bwd_rows, 2 * LANES), BF16),
        rep_t=pltpu.VMEM((LANES, z.bwd_rows), BF16),
        live_v=pltpu.VMEM((z.edges, LANES), F32),
        half_v=pltpu.VMEM((7 * width, width), BF16),
        pown_v=pltpu.VMEM((z.samples * 2 * z.nodes, width), BF16),
        psel_v=pltpu.VMEM((z.samples * z.fwd_chunks * 2 * LANES, width), BF16),
        gath_v=pltpu.VMEM((per_node, width), BF16),
        drep_v=pltpu.VMEM((z.samples * z.bwd_chunks * 2 * LANES, width), BF16),
        recv_v=pltpu.VMEM((per_node, width), F32),
        aown_v=pltpu.VMEM((per_node, width), F32),
        ahalo_v=pltpu.VMEM((per_halo, width), F32),
        table_v=pltpu.VMEM((per_halo, width), BF16),
        gmat_v=pltpu.VMEM((7 * width, width), F32),
        vsum_v=pltpu.VMEM((6 * 8, width), F32),
        edge_sem=pltpu.SemaphoreType.DMA((z.samples,)),
        cot_sem=pltpu.SemaphoreType.DMA((z.samples,)),
        eout_sem=pltpu.SemaphoreType.DMA((z.samples,)),
        egrad_sem=pltpu.SemaphoreType.DMA((z.samples,)),
    )


def build_selectors(z, m, five_ref, send_ref):
    halo, nodes, slots = z.halo, z.nodes, z.slots
    lane = iota((LANES, LANES), 1)
    row = iota((LANES, LANES), 0)
    for g in range(z.edges // LANES):
        rows = slice(g * LANES, (g + 1) * LANES)
        line = jnp.broadcast_to(send_ref[:, rows].astype(F32), (LANES, LANES))
        column = line.T.astype(jnp.int32)
        for h in range(nodes // LANES):
            m.own_v[rows, h * LANES : (h + 1) * LANES] = ones_where(column == lane + (halo + h * LANES))
        place = jnp.where(column < halo, column, jnp.where(column >= halo + nodes, column - nodes, -1))
        in_halo = (place == (lane & (2 * halo - 1))) & (lane < 4 * halo)
        first = slots * (lane & (z.fwd_nodes - 1))
        local = row + (g * LANES) % z.fwd_rows
        m.sel_v[rows, 0:LANES] = ones_where((first <= local) & (local < first + slots))
        m.sel_v[rows, LANES : 2 * LANES] = ones_where(in_halo)
    senders = jnp.broadcast_to(send_ref[...], (8, z.edges))
    for i in range(nodes // 16):
        node = iota((16, z.edges), 0) + (halo + i * 16)
        m.own_t[i * 16 : (i + 1) * 16, :] = ones_where(jnp.broadcast_to(senders[0:1], (16, z.edges)) == node)
    wide = jnp.broadcast_to(senders[0:1], (2 * halo, z.edges))
    node = iota((2 * halo, z.edges), 0)
    node = jnp.where(node < halo, node, node + nodes)
    m.halo_t[...] = ones_where(wide == node)
    first = slots * (iota((z.bwd_rows, 2 * LANES), 1) & (LANES - 1))
    local = iota((z.bwd_rows, 2 * LANES), 0)
    rep = ones_where((first <= local) & (local < first + slots))
    m.rep_v[...] = rep
    first = slots * iota((LANES, z.bwd_rows), 0)
    local = iota((LANES, z.bwd_rows), 1)
    m.rep_t[...] = ones_where((first <= local) & (local < first + slots))
    local = iota((z.bwd_rows, LANES), 0).astype(F32)
    slot = local - slots * jnp.floor((local + 0.5) * (1.0 / slots))
    for h in range(nodes // LANES):
        five = jnp.broadcast_to(five_ref[:, h * LANES : (h + 1) * LANES].astype(F32), (LANES, LANES)).T
        spread = dot_nn(rep[:, :LANES], five.astype(BF16))
        m.live_v[h * z.bwd_rows : (h + 1) * z.bwd_rows, :] = jnp.where(slot < slots - spread, 1.0, 0.0)


def both(column):
    return jnp.concatenate([column, column], 1)


def row_mean(value):
    return jnp.sum(value, -1, keepdims=True) * (1.0 / value.shape[-1])


def centred(value):
    centre = value - row_mean(value)
    return centre, lax.rsqrt(row_mean(centre * centre) + NORM_EPS)


def act_and_slope(half):
    turn = jnp.tanh(half)
    above = 1.0 + turn
    act = half * above
    return act, above + act * (1.0 - turn)


def main_kernel(
    z, names, edge_ref, cot_ref, node_ref, ncot_ref, five_ref, send_ref, weight_ref, halo_ref, vec_ref,
    eout_ref, egrad_ref, nout_ref, ntot_ref, border_ref, grad_ref, gvec_ref, *scratch,
):
    m = type("Held", (), {})()
    for name, ref in zip(names, scratch, strict=True):
        setattr(m, name, ref)
    width, nodes, edges, samples, halo = z.width, z.nodes, z.edges, z.samples, z.halo
    two_halo = 2 * halo

    def sample_copy(source, target, sem, s):
        rows = aligned(s, edges)
        return pltpu.make_async_copy(source.at[rows], target.at[rows], sem.at[s])

    for s in range(samples):
        sample_copy(edge_ref, m.edge_v, m.edge_sem, s).start()
    for s in range(samples):
        sample_copy(cot_ref, m.cot_v, m.cot_sem, s).start()

    build_selectors(z, m, five_ref, send_ref)
    m.half_v[...] = weight_ref[...] * jnp.asarray(0.5, BF16)
    m.gmat_v[...] = jnp.zeros_like(m.gmat_v)
    m.vsum_v[...] = jnp.zeros_like(m.vsum_v)
    m.aown_v[...] = jnp.zeros_like(m.aown_v)
    m.ahalo_v[...] = jnp.zeros_like(m.ahalo_v)
    for s in range(samples):
        for side in range(2):
            m.table_v[s * two_halo + side * halo : s * two_halo + (side + 1) * halo, :] = halo_ref[
                side, s * halo : (s + 1) * halo, :
            ]

    send_half = m.half_v[width : 2 * width, :]
    recv_half = m.half_v[2 * width : 3 * width, :]
    bias_edge, gain_edge, shift_edge = vec_ref[0:1, :] * 0.5, vec_ref[1:2, :], vec_ref[2:3, :]
    bias_node, gain_node, shift_node = vec_ref[3:4, :] * 0.5, vec_ref[4:5, :], vec_ref[5:6, :]

    for s in range(samples):
        node = node_ref[s * nodes : (s + 1) * nodes, :]
        high, low = split(dot_nn(node, send_half))
        m.pown_v[s * 2 * nodes : (s * 2 + 1) * nodes, :] = high
        m.pown_v[(s * 2 + 1) * nodes : (s * 2 + 2) * nodes, :] = low
        high, low = split(dot_nn(node, recv_half) + bias_edge)
        out_high, out_low = split(dot_nn(m.table_v[s * two_halo : (s + 1) * two_halo, :], send_half))
        zero = jnp.zeros((2 * LANES - 2 * z.fwd_nodes - 2 * two_halo, width), BF16)
        for c in range(z.fwd_chunks):
            own = slice(c * z.fwd_nodes, (c + 1) * z.fwd_nodes)
            base = (s * z.fwd_chunks + c) * 2 * LANES
            m.psel_v[base : base + 2 * LANES, :] = jnp.concatenate(
                [high[own], low[own], out_high, out_low, zero], 0
            )

    def forward(i, carry):
        s, c = i // z.fwd_chunks, i % z.fwd_chunks
        rows, local = aligned(i, z.fwd_rows), aligned(c, z.fwd_rows)

        @pl.when(c == 0)
        def _():
            sample_copy(edge_ref, m.edge_v, m.edge_sem, s).wait()

        edge = m.edge_v[rows, :]
        own = m.own_v[local, :]
        left = jnp.concatenate([edge, own, own, m.sel_v[local, :]], 1)
        right = jnp.concatenate(
            [m.half_v[0:width, :], m.pown_v[aligned(s, 2 * nodes), :], m.psel_v[aligned(i, 2 * LANES), :]], 0
        )
        act, slope = act_and_slope(dot_nn(left, right))
        act = act.astype(BF16)
        m.act_v[rows, :] = act
        m.slope_v[rows, :] = slope
        centre, inv = centred(dot_nn(act, weight_ref[3 * width : 4 * width, :]))
        live = m.live_v[local, :]
        inv = inv * live
        m.inv_v[rows, :] = inv
        normed = centre * both(inv)
        m.norm_v[rows, :] = normed.astype(BF16)
        update = normed * gain_edge + both(live) * shift_edge
        m.eout_v[rows, :] = (edge.astype(F32) + update).astype(BF16)
        gathered = dot_nn(m.rep_t[0 : z.fwd_nodes, 0 : z.fwd_rows], update.astype(BF16))
        m.gath_v[aligned(i, z.fwd_nodes), :] = gathered.astype(BF16)

        @pl.when(c == z.fwd_chunks - 1)
        def _():
            sample_copy(m.eout_v, eout_ref, m.eout_sem, s).start()

        return carry

    lax.fori_loop(0, samples * z.fwd_chunks, forward, 0)

    def node_part(i, carry):
        rows = aligned(i, 2 * nodes)
        node, gath = node_ref[rows, :], m.gath_v[rows, :]
        joined = jnp.concatenate([node, gath], 1)
        act, slope = act_and_slope(dot_nn(joined, m.half_v[4 * width : 6 * width, :]) + bias_node)
        act = act.astype(BF16)
        centre, inv = centred(dot_nn(act, weight_ref[6 * width : 7 * width, :]))
        normed = centre * inv
        nout_ref[rows, :] = (node.astype(F32) + normed * gain_node + shift_node).astype(BF16)
        back = ncot_ref[rows, :].astype(F32)
        back_normed = back * normed
        scaled, scaled_normed = back * gain_node, back_normed * gain_node
        d_out = (inv * (scaled - row_mean(scaled) - normed * row_mean(scaled_normed))).astype(BF16)
        m.gmat_v[6 * width : 7 * width, :] += dot_tn(act, d_out)
        m.vsum_v[32:40, :] += fold_rows(back_normed)
        m.vsum_v[40:48, :] += fold_rows(back)
        d_pre = dot_nt(d_out, m.half_v[6 * width : 7 * width, :]) * slope
        d_pre = d_pre.astype(BF16)
        m.vsum_v[24:32, :] += fold_rows(d_pre.astype(F32))
        m.gmat_v[4 * width : 6 * width, :] += dot_tn(joined, d_pre)
        d_joined = dot_nt(d_pre, weight_ref[4 * width : 6 * width, :])
        ntot_ref[rows, :] = back + d_joined[:, :width]
        high, low = split(d_joined[:, width:])
        for k in range(2):
            for c in range(z.bwd_chunks):
                own = slice(k * nodes + c * z.bwd_nodes, k * nodes + (c + 1) * z.bwd_nodes)
                m.drep_v[aligned((i * 2 + k) * z.bwd_chunks + c, 2 * LANES), :] = jnp.concatenate(
                    [high[own], low[own]], 0
                )
        return carry

    lax.fori_loop(0, samples // 2, node_part, 0)

    def backward(i, carry):
        s, c = i // z.bwd_chunks, i % z.bwd_chunks
        rows, local = aligned(i, z.bwd_rows), aligned(c, z.bwd_rows)

        @pl.when(c == 0)
        def _():
            sample_copy(cot_ref, m.cot_v, m.cot_sem, s).wait()

        cot = m.cot_v[rows, :].astype(F32)
        d_update = (cot + dot_nn(m.rep_v[...], m.drep_v[aligned(i, 2 * LANES), :])) * both(m.live_v[local, :])
        normed = m.norm_v[rows, :].astype(F32)
        d_normed = d_update * normed
        m.vsum_v[8:16, :] += fold_rows(d_normed)
        m.vsum_v[16:24, :] += fold_rows(d_update)
        scaled, scaled_normed = d_update * gain_edge, d_normed * gain_edge
        d_out = both(m.inv_v[rows, :]) * (scaled - row_mean(scaled) - normed * row_mean(scaled_normed))
        d_out = d_out.astype(BF16)
        d_pre = dot_nt(d_out, m.half_v[3 * width : 4 * width, :]) * m.slope_v[rows, :]
        d_pre = d_pre.astype(BF16)
        m.gmat_v[3 * width : 4 * width, :] += dot_tn(m.act_v[rows, :], d_out)
        m.gmat_v[0:width, :] += dot_tn(m.edge_v[rows, :], d_pre)
        m.recv_v[aligned(i, z.bwd_nodes), :] = dot_nn(m.rep_t[...], d_pre)
        m.aown_v[aligned(s, nodes), :] += dot_nn(m.own_t[:, local], d_pre)
        m.ahalo_v[aligned(s, two_halo), :] += dot_nn(m.halo_t[:, local], d_pre)
        m.egrad_v[rows, :] = (cot + dot_nt(d_pre, weight_ref[0:width, :])).astype(BF16)

        @pl.when(c == z.bwd_chunks - 1)
        def _():
            sample_copy(m.egrad_v, egrad_ref, m.egrad_sem, s).start()

        return carry

    lax.fori_loop(0, samples * z.bwd_chunks, backward, 0)

    send_full = weight_ref[width : 2 * width, :]
    recv_full = weight_ref[2 * width : 3 * width, :]
    out_high, out_low = split(m.ahalo_v[...])
    border = (dot_nt(out_high, send_full) + dot_nt(out_low, send_full)).astype(BF16)
    for s in range(samples):
        for side in range(2):
            border_ref[side, s * halo : (s + 1) * halo, :] = border[
                s * two_halo + side * halo : s * two_halo + (side + 1) * halo, :
            ]
    table = m.table_v[...]
    grad_send = dot_tn(table, out_high) + dot_tn(table, out_low)
    grad_recv = jnp.zeros((width, width), F32)
    for s in range(samples):
        rows = slice(s * nodes, (s + 1) * nodes)
        recv = m.recv_v[rows, :]
        m.vsum_v[0:8, :] += fold_rows(recv)
        recv_high, recv_low = split(recv)
        own_high, own_low = split(m.aown_v[rows, :])
        node = node_ref[rows, :]
        grad_recv += dot_tn(node, recv_high) + dot_tn(node, recv_low)
        grad_send += dot_tn(node, own_high) + dot_tn(node, own_low)
        ntot_ref[rows, :] += (
            dot_nt(recv_high, recv_full) + dot_nt(recv_low, recv_full)
            + dot_nt(own_high, send_full) + dot_nt(own_low, send_full)
        )
    grad_ref[0:width, :] = m.gmat_v[0:width, :].astype(BF16)
    grad_ref[width : 2 * width, :] = grad_send.astype(BF16)
    grad_ref[2 * width : 3 * width, :] = grad_recv.astype(BF16)
    grad_ref[3 * width :, :] = m.gmat_v[3 * width :, :].astype(BF16)
    for k in range(6):
        gvec_ref[k : k + 1, :] = jnp.sum(m.vsum_v[k * 8 : (k + 1) * 8, :], 0, keepdims=True)
    gvec_ref[6:8, :] = jnp.zeros((2, width), F32)
    for s in range(samples):
        sample_copy(m.eout_v, eout_ref, m.eout_sem, s).wait()
        sample_copy(m.egrad_v, egrad_ref, m.egrad_sem, s).wait()


def main_call(z, edge, cot, node, ncot, five, senders, weights, halo, vectors):
    scratch = main_scratch(z)
    rows, per_node, width = z.samples * z.edges, z.samples * z.nodes, z.width
    whole = pl.BlockSpec(memory_space=pltpu.VMEM)
    anywhere = pl.BlockSpec(memory_space=pl.ANY)
    return pl.pallas_call(
        partial(main_kernel, z, tuple(scratch)),
        out_shape=(
            jax.ShapeDtypeStruct((rows, width), BF16),
            jax.ShapeDtypeStruct((rows, width), BF16),
            jax.ShapeDtypeStruct((per_node, width), BF16),
            jax.ShapeDtypeStruct((per_node, width), F32),
            jax.ShapeDtypeStruct((2, z.samples * z.halo, width), BF16),
            jax.ShapeDtypeStruct((7 * width, width), BF16),
            jax.ShapeDtypeStruct((8, width), F32),
        ),
        in_specs=[anywhere] * 2 + [whole] * 7,
        out_specs=(anywhere, anywhere, whole, whole, whole, whole, whole),
        scratch_shapes=list(scratch.values()),
        compiler_params=pltpu.CompilerParams(vmem_limit_bytes=VMEM_LIMIT),
        name="edge_node_round",
    )(edge, cot, node, ncot, five, senders, weights, halo, vectors)


def dot_exact(left, right, dims):
    return lax.dot_general(left, right, (dims, ((), ())), precision=HIGH, preferred_element_type=F32)


BLOCK = 32
COUNT = 4


def factor_block(packed):
    sub = iota((8, LANES), 0)
    lane = iota((8, LANES), 1)
    tiles = BLOCK // 8
    group = lane & (LANES - BLOCK)
    parts = [packed[8 * r : 8 * r + 8, :] for r in range(tiles)]
    columns = [
        [jnp.take_along_axis(parts[r], group + l, axis=1) if r >= l // 8 else None for r in range(tiles)]
        for l in range(BLOCK)
    ]
    inverse = [jnp.where((lane & (BLOCK - 1)) == sub + 8 * r, 1.0, 0.0) for r in range(tiles)]

    def line(tile, s):
        return jnp.broadcast_to(tile[s : s + 1, :], (8, LANES))

    for j in range(BLOCK):
        rj, sj = j // 8, j % 8
        scale = lax.rsqrt(line(columns[j][rj], sj))
        below = [None if r < rj else columns[j][r] * scale for r in range(tiles)]
        below[rj] = jnp.where(sub > sj, below[rj], 0.0)
        for l in range(j + 1, BLOCK):
            weight = line(below[l // 8], l % 8)
            for r in range(l // 8, tiles):
                columns[l][r] = columns[l][r] - below[r] * weight
        row = line(inverse[rj], sj) * scale
        inverse[rj] = jnp.where(sub == sj, row, inverse[rj] - below[rj] * row)
        for r in range(rj + 1, tiles):
            inverse[r] = inverse[r] - below[r] * row
    return jnp.concatenate(inverse, 0)


def orthogonalize(work_v, width):
    per_half = LANES // BLOCK
    group = iota((BLOCK, LANES), 1) // BLOCK
    for b in range(width // BLOCK):
        half = b // per_half
        first = b * BLOCK
        rows = slice(first, first + BLOCK)
        lanes = slice(half * LANES, (half + 1) * LANES)
        place = [(b + k) % COUNT for k in range(COUNT)]
        packed = work_v[0, rows, lanes]
        for k in range(1, COUNT):
            packed = jnp.where(group == place[k], work_v[k, rows, lanes], packed)
        inverse = factor_block(packed)
        spread = jnp.concatenate([jnp.where(group == place[k], inverse, 0.0) for k in range(COUNT)], 0)
        start = (first + BLOCK) // LANES * LANES
        stack = jnp.concatenate([work_v[(g - b) % COUNT, rows, start:] for g in range(COUNT)], 0)
        solved = dot_exact(spread, stack, ((1,), (0,)))
        for k in range(COUNT):
            work_v[k, rows, width:] = solved[k * BLOCK : (k + 1) * BLOCK, width - start :]
        edges = [first + BLOCK, min(first + 2 * BLOCK, width), width]
        for low, high in zip(edges[:-1], edges[1:], strict=True):
            if low >= high:
                continue
            column = iota((high - low, LANES), 1) // BLOCK
            for k in range(COUNT):
                turned = dot_exact(work_v[k, low:high, lanes], spread, ((1,), (1,)))
                turned = jnp.where(column == k, turned, 0.0)
                work_v[k, low:high, start:] -= dot_exact(turned, solved, ((1,), (0,)))


def matrix_of(row, width):
    return sum((row >= bound * width).astype(jnp.int32) for bound in (3, 4, 6))


def update_kernel(
    grad_ref, gvec_ref, kern_ref, kfirst_ref, ksecond_ref, vec_ref, vfirst_ref, vsecond_ref, stat_ref, bases_ref,
    kern_out, kfirst_out, ksecond_out, half_out, vec_out, vfirst_out, vsecond_out, stat_out, bases_out, work_v,
):
    width = stat_ref.shape[-1]
    shard = kern_ref.shape[0]
    correct = 1.0 - BETA_ONE**STEP
    correct_two = 1.0 - BETA_TWO**STEP
    bounds = [0, 3 * width, 4 * width, 6 * width, 7 * width]
    half = LANES // BLOCK
    for k in range(COUNT):
        rows = grad_ref[bounds[k] : bounds[k + 1], :]
        stat = BETA_TWO * stat_ref[k] + (1.0 - BETA_TWO) * dot_tn(rows, rows)
        stat_out[k] = stat
        turned = dot_exact(bases_ref[k], stat, ((0,), (0,)))
        order = [h * half + (g - k) % half for h in range(width // LANES) for g in range(half)]
        moved = jnp.concatenate([turned[i * BLOCK : (i + 1) * BLOCK, :] for i in order], 0)
        work_v[k, :, 0:width] = dot_exact(turned, moved, ((1,), (1,)))
        work_v[k, :, width:] = turned

    first_row = lax.axis_index("fs") * shard
    grad = grad_ref[pl.ds(pl.multiple_of(first_row, 64), shard), :].astype(F32)
    one = matrix_of(first_row, width)
    two = matrix_of(first_row + shard - 1, width)
    in_two = matrix_of(first_row + iota((shard, width), 0), width) != one
    basis_one, basis_two = bases_ref[one], bases_ref[two]
    rotated = jnp.where(
        in_two, dot_exact(grad, basis_two, ((1,), (0,))), dot_exact(grad, basis_one, ((1,), (0,)))
    )
    first_new = BETA_ONE * kfirst_ref[...] + (1.0 - BETA_ONE) * rotated
    second_new = BETA_TWO * ksecond_ref[...] + (1.0 - BETA_TWO) * rotated * rotated
    kfirst_out[...] = first_new
    ksecond_out[...] = second_new
    step = first_new / correct / (jnp.sqrt(second_new / correct_two) + ADAM_EPS)
    turned = jnp.where(in_two, dot_exact(step, basis_two, ((1,), (1,))), dot_exact(step, basis_one, ((1,), (1,))))
    kern = kern_ref[...]
    kern_new = kern - RATE_MATRIX * (turned + DECAY_RATE * kern)
    kern_out[...] = kern_new
    half_out[...] = kern_new.astype(BF16)
    gvec = gvec_ref[0:6, :]
    first_new = BETA_ONE * vfirst_ref[...] + (1.0 - BETA_ONE) * gvec
    second_new = BETA_TWO * vsecond_ref[...] + (1.0 - BETA_TWO) * gvec * gvec
    vfirst_out[...] = first_new
    vsecond_out[...] = second_new
    vec_out[...] = vec_ref[...] - RATE_VECTOR * (first_new / correct) / (jnp.sqrt(second_new / correct_two) + ADAM_EPS)

    orthogonalize(work_v, width)
    for k in range(COUNT):
        bases_out[k] = work_v[k, :, width:].T


def update_call(grad, gvec, kern, kfirst, ksecond, vec, vfirst, vsecond, stat, bases):
    shard, width = kern.shape
    whole = pl.BlockSpec(memory_space=pltpu.VMEM)
    rows = jax.ShapeDtypeStruct((shard, width), F32)
    six = jax.ShapeDtypeStruct(vec.shape, F32)
    square = jax.ShapeDtypeStruct(stat.shape, F32)
    return pl.pallas_call(
        update_kernel,
        out_shape=(rows, rows, rows, jax.ShapeDtypeStruct((shard, width), BF16), six, six, six, square, square),
        in_specs=[whole] * 10,
        out_specs=(whole,) * 9,
        scratch_shapes=[pltpu.VMEM((COUNT, width, 2 * width), F32)],
        compiler_params=pltpu.CompilerParams(vmem_limit_bytes=VMEM_LIMIT),
        name="update",
    )(grad, gvec, kern, kfirst, ksecond, vec, vfirst, vsecond, stat, bases)


MESH = pl.DeviceIdType.MESH


def greet(partners):
    barrier = pltpu.get_barrier_semaphore()
    count = 0
    for device, exists in partners:
        if exists is None:
            pl.semaphore_signal(barrier, inc=1, device_id=device, device_id_type=MESH)
            count = count + 1
        else:
            pl.when(exists)(partial(pl.semaphore_signal, barrier, inc=1, device_id=device, device_id_type=MESH))
            count = count + exists.astype(jnp.int32)
    pl.semaphore_wait(barrier, count)


def send(source, target, sems, slot, device):
    return pltpu.make_async_remote_copy(
        src_ref=source, dst_ref=target, send_sem=sems.at[0, slot], recv_sem=sems.at[1, slot],
        device_id=device, device_id_type=MESH,
    )


class Gather:
    PARTS = 4

    def __init__(self, rows_v, sems, shard, fs, node):
        self.rows_v, self.sems, self.shard, self.fs, self.node = rows_v, sems, shard, fs, node
        self.next, self.far = (fs ^ 1, node), (fs ^ 2, node)

    def piece(self, owner, part):
        size = self.shard // self.PARTS
        return self.rows_v.at[pl.ds(pl.multiple_of(owner * self.shard + part * size, 16), size)]

    def copy(self, owner, part, slot, device):
        return send(self.piece(owner, part), self.piece(owner, part), self.sems, slot * self.PARTS + part, device)

    def start(self):
        for part in range(self.PARTS):
            self.copy(self.fs, part, 0, self.far).start()
        for part in range(self.PARTS):
            self.copy(self.fs, part, 1, self.next).start()

    def finish(self):
        for part in range(self.PARTS):
            self.copy(self.fs, part, 0, self.far).wait_recv()
            self.copy(self.fs ^ 2, part, 2, self.next).start()
        for part in range(self.PARTS):
            self.copy(self.fs, part, 0, self.far).wait_send()
            self.copy(self.fs, part, 1, self.next).wait()
            self.copy(self.fs ^ 2, part, 2, self.next).wait()


def list_matrix(send_ref, side, nodes):
    halo = send_ref.shape[1]
    listed = jnp.broadcast_to(send_ref[side : side + 1, :], (nodes, halo))
    return ones_where(listed == iota((nodes, halo), 0))


def sides(node, count):
    return ((node - 1, node > 0), (node + 1, node < count - 1))


def fetch_kernel(samples, count, kern_ref, node_ref, send_ref, rows_out, halo_out, rows_v, halo_v, list_v, sems, halo_sems, out_sem):
    fs, node = lax.axis_index("fs"), lax.axis_index("nodes")
    shard = kern_ref.shape[0]
    nodes = node_ref.shape[0] // samples
    halo = send_ref.shape[1]
    gather = Gather(rows_v, sems, shard, fs, node)
    around = sides(node, count)
    rows_v[pl.ds(pl.multiple_of(fs * shard, 16), shard), :] = kern_ref[...].astype(BF16)
    halo_v[...] = jnp.zeros_like(halo_v)
    greet([(gather.next, None), (gather.far, None)] + [((fs, other), exists) for other, exists in around])
    gather.start()
    for side in range(2):
        chosen = list_matrix(send_ref, side, nodes)
        for s in range(samples):
            list_v[side, s * halo : (s + 1) * halo, :] = dot_tn(
                chosen, node_ref[s * nodes : (s + 1) * nodes, :]
            ).astype(BF16)
    for side, (other, exists) in enumerate(around):
        pl.when(exists)(lambda side=side, other=other: send(list_v.at[side], halo_v.at[1 - side], halo_sems, side, (fs, other)).start())
    gather.finish()
    out = pltpu.make_async_copy(rows_v, rows_out, out_sem)
    out.start()
    for side, (other, exists) in enumerate(around):
        def settle(side=side, other=other):
            send(list_v.at[side], halo_v.at[1 - side], halo_sems, side, (fs, other)).wait_send()
            send(list_v.at[1 - side], halo_v.at[side], halo_sems, 1 - side, (fs, other)).wait_recv()
        pl.when(exists)(settle)
    halo_out[...] = halo_v[...]
    out.wait()


def fetch_call(kern, node, send_rows, samples):
    shard, width = kern.shape
    halo = send_rows.shape[1]
    whole, anywhere = pl.BlockSpec(memory_space=pltpu.VMEM), pl.BlockSpec(memory_space=pl.ANY)
    total = lax.axis_size("fs") * shard
    two = (2, samples * halo, width)
    return pl.pallas_call(
        partial(fetch_kernel, samples, lax.axis_size("nodes")),
        out_shape=(jax.ShapeDtypeStruct((total, width), BF16), jax.ShapeDtypeStruct(two, BF16)),
        in_specs=[whole] * 3,
        out_specs=(anywhere, whole),
        scratch_shapes=[
            pltpu.VMEM((total, width), BF16),
            pltpu.VMEM(two, BF16),
            pltpu.VMEM(two, BF16),
            pltpu.SemaphoreType.DMA((2, 3 * Gather.PARTS)),
            pltpu.SemaphoreType.DMA((2, 2)),
            pltpu.SemaphoreType.DMA,
        ],
        compiler_params=pltpu.CompilerParams(
            collective_id=0, has_side_effects=True, vmem_limit_bytes=VMEM_LIMIT
        ),
        name="fetch",
    )(kern, node, send_rows)


def reduce_plan(rows, fs_count, node_count):
    bits = [("fs", b) for b in range(fs_count.bit_length() - 1)] + [
        ("nodes", b) for b in range(node_count.bit_length() - 1)
    ]
    steps = []
    for i, (axis, bit) in enumerate(bits):
        halved = rows % 32 == 0 and i < len(bits) - 1
        rows = rows // 2 if halved else rows
        steps.append((axis, bit, rows, halved))
    return steps


def reduce_kernel(
    samples, plan, count, grad_ref, gvec_ref, border_ref, total_ref, send_ref,
    grad_out, gvec_out, node_out, sum_v, out_v, land_v, send_v, vland_v, vsend_v, ret_v, sems, vsems, halo_sems, out_sem,
):
    fs, node = lax.axis_index("fs"), lax.axis_index("nodes")
    nodes = total_ref.shape[0] // samples
    halo = send_ref.shape[1]
    width = grad_ref.shape[1]
    around = sides(node, count)

    def partner(axis, bit):
        return (fs ^ (1 << bit), node) if axis == "fs" else (fs, node ^ (1 << bit))

    ret_v[...] = jnp.zeros_like(ret_v)
    greet(
        [(partner(axis, bit), None) for axis, bit, _, _ in plan] + [((fs, other), exists) for other, exists in around]
    )

    def give_back(side, other):
        return send(border_ref.at[side], ret_v.at[1 - side], halo_sems, side, (fs, other))

    for side, (other, exists) in enumerate(around):
        pl.when(exists)(lambda side=side, other=other: give_back(side, other).start())

    first, place, copies, regions = 0, 0, [], []
    vsum = gvec_ref[...]
    for i, (axis, bit, rows, halved) in enumerate(plan):
        mine = ((fs if axis == "fs" else node) >> bit) & 1
        keep = pl.multiple_of(first + mine * rows, 16) if halved else first
        give = pl.multiple_of(first + (1 - mine) * rows, 16) if halved else first
        if i == 0:
            source = grad_ref.at[pl.ds(give, rows)]
        else:
            source = send_v.at[pl.ds(place, rows)]
            source[...] = sum_v[pl.ds(give, rows), :].astype(BF16)
        copy = send(source, land_v.at[pl.ds(place, rows)], sems, i, partner(axis, bit))
        copy.start()
        vsend_v[i] = vsum
        vcopy = send(vsend_v.at[i], vland_v.at[i], vsems, i, partner(axis, bit))
        vcopy.start()
        copy.wait_recv()
        held = grad_ref if i == 0 else sum_v if halved else send_v
        own = keep if i == 0 or halved else place
        total = held[pl.ds(own, rows), :].astype(F32) + land_v[pl.ds(place, rows), :].astype(F32)
        if i == len(plan) - 1:
            out_v[pl.ds(keep, rows), :] = total.astype(BF16)
        else:
            sum_v[pl.ds(keep, rows), :] = total
        vcopy.wait_recv()
        vsum = vsum + vland_v[i]
        copies += [copy, vcopy]
        regions.append((axis, bit, rows, halved, keep))
        first, place = keep, place + rows
    for side, (other, exists) in enumerate(around):
        def settle(side=side, other=other):
            give_back(side, other).wait_send()
            give_back(1 - side, other).wait_recv()
        pl.when(exists)(settle)
    slot = len(plan)
    for axis, bit, rows, halved, keep in reversed(regions):
        if not halved:
            continue
        region = out_v.at[pl.ds(keep, rows)]
        copy = send(region, region, sems, slot, partner(axis, bit))
        copy.start()
        copies.append(copy)
        slot += 1
        if axis == "fs" and bit == 0:
            low, high = (list_matrix(send_ref, side, nodes) for side in range(2))
            for s in range(samples):
                rows_s = slice(s * nodes, (s + 1) * nodes)
                part = slice(s * halo, (s + 1) * halo)
                node_out[rows_s, :] = (
                    total_ref[rows_s, :] + dot_nn(low, ret_v[0, part, :]) + dot_nn(high, ret_v[1, part, :])
                ).astype(BF16)
            gvec_out[...] = vsum
        copy.wait_recv()
    out = pltpu.make_async_copy(out_v, grad_out, out_sem)
    out.start()
    for copy in copies:
        copy.wait_send()
    out.wait()


def reduce_call(grad, gvec, border, total, send_rows, samples):
    rows, width = grad.shape
    count = lax.axis_size("nodes")
    plan = reduce_plan(rows, lax.axis_size("fs"), count)
    landing = sum(step[2] for step in plan)
    gathers = sum(step[3] for step in plan)
    whole, anywhere = pl.BlockSpec(memory_space=pltpu.VMEM), pl.BlockSpec(memory_space=pl.ANY)
    return pl.pallas_call(
        partial(reduce_kernel, samples, plan, count),
        out_shape=(
            jax.ShapeDtypeStruct(grad.shape, BF16),
            jax.ShapeDtypeStruct(gvec.shape, F32),
            jax.ShapeDtypeStruct(total.shape, BF16),
        ),
        in_specs=[whole] * 5,
        out_specs=(anywhere, whole, whole),
        scratch_shapes=[
            pltpu.VMEM((rows, width), F32),
            pltpu.VMEM((rows, width), BF16),
            pltpu.VMEM((landing, width), BF16),
            pltpu.VMEM((landing, width), BF16),
            pltpu.VMEM((len(plan),) + gvec.shape, F32),
            pltpu.VMEM((len(plan),) + gvec.shape, F32),
            pltpu.VMEM(border.shape, BF16),
            pltpu.SemaphoreType.DMA((2, len(plan) + gathers)),
            pltpu.SemaphoreType.DMA((2, len(plan))),
            pltpu.SemaphoreType.DMA((2, 2)),
            pltpu.SemaphoreType.DMA,
        ],
        compiler_params=pltpu.CompilerParams(
            collective_id=1, has_side_effects=True, vmem_limit_bytes=VMEM_LIMIT
        ),
        name="reduce",
    )(grad, gvec, border, total, send_rows)


def on_device(
    edge_latent, node_latent, edge_cot, node_cot, five_flag, senders, send_rows, kernels, kernel_first, kernel_second,
    vectors, vector_first, vector_second, statistics, bases,
):
    samples, nodes, width = node_latent.shape
    slots = senders.shape[0] // nodes
    halo = send_rows.shape[1]
    z = Sizes(samples, nodes, slots, halo, width)
    weights, around = fetch_call(kernels, node_latent.reshape(-1, width), send_rows, samples)
    edge_out, edge_grad, node_out, node_total, border, grad, gvec = main_call(
        z,
        edge_latent.reshape(-1, width),
        edge_cot.reshape(-1, width),
        node_latent.reshape(-1, width),
        node_cot.reshape(-1, width),
        five_flag.reshape(1, -1),
        senders.reshape(1, -1),
        weights,
        around,
        vectors,
    )
    grad, gvec, node_grad = reduce_call(grad, gvec, border, node_total, send_rows, samples)
    kernel_new, first_new, second_new, half, vec_new, vfirst_new, vsecond_new, stat_new, bases_new = update_call(
        grad, gvec, kernels, kernel_first, kernel_second, vectors, vector_first, vector_second, statistics, bases
    )
    weights_half = lax.all_gather(half, "fs", axis=0, tiled=True)
    return (
        edge_out.reshape(edge_latent.shape),
        node_out.reshape(node_latent.shape),
        edge_grad.reshape(edge_latent.shape),
        node_grad.reshape(node_latent.shape),
        kernel_new, first_new, second_new, vec_new, vfirst_new, vsecond_new, stat_new, bases_new, weights_half,
    )


def solution(mesh):
    in_specs = (
        P("fs", "nodes", None),
        P("fs", "nodes", None),
        P("fs", "nodes", None),
        P("fs", "nodes", None),
        P("nodes"),
        P("nodes"),
        P("nodes", None),
        P("fs", None),
        P("fs", None),
        P("fs", None),
        P(),
        P(),
        P(),
        P(),
        P(),
    )
    out_specs = (
        P("fs", "nodes", None),
        P("fs", "nodes", None),
        P("fs", "nodes", None),
        P("fs", "nodes", None),
        P("fs", None),
        P("fs", None),
        P("fs", None),
        P(),
        P(),
        P(),
        P(),
        P(),
        P(),
    )
    return jax.shard_map(
        on_device, mesh=mesh, in_specs=in_specs, out_specs=out_specs, check_vma=False
    )
```

```python
from functools import partial

import jax
import jax.numpy as jnp
from jax import lax
from jax.experimental import pallas as pl
from jax.experimental.pallas import tpu as pltpu
from jax.sharding import PartitionSpec as P

STEP = 5

NORM_EPS = 1e-05
BETA_ONE = 0.5
BETA_TWO = 0.5
RATE_MATRIX = 0.05
RATE_VECTOR = 0.2
DECAY_RATE = 0.01
ADAM_EPS = 1e-08
HIGH = lax.Precision.HIGHEST
F32 = jnp.float32
BF16 = jnp.bfloat16
LANES = 128
VMEM_LIMIT = 56 * 1024 * 1024


def dot_nn(left, right):
    return lax.dot_general(left, right, (((1,), (0,)), ((), ())), preferred_element_type=F32)


def dot_nt(left, right):
    return lax.dot_general(left, right, (((1,), (1,)), ((), ())), preferred_element_type=F32)


def dot_tn(left, right):
    return lax.dot_general(left, right, (((0,), (0,)), ((), ())), preferred_element_type=F32)


def split(value):
    high = value.astype(BF16)
    return high, (value - high.astype(F32)).astype(BF16)


def iota(shape, dim):
    return lax.broadcasted_iota(jnp.int32, shape, dim)


def ones_where(mask):
    return jnp.where(mask, 1.0, 0.0).astype(BF16)


def fold_rows(value):
    rows, width = value.shape
    return jnp.sum(value.reshape(rows // 8, 8, width), 0)


def aligned(index, step):
    return pl.ds(pl.multiple_of(index * step, step), step)


class Sizes:
    def __init__(self, samples, nodes, slots, halo, width):
        self.samples, self.nodes, self.slots = samples, nodes, slots
        self.halo, self.width = halo, width
        self.edges = nodes * slots
        self.fwd_nodes, self.bwd_nodes = 64, 128
        self.fwd_rows = self.fwd_nodes * slots
        self.bwd_rows = self.bwd_nodes * slots
        self.fwd_chunks = nodes // self.fwd_nodes
        self.bwd_chunks = nodes // self.bwd_nodes


def main_scratch(z):
    rows, width = z.samples * z.edges, z.width
    per_node = z.samples * z.nodes
    per_halo = z.samples * 2 * z.halo
    return dict(
        edge_v=pltpu.VMEM((rows, width), BF16),
        cot_v=pltpu.VMEM((rows, width), BF16),
        eout_v=pltpu.VMEM((rows, width), BF16),
        egrad_v=pltpu.VMEM((rows, width), BF16),
        act_v=pltpu.VMEM((rows, width), BF16),
        slope_v=pltpu.VMEM((rows, width), F32),
        norm_v=pltpu.VMEM((rows, width), BF16),
        inv_v=pltpu.VMEM((rows, LANES), F32),
        own_v=pltpu.VMEM((z.edges, z.nodes), BF16),
        own_t=pltpu.VMEM((z.nodes, z.edges), BF16),
        halo_t=pltpu.VMEM((2 * z.halo, z.edges), BF16),
        sel_v=pltpu.VMEM((z.edges, 2 * LANES), BF16),
        rep_v=pltpu.VMEM((z.bwd_rows, 2 * LANES), BF16),
        rep_t=pltpu.VMEM((LANES, z.bwd_rows), BF16),
        live_v=pltpu.VMEM((z.edges, LANES), F32),
        half_v=pltpu.VMEM((7 * width, width), BF16),
        pown_v=pltpu.VMEM((z.samples * 2 * z.nodes, width), BF16),
        psel_v=pltpu.VMEM((z.samples * z.fwd_chunks * 2 * LANES, width), BF16),
        gath_v=pltpu.VMEM((per_node, width), BF16),
        drep_v=pltpu.VMEM((z.samples * z.bwd_chunks * 2 * LANES, width), BF16),
        recv_v=pltpu.VMEM((per_node, width), F32),
        aown_v=pltpu.VMEM((per_node, width), F32),
        ahalo_v=pltpu.VMEM((per_halo, width), F32),
        table_v=pltpu.VMEM((per_halo, width), BF16),
        gmat_v=pltpu.VMEM((7 * width, width), F32),
        vsum_v=pltpu.VMEM((6 * 8, width), F32),
        pre_v=pltpu.VMEM((2, z.fwd_rows, width), F32),
        raw_v=pltpu.VMEM((2, z.fwd_rows, width), F32),
        upd_v=pltpu.VMEM((2, z.fwd_rows, width), BF16),
        dout_v=pltpu.VMEM((2, z.bwd_rows, width), BF16),
        dpre_v=pltpu.VMEM((2, z.bwd_rows, width), BF16),
        edge_sem=pltpu.SemaphoreType.DMA((z.samples,)),
        cot_sem=pltpu.SemaphoreType.DMA((z.samples,)),
        eout_sem=pltpu.SemaphoreType.DMA((z.samples,)),
        egrad_sem=pltpu.SemaphoreType.DMA((z.samples,)),
    )


def build_selectors(z, m, five_ref, send_ref):
    halo, nodes, slots = z.halo, z.nodes, z.slots
    lane = iota((LANES, LANES), 1)
    row = iota((LANES, LANES), 0)
    for g in range(z.edges // LANES):
        rows = slice(g * LANES, (g + 1) * LANES)
        line = jnp.broadcast_to(send_ref[:, rows].astype(F32), (LANES, LANES))
        column = line.T.astype(jnp.int32)
        for h in range(nodes // LANES):
            m.own_v[rows, h * LANES : (h + 1) * LANES] = ones_where(column == lane + (halo + h * LANES))
        place = jnp.where(column < halo, column, jnp.where(column >= halo + nodes, column - nodes, -1))
        in_halo = (place == (lane & (2 * halo - 1))) & (lane < 4 * halo)
        first = slots * (lane & (z.fwd_nodes - 1))
        local = row + (g * LANES) % z.fwd_rows
        m.sel_v[rows, 0:LANES] = ones_where((first <= local) & (local < first + slots))
        m.sel_v[rows, LANES : 2 * LANES] = ones_where(in_halo)
    senders = jnp.broadcast_to(send_ref[...], (8, z.edges))
    for i in range(nodes // 16):
        node = iota((16, z.edges), 0) + (halo + i * 16)
        m.own_t[i * 16 : (i + 1) * 16, :] = ones_where(jnp.broadcast_to(senders[0:1], (16, z.edges)) == node)
    wide = jnp.broadcast_to(senders[0:1], (2 * halo, z.edges))
    node = iota((2 * halo, z.edges), 0)
    node = jnp.where(node < halo, node, node + nodes)
    m.halo_t[...] = ones_where(wide == node)
    first = slots * (iota((z.bwd_rows, 2 * LANES), 1) & (LANES - 1))
    local = iota((z.bwd_rows, 2 * LANES), 0)
    rep = ones_where((first <= local) & (local < first + slots))
    m.rep_v[...] = rep
    first = slots * iota((LANES, z.bwd_rows), 0)
    local = iota((LANES, z.bwd_rows), 1)
    m.rep_t[...] = ones_where((first <= local) & (local < first + slots))
    local = iota((z.bwd_rows, LANES), 0).astype(F32)
    slot = local - slots * jnp.floor((local + 0.5) * (1.0 / slots))
    for h in range(nodes // LANES):
        five = jnp.broadcast_to(five_ref[:, h * LANES : (h + 1) * LANES].astype(F32), (LANES, LANES)).T
        spread = dot_nn(rep[:, :LANES], five.astype(BF16))
        m.live_v[h * z.bwd_rows : (h + 1) * z.bwd_rows, :] = jnp.where(slot < slots - spread, 1.0, 0.0)


def both(column):
    return jnp.concatenate([column, column], 1)


def row_mean(value):
    return jnp.sum(value, -1, keepdims=True) * (1.0 / value.shape[-1])


def centred(value):
    centre = value - row_mean(value)
    return centre, lax.rsqrt(row_mean(centre * centre) + NORM_EPS)


def act_and_slope(half):
    turn = jnp.tanh(half)
    above = 1.0 + turn
    act = half * above
    return act, above + act * (1.0 - turn)


def main_kernel(
    z, names, edge_ref, cot_ref, node_ref, ncot_ref, five_ref, send_ref, weight_ref, halo_ref, vec_ref,
    eout_ref, egrad_ref, nout_ref, ntot_ref, border_ref, grad_ref, gvec_ref, *scratch,
):
    m = type("Held", (), {})()
    for name, ref in zip(names, scratch, strict=True):
        setattr(m, name, ref)
    width, nodes, edges, samples, halo = z.width, z.nodes, z.edges, z.samples, z.halo
    two_halo = 2 * halo

    def sample_copy(source, target, sem, s):
        rows = aligned(s, edges)
        return pltpu.make_async_copy(source.at[rows], target.at[rows], sem.at[s])

    for s in range(samples):
        sample_copy(edge_ref, m.edge_v, m.edge_sem, s).start()
    for s in range(samples):
        sample_copy(cot_ref, m.cot_v, m.cot_sem, s).start()

    build_selectors(z, m, five_ref, send_ref)
    m.half_v[...] = weight_ref[...] * jnp.asarray(0.5, BF16)
    m.gmat_v[...] = jnp.zeros_like(m.gmat_v)
    m.vsum_v[...] = jnp.zeros_like(m.vsum_v)
    m.aown_v[...] = jnp.zeros_like(m.aown_v)
    m.ahalo_v[...] = jnp.zeros_like(m.ahalo_v)
    for s in range(samples):
        for side in range(2):
            m.table_v[s * two_halo + side * halo : s * two_halo + (side + 1) * halo, :] = halo_ref[
                side, s * halo : (s + 1) * halo, :
            ]

    send_half = m.half_v[width : 2 * width, :]
    recv_half = m.half_v[2 * width : 3 * width, :]
    bias_edge, gain_edge, shift_edge = vec_ref[0:1, :] * 0.5, vec_ref[1:2, :], vec_ref[2:3, :]
    bias_node, gain_node, shift_node = vec_ref[3:4, :] * 0.5, vec_ref[4:5, :], vec_ref[5:6, :]

    for s in range(samples):
        node = node_ref[s * nodes : (s + 1) * nodes, :]
        high, low = split(dot_nn(node, send_half))
        m.pown_v[s * 2 * nodes : (s * 2 + 1) * nodes, :] = high
        m.pown_v[(s * 2 + 1) * nodes : (s * 2 + 2) * nodes, :] = low
        high, low = split(dot_nn(node, recv_half) + bias_edge)
        out_high, out_low = split(dot_nn(m.table_v[s * two_halo : (s + 1) * two_halo, :], send_half))
        zero = jnp.zeros((2 * LANES - 2 * z.fwd_nodes - 2 * two_halo, width), BF16)
        for c in range(z.fwd_chunks):
            own = slice(c * z.fwd_nodes, (c + 1) * z.fwd_nodes)
            base = (s * z.fwd_chunks + c) * 2 * LANES
            m.psel_v[base : base + 2 * LANES, :] = jnp.concatenate(
                [high[own], low[own], out_high, out_low, zero], 0
            )

    per = z.fwd_chunks
    last = samples * per - 1

    def join_edges(i, slot):
        s, c = i // per, i % per
        local = aligned(c, z.fwd_rows)
        own = m.own_v[local, :]
        left = jnp.concatenate([m.edge_v[aligned(i, z.fwd_rows), :], own, own, m.sel_v[local, :]], 1)
        right = jnp.concatenate(
            [m.half_v[0:width, :], m.pown_v[aligned(s, 2 * nodes), :], m.psel_v[aligned(i, 2 * LANES), :]], 0
        )
        m.pre_v[slot] = dot_nn(left, right)

    def activate(i, slot):
        rows = aligned(i, z.fwd_rows)
        act, slope = act_and_slope(m.pre_v[slot])
        act = act.astype(BF16)
        m.act_v[rows, :] = act
        m.slope_v[rows, :] = slope
        m.raw_v[slot] = dot_nn(act, weight_ref[3 * width : 4 * width, :])

    def update_edges(i, slot):
        rows, local = aligned(i, z.fwd_rows), aligned(i % per, z.fwd_rows)
        centre, inv = centred(m.raw_v[slot])
        live = m.live_v[local, :]
        inv = inv * live
        m.inv_v[rows, :] = inv
        normed = centre * both(inv)
        m.norm_v[rows, :] = normed.astype(BF16)
        update = normed * gain_edge + both(live) * shift_edge
        m.eout_v[rows, :] = (m.edge_v[rows, :].astype(F32) + update).astype(BF16)
        m.upd_v[slot] = update.astype(BF16)

    def gather_updates(i, slot):
        gathered = dot_nn(m.rep_t[0 : z.fwd_nodes, 0 : z.fwd_rows], m.upd_v[slot])
        m.gath_v[aligned(i, z.fwd_nodes), :] = gathered.astype(BF16)

    def edge_in(s):
        return sample_copy(edge_ref, m.edge_v, m.edge_sem, s)

    edge_in(0).wait()
    join_edges(0, 0)

    def forward(s, carry):
        pl.when(s < samples - 1)(lambda: edge_in(s + 1).wait())
        for c in range(per):
            i = s * per + c
            join_edges(jnp.minimum(i + 1, last), (c + 1) % 2)
            gather_updates(jnp.maximum(i - 2, 0), c % 2)
            activate(i, c % 2)
            update_edges(jnp.maximum(i - 1, 0), (c + 1) % 2)
        pl.when(s > 0)(lambda: sample_copy(m.eout_v, eout_ref, m.eout_sem, s - 1).start())
        return carry

    lax.fori_loop(0, samples, forward, 0)
    gather_updates(last - 1, 0)
    update_edges(last, 1)
    gather_updates(last, 1)
    sample_copy(m.eout_v, eout_ref, m.eout_sem, samples - 1).start()

    def node_part(i, carry):
        rows = aligned(i, 2 * nodes)
        node, gath = node_ref[rows, :], m.gath_v[rows, :]
        joined = jnp.concatenate([node, gath], 1)
        act, slope = act_and_slope(dot_nn(joined, m.half_v[4 * width : 6 * width, :]) + bias_node)
        act = act.astype(BF16)
        centre, inv = centred(dot_nn(act, weight_ref[6 * width : 7 * width, :]))
        normed = centre * inv
        nout_ref[rows, :] = (node.astype(F32) + normed * gain_node + shift_node).astype(BF16)
        back = ncot_ref[rows, :].astype(F32)
        back_normed = back * normed
        scaled, scaled_normed = back * gain_node, back_normed * gain_node
        d_out = (inv * (scaled - row_mean(scaled) - normed * row_mean(scaled_normed))).astype(BF16)
        m.gmat_v[6 * width : 7 * width, :] += dot_tn(act, d_out)
        m.vsum_v[32:40, :] += fold_rows(back_normed)
        m.vsum_v[40:48, :] += fold_rows(back)
        d_pre = dot_nt(d_out, m.half_v[6 * width : 7 * width, :]) * slope
        d_pre = d_pre.astype(BF16)
        m.vsum_v[24:32, :] += fold_rows(d_pre.astype(F32))
        m.gmat_v[4 * width : 6 * width, :] += dot_tn(joined, d_pre)
        d_joined = dot_nt(d_pre, weight_ref[4 * width : 6 * width, :])
        ntot_ref[rows, :] = back + d_joined[:, :width]
        high, low = split(d_joined[:, width:])
        for k in range(2):
            for c in range(z.bwd_chunks):
                own = slice(k * nodes + c * z.bwd_nodes, k * nodes + (c + 1) * z.bwd_nodes)
                m.drep_v[aligned((i * 2 + k) * z.bwd_chunks + c, 2 * LANES), :] = jnp.concatenate(
                    [high[own], low[own]], 0
                )
        return carry

    lax.fori_loop(0, samples // 2, node_part, 0)

    halves = z.bwd_rows // z.fwd_rows
    pairs = samples * z.bwd_chunks

    def spread_back(i, slot):
        half = slice((slot % halves) * z.fwd_rows, (slot % halves + 1) * z.fwd_rows)
        m.pre_v[slot] = dot_nn(m.rep_v[half, :], m.drep_v[aligned(i // halves, 2 * LANES), :])

    def norm_back(i, slot, pair):
        rows, local = aligned(i, z.fwd_rows), aligned(i % per, z.fwd_rows)
        d_update = (m.cot_v[rows, :].astype(F32) + m.pre_v[slot]) * both(m.live_v[local, :])
        normed = m.norm_v[rows, :].astype(F32)
        d_normed = d_update * normed
        m.vsum_v[8:16, :] += fold_rows(d_normed)
        m.vsum_v[16:24, :] += fold_rows(d_update)
        scaled, scaled_normed = d_update * gain_edge, d_normed * gain_edge
        d_out = both(m.inv_v[rows, :]) * (scaled - row_mean(scaled) - normed * row_mean(scaled_normed))
        m.dout_v[pair, slot * z.fwd_rows : (slot + 1) * z.fwd_rows, :] = d_out.astype(BF16)

    def activate_back(i, slot, pair):
        part = slice(slot * z.fwd_rows, (slot + 1) * z.fwd_rows)
        d_act = dot_nt(m.dout_v[pair, part, :], m.half_v[3 * width : 4 * width, :])
        m.dpre_v[pair, part, :] = (d_act * m.slope_v[aligned(i, z.fwd_rows), :]).astype(BF16)

    def weights_back(p, pair):
        s, c = p // z.bwd_chunks, p % z.bwd_chunks
        rows, local = aligned(p, z.bwd_rows), aligned(c, z.bwd_rows)
        d_out, d_pre = m.dout_v[pair], m.dpre_v[pair]
        m.gmat_v[3 * width : 4 * width, :] += dot_tn(m.act_v[rows, :], d_out)
        m.gmat_v[0:width, :] += dot_tn(m.edge_v[rows, :], d_pre)
        m.recv_v[aligned(p, z.bwd_nodes), :] = dot_nn(m.rep_t[...], d_pre)
        m.aown_v[aligned(s, nodes), :] += dot_nn(m.own_t[:, local], d_pre)
        m.ahalo_v[aligned(s, two_halo), :] += dot_nn(m.halo_t[:, local], d_pre)
        m.egrad_v[rows, :] = (m.cot_v[rows, :].astype(F32) + dot_nt(d_pre, weight_ref[0:width, :])).astype(BF16)

    m.dout_v[1] = jnp.zeros_like(m.dout_v[1])
    m.dpre_v[1] = jnp.zeros_like(m.dpre_v[1])
    spread_back(0, 0)

    def backward(s, carry):
        sample_copy(cot_ref, m.cot_v, m.cot_sem, s).wait()
        for k in range(z.bwd_chunks):
            p = s * z.bwd_chunks + k
            i = p * halves
            spread_back(i + 1, 1)
            activate_back(jnp.maximum(i - 1, 0), 1, 1 - k)
            norm_back(i, 0, k)
            weights_back(jnp.maximum(p - 1, 0), 1 - k)
            spread_back(jnp.minimum(i + 2, last), 0)
            activate_back(i, 0, k)
            norm_back(i + 1, 1, k)
        pl.when(s > 0)(lambda: sample_copy(m.egrad_v, egrad_ref, m.egrad_sem, s - 1).start())
        return carry

    lax.fori_loop(0, samples, backward, 0)
    activate_back(last, 1, 1)
    weights_back(pairs - 1, 1)
    sample_copy(m.egrad_v, egrad_ref, m.egrad_sem, samples - 1).start()

    send_full = weight_ref[width : 2 * width, :]
    recv_full = weight_ref[2 * width : 3 * width, :]
    out_high, out_low = split(m.ahalo_v[...])
    border = (dot_nt(out_high, send_full) + dot_nt(out_low, send_full)).astype(BF16)
    for s in range(samples):
        for side in range(2):
            border_ref[side, s * halo : (s + 1) * halo, :] = border[
                s * two_halo + side * halo : s * two_halo + (side + 1) * halo, :
            ]
    table = m.table_v[...]
    grad_send = dot_tn(table, out_high) + dot_tn(table, out_low)
    grad_recv = jnp.zeros((width, width), F32)
    for s in range(samples):
        rows = slice(s * nodes, (s + 1) * nodes)
        recv = m.recv_v[rows, :]
        m.vsum_v[0:8, :] += fold_rows(recv)
        recv_high, recv_low = split(recv)
        own_high, own_low = split(m.aown_v[rows, :])
        node = node_ref[rows, :]
        grad_recv += dot_tn(node, recv_high) + dot_tn(node, recv_low)
        grad_send += dot_tn(node, own_high) + dot_tn(node, own_low)
        ntot_ref[rows, :] += (
            dot_nt(recv_high, recv_full) + dot_nt(recv_low, recv_full)
            + dot_nt(own_high, send_full) + dot_nt(own_low, send_full)
        )
    grad_ref[0:width, :] = m.gmat_v[0:width, :].astype(BF16)
    grad_ref[width : 2 * width, :] = grad_send.astype(BF16)
    grad_ref[2 * width : 3 * width, :] = grad_recv.astype(BF16)
    grad_ref[3 * width :, :] = m.gmat_v[3 * width :, :].astype(BF16)
    for k in range(6):
        gvec_ref[k : k + 1, :] = jnp.sum(m.vsum_v[k * 8 : (k + 1) * 8, :], 0, keepdims=True)
    gvec_ref[6:8, :] = jnp.zeros((2, width), F32)
    for s in range(samples):
        sample_copy(m.eout_v, eout_ref, m.eout_sem, s).wait()
        sample_copy(m.egrad_v, egrad_ref, m.egrad_sem, s).wait()


def main_call(z, edge, cot, node, ncot, five, senders, weights, halo, vectors):
    scratch = main_scratch(z)
    rows, per_node, width = z.samples * z.edges, z.samples * z.nodes, z.width
    whole = pl.BlockSpec(memory_space=pltpu.VMEM)
    anywhere = pl.BlockSpec(memory_space=pl.ANY)
    return pl.pallas_call(
        partial(main_kernel, z, tuple(scratch)),
        out_shape=(
            jax.ShapeDtypeStruct((rows, width), BF16),
            jax.ShapeDtypeStruct((rows, width), BF16),
            jax.ShapeDtypeStruct((per_node, width), BF16),
            jax.ShapeDtypeStruct((per_node, width), F32),
            jax.ShapeDtypeStruct((2, z.samples * z.halo, width), BF16),
            jax.ShapeDtypeStruct((7 * width, width), BF16),
            jax.ShapeDtypeStruct((8, width), F32),
        ),
        in_specs=[anywhere] * 2 + [whole] * 7,
        out_specs=(anywhere, anywhere, whole, whole, whole, whole, whole),
        scratch_shapes=list(scratch.values()),
        compiler_params=pltpu.CompilerParams(vmem_limit_bytes=VMEM_LIMIT),
        name="edge_node_round",
    )(edge, cot, node, ncot, five, senders, weights, halo, vectors)


def dot_exact(left, right, dims):
    return lax.dot_general(left, right, (dims, ((), ())), precision=HIGH, preferred_element_type=F32)


BLOCK = 32
COUNT = 4
HALF = LANES // BLOCK


def wide_left(value):
    high, low = split(value)
    return jnp.concatenate([high, high, low], 1)


def wide_right(value):
    high, low = split(value)
    return jnp.concatenate([high, low, high], 1)


def dot_three(left, right):
    return dot_nt(wide_left(left), wide_right(right))


def factor_block(packed):
    sub = iota((8, LANES), 0)
    lane = iota((8, LANES), 1)
    tiles = BLOCK // 8
    group = lane & (LANES - BLOCK)
    parts = [packed[8 * r : 8 * r + 8, :] for r in range(tiles)]
    columns = [
        [jnp.take_along_axis(parts[r], group + l, axis=1) if r >= l // 8 else None for r in range(tiles)]
        for l in range(BLOCK)
    ]
    inverse = [jnp.where((lane & (BLOCK - 1)) == sub + 8 * r, 1.0, 0.0) for r in range(tiles)]

    def line(tile, s):
        return jnp.broadcast_to(tile[s : s + 1, :], (8, LANES))

    for j in range(BLOCK):
        rj, sj = j // 8, j % 8
        scale = lax.rsqrt(line(columns[j][rj], sj))
        below = [None if r < rj else columns[j][r] * scale for r in range(tiles)]
        below[rj] = jnp.where(sub > sj, below[rj], 0.0)
        for l in range(j + 1, BLOCK):
            weight = line(below[l // 8], l % 8)
            for r in range(l // 8, tiles):
                columns[l][r] = columns[l][r] - below[r] * weight
        row = line(inverse[rj], sj) * scale
        inverse[rj] = jnp.where(sub == sj, row, inverse[rj] - below[rj] * row)
        for r in range(rj + 1, tiles):
            inverse[r] = inverse[r] - below[r] * row
    return jnp.concatenate(inverse, 0)


def turned_blocks(k, width):
    return [h * HALF + (g - k) % HALF for h in range(width // LANES) for g in range(HALF)]


def pick_rows(value, blocks):
    return jnp.concatenate([value[i * BLOCK : (i + 1) * BLOCK, :] for i in blocks], 0)


def orthogonalize(work_v, bases_out, width, halfway):
    blocks = width // BLOCK
    group = iota((BLOCK, LANES), 1) // BLOCK
    square = iota((LANES, LANES), 0) // BLOCK == iota((LANES, LANES), 1) // BLOCK

    def placed(values, b):
        return [jnp.where(group == (b + k) % COUNT, values[k], jnp.zeros_like(values[k])) for k in range(COUNT)]

    def lanes_of(b):
        return slice(b // HALF * LANES, (b // HALF + 1) * LANES)

    def rows_of(b):
        return slice(b * BLOCK, (b + 1) * BLOCK)

    packed = sum(placed([work_v[k, rows_of(0), lanes_of(0)] for k in range(COUNT)], 0))
    for b in range(blocks):
        if b == blocks // 2:
            halfway()
        lanes, after = lanes_of(b), (b + 1) * BLOCK
        high, low = split(factor_block(packed).astype(F32))
        high, low = placed([high] * COUNT, b), placed([low] * COUNT, b)
        if b < blocks - 1:
            spread_high, spread_low = jnp.concatenate(high, 0), jnp.concatenate(low, 0)
            spread = jnp.concatenate([spread_high, spread_low, spread_high], 1)
            ahead = jnp.concatenate([work_v[k, rows_of(b + 1), lanes] for k in range(COUNT)], 0)
            turned = jnp.where(square, dot_nt(wide_left(ahead), spread), 0.0)
            order = [(g - b - 1) % COUNT for g in range(COUNT)]
            update = dot_nt(wide_left(turned), pick_rows(wide_right(turned), order))
            current = placed([work_v[k, rows_of(b + 1), lanes_of(b + 1)] for k in range(COUNT)], b + 1)
            packed = sum(current) - sum(update[rows_of(k), :] for k in range(COUNT))
        start = after // LANES * LANES
        for k in range(COUNT):
            four_high = jnp.concatenate([high[k]] * HALF, 0)
            four_low = jnp.concatenate([low[k]] * HALF, 0)
            below = wide_left(work_v[k, after:, lanes])
            turned = dot_nt(below, jnp.concatenate([four_high, four_low, four_high], 1))
            mine = iota((width, LANES), 1) // BLOCK == b % HALF
            bases_out[k, :, lanes] = jnp.where(mine, turned[width - after :, :], bases_out[k, :, lanes])
            if b == blocks - 1:
                continue
            turned_high, turned_low = split(turned)
            part = iota(turned.shape, 1) // BLOCK
            zero = jnp.zeros_like(turned_high)
            left = jnp.where(part == 2, turned_low, jnp.where(part == 3, zero, turned_high))
            right = jnp.where(part == 1, turned_low, jnp.where(part == 3, zero, turned_high))
            right = jnp.concatenate(
                [
                    right[(i - b - 1) * BLOCK : (i - b) * BLOCK, :] if i > b else zero[0:BLOCK, :]
                    for i in turned_blocks(k, width)[start // BLOCK :]
                ],
                0,
            )
            work_v[k, after:, start:] -= dot_nt(left, right)


def matrix_bounds(width):
    return [0, 3 * width, 4 * width, 6 * width, 7 * width]


def new_statistics(grad_ref, stat_ref, k):
    width = stat_ref.shape[-1]
    bounds = matrix_bounds(width)
    rows = grad_ref[bounds[k] : bounds[k + 1], :]
    return BETA_TWO * stat_ref[k] + (1.0 - BETA_TWO) * dot_tn(rows, rows)


def matrix_of(row, width):
    return sum((row >= bound).astype(jnp.int32) for bound in matrix_bounds(width)[1:-1])


def adam_kernel(
    grad_ref, gvec_ref, kern_ref, kfirst_ref, ksecond_ref, vec_ref, vfirst_ref, vsecond_ref, stat_ref, bases_ref,
    kern_out, kfirst_out, ksecond_out, half_out, vec_out, vfirst_out, vsecond_out, stat_out,
):
    width = stat_ref.shape[-1]
    shard = kern_ref.shape[0]
    correct = 1.0 - BETA_ONE**STEP
    correct_two = 1.0 - BETA_TWO**STEP
    first_row = lax.axis_index("fs") * shard
    grad = grad_ref[pl.ds(pl.multiple_of(first_row, 64), shard), :]
    one = matrix_of(first_row, width)
    two = matrix_of(first_row + shard - 1, width)
    in_two = matrix_of(first_row + iota((shard, width), 0), width) != one
    basis_one, basis_two = bases_ref[one], bases_ref[two]

    def turn(basis):
        high, low = split(basis)
        return dot_nn(grad, high) + dot_nn(grad, low)

    rotated = jnp.where(in_two, turn(basis_two), turn(basis_one))
    first_new = BETA_ONE * kfirst_ref[...] + (1.0 - BETA_ONE) * rotated
    second_new = BETA_TWO * ksecond_ref[...] + (1.0 - BETA_TWO) * rotated * rotated
    kfirst_out[...] = first_new
    ksecond_out[...] = second_new
    step = first_new / correct / (jnp.sqrt(second_new / correct_two) + ADAM_EPS)
    turned = jnp.where(in_two, dot_three(step, basis_two), dot_three(step, basis_one))
    kern = kern_ref[...]
    kern_new = kern - RATE_MATRIX * (turned + DECAY_RATE * kern)
    kern_out[...] = kern_new
    half_out[...] = kern_new.astype(BF16)
    gvec = gvec_ref[0:6, :]
    first_new = BETA_ONE * vfirst_ref[...] + (1.0 - BETA_ONE) * gvec
    second_new = BETA_TWO * vsecond_ref[...] + (1.0 - BETA_TWO) * gvec * gvec
    vfirst_out[...] = first_new
    vsecond_out[...] = second_new
    vec_out[...] = vec_ref[...] - RATE_VECTOR * (first_new / correct) / (jnp.sqrt(second_new / correct_two) + ADAM_EPS)
    for k in range(COUNT):
        stat_out[k] = new_statistics(grad_ref, stat_ref, k)


def adam_call(grad, gvec, kern, kfirst, ksecond, vec, vfirst, vsecond, stat, bases):
    shard, width = kern.shape
    whole = pl.BlockSpec(memory_space=pltpu.VMEM)
    rows = jax.ShapeDtypeStruct((shard, width), F32)
    six = jax.ShapeDtypeStruct(vec.shape, F32)
    return pl.pallas_call(
        adam_kernel,
        out_shape=(
            rows, rows, rows, jax.ShapeDtypeStruct((shard, width), BF16), six, six, six,
            jax.ShapeDtypeStruct(stat.shape, F32),
        ),
        in_specs=[whole] * 10,
        out_specs=(whole,) * 8,
        compiler_params=pltpu.CompilerParams(vmem_limit_bytes=VMEM_LIMIT),
        name="adam",
    )(grad, gvec, kern, kfirst, ksecond, vec, vfirst, vsecond, stat, bases)


def prepare_bases(stat_ref, bases_ref, work_v, width):
    for k in range(COUNT):
        order = turned_blocks(k, width)
        stat = stat_ref[k]
        flipped = bases_ref[k].T
        proj_rows = dot_three(flipped, stat)
        work_v[k, 0:width, :] = dot_three(proj_rows, pick_rows(proj_rows, order))
        work_v[k, width:, :] = dot_three(stat, pick_rows(flipped, order))


MESH = pl.DeviceIdType.MESH


def greet(partners):
    barrier = pltpu.get_barrier_semaphore()
    count = 0
    for device, exists in partners:
        if exists is None:
            pl.semaphore_signal(barrier, inc=1, device_id=device, device_id_type=MESH)
            count = count + 1
        else:
            pl.when(exists)(partial(pl.semaphore_signal, barrier, inc=1, device_id=device, device_id_type=MESH))
            count = count + exists.astype(jnp.int32)
    pl.semaphore_wait(barrier, count)


def send(source, target, sems, slot, device):
    return pltpu.make_async_remote_copy(
        src_ref=source, dst_ref=target, send_sem=sems.at[0, slot], recv_sem=sems.at[1, slot],
        device_id=device, device_id_type=MESH,
    )


class Gather:
    PARTS = 4

    def __init__(self, rows_v, sems, shard, fs, node):
        self.rows_v, self.sems, self.shard, self.fs, self.node = rows_v, sems, shard, fs, node
        self.next, self.far = (fs ^ 1, node), (fs ^ 2, node)

    def piece(self, owner, part):
        size = self.shard // self.PARTS
        return self.rows_v.at[pl.ds(pl.multiple_of(owner * self.shard + part * size, 16), size)]

    def copy(self, owner, part, slot, device):
        return send(self.piece(owner, part), self.piece(owner, part), self.sems, slot * self.PARTS + part, device)

    def start(self):
        for part in range(self.PARTS):
            self.copy(self.fs, part, 0, self.far).start()
        for part in range(self.PARTS):
            self.copy(self.fs, part, 1, self.next).start()

    def forward(self):
        for part in range(self.PARTS):
            self.copy(self.fs, part, 0, self.far).wait_recv()
            self.copy(self.fs ^ 2, part, 2, self.next).start()

    def finish(self):
        for part in range(self.PARTS):
            self.copy(self.fs, part, 0, self.far).wait_send()
            self.copy(self.fs, part, 1, self.next).wait()
            self.copy(self.fs ^ 2, part, 2, self.next).wait()


def list_matrix(send_ref, side, nodes):
    halo = send_ref.shape[1]
    listed = jnp.broadcast_to(send_ref[side : side + 1, :], (nodes, halo))
    return ones_where(listed == iota((nodes, halo), 0))


def sides(node, count):
    return ((node - 1, node > 0), (node + 1, node < count - 1))


def fetch_kernel(samples, count, kern_ref, node_ref, send_ref, rows_out, halo_out, rows_v, halo_v, list_v, sems, halo_sems, out_sem):
    fs, node = lax.axis_index("fs"), lax.axis_index("nodes")
    shard = kern_ref.shape[0]
    nodes = node_ref.shape[0] // samples
    halo = send_ref.shape[1]
    gather = Gather(rows_v, sems, shard, fs, node)
    around = sides(node, count)
    rows_v[pl.ds(pl.multiple_of(fs * shard, 16), shard), :] = kern_ref[...].astype(BF16)
    halo_v[...] = jnp.zeros_like(halo_v)
    greet([(gather.next, None), (gather.far, None)] + [((fs, other), exists) for other, exists in around])
    gather.start()
    for side in range(2):
        chosen = list_matrix(send_ref, side, nodes)
        for s in range(samples):
            list_v[side, s * halo : (s + 1) * halo, :] = dot_tn(
                chosen, node_ref[s * nodes : (s + 1) * nodes, :]
            ).astype(BF16)
    for side, (other, exists) in enumerate(around):
        pl.when(exists)(lambda side=side, other=other: send(list_v.at[side], halo_v.at[1 - side], halo_sems, side, (fs, other)).start())
    gather.forward()
    gather.finish()
    out = pltpu.make_async_copy(rows_v, rows_out, out_sem)
    out.start()
    for side, (other, exists) in enumerate(around):
        def settle(side=side, other=other):
            send(list_v.at[side], halo_v.at[1 - side], halo_sems, side, (fs, other)).wait_send()
            send(list_v.at[1 - side], halo_v.at[side], halo_sems, 1 - side, (fs, other)).wait_recv()
        pl.when(exists)(settle)
    halo_out[...] = halo_v[...]
    out.wait()


def fetch_call(kern, node, send_rows, samples):
    shard, width = kern.shape
    halo = send_rows.shape[1]
    whole, anywhere = pl.BlockSpec(memory_space=pltpu.VMEM), pl.BlockSpec(memory_space=pl.ANY)
    total = lax.axis_size("fs") * shard
    two = (2, samples * halo, width)
    return pl.pallas_call(
        partial(fetch_kernel, samples, lax.axis_size("nodes")),
        out_shape=(jax.ShapeDtypeStruct((total, width), BF16), jax.ShapeDtypeStruct(two, BF16)),
        in_specs=[whole] * 3,
        out_specs=(anywhere, whole),
        scratch_shapes=[
            pltpu.VMEM((total, width), BF16),
            pltpu.VMEM(two, BF16),
            pltpu.VMEM(two, BF16),
            pltpu.SemaphoreType.DMA((2, 3 * Gather.PARTS)),
            pltpu.SemaphoreType.DMA((2, 2)),
            pltpu.SemaphoreType.DMA,
        ],
        compiler_params=pltpu.CompilerParams(
            collective_id=0, has_side_effects=True, vmem_limit_bytes=VMEM_LIMIT
        ),
        name="fetch",
    )(kern, node, send_rows)


class Cube:
    def __init__(self, count, fs=None, node=None):
        bits = count.bit_length() - 1
        self.node_bits = min(2, bits)
        self.size = 2 << self.node_bits
        self.extra = list(range(self.node_bits, bits))
        self.fs, self.node = fs, node
        if fs is not None:
            self.me = (fs >> 1) + 2 * (node & ((1 << self.node_bits) - 1))
        self.far_first = sorted(range(1, self.size), key=lambda r: (-r.bit_count(), -r))

    def device(self, r):
        return self.fs ^ (2 * (r & 1)), self.node ^ (r >> 1)

    def over(self, bit):
        return self.fs, self.node ^ (1 << bit)


def tree_sum(parts):
    while len(parts) > 1:
        parts = [left + right for left, right in zip(parts[::2], parts[1::2], strict=True)]
    return parts[0]


def reduce_kernel(
    samples, count, grad_ref, gvec_ref, border_ref, total_ref, send_ref,
    grad_out, gvec_out, node_out, half_v, land_v, sum_v, cube_v, extra_v, out_v, total_v, vsend_v, vland_v, ret_v,
    core_sems, cube_sems, extra_sems, back_sems, last_sems, vec_sems, halo_sems, local_sems,
):
    fs, node = lax.axis_index("fs"), lax.axis_index("nodes")
    cube = Cube(count, fs, node)
    nodes = total_ref.shape[0] // samples
    halo = send_ref.shape[1]
    rows = grad_ref.shape[0] // 2
    size = rows // cube.size
    around = sides(node, count)
    twin = (fs ^ 1, node)
    keep, give = (fs & 1) * rows, (1 - (fs & 1)) * rows

    def chunk(ref, r, base=0):
        return ref.at[pl.ds(pl.multiple_of(base + (cube.me ^ r) * size, 16), size)]

    mine = pltpu.make_async_copy(grad_ref.at[pl.ds(pl.multiple_of(keep, 16), rows)], half_v, local_sems.at[0])
    mine.start()
    fetch_total = pltpu.make_async_copy(total_ref, total_v, local_sems.at[1])
    fetch_total.start()
    ret_v[...] = jnp.zeros_like(ret_v)
    vsend_v[0] = gvec_ref[...]
    greet(
        [(twin, None)]
        + [(cube.device(r), None) for r in range(1, cube.size)]
        + [(cube.over(bit), None) for bit in cube.extra]
        + [((fs, other), exists) for other, exists in around]
    )

    def give_back(side, other):
        return send(border_ref.at[side], ret_v.at[1 - side], halo_sems, side, (fs, other))

    started = []

    def begin(copy):
        copy.start()
        started.append(copy)
        return copy

    order = cube.far_first + [0]
    core = {r: begin(send(chunk(grad_ref, r, give), chunk(land_v, r), core_sems, r, twin)) for r in order}
    vec = begin(send(vsend_v.at[0], vland_v.at[0], vec_sems, 0, twin))
    for side, (other, exists) in enumerate(around):
        pl.when(exists)(lambda side=side, other=other: give_back(side, other).start())
    mine.wait()
    spread, total = {}, None
    for r in order:
        core[r].wait_recv()
        total = chunk(half_v, r)[...].astype(F32) + chunk(land_v, r)[...].astype(F32)
        if r:
            chunk(sum_v, r)[...] = total.astype(BF16)
            spread[r] = begin(send(chunk(sum_v, r), cube_v.at[r], cube_sems, r, cube.device(r)))
    vec.wait_recv()
    vsum = vsend_v[0] + vland_v[0]
    vsend_v[1] = vsum
    vec = {r: begin(send(vsend_v.at[1], vland_v.at[r], vec_sems, r, cube.device(r))) for r in range(1, cube.size)}
    for r in reversed(cube.far_first):
        spread[r].wait_recv()
        total = total + cube_v[r].astype(F32)
    for copy in vec.values():
        copy.wait_recv()
    vsum = tree_sum([vsum] + [vland_v[r] for r in range(1, cube.size)])
    for e, bit in enumerate(cube.extra):
        extra_v[2 * e] = total.astype(BF16)
        vsend_v[2 + e] = vsum
        copy = begin(send(extra_v.at[2 * e], extra_v.at[2 * e + 1], extra_sems, e, cube.over(bit)))
        slot = cube.size + e
        vcopy = begin(send(vsend_v.at[2 + e], vland_v.at[slot], vec_sems, slot, cube.over(bit)))
        copy.wait_recv()
        total = extra_v[2 * e].astype(F32) + extra_v[2 * e + 1].astype(F32)
        vcopy.wait_recv()
        vsum = vsum + vland_v[slot]
    own = chunk(out_v, 0, keep)
    own[...] = total.astype(BF16)
    back = {r: begin(send(own, own, back_sems, r, cube.device(r))) for r in cube.far_first}
    last = {0: begin(send(own, own, last_sems, 0, twin))}
    gvec_out[...] = vsum
    for side, (other, exists) in enumerate(around):
        def settle(side=side, other=other):
            give_back(side, other).wait_send()
            give_back(1 - side, other).wait_recv()
        pl.when(exists)(settle)
    fetch_total.wait()
    low, high = (list_matrix(send_ref, side, nodes) for side in range(2))
    for s in range(samples):
        rows_s = slice(s * nodes, (s + 1) * nodes)
        part = slice(s * halo, (s + 1) * halo)
        node_out[rows_s, :] = (
            total_v[rows_s, :] + dot_nn(low, ret_v[0, part, :]) + dot_nn(high, ret_v[1, part, :])
        ).astype(BF16)
    for r in reversed(cube.far_first):
        back[r].wait_recv()
        part = chunk(out_v, r, keep)
        last[r] = begin(send(part, part, last_sems, r, twin))
    out = pltpu.make_async_copy(
        out_v.at[pl.ds(pl.multiple_of(keep, 16), rows)], grad_out.at[pl.ds(pl.multiple_of(keep, 16), rows)], local_sems.at[0]
    )
    out.start()
    for copy in last.values():
        copy.wait_recv()
    rest = pltpu.make_async_copy(
        out_v.at[pl.ds(pl.multiple_of(give, 16), rows)], grad_out.at[pl.ds(pl.multiple_of(give, 16), rows)], local_sems.at[1]
    )
    rest.start()
    for copy in started:
        copy.wait_send()
    out.wait()
    rest.wait()


def reduce_call(grad, gvec, border, total, send_rows, samples):
    rows, width = grad.shape
    count = lax.axis_size("nodes")
    cube = Cube(count)
    extra = len(cube.extra)
    half, size = rows // 2, rows // 2 // cube.size
    whole, anywhere = pl.BlockSpec(memory_space=pltpu.VMEM), pl.BlockSpec(memory_space=pl.ANY)
    return pl.pallas_call(
        partial(reduce_kernel, samples, count),
        out_shape=(
            jax.ShapeDtypeStruct(grad.shape, BF16),
            jax.ShapeDtypeStruct(gvec.shape, F32),
            jax.ShapeDtypeStruct(total.shape, BF16),
        ),
        in_specs=[anywhere, whole, whole, anywhere, whole],
        out_specs=(anywhere, whole, whole),
        scratch_shapes=[
            pltpu.VMEM((half, width), BF16),
            pltpu.VMEM((half, width), BF16),
            pltpu.VMEM((half, width), BF16),
            pltpu.VMEM((cube.size, size, width), BF16),
            pltpu.VMEM((max(2 * extra, 1), size, width), BF16),
            pltpu.VMEM((rows, width), BF16),
            pltpu.VMEM(total.shape, F32),
            pltpu.VMEM((2 + extra,) + gvec.shape, F32),
            pltpu.VMEM((cube.size + extra,) + gvec.shape, F32),
            pltpu.VMEM(border.shape, BF16),
            pltpu.SemaphoreType.DMA((2, cube.size)),
            pltpu.SemaphoreType.DMA((2, cube.size)),
            pltpu.SemaphoreType.DMA((2, max(extra, 1))),
            pltpu.SemaphoreType.DMA((2, cube.size)),
            pltpu.SemaphoreType.DMA((2, cube.size)),
            pltpu.SemaphoreType.DMA((2, cube.size + extra)),
            pltpu.SemaphoreType.DMA((2, 2)),
            pltpu.SemaphoreType.DMA((2,)),
        ],
        compiler_params=pltpu.CompilerParams(
            collective_id=1, has_side_effects=True, vmem_limit_bytes=VMEM_LIMIT
        ),
        name="reduce",
    )(grad, gvec, border, total, send_rows)


def finish_kernel(half_ref, stat_ref, bases_ref, bases_out, rows_out, work_v, rows_v, sems, out_sem):
    fs, node = lax.axis_index("fs"), lax.axis_index("nodes")
    shard = half_ref.shape[0]
    width = stat_ref.shape[-1]
    gather = Gather(rows_v, sems, shard, fs, node)
    rows_v[pl.ds(pl.multiple_of(fs * shard, 16), shard), :] = half_ref[...]
    greet([(gather.next, None), (gather.far, None)])
    gather.start()
    prepare_bases(stat_ref, bases_ref, work_v, width)
    bases_out[...] = jnp.zeros_like(bases_out)
    orthogonalize(work_v, bases_out, width, gather.forward)
    gather.finish()
    out = pltpu.make_async_copy(rows_v, rows_out, out_sem)
    out.start()
    out.wait()


def finish_call(half, stat, bases):
    shard, width = half.shape
    whole, anywhere = pl.BlockSpec(memory_space=pltpu.VMEM), pl.BlockSpec(memory_space=pl.ANY)
    total = lax.axis_size("fs") * shard
    return pl.pallas_call(
        finish_kernel,
        out_shape=(jax.ShapeDtypeStruct(stat.shape, F32), jax.ShapeDtypeStruct((total, width), BF16)),
        in_specs=[whole] * 3,
        out_specs=(whole, anywhere),
        scratch_shapes=[
            pltpu.VMEM((COUNT, 2 * width, width), F32),
            pltpu.VMEM((total, width), BF16),
            pltpu.SemaphoreType.DMA((2, 3 * Gather.PARTS)),
            pltpu.SemaphoreType.DMA,
        ],
        compiler_params=pltpu.CompilerParams(
            collective_id=2, has_side_effects=True, vmem_limit_bytes=VMEM_LIMIT
        ),
        name="finish",
    )(half, stat, bases)


def on_device(
    edge_latent, node_latent, edge_cot, node_cot, five_flag, senders, send_rows, kernels, kernel_first, kernel_second,
    vectors, vector_first, vector_second, statistics, bases,
):
    samples, nodes, width = node_latent.shape
    slots = senders.shape[0] // nodes
    halo = send_rows.shape[1]
    z = Sizes(samples, nodes, slots, halo, width)
    weights, around = fetch_call(kernels, node_latent.reshape(-1, width), send_rows, samples)
    edge_out, edge_grad, node_out, node_total, border, grad, gvec = main_call(
        z,
        edge_latent.reshape(-1, width),
        edge_cot.reshape(-1, width),
        node_latent.reshape(-1, width),
        node_cot.reshape(-1, width),
        five_flag.reshape(1, -1),
        senders.reshape(1, -1),
        weights,
        around,
        vectors,
    )
    grad, gvec, node_grad = reduce_call(grad, gvec, border, node_total, send_rows, samples)
    kernel_new, first_new, second_new, half, vec_new, vfirst_new, vsecond_new, stat_new = adam_call(
        grad, gvec, kernels, kernel_first, kernel_second, vectors, vector_first, vector_second, statistics, bases
    )
    bases_new, weights_half = finish_call(half, stat_new, bases)
    return (
        edge_out.reshape(edge_latent.shape),
        node_out.reshape(node_latent.shape),
        edge_grad.reshape(edge_latent.shape),
        node_grad.reshape(node_latent.shape),
        kernel_new, first_new, second_new, vec_new, vfirst_new, vsecond_new, stat_new, bases_new, weights_half,
    )


def solution(mesh):
    in_specs = (
        P("fs", "nodes", None),
        P("fs", "nodes", None),
        P("fs", "nodes", None),
        P("fs", "nodes", None),
        P("nodes"),
        P("nodes"),
        P("nodes", None),
        P("fs", None),
        P("fs", None),
        P("fs", None),
        P(),
        P(),
        P(),
        P(),
        P(),
    )
    out_specs = (
        P("fs", "nodes", None),
        P("fs", "nodes", None),
        P("fs", "nodes", None),
        P("fs", "nodes", None),
        P("fs", None),
        P("fs", None),
        P("fs", None),
        P(),
        P(),
        P(),
        P(),
        P(),
        P(),
    )
    return jax.shard_map(
        on_device, mesh=mesh, in_specs=in_specs, out_specs=out_specs, check_vma=False
    )
```

```python
from functools import partial

import jax
import jax.numpy as jnp
from jax import lax
from jax.experimental import pallas as pl
from jax.experimental.pallas import tpu as pltpu
from jax.sharding import PartitionSpec as P

STEP = 5

NORM_EPS = 1e-05
BETA_ONE = 0.5
BETA_TWO = 0.5
RATE_MATRIX = 0.05
RATE_VECTOR = 0.2
DECAY_RATE = 0.01
ADAM_EPS = 1e-08
HIGH = lax.Precision.HIGHEST
F32 = jnp.float32
BF16 = jnp.bfloat16
LANES = 128
VMEM_LIMIT = 56 * 1024 * 1024


def dot_nn(left, right):
    return lax.dot_general(left, right, (((1,), (0,)), ((), ())), preferred_element_type=F32)


def dot_nt(left, right):
    return lax.dot_general(left, right, (((1,), (1,)), ((), ())), preferred_element_type=F32)


def dot_tn(left, right):
    return lax.dot_general(left, right, (((0,), (0,)), ((), ())), preferred_element_type=F32)


def split(value):
    high = value.astype(BF16)
    return high, (value - high.astype(F32)).astype(BF16)


def iota(shape, dim):
    return lax.broadcasted_iota(jnp.int32, shape, dim)


def ones_where(mask):
    return jnp.where(mask, 1.0, 0.0).astype(BF16)


def fold_rows(value):
    rows, width = value.shape
    return jnp.sum(value.reshape(rows // 8, 8, width), 0)


def aligned(index, step):
    return pl.ds(pl.multiple_of(index * step, step), step)


class Sizes:
    def __init__(self, samples, nodes, slots, halo, width):
        self.samples, self.nodes, self.slots = samples, nodes, slots
        self.halo, self.width = halo, width
        self.edges = nodes * slots
        self.fwd_nodes, self.bwd_nodes = 64, 128
        self.fwd_rows = self.fwd_nodes * slots
        self.bwd_rows = self.bwd_nodes * slots
        self.fwd_chunks = nodes // self.fwd_nodes
        self.bwd_chunks = nodes // self.bwd_nodes


def main_scratch(z, shard):
    rows, width = z.samples * z.edges, z.width
    per_node = z.samples * z.nodes
    per_halo = z.samples * 2 * z.halo
    return dict(
        edge_v=pltpu.VMEM((rows, width), BF16),
        cot_v=pltpu.VMEM((rows, width), BF16),
        edge_out_v=pltpu.VMEM((rows, width), BF16),
        act_v=pltpu.VMEM((rows, width), BF16),
        slope_v=pltpu.VMEM((rows, width), F32),
        norm_v=pltpu.VMEM((rows, width), BF16),
        inv_v=pltpu.VMEM((rows, LANES), F32),
        own_v=pltpu.VMEM((z.edges, z.nodes), BF16),
        own_t=pltpu.VMEM((z.nodes, z.edges), BF16),
        halo_t=pltpu.VMEM((2 * z.halo, z.edges), BF16),
        sel_v=pltpu.VMEM((z.edges, 2 * LANES), BF16),
        rep_v=pltpu.VMEM((z.bwd_rows, 2 * LANES), BF16),
        rep_t=pltpu.VMEM((LANES, z.bwd_rows), BF16),
        live_v=pltpu.VMEM((z.edges, LANES), F32),
        half_v=pltpu.VMEM((7 * width, width), BF16),
        pown_v=pltpu.VMEM((z.samples * 2 * z.nodes, width), BF16),
        psel_v=pltpu.VMEM((z.samples * z.fwd_chunks * 2 * LANES, width), BF16),
        gath_v=pltpu.VMEM((per_node, width), BF16),
        drep_v=pltpu.VMEM((z.samples * z.bwd_chunks * 2 * LANES, width), BF16),
        recv_v=pltpu.VMEM((per_node, width), F32),
        aown_v=pltpu.VMEM((per_node, width), F32),
        ahalo_v=pltpu.VMEM((per_halo, width), F32),
        table_v=pltpu.VMEM((per_halo, width), BF16),
        gmat_v=pltpu.VMEM((7 * width, width), F32),
        vsum_v=pltpu.VMEM((6 * 8, width), F32),
        pre_v=pltpu.VMEM((2, z.fwd_rows, width), F32),
        raw_v=pltpu.VMEM((2, z.fwd_rows, width), F32),
        upd_v=pltpu.VMEM((2, z.fwd_rows, width), BF16),
        dout_v=pltpu.VMEM((2, z.bwd_rows, width), BF16),
        dpre_v=pltpu.VMEM((2, z.bwd_rows, width), BF16),
        ncot_v=pltpu.VMEM((per_node, width), BF16),
        total_v=pltpu.VMEM((per_node, width), F32),
        rows_v=pltpu.VMEM((7 * width, width), BF16),
        first_v=pltpu.VMEM((7 * width, width), BF16),
        second_v=pltpu.VMEM((7 * width, width), BF16),
        mom_v=pltpu.VMEM((2, shard, width), F32),
        list_v=pltpu.VMEM((2, z.samples * z.halo, width), BF16),
        halo_v=pltpu.VMEM((2, z.samples * z.halo, width), BF16),
        border_v=pltpu.VMEM((2, z.samples * z.halo, width), BF16),
        ret_v=pltpu.VMEM((2, z.samples * z.halo, width), BF16),
        gout_v=pltpu.VMEM((7 * width, width), BF16),
        edge_sem=pltpu.SemaphoreType.DMA((z.samples,)),
        cot_sem=pltpu.SemaphoreType.DMA((z.samples,)),
        eout_sem=pltpu.SemaphoreType.DMA((z.samples,)),
        egrad_sem=pltpu.SemaphoreType.DMA((z.samples,)),
        local_sem=pltpu.SemaphoreType.DMA((8,)),
        rows_sem=pltpu.SemaphoreType.DMA((2, 12)),
        first_sem=pltpu.SemaphoreType.DMA((2, 3)),
        second_sem=pltpu.SemaphoreType.DMA((2, 3)),
        halo_sem=pltpu.SemaphoreType.DMA((2, 2)),
        ret_sem=pltpu.SemaphoreType.DMA((2, 2)),
    )


def build_selectors(z, m, five_ref, send_ref):
    halo, nodes, slots = z.halo, z.nodes, z.slots
    lane = iota((LANES, LANES), 1)
    row = iota((LANES, LANES), 0)
    for g in range(z.edges // LANES):
        rows = slice(g * LANES, (g + 1) * LANES)
        line = jnp.broadcast_to(send_ref[:, rows].astype(F32), (LANES, LANES))
        column = line.T.astype(jnp.int32)
        for h in range(nodes // LANES):
            m.own_v[rows, h * LANES : (h + 1) * LANES] = ones_where(column == lane + (halo + h * LANES))
        place = jnp.where(column < halo, column, jnp.where(column >= halo + nodes, column - nodes, -1))
        in_halo = (place == (lane & (2 * halo - 1))) & (lane < 4 * halo)
        first = slots * (lane & (z.fwd_nodes - 1))
        local = row + (g * LANES) % z.fwd_rows
        m.sel_v[rows, 0:LANES] = ones_where((first <= local) & (local < first + slots))
        m.sel_v[rows, LANES : 2 * LANES] = ones_where(in_halo)
    senders = jnp.broadcast_to(send_ref[...], (8, z.edges))
    for i in range(nodes // 16):
        node = iota((16, z.edges), 0) + (halo + i * 16)
        m.own_t[i * 16 : (i + 1) * 16, :] = ones_where(jnp.broadcast_to(senders[0:1], (16, z.edges)) == node)
    wide = jnp.broadcast_to(senders[0:1], (2 * halo, z.edges))
    node = iota((2 * halo, z.edges), 0)
    node = jnp.where(node < halo, node, node + nodes)
    m.halo_t[...] = ones_where(wide == node)
    first = slots * (iota((z.bwd_rows, 2 * LANES), 1) & (LANES - 1))
    local = iota((z.bwd_rows, 2 * LANES), 0)
    rep = ones_where((first <= local) & (local < first + slots))
    m.rep_v[...] = rep
    first = slots * iota((LANES, z.bwd_rows), 0)
    local = iota((LANES, z.bwd_rows), 1)
    m.rep_t[...] = ones_where((first <= local) & (local < first + slots))
    local = iota((z.bwd_rows, LANES), 0).astype(F32)
    slot = local - slots * jnp.floor((local + 0.5) * (1.0 / slots))
    for h in range(nodes // LANES):
        five = jnp.broadcast_to(five_ref[:, h * LANES : (h + 1) * LANES].astype(F32), (LANES, LANES)).T
        spread = dot_nn(rep[:, :LANES], five.astype(BF16))
        m.live_v[h * z.bwd_rows : (h + 1) * z.bwd_rows, :] = jnp.where(slot < slots - spread, 1.0, 0.0)


def both(column):
    return jnp.concatenate([column, column], 1)


def row_mean(value):
    return jnp.sum(value, -1, keepdims=True) * (1.0 / value.shape[-1])


def centred(value):
    centre = value - row_mean(value)
    return centre, lax.rsqrt(row_mean(centre * centre) + NORM_EPS)


def act_and_slope(half):
    turn = jnp.tanh(half)
    above = 1.0 + turn
    act = half * above
    return act, above + act * (1.0 - turn)


MESH = pl.DeviceIdType.MESH


def greet(partners):
    barrier = pltpu.get_barrier_semaphore()
    count = 0
    for device, exists in partners:
        if exists is None:
            pl.semaphore_signal(barrier, inc=1, device_id=device, device_id_type=MESH)
            count = count + 1
        else:
            pl.when(exists)(partial(pl.semaphore_signal, barrier, inc=1, device_id=device, device_id_type=MESH))
            count = count + exists.astype(jnp.int32)
    pl.semaphore_wait(barrier, count)


def send(source, target, sems, slot, device):
    return pltpu.make_async_remote_copy(
        src_ref=source, dst_ref=target, send_sem=sems.at[0, slot], recv_sem=sems.at[1, slot],
        device_id=device, device_id_type=MESH,
    )


class Gather:
    def __init__(self, rows_v, sems, shard, fs, node):
        self.rows_v, self.sems, self.shard, self.fs = rows_v, sems, shard, fs
        self.parts = sems.shape[1] // 3
        self.next, self.far = (fs ^ 1, node), (fs ^ 2, node)

    def piece(self, owner, part):
        size = self.shard // self.parts
        return self.rows_v.at[pl.ds(pl.multiple_of(owner * self.shard + part * size, 16), size)]

    def copy(self, owner, part, slot, device):
        return send(self.piece(owner, part), self.piece(owner, part), self.sems, slot * self.parts + part, device)

    def start(self):
        for part in range(self.parts):
            self.copy(self.fs, part, 0, self.far).start()
        for part in range(self.parts):
            self.copy(self.fs, part, 1, self.next).start()

    def forward(self):
        for part in range(self.parts):
            self.copy(self.fs, part, 0, self.far).wait_recv()
            self.copy(self.fs ^ 2, part, 2, self.next).start()

    def finish(self):
        for part in range(self.parts):
            self.copy(self.fs, part, 0, self.far).wait_send()
            self.copy(self.fs, part, 1, self.next).wait()
            self.copy(self.fs ^ 2, part, 2, self.next).wait()


def list_matrix(send_ref, side, nodes):
    halo = send_ref.shape[1]
    listed = jnp.broadcast_to(send_ref[side : side + 1, :], (nodes, halo))
    return ones_where(listed == iota((nodes, halo), 0))


def sides(node, count):
    return ((node - 1, node > 0), (node + 1, node < count - 1))


class Cube:
    def __init__(self, count, fs=None, node=None):
        bits = count.bit_length() - 1
        self.node_bits = min(2, bits)
        self.size = 2 << self.node_bits
        self.extra = list(range(self.node_bits, bits))
        self.fs, self.node = fs, node
        if fs is not None:
            self.me = (fs >> 1) + 2 * (node & ((1 << self.node_bits) - 1))
        self.far_first = sorted(range(1, self.size), key=lambda r: (-r.bit_count(), -r))

    def device(self, r):
        return self.fs ^ (2 * (r & 1)), self.node ^ (r >> 1)

    def over(self, bit):
        return self.fs, self.node ^ (1 << bit)


def tree_sum(parts):
    while len(parts) > 1:
        parts = [left + right for left, right in zip(parts[::2], parts[1::2], strict=True)]
    return parts[0]


class Reduce:
    def __init__(self, cube, first, rows, sum_v, out_v, buffers):
        self.cube, self.sum_v, self.out_v = cube, sum_v, out_v
        self.give_v, self.land_v, self.near_v, self.cube_v, self.acc_v, self.extra_v, self.sems = buffers
        self.half = rows // 2
        self.size = self.half // cube.size
        core = cube.fs & 1
        self.keep, self.give = first + core * self.half, first + (1 - core) * self.half
        self.twin = (cube.fs ^ 1, cube.node)
        self.order = cube.far_first + [0]
        self.started = []

    @staticmethod
    def scratch(cube, rows, width):
        half, extra = rows // 2, max(2 * len(cube.extra), 1)
        size = half // cube.size
        return [
            pltpu.VMEM((half, width), BF16),
            pltpu.VMEM((half, width), BF16),
            pltpu.VMEM((half, width), BF16),
            pltpu.VMEM((cube.size, size, width), BF16),
            pltpu.VMEM((size, width), F32),
            pltpu.VMEM((extra, size, width), BF16),
            pltpu.SemaphoreType.DMA((2, 4 * cube.size + extra)),
        ]

    def rows(self, r, base=0):
        return pl.ds(pl.multiple_of(base + (self.cube.me ^ r) * self.size, 16), self.size)

    def launch(self, source, target, slot, device):
        copy = send(source, target, self.sems, slot, device)
        copy.start()
        self.started.append(copy)
        return copy

    def begin(self):
        self.core = {}
        for r in self.order:
            part = self.give_v.at[self.rows(r)]
            part[...] = self.sum_v[self.rows(r, self.give), :].astype(BF16)
            self.core[r] = self.launch(part, self.land_v.at[self.rows(r)], r, self.twin)

    def spread(self):
        self.near = {}
        for r in self.order:
            self.core[r].wait_recv()
            total = self.sum_v[self.rows(r, self.keep), :] + self.land_v[self.rows(r), :].astype(F32)
            if r:
                part = self.near_v.at[self.rows(r)]
                part[...] = total.astype(BF16)
                self.near[r] = self.launch(part, self.cube_v.at[r], self.cube.size + r, self.cube.device(r))
            else:
                self.acc_v[...] = total

    def meet(self):
        total = self.acc_v[...]
        for r in reversed(self.cube.far_first):
            self.near[r].wait_recv()
            total = total + self.cube_v[r].astype(F32)
        self.far = None
        if self.cube.extra:
            self.exchange(total, 0)
        else:
            self.acc_v[...] = total

    def exchange(self, total, e):
        self.extra_v[2 * e] = total.astype(BF16)
        self.far = self.launch(
            self.extra_v.at[2 * e], self.extra_v.at[2 * e + 1], 4 * self.cube.size + e, self.cube.over(self.cube.extra[e])
        )

    def settle(self):
        total = self.acc_v[...]
        for e in range(len(self.cube.extra)):
            self.far.wait_recv()
            total = self.extra_v[2 * e].astype(F32) + self.extra_v[2 * e + 1].astype(F32)
            if e + 1 < len(self.cube.extra):
                self.exchange(total, e + 1)
        own = self.out_v.at[self.rows(0, self.keep)]
        own[...] = total.astype(BF16)
        size = self.cube.size
        self.back = {r: self.launch(own, own, 2 * size + r, self.cube.device(r)) for r in self.cube.far_first}
        self.last = [self.launch(own, own, 3 * size, self.twin)]

    def forward(self):
        for r in reversed(self.cube.far_first):
            self.back[r].wait_recv()
            part = self.out_v.at[self.rows(r, self.keep)]
            self.last.append(self.launch(part, part, 3 * self.cube.size + r, self.twin))

    def end(self):
        for copy in self.last:
            copy.wait_recv()
        for copy in self.started:
            copy.wait_send()


class VectorSum:
    def __init__(self, cube, send_v, land_v, sems):
        self.cube, self.send_v, self.land_v, self.sems = cube, send_v, land_v, sems
        self.started = []

    @staticmethod
    def scratch(cube, shape):
        extra = len(cube.extra)
        return [
            pltpu.VMEM((2 + extra,) + shape, F32),
            pltpu.VMEM((cube.size + extra,) + shape, F32),
            pltpu.SemaphoreType.DMA((2, cube.size + extra)),
        ]

    def launch(self, source, slot, device):
        copy = send(self.send_v.at[source], self.land_v.at[slot], self.sems, slot, device)
        copy.start()
        self.started.append(copy)
        return copy

    def begin(self, value):
        self.send_v[0] = value
        self.core = self.launch(0, 0, (self.cube.fs ^ 1, self.cube.node))

    def spread(self):
        self.core.wait_recv()
        self.send_v[1] = self.send_v[0] + self.land_v[0]
        self.near = [self.launch(1, r, self.cube.device(r)) for r in range(1, self.cube.size)]

    def meet(self):
        for copy in self.near:
            copy.wait_recv()
        self.total = tree_sum([self.send_v[1]] + [self.land_v[r] for r in range(1, self.cube.size)])
        self.far = self.exchange(0) if self.cube.extra else None

    def exchange(self, e):
        self.send_v[2 + e] = self.total
        return self.launch(2 + e, self.cube.size + e, self.cube.over(self.cube.extra[e]))

    def settle(self):
        for e in range(len(self.cube.extra)):
            self.far.wait_recv()
            self.total = self.total + self.land_v[self.cube.size + e]
            if e + 1 < len(self.cube.extra):
                self.far = self.exchange(e + 1)
        return self.total

    def end(self):
        for copy in self.started:
            copy.wait_send()


def round_kernel(
    z, names, count, edge_ref, cot_ref, node_ref, ncot_ref, five_ref, send_ref, list_ref, kern_ref, kfirst_ref, ksecond_ref,
    vec_ref, eout_ref, egrad_ref, nout_ref, ngrad_ref, grad_ref, gvec_ref, rows_ref, first_ref, second_ref, *scratch,
):
    m = type("Held", (), {})()
    for name, ref in zip(names, scratch[: len(names)], strict=True):
        setattr(m, name, ref)
    spare = scratch[len(names) :]
    fs, node_id = lax.axis_index("fs"), lax.axis_index("nodes")
    cube = Cube(count, fs, node_id)
    around = sides(node_id, count)
    shard = kern_ref.shape[0]
    width, nodes, edges, samples, halo = z.width, z.nodes, z.edges, z.samples, z.halo
    two_halo = 2 * halo

    def sample_copy(source, target, sem, s):
        rows = aligned(s, edges)
        return pltpu.make_async_copy(source.at[rows], target.at[rows], sem.at[s])

    locals_in = [
        pltpu.make_async_copy(source, target, m.local_sem.at[i])
        for i, (source, target) in enumerate(
            [(ncot_ref, m.ncot_v), (kfirst_ref, m.mom_v.at[0]), (ksecond_ref, m.mom_v.at[1])]
        )
    ]
    weight_ref = m.rows_v
    mine = pl.ds(pl.multiple_of(fs * shard, 16), shard)
    weight_ref[mine, :] = kern_ref[...].astype(BF16)
    m.halo_v[...] = jnp.zeros_like(m.halo_v)
    m.ret_v[...] = jnp.zeros_like(m.ret_v)
    gather = Gather(weight_ref, m.rows_sem, shard, fs, node_id)
    moments = [Gather(m.first_v, m.first_sem, shard, fs, node_id), Gather(m.second_v, m.second_sem, shard, fs, node_id)]
    greet(
        [(gather.next, None)]
        + [(cube.device(r), None) for r in range(1, cube.size)]
        + [(cube.over(bit), None) for bit in cube.extra]
        + [((fs, other), exists) for other, exists in around]
    )
    gather.start()
    for copy in locals_in:
        copy.start()
    for s in range(samples):
        sample_copy(edge_ref, m.edge_v, m.edge_sem, s).start()
    for s in range(samples):
        sample_copy(cot_ref, m.cot_v, m.cot_sem, s).start()

    def to_side(source, target, sems, side, other):
        return send(source.at[side], target.at[1 - side], sems, side, (fs, other))

    def start_sides(source, target, sems):
        for side, (other, exists) in enumerate(around):
            pl.when(exists)(lambda side=side, other=other: to_side(source, target, sems, side, other).start())

    def finish_sides(source, target, sems):
        for side, (other, exists) in enumerate(around):
            def settle(side=side, other=other):
                to_side(source, target, sems, side, other).wait_send()
                to_side(source, target, sems, 1 - side, other).wait_recv()
            pl.when(exists)(settle)

    for side in range(2):
        chosen = list_matrix(list_ref, side, nodes)
        for s in range(samples):
            m.list_v[side, s * halo : (s + 1) * halo, :] = dot_tn(
                chosen, node_ref[s * nodes : (s + 1) * nodes, :]
            ).astype(BF16)
    start_sides(m.list_v, m.halo_v, m.halo_sem)
    build_selectors(z, m, five_ref, send_ref)
    gather.forward()
    gather.finish()
    finish_sides(m.list_v, m.halo_v, m.halo_sem)
    rows_out = pltpu.make_async_copy(weight_ref, rows_ref, m.local_sem.at[3])
    rows_out.start()
    for copy in locals_in:
        copy.wait()
    for k, (moment, held) in enumerate(zip(moments, (m.first_v, m.second_v), strict=True)):
        held[mine, :] = m.mom_v[k].astype(BF16)
        moment.start()
    m.half_v[...] = weight_ref[...] * jnp.asarray(0.5, BF16)
    m.gmat_v[...] = jnp.zeros_like(m.gmat_v)
    m.vsum_v[...] = jnp.zeros_like(m.vsum_v)
    m.aown_v[...] = jnp.zeros_like(m.aown_v)
    m.ahalo_v[...] = jnp.zeros_like(m.ahalo_v)
    for s in range(samples):
        for side in range(2):
            m.table_v[s * two_halo + side * halo : s * two_halo + (side + 1) * halo, :] = m.halo_v[
                side, s * halo : (s + 1) * halo, :
            ]

    send_half = m.half_v[width : 2 * width, :]
    recv_half = m.half_v[2 * width : 3 * width, :]
    bias_edge, gain_edge, shift_edge = vec_ref[0:1, :] * 0.5, vec_ref[1:2, :], vec_ref[2:3, :]
    bias_node, gain_node, shift_node = vec_ref[3:4, :] * 0.5, vec_ref[4:5, :], vec_ref[5:6, :]

    for s in range(samples):
        node = node_ref[s * nodes : (s + 1) * nodes, :]
        high, low = split(dot_nn(node, send_half))
        m.pown_v[s * 2 * nodes : (s * 2 + 1) * nodes, :] = high
        m.pown_v[(s * 2 + 1) * nodes : (s * 2 + 2) * nodes, :] = low
        high, low = split(dot_nn(node, recv_half) + bias_edge)
        out_high, out_low = split(dot_nn(m.table_v[s * two_halo : (s + 1) * two_halo, :], send_half))
        zero = jnp.zeros((2 * LANES - 2 * z.fwd_nodes - 2 * two_halo, width), BF16)
        for c in range(z.fwd_chunks):
            own = slice(c * z.fwd_nodes, (c + 1) * z.fwd_nodes)
            base = (s * z.fwd_chunks + c) * 2 * LANES
            m.psel_v[base : base + 2 * LANES, :] = jnp.concatenate(
                [high[own], low[own], out_high, out_low, zero], 0
            )

    per = z.fwd_chunks
    last = samples * per - 1

    def join_edges(i, slot):
        s, c = i // per, i % per
        local = aligned(c, z.fwd_rows)
        own = m.own_v[local, :]
        left = jnp.concatenate([m.edge_v[aligned(i, z.fwd_rows), :], own, own, m.sel_v[local, :]], 1)
        right = jnp.concatenate(
            [m.half_v[0:width, :], m.pown_v[aligned(s, 2 * nodes), :], m.psel_v[aligned(i, 2 * LANES), :]], 0
        )
        m.pre_v[slot] = dot_nn(left, right)

    def activate(i, slot):
        rows = aligned(i, z.fwd_rows)
        act, slope = act_and_slope(m.pre_v[slot])
        act = act.astype(BF16)
        m.act_v[rows, :] = act
        m.slope_v[rows, :] = slope
        m.raw_v[slot] = dot_nn(act, weight_ref[3 * width : 4 * width, :])

    def update_edges(i, slot):
        rows, local = aligned(i, z.fwd_rows), aligned(i % per, z.fwd_rows)
        centre, inv = centred(m.raw_v[slot])
        live = m.live_v[local, :]
        inv = inv * live
        m.inv_v[rows, :] = inv
        normed = centre * both(inv)
        m.norm_v[rows, :] = normed.astype(BF16)
        update = normed * gain_edge + both(live) * shift_edge
        m.edge_out_v[rows, :] = (m.edge_v[rows, :].astype(F32) + update).astype(BF16)
        m.upd_v[slot] = update.astype(BF16)

    def gather_updates(i, slot):
        gathered = dot_nn(m.rep_t[0 : z.fwd_nodes, 0 : z.fwd_rows], m.upd_v[slot])
        m.gath_v[aligned(i, z.fwd_nodes), :] = gathered.astype(BF16)

    def edge_in(s):
        return sample_copy(edge_ref, m.edge_v, m.edge_sem, s)

    edge_in(0).wait()
    join_edges(0, 0)

    def forward(s, carry):
        pl.when(s < samples - 1)(lambda: edge_in(s + 1).wait())
        for c in range(per):
            i = s * per + c
            join_edges(jnp.minimum(i + 1, last), (c + 1) % 2)
            gather_updates(jnp.maximum(i - 2, 0), c % 2)
            activate(i, c % 2)
            update_edges(jnp.maximum(i - 1, 0), (c + 1) % 2)
        pl.when(s > 0)(lambda: sample_copy(m.edge_out_v, eout_ref, m.eout_sem, s - 1).start())
        return carry

    lax.fori_loop(0, samples, forward, 0)
    gather_updates(last - 1, 0)
    update_edges(last, 1)
    gather_updates(last, 1)
    sample_copy(m.edge_out_v, eout_ref, m.eout_sem, samples - 1).start()

    def node_part(i, carry):
        rows = aligned(i, 2 * nodes)
        node, gath = node_ref[rows, :], m.gath_v[rows, :]
        joined = jnp.concatenate([node, gath], 1)
        act, slope = act_and_slope(dot_nn(joined, m.half_v[4 * width : 6 * width, :]) + bias_node)
        act = act.astype(BF16)
        centre, inv = centred(dot_nn(act, weight_ref[6 * width : 7 * width, :]))
        normed = centre * inv
        nout_ref[rows, :] = (node.astype(F32) + normed * gain_node + shift_node).astype(BF16)
        back = m.ncot_v[rows, :].astype(F32)
        back_normed = back * normed
        scaled, scaled_normed = back * gain_node, back_normed * gain_node
        d_out = (inv * (scaled - row_mean(scaled) - normed * row_mean(scaled_normed))).astype(BF16)
        m.gmat_v[6 * width : 7 * width, :] += dot_tn(act, d_out)
        m.vsum_v[32:40, :] += fold_rows(back_normed)
        m.vsum_v[40:48, :] += fold_rows(back)
        d_pre = dot_nt(d_out, m.half_v[6 * width : 7 * width, :]) * slope
        d_pre = d_pre.astype(BF16)
        m.vsum_v[24:32, :] += fold_rows(d_pre.astype(F32))
        m.gmat_v[4 * width : 6 * width, :] += dot_tn(joined, d_pre)
        d_joined = dot_nt(d_pre, weight_ref[4 * width : 6 * width, :])
        m.total_v[rows, :] = back + d_joined[:, :width]
        high, low = split(d_joined[:, width:])
        for k in range(2):
            for c in range(z.bwd_chunks):
                own = slice(k * nodes + c * z.bwd_nodes, k * nodes + (c + 1) * z.bwd_nodes)
                m.drep_v[aligned((i * 2 + k) * z.bwd_chunks + c, 2 * LANES), :] = jnp.concatenate(
                    [high[own], low[own]], 0
                )
        return carry

    lax.fori_loop(0, samples // 2, node_part, 0)

    halves = z.bwd_rows // z.fwd_rows
    pairs = samples * z.bwd_chunks

    def spread_back(i, slot):
        half = slice((slot % halves) * z.fwd_rows, (slot % halves + 1) * z.fwd_rows)
        m.pre_v[slot] = dot_nn(m.rep_v[half, :], m.drep_v[aligned(i // halves, 2 * LANES), :])

    def norm_back(i, slot, pair):
        rows, local = aligned(i, z.fwd_rows), aligned(i % per, z.fwd_rows)
        d_update = (m.cot_v[rows, :].astype(F32) + m.pre_v[slot]) * both(m.live_v[local, :])
        normed = m.norm_v[rows, :].astype(F32)
        d_normed = d_update * normed
        m.vsum_v[8:16, :] += fold_rows(d_normed)
        m.vsum_v[16:24, :] += fold_rows(d_update)
        scaled, scaled_normed = d_update * gain_edge, d_normed * gain_edge
        d_out = both(m.inv_v[rows, :]) * (scaled - row_mean(scaled) - normed * row_mean(scaled_normed))
        m.dout_v[pair, slot * z.fwd_rows : (slot + 1) * z.fwd_rows, :] = d_out.astype(BF16)

    def activate_back(i, slot, pair):
        part = slice(slot * z.fwd_rows, (slot + 1) * z.fwd_rows)
        d_act = dot_nt(m.dout_v[pair, part, :], m.half_v[3 * width : 4 * width, :])
        m.dpre_v[pair, part, :] = (d_act * m.slope_v[aligned(i, z.fwd_rows), :]).astype(BF16)

    def weights_back(p, pair):
        s, c = p // z.bwd_chunks, p % z.bwd_chunks
        rows, local = aligned(p, z.bwd_rows), aligned(c, z.bwd_rows)
        d_out, d_pre = m.dout_v[pair], m.dpre_v[pair]
        m.gmat_v[3 * width : 4 * width, :] += dot_tn(m.act_v[rows, :], d_out)
        m.gmat_v[0:width, :] += dot_tn(m.edge_v[rows, :], d_pre)
        m.recv_v[aligned(p, z.bwd_nodes), :] = dot_nn(m.rep_t[...], d_pre)
        m.aown_v[aligned(s, nodes), :] += dot_nn(m.own_t[:, local], d_pre)
        m.ahalo_v[aligned(s, two_halo), :] += dot_nn(m.halo_t[:, local], d_pre)
        m.edge_out_v[rows, :] = (m.cot_v[rows, :].astype(F32) + dot_nt(d_pre, weight_ref[0:width, :])).astype(BF16)

    for s in range(samples):
        sample_copy(m.edge_out_v, eout_ref, m.eout_sem, s).wait()
    m.dout_v[1] = jnp.zeros_like(m.dout_v[1])
    m.dpre_v[1] = jnp.zeros_like(m.dpre_v[1])
    spread_back(0, 0)

    def backward(s, carry):
        sample_copy(cot_ref, m.cot_v, m.cot_sem, s).wait()
        for k in range(z.bwd_chunks):
            p = s * z.bwd_chunks + k
            i = p * halves
            spread_back(i + 1, 1)
            activate_back(jnp.maximum(i - 1, 0), 1, 1 - k)
            norm_back(i, 0, k)
            weights_back(jnp.maximum(p - 1, 0), 1 - k)
            spread_back(jnp.minimum(i + 2, last), 0)
            activate_back(i, 0, k)
            norm_back(i + 1, 1, k)
        pl.when(s > 0)(lambda: sample_copy(m.edge_out_v, egrad_ref, m.egrad_sem, s - 1).start())
        return carry

    lax.fori_loop(0, samples, backward, 0)
    activate_back(last, 1, 1)
    weights_back(pairs - 1, 1)
    sample_copy(m.edge_out_v, egrad_ref, m.egrad_sem, samples - 1).start()

    send_full = weight_ref[width : 2 * width, :]
    recv_full = weight_ref[2 * width : 3 * width, :]
    table = m.table_v[...]
    out_high, out_low = split(m.ahalo_v[...])
    grad_send = dot_tn(table, out_high) + dot_tn(table, out_low)
    grad_recv = jnp.zeros((width, width), F32)
    for s in range(samples):
        rows = slice(s * nodes, (s + 1) * nodes)
        recv_high, recv_low = split(m.recv_v[rows, :])
        own_high, own_low = split(m.aown_v[rows, :])
        node = node_ref[rows, :]
        grad_recv += dot_tn(node, recv_high) + dot_tn(node, recv_low)
        grad_send += dot_tn(node, own_high) + dot_tn(node, own_low)
    m.gmat_v[width : 2 * width, :] = grad_send
    m.gmat_v[2 * width : 3 * width, :] = grad_recv
    reduce = Reduce(cube, 0, 7 * width, m.gmat_v, m.gout_v, spare[:7])
    vectors = VectorSum(cube, *spare[7:])
    reduce.begin()
    border = (dot_nt(out_high, send_full) + dot_nt(out_low, send_full)).astype(BF16)
    for s in range(samples):
        for side in range(2):
            m.border_v[side, s * halo : (s + 1) * halo, :] = border[
                s * two_halo + side * halo : s * two_halo + (side + 1) * halo, :
            ]
    start_sides(m.border_v, m.ret_v, m.ret_sem)
    for s in range(samples):
        m.vsum_v[0:8, :] += fold_rows(m.recv_v[s * nodes : (s + 1) * nodes, :])
    vectors.begin(
        jnp.concatenate(
            [jnp.sum(m.vsum_v[k * 8 : (k + 1) * 8, :], 0, keepdims=True) for k in range(6)]
            + [jnp.zeros((2, width), F32)],
            0,
        )
    )
    reduce.spread()
    vectors.spread()
    for moment in moments:
        moment.forward()
    for s in range(samples):
        rows = slice(s * nodes, (s + 1) * nodes)
        recv_high, recv_low = split(m.recv_v[rows, :])
        own_high, own_low = split(m.aown_v[rows, :])
        m.total_v[rows, :] += (
            dot_nt(recv_high, recv_full) + dot_nt(recv_low, recv_full)
            + dot_nt(own_high, send_full) + dot_nt(own_low, send_full)
        )
    reduce.meet()
    vectors.meet()
    finish_sides(m.border_v, m.ret_v, m.ret_sem)
    low, high = (list_matrix(list_ref, side, nodes) for side in range(2))
    for s in range(samples):
        rows, part = slice(s * nodes, (s + 1) * nodes), slice(s * halo, (s + 1) * halo)
        ngrad_ref[rows, :] = (
            m.total_v[rows, :] + dot_nn(low, m.ret_v[0, part, :]) + dot_nn(high, m.ret_v[1, part, :])
        ).astype(BF16)
    reduce.settle()
    gvec_ref[...] = vectors.settle()
    for moment in moments:
        moment.finish()
    moments_out = [
        pltpu.make_async_copy(m.first_v, first_ref, m.local_sem.at[4]),
        pltpu.make_async_copy(m.second_v, second_ref, m.local_sem.at[5]),
    ]
    for copy in moments_out:
        copy.start()
    for s in range(samples):
        sample_copy(m.edge_out_v, egrad_ref, m.egrad_sem, s).wait()
    for copy in moments_out + [rows_out]:
        copy.wait()
    reduce.forward()
    reduce.end()
    vectors.end()
    grad_out = pltpu.make_async_copy(m.gout_v, grad_ref, m.local_sem.at[6])
    grad_out.start()
    grad_out.wait()


def round_call(z, count, edge, cot, node, ncot, five, senders, send_rows, kern, kfirst, ksecond, vectors):
    shard, width = kern.shape
    scratch = main_scratch(z, shard)
    cube = Cube(count)
    spare = Reduce.scratch(cube, 7 * width, width) + VectorSum.scratch(cube, (8, width))
    rows, per_node = z.samples * z.edges, z.samples * z.nodes
    whole = pl.BlockSpec(memory_space=pltpu.VMEM)
    anywhere = pl.BlockSpec(memory_space=pl.ANY)
    total = jax.ShapeDtypeStruct((7 * width, width), BF16)
    return pl.pallas_call(
        partial(round_kernel, z, tuple(scratch), count),
        out_shape=(
            jax.ShapeDtypeStruct((rows, width), BF16),
            jax.ShapeDtypeStruct((rows, width), BF16),
            jax.ShapeDtypeStruct((per_node, width), BF16),
            jax.ShapeDtypeStruct((per_node, width), BF16),
            total,
            jax.ShapeDtypeStruct((8, width), F32),
            total, total, total,
        ),
        in_specs=[anywhere, anywhere, whole, anywhere, whole, whole, whole, whole, anywhere, anywhere, whole],
        out_specs=(anywhere, anywhere, whole, whole, anywhere, whole, anywhere, anywhere, anywhere),
        scratch_shapes=list(scratch.values()) + spare,
        compiler_params=pltpu.CompilerParams(
            collective_id=0, has_side_effects=True, vmem_limit_bytes=VMEM_LIMIT
        ),
        name="edge_node_round",
    )(edge, cot, node, ncot, five, senders, send_rows, kern, kfirst, ksecond, vectors)


def dot_exact(left, right, dims):
    return lax.dot_general(left, right, (dims, ((), ())), precision=HIGH, preferred_element_type=F32)


BLOCK = 32
COUNT = 4
HALF = LANES // BLOCK


def wide_left(value):
    high, low = split(value)
    return jnp.concatenate([high, high, low], 1)


def wide_right(value):
    high, low = split(value)
    return jnp.concatenate([high, low, high], 1)


def dot_three(left, right):
    return dot_nt(wide_left(left), wide_right(right))


def factor_block(packed):
    sub = iota((8, LANES), 0)
    lane = iota((8, LANES), 1)
    tiles = BLOCK // 8
    group = lane & (LANES - BLOCK)
    parts = [packed[8 * r : 8 * r + 8, :] for r in range(tiles)]
    columns = [
        [jnp.take_along_axis(parts[r], group + l, axis=1) if r >= l // 8 else None for r in range(tiles)]
        for l in range(BLOCK)
    ]
    inverse = [jnp.where((lane & (BLOCK - 1)) == sub + 8 * r, 1.0, 0.0) for r in range(tiles)]

    def line(tile, s):
        return jnp.broadcast_to(tile[s : s + 1, :], (8, LANES))

    for j in range(BLOCK):
        rj, sj = j // 8, j % 8
        scale = lax.rsqrt(line(columns[j][rj], sj))
        below = [None if r < rj else columns[j][r] * scale for r in range(tiles)]
        below[rj] = jnp.where(sub > sj, below[rj], 0.0)
        for l in range(j + 1, BLOCK):
            weight = line(below[l // 8], l % 8)
            for r in range(l // 8, tiles):
                columns[l][r] = columns[l][r] - below[r] * weight
        row = line(inverse[rj], sj) * scale
        inverse[rj] = jnp.where(sub == sj, row, inverse[rj] - below[rj] * row)
        for r in range(rj + 1, tiles):
            inverse[r] = inverse[r] - below[r] * row
    return jnp.concatenate(inverse, 0)


def turned_blocks(k, width):
    return [h * HALF + (g - k) % HALF for h in range(width // LANES) for g in range(HALF)]


def pick_rows(value, blocks):
    return jnp.concatenate([value[i * BLOCK : (i + 1) * BLOCK, :] for i in blocks], 0)


def orthogonalize(work_v, bases_out, width, beside):
    blocks = width // BLOCK
    group = iota((BLOCK, LANES), 1) // BLOCK
    square = iota((LANES, LANES), 0) // BLOCK == iota((LANES, LANES), 1) // BLOCK

    def placed(values, b):
        return [jnp.where(group == (b + k) % COUNT, values[k], jnp.zeros_like(values[k])) for k in range(COUNT)]

    def lanes_of(b):
        return slice(b // HALF * LANES, (b // HALF + 1) * LANES)

    def rows_of(b):
        return slice(b * BLOCK, (b + 1) * BLOCK)

    packed = sum(placed([work_v[k, rows_of(0), lanes_of(0)] for k in range(COUNT)], 0))
    for b in range(blocks):
        beside(b)
        lanes, after = lanes_of(b), (b + 1) * BLOCK
        high, low = split(factor_block(packed).astype(F32))
        high, low = placed([high] * COUNT, b), placed([low] * COUNT, b)
        if b < blocks - 1:
            spread_high, spread_low = jnp.concatenate(high, 0), jnp.concatenate(low, 0)
            spread = jnp.concatenate([spread_high, spread_low, spread_high], 1)
            ahead = jnp.concatenate([work_v[k, rows_of(b + 1), lanes] for k in range(COUNT)], 0)
            turned = jnp.where(square, dot_nt(wide_left(ahead), spread), 0.0)
            order = [(g - b - 1) % COUNT for g in range(COUNT)]
            update = dot_nt(wide_left(turned), pick_rows(wide_right(turned), order))
            current = placed([work_v[k, rows_of(b + 1), lanes_of(b + 1)] for k in range(COUNT)], b + 1)
            packed = sum(current) - sum(update[rows_of(k), :] for k in range(COUNT))
        start = after // LANES * LANES
        for k in range(COUNT):
            four_high = jnp.concatenate([high[k]] * HALF, 0)
            four_low = jnp.concatenate([low[k]] * HALF, 0)
            below = wide_left(work_v[k, after:, lanes])
            turned = dot_nt(below, jnp.concatenate([four_high, four_low, four_high], 1))
            mine = iota((width, LANES), 1) // BLOCK == b % HALF
            bases_out[k, :, lanes] = jnp.where(mine, turned[width - after :, :], bases_out[k, :, lanes])
            if b == blocks - 1:
                continue
            turned_high, turned_low = split(turned)
            part = iota(turned.shape, 1) // BLOCK
            zero = jnp.zeros_like(turned_high)
            left = jnp.where(part == 2, turned_low, jnp.where(part == 3, zero, turned_high))
            right = jnp.where(part == 1, turned_low, jnp.where(part == 3, zero, turned_high))
            right = jnp.concatenate(
                [
                    right[(i - b - 1) * BLOCK : (i - b) * BLOCK, :] if i > b else zero[0:BLOCK, :]
                    for i in turned_blocks(k, width)[start // BLOCK :]
                ],
                0,
            )
            work_v[k, after:, start:] -= dot_nt(left, right)


def matrix_bounds(width):
    return [0, 3 * width, 4 * width, 6 * width, 7 * width]


def new_statistics(grad_ref, stat_ref, k):
    width = stat_ref.shape[-1]
    bounds = matrix_bounds(width)
    rows = grad_ref[bounds[k] : bounds[k + 1], :]
    return BETA_TWO * stat_ref[k] + (1.0 - BETA_TWO) * dot_tn(rows, rows)


def matrix_of(row, width):
    return sum((row >= bound).astype(jnp.int32) for bound in matrix_bounds(width)[1:-1])


def prepare_bases(stat_ref, bases_ref, work_v, width):
    for k in range(COUNT):
        order = turned_blocks(k, width)
        stat = stat_ref[k]
        flipped = bases_ref[k].T
        proj_rows = dot_three(flipped, stat)
        work_v[k, 0:width, :] = dot_three(proj_rows, pick_rows(proj_rows, order))
        work_v[k, width:, :] = dot_three(stat, pick_rows(flipped, order))


def adam_step(first, second, rotated):
    first = BETA_ONE * first + (1.0 - BETA_ONE) * rotated
    second = BETA_TWO * second + (1.0 - BETA_TWO) * rotated * rotated
    step = first / (1.0 - BETA_ONE**STEP) / (jnp.sqrt(second / (1.0 - BETA_TWO**STEP)) + ADAM_EPS)
    return first, second, step


def turn(rows, basis):
    high, low = split(basis)
    return dot_nn(rows, high) + dot_nn(rows, low)


def decayed(kern, turned):
    return kern - RATE_MATRIX * (turned + DECAY_RATE * kern)


def update_kernel(
    grad_ref, stat_ref, bases_ref, kern_ref, kfirst_ref, ksecond_ref, rows_ref, first_ref, second_ref,
    gvec_ref, vec_ref, vfirst_ref, vsecond_ref, eout_ref, egrad_ref, nout_ref, ngrad_ref,
    eout_out, egrad_out, nout_out, ngrad_out, kern_out, kfirst_out, ksecond_out, vec_out, vfirst_out, vsecond_out,
    stat_out, bases_out, half_out,
    grad_v, stat_v, bases_v, kern_v, kfirst_v, ksecond_v, rows_v, first_v, second_v,
    work_v, kern_new, kfirst_new, ksecond_new, stat_new, bases_new, half_v, eout_v, egrad_v, nout_v, ngrad_v, in_sem, out_sem, pass_sem,
):
    shard, width = kern_v.shape
    copies = [
        pltpu.make_async_copy(source, target, in_sem.at[i])
        for i, (source, target) in enumerate(
            [
                (bases_ref, bases_v), (stat_ref, stat_v), (grad_ref, grad_v), (kern_ref, kern_v), (kfirst_ref, kfirst_v),
                (ksecond_ref, ksecond_v), (rows_ref, rows_v), (first_ref, first_v), (second_ref, second_v),
            ]
        )
    ]
    passed = [
        (pltpu.make_async_copy(source, held, pass_sem.at[0, i]), pltpu.make_async_copy(held, target, pass_sem.at[1, i]))
        for i, (source, held, target) in enumerate(
            [
                (eout_ref, eout_v, eout_out), (egrad_ref, egrad_v, egrad_out),
                (nout_ref, nout_v, nout_out), (ngrad_ref, ngrad_v, ngrad_out),
            ]
        )
    ]
    outs = [
        pltpu.make_async_copy(source, target, out_sem.at[i])
        for i, (source, target) in enumerate(
            [
                (stat_new, stat_out), (kern_new, kern_out), (kfirst_new, kfirst_out), (ksecond_new, ksecond_out),
                (half_v, half_out), (bases_new, bases_out),
            ]
        )
    ]
    for copy in copies:
        copy.start()
    bases_new[...] = jnp.zeros_like(bases_new)
    for copy in copies[:3]:
        copy.wait()
    for k in range(COUNT):
        stat_new[k] = new_statistics(grad_v, stat_v, k)
    outs[0].start()
    for copy in copies[3:]:
        copy.wait()
    for copy, _ in passed:
        copy.start()
    prepare_bases(stat_new, bases_v, work_v, width)

    def own_rows():
        first_row = lax.axis_index("fs") * shard
        grad = grad_v[pl.ds(pl.multiple_of(first_row, 64), shard), :]
        one = matrix_of(first_row, width)
        two = matrix_of(first_row + shard - 1, width)
        in_two = matrix_of(first_row + iota((shard, width), 0), width) != one
        basis_one, basis_two = bases_v[one], bases_v[two]
        rotated = jnp.where(in_two, turn(grad, basis_two), turn(grad, basis_one))
        kfirst_new[...], ksecond_new[...], step = adam_step(kfirst_v[...], ksecond_v[...], rotated)
        turned = jnp.where(in_two, dot_three(step, basis_two), dot_three(step, basis_one))
        kern_new[...] = decayed(kern_v[...], turned)

    def all_rows(k):
        bounds = matrix_bounds(width)
        rows = slice(bounds[k], bounds[k + 1])
        rotated = turn(grad_v[rows, :], bases_v[k])
        _, _, step = adam_step(first_v[rows, :].astype(F32), second_v[rows, :].astype(F32), rotated)
        turned = dot_nt(step.astype(BF16), bases_v[k].astype(BF16))
        half_v[rows, :] = decayed(rows_v[rows, :].astype(F32), turned).astype(BF16)

    def vector_rows():
        first, second, step = adam_step(vfirst_ref[...], vsecond_ref[...], gvec_ref[0:6, :])
        vfirst_out[...], vsecond_out[...] = first, second
        vec_out[...] = vec_ref[...] - RATE_VECTOR * step

    def beside(b):
        if b < COUNT:
            all_rows(b)
        elif b == COUNT:
            own_rows()
        elif b == COUNT + 1:
            vector_rows()
            for arrived, leaving in passed:
                arrived.wait()
                leaving.start()
            for copy in outs[1:5]:
                copy.start()

    orthogonalize(work_v, bases_new, width, beside)
    outs[5].start()
    for copy in outs + [leaving for _, leaving in passed]:
        copy.wait()


def update_call(grad, stat, bases, kern, kfirst, ksecond, rows, first, second, gvec, vec, vfirst, vsecond, *through):
    shard, width = kern.shape
    whole, anywhere = pl.BlockSpec(memory_space=pltpu.VMEM), pl.BlockSpec(memory_space=pl.ANY)

    def like(array):
        return jax.ShapeDtypeStruct(array.shape, array.dtype)

    def held(array):
        return pltpu.VMEM(array.shape, array.dtype)

    loaded = (grad, stat, bases, kern, kfirst, ksecond, rows, first, second)
    return pl.pallas_call(
        update_kernel,
        out_shape=tuple(map(like, through))
        + (like(kern), like(kern), like(kern), like(vec), like(vec), like(vec), like(stat), like(stat), like(grad)),
        in_specs=[anywhere] * 9 + [whole] * 4 + [anywhere] * 4,
        out_specs=(anywhere,) * 7 + (whole,) * 3 + (anywhere,) * 3,
        scratch_shapes=[held(array) for array in loaded]
        + [pltpu.VMEM((COUNT, 2 * width, width), F32)]
        + [held(array) for array in (kern, kern, kern, stat, stat, grad) + through]
        + [pltpu.SemaphoreType.DMA((9,)), pltpu.SemaphoreType.DMA((6,)), pltpu.SemaphoreType.DMA((2, 4))],
        compiler_params=pltpu.CompilerParams(vmem_limit_bytes=VMEM_LIMIT),
        name="update",
    )(*loaded, gvec, vec, vfirst, vsecond, *through)


def on_device(
    edge_latent, node_latent, edge_cot, node_cot, five_flag, senders, send_rows, kernels, kernel_first, kernel_second,
    vectors, vector_first, vector_second, statistics, bases,
):
    samples, nodes, width = node_latent.shape
    slots = senders.shape[0] // nodes
    z = Sizes(samples, nodes, slots, send_rows.shape[1], width)
    edge_out, edge_grad, node_out, node_grad, grad, gvec, rows, first, second = round_call(
        z,
        lax.axis_size("nodes"),
        edge_latent.reshape(-1, width),
        edge_cot.reshape(-1, width),
        node_latent.reshape(-1, width),
        node_cot.reshape(-1, width),
        five_flag.reshape(1, -1),
        senders.reshape(1, -1),
        send_rows,
        kernels,
        kernel_first,
        kernel_second,
        vectors,
    )
    edge_out, edge_grad, node_out, node_grad, *rest = update_call(
        grad, statistics, bases, kernels, kernel_first, kernel_second, rows, first, second, gvec,
        vectors, vector_first, vector_second, edge_out, edge_grad, node_out, node_grad,
    )
    return (
        edge_out.reshape(edge_latent.shape),
        node_out.reshape(node_latent.shape),
        edge_grad.reshape(edge_latent.shape),
        node_grad.reshape(node_latent.shape),
        *rest,
    )


def solution(mesh):
    in_specs = (
        P("fs", "nodes", None),
        P("fs", "nodes", None),
        P("fs", "nodes", None),
        P("fs", "nodes", None),
        P("nodes"),
        P("nodes"),
        P("nodes", None),
        P("fs", None),
        P("fs", None),
        P("fs", None),
        P(),
        P(),
        P(),
        P(),
        P(),
    )
    out_specs = (
        P("fs", "nodes", None),
        P("fs", "nodes", None),
        P("fs", "nodes", None),
        P("fs", "nodes", None),
        P("fs", None),
        P("fs", None),
        P("fs", None),
        P(),
        P(),
        P(),
        P(),
        P(),
        P(),
    )
    return jax.shard_map(
        on_device, mesh=mesh, in_specs=in_specs, out_specs=out_specs, check_vma=False
    )
```

```python
from functools import partial

import jax
import jax.numpy as jnp
from jax import lax
from jax.experimental import pallas as pl
from jax.experimental.pallas import tpu as pltpu
from jax.sharding import PartitionSpec as P

STEP = 5

NORM_EPS = 1e-05
BETA_ONE = 0.5
BETA_TWO = 0.5
RATE_MATRIX = 0.05
RATE_VECTOR = 0.2
DECAY_RATE = 0.01
ADAM_EPS = 1e-08
TINY = 1e-37
HIGH = lax.Precision.HIGHEST
F32 = jnp.float32
BF16 = jnp.bfloat16
LANES = 128
VMEM_LIMIT = 61 * 1024 * 1024


def dot_nn(left, right):
    return lax.dot_general(left, right, (((1,), (0,)), ((), ())), preferred_element_type=F32)


def dot_nt(left, right):
    return lax.dot_general(left, right, (((1,), (1,)), ((), ())), preferred_element_type=F32)


def dot_tn(left, right):
    return lax.dot_general(left, right, (((0,), (0,)), ((), ())), preferred_element_type=F32)


def split(value):
    high = value.astype(BF16)
    return high, (value - high.astype(F32)).astype(BF16)


def iota(shape, dim):
    return lax.broadcasted_iota(jnp.int32, shape, dim)


def ones_where(mask):
    return jnp.where(mask, 1.0, 0.0).astype(BF16)


def fold_rows(value):
    rows, width = value.shape
    return jnp.sum(value.reshape(rows // 8, 8, width), 0)


def aligned(index, step):
    return pl.ds(pl.multiple_of(index * step, step), step)


class Sizes:
    def __init__(self, samples, nodes, slots, halo, width):
        self.samples, self.nodes, self.slots = samples, nodes, slots
        self.halo, self.width = halo, width
        self.edges = nodes * slots
        self.fwd_nodes, self.bwd_nodes = 64, 128
        self.fwd_rows = self.fwd_nodes * slots
        self.bwd_rows = self.bwd_nodes * slots
        self.fwd_chunks = nodes // self.fwd_nodes
        self.bwd_chunks = nodes // self.bwd_nodes


def main_scratch(z):
    rows, width = z.samples * z.edges, z.width
    per_node = z.samples * z.nodes
    per_halo = z.samples * 2 * z.halo
    return dict(
        edge_v=pltpu.VMEM((rows, width), BF16),
        cot_v=pltpu.VMEM((rows, width), BF16),
        edge_out_v=pltpu.VMEM((rows, width), BF16),
        act_v=pltpu.VMEM((rows, width), BF16),
        slope_v=pltpu.VMEM((rows, width), F32),
        norm_v=pltpu.VMEM((rows, width), BF16),
        inv_v=pltpu.VMEM((rows, LANES), F32),
        own_v=pltpu.VMEM((z.edges, z.nodes), BF16),
        scat_v=pltpu.VMEM((z.bwd_chunks, z.nodes + 2 * z.halo + LANES, z.bwd_rows), BF16),
        sel_v=pltpu.VMEM((z.edges, 2 * LANES), BF16),
        rep_v=pltpu.VMEM((z.bwd_rows, 2 * LANES), BF16),
        live_v=pltpu.VMEM((z.edges, LANES), F32),
        half_v=pltpu.VMEM((7 * width, width), BF16),
        pown_v=pltpu.VMEM((per_node, width), BF16),
        psel_v=pltpu.VMEM((z.samples * z.fwd_chunks * 2 * LANES, width), BF16),
        gath_v=pltpu.VMEM((per_node, width), BF16),
        drep_v=pltpu.VMEM((z.samples * z.bwd_chunks * 2 * LANES, width), BF16),
        recv_v=pltpu.VMEM((per_node, width), F32),
        aown_v=pltpu.VMEM((per_node, width), F32),
        ahalo_v=pltpu.VMEM((per_halo, width), F32),
        table_v=pltpu.VMEM((per_halo, width), BF16),
        gmat_v=pltpu.VMEM((7 * width, width), F32),
        vsum_v=pltpu.VMEM((6 * 8, width), F32),
        pre_v=pltpu.VMEM((2, z.fwd_rows, width), F32),
        raw_v=pltpu.VMEM((2, z.fwd_rows, width), F32),
        upd_v=pltpu.VMEM((2, z.fwd_rows, width), BF16),
        dout_v=pltpu.VMEM((2, z.bwd_rows, width), BF16),
        dpre_v=pltpu.VMEM((2, z.bwd_rows, width), BF16),
        dall_v=pltpu.VMEM((rows, width), BF16),
        ncot_v=pltpu.VMEM((per_node, width), BF16),
        total_v=pltpu.VMEM((per_node, width), F32),
        rows_v=pltpu.VMEM((7 * width, width), BF16),
        first_v=pltpu.VMEM((7 * width, width), BF16),
        second_v=pltpu.VMEM((7 * width, width), BF16),
        list_v=pltpu.VMEM((2, z.samples * z.halo, width), BF16),
        halo_v=pltpu.VMEM((2, z.samples * z.halo, width), BF16),
        border_v=pltpu.VMEM((2, z.samples * z.halo, width), BF16),
        ret_v=pltpu.VMEM((2, z.samples * z.halo, width), BF16),
        gout_v=pltpu.VMEM((7 * width, width), BF16),
        edge_sem=pltpu.SemaphoreType.DMA((z.samples,)),
        cot_sem=pltpu.SemaphoreType.DMA((z.samples,)),
        eout_sem=pltpu.SemaphoreType.DMA((z.samples,)),
        egrad_sem=pltpu.SemaphoreType.DMA((z.samples,)),
        stat_v=pltpu.VMEM((PAIR, width, width), F32),
        bases_v=pltpu.VMEM((PAIR, width, width), F32),
        node_v=pltpu.VMEM((per_node, width), BF16),
        nout_v=pltpu.VMEM((per_node, width), BF16),
        ngrad_v=pltpu.VMEM((per_node, width), BF16),
        snew_v=pltpu.VMEM((PAIR, width, width), F32),
        work_v=pltpu.VMEM((PAIR, 2 * width, width), F32),
        hnew_v=pltpu.VMEM((3 * width, width), BF16),
        local_sem=pltpu.SemaphoreType.DMA((7,)),
        out_sem=pltpu.SemaphoreType.DMA((10,)),
        rows_sem=pltpu.SemaphoreType.DMA((2, 12)),
        first_sem=pltpu.SemaphoreType.DMA((2, 3)),
        second_sem=pltpu.SemaphoreType.DMA((2, 3)),
        halo_sem=pltpu.SemaphoreType.DMA((2, 2)),
        ret_sem=pltpu.SemaphoreType.DMA((2, 2)),
    )


def build_selectors(z, m, five_ref, send_ref):
    halo, nodes, slots = z.halo, z.nodes, z.slots
    lane = iota((LANES, LANES), 1)
    row = iota((LANES, LANES), 0)
    for g in range(z.edges // LANES):
        rows = slice(g * LANES, (g + 1) * LANES)
        line = jnp.broadcast_to(send_ref[g : g + 1, :].astype(F32), (LANES, LANES))
        column = line.T.astype(jnp.int32)
        for h in range(nodes // LANES):
            m.own_v[rows, h * LANES : (h + 1) * LANES] = ones_where(column == lane + (halo + h * LANES))
        place = jnp.where(column < halo, column, jnp.where(column >= halo + nodes, column - nodes, -1))
        in_halo = (place == (lane & (2 * halo - 1))) & (lane < 4 * halo)
        first = slots * (lane & (z.fwd_nodes - 1))
        local = row + (g * LANES) % z.fwd_rows
        m.sel_v[rows, 0:LANES] = ones_where((first <= local) & (local < first + slots))
        m.sel_v[rows, LANES : 2 * LANES] = ones_where(in_halo)
    place = iota((nodes + 2 * halo, z.bwd_rows), 0)
    place = jnp.where(place < nodes, place + halo, jnp.where(place < nodes + halo, place - nodes, place))
    first = slots * iota((LANES, z.bwd_rows), 0)
    local = iota((LANES, z.bwd_rows), 1)
    rep_t = ones_where((first <= local) & (local < first + slots))
    for c in range(z.bwd_chunks):
        lines = range(c * z.bwd_rows // LANES, (c + 1) * z.bwd_rows // LANES)
        senders = jnp.concatenate([send_ref[g : g + 1, :] for g in lines], 1)
        senders = jnp.broadcast_to(senders, place.shape)
        m.scat_v[c, 0 : nodes + 2 * halo, :] = ones_where(senders == place)
        m.scat_v[c, nodes + 2 * halo :, :] = rep_t
    first = slots * (iota((z.bwd_rows, 2 * LANES), 1) & (LANES - 1))
    local = iota((z.bwd_rows, 2 * LANES), 0)
    rep = ones_where((first <= local) & (local < first + slots))
    m.rep_v[...] = rep
    local = iota((z.bwd_rows, LANES), 0).astype(F32)
    slot = local - slots * jnp.floor((local + 0.5) * (1.0 / slots))
    for h in range(nodes // LANES):
        five = jnp.broadcast_to(five_ref[:, h * LANES : (h + 1) * LANES].astype(F32), (LANES, LANES)).T
        spread = dot_nn(rep[:, :LANES], five.astype(BF16))
        m.live_v[h * z.bwd_rows : (h + 1) * z.bwd_rows, :] = jnp.where(slot < slots - spread, 1.0, 0.0)


def both(column):
    return jnp.concatenate([column, column], 1)


def row_mean(value):
    return jnp.sum(value, -1, keepdims=True) * (1.0 / value.shape[-1])


def centred(value):
    centre = value - row_mean(value)
    return centre, lax.rsqrt(row_mean(centre * centre) + NORM_EPS)


def act_and_slope(half):
    turn = jnp.tanh(half)
    above = 1.0 + turn
    act = half * above
    return act, above + act * (1.0 - turn)


MESH = pl.DeviceIdType.MESH


def greet(partners):
    barrier = pltpu.get_barrier_semaphore()
    count = 0
    for device, exists in partners:
        if exists is None:
            pl.semaphore_signal(barrier, inc=1, device_id=device, device_id_type=MESH)
            count = count + 1
        else:
            pl.when(exists)(partial(pl.semaphore_signal, barrier, inc=1, device_id=device, device_id_type=MESH))
            count = count + exists.astype(jnp.int32)
    return lambda: pl.semaphore_wait(barrier, count)


def send(source, target, sems, slot, device):
    return pltpu.make_async_remote_copy(
        src_ref=source, dst_ref=target, send_sem=sems.at[0, slot], recv_sem=sems.at[1, slot],
        device_id=device, device_id_type=MESH,
    )


class Gather:
    def __init__(self, rows_v, sems, shard, fs, node):
        self.rows_v, self.sems, self.shard, self.fs = rows_v, sems, shard, fs
        self.parts = sems.shape[1] // 3
        self.next, self.far = (fs ^ 1, node), (fs ^ 2, node)

    def piece(self, owner, part):
        size = self.shard // self.parts
        return self.rows_v.at[pl.ds(pl.multiple_of(owner * self.shard + part * size, 16), size)]

    def copy(self, owner, part, slot, device):
        return send(self.piece(owner, part), self.piece(owner, part), self.sems, slot * self.parts + part, device)

    def start(self):
        for part in range(self.parts):
            self.copy(self.fs, part, 0, self.far).start()
        for part in range(self.parts):
            self.copy(self.fs, part, 1, self.next).start()

    def forward(self):
        for part in range(self.parts):
            self.copy(self.fs, part, 0, self.far).wait_recv()
            self.copy(self.fs ^ 2, part, 2, self.next).start()

    def finish(self):
        for part in range(self.parts):
            self.copy(self.fs, part, 0, self.far).wait_send()
            self.copy(self.fs, part, 1, self.next).wait()
            self.copy(self.fs ^ 2, part, 2, self.next).wait()


def list_matrix(send_ref, side, nodes):
    halo = send_ref.shape[1]
    listed = jnp.broadcast_to(send_ref[side : side + 1, :], (nodes, halo))
    return ones_where(listed == iota((nodes, halo), 0))


def sides(node, count):
    return ((node - 1, node > 0), (node + 1, node < count - 1))


class Cube:
    def __init__(self, count, fs=None, node=None):
        bits = count.bit_length() - 1
        self.node_bits = min(2, bits)
        self.size = 2 << self.node_bits
        self.extra = list(range(self.node_bits, bits))
        self.fs, self.node = fs, node
        if fs is not None:
            self.me = (fs >> 1) + 2 * (node & ((1 << self.node_bits) - 1))
        self.far_first = sorted(range(1, self.size), key=lambda r: (-r.bit_count(), -r))

    def device(self, r):
        return self.fs ^ (2 * (r & 1)), self.node ^ (r >> 1)

    def over(self, bit):
        return self.fs, self.node ^ (1 << bit)


def tree_sum(parts):
    while len(parts) > 1:
        parts = [left + right for left, right in zip(parts[::2], parts[1::2], strict=True)]
    return parts[0]


class Reduce:
    def __init__(self, cube, first, rows, sum_v, out_v, buffers):
        self.cube, self.sum_v, self.out_v = cube, sum_v, out_v
        self.give_v, self.land_v, self.near_v, self.cube_v, self.acc_v, self.extra_v, self.sems = buffers
        self.half = rows // 2
        self.size = self.half // cube.size
        core = cube.fs & 1
        self.keep, self.give = first + core * self.half, first + (1 - core) * self.half
        self.twin = (cube.fs ^ 1, cube.node)
        self.order = cube.far_first + [0]
        self.started = []

    @staticmethod
    def scratch(cube, rows, width):
        half, extra = rows // 2, max(2 * len(cube.extra), 1)
        size = half // cube.size
        return [
            pltpu.VMEM((half, width), BF16),
            pltpu.VMEM((half, width), BF16),
            pltpu.VMEM((half, width), BF16),
            pltpu.VMEM((cube.size, size, width), BF16),
            pltpu.VMEM((size, width), F32),
            pltpu.VMEM((extra, size, width), BF16),
            pltpu.SemaphoreType.DMA((2, 4 * cube.size + extra)),
        ]

    def rows(self, r, base=0):
        return pl.ds(pl.multiple_of(base + (self.cube.me ^ r) * self.size, 16), self.size)

    def launch(self, source, target, slot, device):
        copy = send(source, target, self.sems, slot, device)
        copy.start()
        self.started.append(copy)
        return copy

    def begin(self):
        self.core = {}
        for r in self.order:
            part = self.give_v.at[self.rows(r)]
            part[...] = self.sum_v[self.rows(r, self.give), :].astype(BF16)
            self.core[r] = self.launch(part, self.land_v.at[self.rows(r)], r, self.twin)

    def spread(self):
        self.near = {}
        for r in self.order:
            self.core[r].wait_recv()
            total = self.sum_v[self.rows(r, self.keep), :] + self.land_v[self.rows(r), :].astype(F32)
            if r:
                part = self.near_v.at[self.rows(r)]
                part[...] = total.astype(BF16)
                self.near[r] = self.launch(part, self.cube_v.at[r], self.cube.size + r, self.cube.device(r))
            else:
                self.acc_v[...] = total

    def meet(self):
        total = self.acc_v[...]
        for r in reversed(self.cube.far_first):
            self.near[r].wait_recv()
            total = total + self.cube_v[r].astype(F32)
        self.far = None
        if self.cube.extra:
            self.exchange(total, 0)
        else:
            self.acc_v[...] = total

    def exchange(self, total, e):
        self.extra_v[2 * e] = total.astype(BF16)
        self.far = self.launch(
            self.extra_v.at[2 * e], self.extra_v.at[2 * e + 1], 4 * self.cube.size + e, self.cube.over(self.cube.extra[e])
        )

    def settle(self):
        total = self.acc_v[...]
        for e in range(len(self.cube.extra)):
            self.far.wait_recv()
            total = self.extra_v[2 * e].astype(F32) + self.extra_v[2 * e + 1].astype(F32)
            if e + 1 < len(self.cube.extra):
                self.exchange(total, e + 1)
        own = self.out_v.at[self.rows(0, self.keep)]
        own[...] = total.astype(BF16)
        size = self.cube.size
        self.back = {r: self.launch(own, own, 2 * size + r, self.cube.device(r)) for r in self.cube.far_first}
        self.last = [self.launch(own, own, 3 * size, self.twin)]

    def forward(self):
        for r in reversed(self.cube.far_first):
            self.back[r].wait_recv()
            part = self.out_v.at[self.rows(r, self.keep)]
            self.last.append(self.launch(part, part, 3 * self.cube.size + r, self.twin))

    def arrive(self):
        for copy in self.last:
            copy.wait_recv()

    def end(self):
        for copy in self.started:
            copy.wait_send()


class VectorSum:
    def __init__(self, cube, send_v, land_v, sems):
        self.cube, self.send_v, self.land_v, self.sems = cube, send_v, land_v, sems
        self.started = []

    @staticmethod
    def scratch(cube, shape):
        extra = len(cube.extra)
        return [
            pltpu.VMEM((2 + extra,) + shape, F32),
            pltpu.VMEM((cube.size + extra,) + shape, F32),
            pltpu.SemaphoreType.DMA((2, cube.size + extra)),
        ]

    def launch(self, source, slot, device):
        copy = send(self.send_v.at[source], self.land_v.at[slot], self.sems, slot, device)
        copy.start()
        self.started.append(copy)
        return copy

    def begin(self, value):
        self.send_v[0] = value
        self.core = self.launch(0, 0, (self.cube.fs ^ 1, self.cube.node))

    def spread(self):
        self.core.wait_recv()
        self.send_v[1] = self.send_v[0] + self.land_v[0]
        self.near = [self.launch(1, r, self.cube.device(r)) for r in range(1, self.cube.size)]

    def meet(self):
        for copy in self.near:
            copy.wait_recv()
        self.total = tree_sum([self.send_v[1]] + [self.land_v[r] for r in range(1, self.cube.size)])
        self.far = self.exchange(0) if self.cube.extra else None

    def exchange(self, e):
        self.send_v[2 + e] = self.total
        return self.launch(2 + e, self.cube.size + e, self.cube.over(self.cube.extra[e]))

    def settle(self):
        for e in range(len(self.cube.extra)):
            self.far.wait_recv()
            self.total = self.total + self.land_v[self.cube.size + e]
            if e + 1 < len(self.cube.extra):
                self.far = self.exchange(e + 1)
        return self.total

    def end(self):
        for copy in self.started:
            copy.wait_send()


BLOCK = 32
COUNT = 4
PAIR = 2
AHEAD = 4
HALF = LANES // BLOCK


def wide_left(value):
    high, low = split(value)
    return jnp.concatenate([high, high, low], 1)


def wide_right(value):
    high, low = split(value)
    return jnp.concatenate([high, low, high], 1)


def dot_three(left, right):
    return dot_nt(wide_left(left), wide_right(right))


def factor_block(packed):
    sub = iota((8, LANES), 0)
    lane = iota((8, LANES), 1)
    tiles = BLOCK // 8
    group = lane & (LANES - BLOCK)
    plain = [packed[8 * r : 8 * r + 8, :] for r in range(tiles)]
    columns = {}

    def take_columns(panel):
        for l in range(8 * panel, 8 * panel + 8):
            columns[l] = [None] * panel + [jnp.take_along_axis(part, group + l, axis=1) for part in plain[panel:]]

    take_columns(0)
    inverse = [jnp.where((lane & (BLOCK - 1)) == sub + 8 * r, 1.0, 0.0) for r in range(tiles)]

    def line(tile, s):
        return jnp.broadcast_to(tile[s : s + 1, :], (8, LANES))

    for j in range(BLOCK):
        rj, sj = j // 8, j % 8
        scale = lax.rsqrt(line(columns[j][rj], sj))
        below = [None if r < rj else columns[j][r] * scale for r in range(tiles)]
        below[rj] = jnp.where(sub > sj, below[rj], 0.0)
        for l in [l for l in columns if l > j]:
            weight = line(below[l // 8], l % 8)
            for r in range(l // 8, tiles):
                columns[l][r] = columns[l][r] - below[r] * weight
        if j < BLOCK - 8 - AHEAD:
            row = line(plain[rj], sj) * scale
            for r in range(rj, tiles):
                plain[r] = plain[r] - below[r] * row
        if j % 8 == 7 - AHEAD and j < BLOCK - 8:
            take_columns(rj + 1)
        row = line(inverse[rj], sj) * scale
        inverse[rj] = jnp.where(sub == sj, row, inverse[rj] - below[rj] * row)
        for r in range(rj + 1, tiles):
            inverse[r] = inverse[r] - below[r] * row
    return jnp.concatenate(inverse, 0)


def turned_blocks(k, width):
    return [h * HALF + (g - k) % HALF for h in range(width // LANES) for g in range(HALF)]


def pick_rows(value, blocks):
    return jnp.concatenate([value[i * BLOCK : (i + 1) * BLOCK, :] for i in blocks], 0)


def orthogonalize(work_v, bases_out, width, beside):
    blocks = width // BLOCK
    group = iota((BLOCK, LANES), 1) // BLOCK
    square = iota((LANES, LANES), 0) // BLOCK == iota((LANES, LANES), 1) // BLOCK

    def placed(values, b):
        return [jnp.where(group == (b + k) % COUNT, values[k], jnp.zeros_like(values[k])) for k in range(COUNT)]

    def lanes_of(b):
        return slice(b // HALF * LANES, (b // HALF + 1) * LANES)

    def rows_of(b):
        return slice(b * BLOCK, (b + 1) * BLOCK)

    packed = sum(placed([work_v[k, rows_of(0), lanes_of(0)] for k in range(COUNT)], 0))
    for b in range(blocks):
        beside(b)
        lanes, after = lanes_of(b), (b + 1) * BLOCK
        high, low = split(factor_block(packed).astype(F32))
        high, low = placed([high] * COUNT, b), placed([low] * COUNT, b)
        if b < blocks - 1:
            spread_high, spread_low = jnp.concatenate(high, 0), jnp.concatenate(low, 0)
            spread = jnp.concatenate([spread_high, spread_low, spread_high], 1)
            ahead = jnp.concatenate([work_v[k, rows_of(b + 1), lanes] for k in range(COUNT)], 0)
            turned = jnp.where(square, dot_nt(wide_left(ahead), spread), 0.0)
            order = [(g - b - 1) % COUNT for g in range(COUNT)]
            update = dot_nt(wide_left(turned), pick_rows(wide_right(turned), order))
            current = placed([work_v[k, rows_of(b + 1), lanes_of(b + 1)] for k in range(COUNT)], b + 1)
            packed = sum(current) - sum(update[rows_of(k), :] for k in range(COUNT))
        start = after // LANES * LANES
        for k in range(COUNT):
            four_high = jnp.concatenate([high[k]] * HALF, 0)
            four_low = jnp.concatenate([low[k]] * HALF, 0)
            below = wide_left(work_v[k, after:, lanes])
            turned = dot_nt(below, jnp.concatenate([four_high, four_low, four_high], 1))
            mine = iota((width, LANES), 1) // BLOCK == b % HALF
            bases_out[k, :, lanes] = jnp.where(mine, turned[width - after :, :], bases_out[k, :, lanes])
            if b == blocks - 1:
                continue
            turned_high, turned_low = split(turned)
            part = iota(turned.shape, 1) // BLOCK
            zero = jnp.zeros_like(turned_high)
            left = jnp.where(part == 2, turned_low, jnp.where(part == 3, zero, turned_high))
            right = jnp.where(part == 1, turned_low, jnp.where(part == 3, zero, turned_high))
            right = jnp.concatenate(
                [
                    right[(i - b - 1) * BLOCK : (i - b) * BLOCK, :] if i > b else zero[0:BLOCK, :]
                    for i in turned_blocks(k, width)[start // BLOCK :]
                ],
                0,
            )
            work_v[k, after:, start:] -= dot_nt(left, right)


def matrix_bounds(width):
    return [0, 3 * width, 4 * width, 6 * width, 7 * width]


def new_statistics(rows, stat):
    return BETA_TWO * stat + (1.0 - BETA_TWO) * dot_tn(rows, rows)


def matrix_of(row, width):
    return sum((row >= bound).astype(jnp.int32) for bound in matrix_bounds(width)[1:-1])


def prepare_bases(stat, basis, k):
    width = stat.shape[-1]
    order = turned_blocks(k, width)
    flipped = basis.T
    proj_rows = dot_three(flipped, stat)
    gram = dot_three(proj_rows, pick_rows(proj_rows, order))
    return gram, dot_three(stat, pick_rows(flipped, order))


def adam_step(first, second, rotated):
    first = BETA_ONE * first + (1.0 - BETA_ONE) * rotated
    second = BETA_TWO * second + (1.0 - BETA_TWO) * rotated * rotated
    square = second * (1.0 / (1.0 - BETA_TWO**STEP))
    root = square * lax.rsqrt(jnp.maximum(square, TINY))
    return first, second, first * (1.0 / (1.0 - BETA_ONE**STEP)) * (1.0 / (root + ADAM_EPS))


def turn(rows, basis):
    high, low = split(basis)
    return dot_nn(rows, high) + dot_nn(rows, low)


def decayed(kern, turned):
    return kern - RATE_MATRIX * (turned + DECAY_RATE * kern)


def rounded_rows(grad, basis, kern, first, second):
    _, _, step = adam_step(first.astype(F32), second.astype(F32), turn(grad, basis))
    return decayed(kern.astype(F32), dot_nt(step.astype(BF16), basis.astype(BF16))).astype(BF16)


def round_kernel(
    z, names, count, edge_ref, cot_ref, node_hbm, ncot_ref, five_ref, send_ref, list_ref, kern_ref, kfirst_ref, ksecond_ref,
    vec_ref, stat_ref, bases_ref, eout_ref, egrad_ref, nout_hbm, ngrad_hbm, grad_ref, gvec_ref, rows_ref, first_ref, second_ref,
    stat_hbm, work_hbm, half_hbm, *scratch,
):
    m = type("Held", (), {})()
    for name, ref in zip(names, scratch[: len(names)], strict=True):
        setattr(m, name, ref)
    spare = scratch[len(names) :]
    fs, node_id = lax.axis_index("fs"), lax.axis_index("nodes")
    cube = Cube(count, fs, node_id)
    around = sides(node_id, count)
    shard = kern_ref.shape[0]
    width, nodes, edges, samples, halo = z.width, z.nodes, z.edges, z.samples, z.halo
    two_halo = 2 * halo

    def sample_copy(source, target, sem, s):
        rows = aligned(s, edges)
        return pltpu.make_async_copy(source.at[rows], target.at[rows], sem.at[s])

    weight_ref = m.rows_v
    mine = pl.ds(pl.multiple_of(fs * shard, 16), shard)
    staged = [pl.ds(i * shard, shard) for i in range(3)]
    locals_in = [
        pltpu.make_async_copy(source, target, m.local_sem.at[i])
        for i, (source, target) in enumerate(
            [
                (kern_ref, m.slope_v.at[staged[0]]), (node_hbm, m.node_v), (kfirst_ref, m.slope_v.at[staged[1]]),
                (ksecond_ref, m.slope_v.at[staged[2]]), (ncot_ref, m.ncot_v),
                (stat_ref.at[pl.ds(PAIR, PAIR)], m.stat_v), (bases_ref.at[pl.ds(PAIR, PAIR)], m.bases_v),
            ]
        )
    ]
    node_ref, nout_ref, ngrad_ref = m.node_v, m.nout_v, m.ngrad_v
    stat_out, work_out, half_out = m.snew_v, m.work_v, m.hnew_v

    def start_out(i, source, target):
        copy = pltpu.make_async_copy(source, target, m.out_sem.at[i])
        copy.start()
        outs.append(copy)

    outs = []
    gather = Gather(weight_ref, m.rows_sem, shard, fs, node_id)
    moments = [Gather(m.first_v, m.first_sem, shard, fs, node_id), Gather(m.second_v, m.second_sem, shard, fs, node_id)]
    for copy in locals_in[:2]:
        copy.start()
    m.halo_v[...] = jnp.zeros_like(m.halo_v)
    m.ret_v[...] = jnp.zeros_like(m.ret_v)
    all_in = greet(
        [(gather.next, None)]
        + [(cube.device(r), None) for r in range(1, cube.size)]
        + [(cube.over(bit), None) for bit in cube.extra]
        + [((fs, other), exists) for other, exists in around]
    )
    locals_in[0].wait()
    weight_ref[mine, :] = m.slope_v[staged[0], :].astype(BF16)
    all_in()
    gather.start()
    for copy in locals_in[2:]:
        copy.start()
    for s in range(samples):
        sample_copy(edge_ref, m.edge_v, m.edge_sem, s).start()
    for s in range(samples):
        sample_copy(cot_ref, m.cot_v, m.cot_sem, s).start()

    def to_side(source, target, sems, side, other):
        return send(source.at[side], target.at[1 - side], sems, side, (fs, other))

    def start_sides(source, target, sems):
        for side, (other, exists) in enumerate(around):
            pl.when(exists)(lambda side=side, other=other: to_side(source, target, sems, side, other).start())

    def finish_sides(source, target, sems):
        for side, (other, exists) in enumerate(around):
            def settle(side=side, other=other):
                to_side(source, target, sems, side, other).wait_send()
                to_side(source, target, sems, 1 - side, other).wait_recv()
            pl.when(exists)(settle)

    locals_in[1].wait()
    for side in range(2):
        chosen = list_matrix(list_ref, side, nodes)
        for s in range(samples):
            m.list_v[side, s * halo : (s + 1) * halo, :] = dot_tn(
                chosen, node_ref[s * nodes : (s + 1) * nodes, :]
            ).astype(BF16)
    start_sides(m.list_v, m.halo_v, m.halo_sem)
    build_selectors(z, m, five_ref, send_ref)
    gather.forward()
    gather.finish()
    finish_sides(m.list_v, m.halo_v, m.halo_sem)
    start_out(0, weight_ref, rows_ref)
    for copy in locals_in[2:]:
        copy.wait()
    for k, (moment, held) in enumerate(zip(moments, (m.first_v, m.second_v), strict=True)):
        held[mine, :] = m.slope_v[staged[k + 1], :].astype(BF16)
        moment.start()
    m.half_v[...] = weight_ref[...] * jnp.asarray(0.5, BF16)
    m.gmat_v[...] = jnp.zeros_like(m.gmat_v)
    m.vsum_v[...] = jnp.zeros_like(m.vsum_v)
    m.aown_v[...] = jnp.zeros_like(m.aown_v)
    m.ahalo_v[...] = jnp.zeros_like(m.ahalo_v)
    for s in range(samples):
        for side in range(2):
            m.table_v[s * two_halo + side * halo : s * two_halo + (side + 1) * halo, :] = m.halo_v[
                side, s * halo : (s + 1) * halo, :
            ]

    send_half = m.half_v[width : 2 * width, :]
    recv_half = m.half_v[2 * width : 3 * width, :]
    bias_edge, gain_edge, shift_edge = vec_ref[0:1, :] * 0.5, vec_ref[1:2, :], vec_ref[2:3, :]
    bias_node, gain_node, shift_node = vec_ref[3:4, :] * 0.5, vec_ref[4:5, :], vec_ref[5:6, :]

    for s in range(samples):
        node = node_ref[s * nodes : (s + 1) * nodes, :]
        m.pown_v[s * nodes : (s + 1) * nodes, :] = dot_nn(node, send_half).astype(BF16)
        high, low = split(dot_nn(node, recv_half) + bias_edge)
        out_high, out_low = split(dot_nn(m.table_v[s * two_halo : (s + 1) * two_halo, :], send_half))
        zero = jnp.zeros((2 * LANES - 2 * z.fwd_nodes - 2 * two_halo, width), BF16)
        for c in range(z.fwd_chunks):
            own = slice(c * z.fwd_nodes, (c + 1) * z.fwd_nodes)
            base = (s * z.fwd_chunks + c) * 2 * LANES
            m.psel_v[base : base + 2 * LANES, :] = jnp.concatenate(
                [high[own], low[own], out_high, out_low, zero], 0
            )

    per = z.fwd_chunks
    last = samples * per - 1

    def join_edges(i, slot):
        s, c = i // per, i % per
        local = aligned(c, z.fwd_rows)
        left = jnp.concatenate([m.edge_v[aligned(i, z.fwd_rows), :], m.own_v[local, :], m.sel_v[local, :]], 1)
        right = jnp.concatenate(
            [m.half_v[0:width, :], m.pown_v[aligned(s, nodes), :], m.psel_v[aligned(i, 2 * LANES), :]], 0
        )
        m.pre_v[slot] = dot_nn(left, right)

    def activate(i, slot):
        rows = aligned(i, z.fwd_rows)
        act, slope = act_and_slope(m.pre_v[slot])
        act = act.astype(BF16)
        m.act_v[rows, :] = act
        m.slope_v[rows, :] = slope
        m.raw_v[slot] = dot_nn(act, weight_ref[3 * width : 4 * width, :])

    def update_edges(i, slot):
        rows, local = aligned(i, z.fwd_rows), aligned(i % per, z.fwd_rows)
        centre, inv = centred(m.raw_v[slot])
        live = m.live_v[local, :]
        inv = inv * live
        m.inv_v[rows, :] = inv
        normed = centre * both(inv)
        m.norm_v[rows, :] = normed.astype(BF16)
        update = normed * gain_edge + both(live) * shift_edge
        m.edge_out_v[rows, :] = (m.edge_v[rows, :].astype(F32) + update).astype(BF16)
        m.upd_v[slot] = update.astype(BF16)

    def gather_updates(i, slot):
        take = slice(nodes + two_halo, nodes + two_halo + z.fwd_nodes)
        gathered = dot_nn(m.scat_v[0, take, 0 : z.fwd_rows], m.upd_v[slot])
        m.gath_v[aligned(i, z.fwd_nodes), :] = gathered.astype(BF16)

    def edge_in(s):
        return sample_copy(edge_ref, m.edge_v, m.edge_sem, s)

    edge_in(0).wait()
    join_edges(0, 0)

    def forward(s, carry):
        pl.when(s < samples - 1)(lambda: edge_in(s + 1).wait())
        for c in range(per):
            i = s * per + c
            join_edges(jnp.minimum(i + 1, last), (c + 1) % 2)
            gather_updates(jnp.maximum(i - 2, 0), c % 2)
            activate(i, c % 2)
            update_edges(jnp.maximum(i - 1, 0), (c + 1) % 2)
        pl.when(s > 0)(lambda: sample_copy(m.edge_out_v, eout_ref, m.eout_sem, s - 1).start())
        return carry

    lax.fori_loop(0, samples, forward, 0)
    gather_updates(last - 1, 0)
    update_edges(last, 1)
    gather_updates(last, 1)
    sample_copy(m.edge_out_v, eout_ref, m.eout_sem, samples - 1).start()

    def node_part(i, carry):
        rows = aligned(i, 2 * nodes)
        node, gath = node_ref[rows, :], m.gath_v[rows, :]
        joined = jnp.concatenate([node, gath], 1)
        act, slope = act_and_slope(dot_nn(joined, m.half_v[4 * width : 6 * width, :]) + bias_node)
        act = act.astype(BF16)
        centre, inv = centred(dot_nn(act, weight_ref[6 * width : 7 * width, :]))
        normed = centre * inv
        nout_ref[rows, :] = (node.astype(F32) + normed * gain_node + shift_node).astype(BF16)
        back = m.ncot_v[rows, :].astype(F32)
        back_normed = back * normed
        scaled, scaled_normed = back * gain_node, back_normed * gain_node
        d_out = (inv * (scaled - row_mean(scaled) - normed * row_mean(scaled_normed))).astype(BF16)
        m.gmat_v[6 * width : 7 * width, :] += dot_tn(act, d_out)
        m.vsum_v[32:40, :] += fold_rows(back_normed)
        m.vsum_v[40:48, :] += fold_rows(back)
        d_pre = dot_nt(d_out, m.half_v[6 * width : 7 * width, :]) * slope
        d_pre = d_pre.astype(BF16)
        m.vsum_v[24:32, :] += fold_rows(d_pre.astype(F32))
        m.gmat_v[4 * width : 6 * width, :] += dot_tn(joined, d_pre)
        d_joined = dot_nt(d_pre, weight_ref[4 * width : 6 * width, :])
        m.total_v[rows, :] = back + d_joined[:, :width]
        high, low = split(d_joined[:, width:])
        for k in range(2):
            for c in range(z.bwd_chunks):
                own = slice(k * nodes + c * z.bwd_nodes, k * nodes + (c + 1) * z.bwd_nodes)
                m.drep_v[aligned((i * 2 + k) * z.bwd_chunks + c, 2 * LANES), :] = jnp.concatenate(
                    [high[own], low[own]], 0
                )
        return carry

    lax.fori_loop(0, samples // 2, node_part, 0)

    halves = z.bwd_rows // z.fwd_rows
    pairs = samples * z.bwd_chunks

    def spread_back(i, slot):
        half = slice((slot % halves) * z.fwd_rows, (slot % halves + 1) * z.fwd_rows)
        m.pre_v[slot] = dot_nn(m.rep_v[half, :], m.drep_v[aligned(i // halves, 2 * LANES), :])

    def norm_back(i, slot, pair):
        rows, local = aligned(i, z.fwd_rows), aligned(i % per, z.fwd_rows)
        d_update = (m.cot_v[rows, :].astype(F32) + m.pre_v[slot]) * both(m.live_v[local, :])
        normed = m.norm_v[rows, :].astype(F32)
        d_normed = d_update * normed
        m.vsum_v[8:16, :] += fold_rows(d_normed)
        m.vsum_v[16:24, :] += fold_rows(d_update)
        scaled, scaled_normed = d_update * gain_edge, d_normed * gain_edge
        d_out = both(m.inv_v[rows, :]) * (scaled - row_mean(scaled) - normed * row_mean(scaled_normed))
        m.dout_v[pair, slot * z.fwd_rows : (slot + 1) * z.fwd_rows, :] = d_out.astype(BF16)

    def activate_back(i, slot, pair):
        part = slice(slot * z.fwd_rows, (slot + 1) * z.fwd_rows)
        d_act = dot_nt(m.dout_v[pair, part, :], m.half_v[3 * width : 4 * width, :])
        d_pre = (d_act * m.slope_v[aligned(i, z.fwd_rows), :]).astype(BF16)
        m.dpre_v[pair, part, :] = d_pre
        m.dall_v[aligned(i, z.fwd_rows), :] = d_pre

    def weights_back(p, pair):
        s, c = p // z.bwd_chunks, p % z.bwd_chunks
        rows = aligned(p, z.bwd_rows)
        d_out, d_pre = m.dout_v[pair], m.dpre_v[pair]
        m.gmat_v[3 * width : 4 * width, :] += dot_tn(m.act_v[rows, :], d_out)
        m.gmat_v[0:width, :] += dot_tn(m.edge_v[rows, :], d_pre)
        sums = dot_nn(m.scat_v[c], d_pre)
        m.aown_v[aligned(s, nodes), :] += sums[0:nodes, :]
        m.ahalo_v[aligned(s, two_halo), :] += sums[nodes : nodes + two_halo, :]
        m.recv_v[aligned(p, z.bwd_nodes), :] = sums[nodes + two_halo :, :]

    m.dout_v[1] = jnp.zeros_like(m.dout_v[1])
    m.dpre_v[1] = jnp.zeros_like(m.dpre_v[1])
    spread_back(0, 0)

    def backward(s, carry):
        sample_copy(cot_ref, m.cot_v, m.cot_sem, s).wait()
        for k in range(z.bwd_chunks):
            p = s * z.bwd_chunks + k
            i = p * halves
            spread_back(i + 1, 1)
            activate_back(jnp.maximum(i - 1, 0), 1, 1 - k)
            norm_back(i, 0, k)
            weights_back(jnp.maximum(p - 1, 0), 1 - k)
            spread_back(jnp.minimum(i + 2, last), 0)
            activate_back(i, 0, k)
            norm_back(i + 1, 1, k)
        return carry

    nodes_sum = Reduce(cube, 4 * width, 3 * width, m.gmat_v, m.gout_v, spare[7:14])
    nodes_sum.begin()
    start_out(1, nout_ref, nout_hbm)
    lax.fori_loop(0, 1, backward, 0)
    nodes_sum.spread()
    lax.fori_loop(1, samples, backward, 0)
    activate_back(last, 1, 1)
    weights_back(pairs - 1, 1)

    def edge_gradient(s, carry):
        for c in range(per):
            rows = aligned(s * per + c, z.fwd_rows)
            d_edge = dot_nt(m.dall_v[rows, :], weight_ref[0:width, :])
            m.edge_out_v[rows, :] = (m.cot_v[rows, :].astype(F32) + d_edge).astype(BF16)
        sample_copy(m.edge_out_v, egrad_ref, m.egrad_sem, s).start()
        return carry

    send_full = weight_ref[width : 2 * width, :]
    recv_full = weight_ref[2 * width : 3 * width, :]
    table = m.table_v[...]
    out_high, out_low = split(m.ahalo_v[...])
    nodes_all = node_ref[...]
    grad_send = dot_tn(table, out_high) + dot_tn(nodes_all, m.aown_v[...].astype(BF16))
    grad_recv = dot_tn(nodes_all, m.recv_v[...].astype(BF16))
    m.gmat_v[width : 2 * width, :] = grad_send
    m.gmat_v[2 * width : 3 * width, :] = grad_recv
    reduce = Reduce(cube, 0, 4 * width, m.gmat_v, m.gout_v, spare[:7])
    vectors = VectorSum(cube, *spare[14:])
    reduce.begin()
    nodes_sum.meet()
    border = (dot_nt(out_high, send_full) + dot_nt(out_low, send_full)).astype(BF16)
    for s in range(samples):
        for side in range(2):
            m.border_v[side, s * halo : (s + 1) * halo, :] = border[
                s * two_halo + side * halo : s * two_halo + (side + 1) * halo, :
            ]
    start_sides(m.border_v, m.ret_v, m.ret_sem)
    for s in range(samples):
        m.vsum_v[0:8, :] += fold_rows(m.recv_v[s * nodes : (s + 1) * nodes, :])
    vectors.begin(
        jnp.concatenate(
            [jnp.sum(m.vsum_v[k * 8 : (k + 1) * 8, :], 0, keepdims=True) for k in range(6)]
            + [jnp.zeros((2, width), F32)],
            0,
        )
    )
    reduce.spread()
    vectors.spread()
    for moment in moments:
        moment.forward()
    for s in range(samples):
        sample_copy(m.edge_out_v, eout_ref, m.eout_sem, s).wait()
    lax.fori_loop(0, samples, edge_gradient, 0)
    nodes_sum.settle()
    for s in range(samples):
        rows = slice(s * nodes, (s + 1) * nodes)
        recv_high, recv_low = split(m.recv_v[rows, :])
        own_high, own_low = split(m.aown_v[rows, :])
        m.total_v[rows, :] += (
            dot_nt(recv_high, recv_full) + dot_nt(recv_low, recv_full)
            + dot_nt(own_high, send_full) + dot_nt(own_low, send_full)
        )
    reduce.meet()
    vectors.meet()
    nodes_sum.forward()
    finish_sides(m.border_v, m.ret_v, m.ret_sem)
    low, high = (list_matrix(list_ref, side, nodes) for side in range(2))
    for s in range(samples):
        rows, part = slice(s * nodes, (s + 1) * nodes), slice(s * halo, (s + 1) * halo)
        ngrad_ref[rows, :] = (
            m.total_v[rows, :] + dot_nn(low, m.ret_v[0, part, :]) + dot_nn(high, m.ret_v[1, part, :])
        ).astype(BF16)
    start_out(2, ngrad_ref, ngrad_hbm)
    reduce.settle()
    gvec_ref[...] = vectors.settle()
    nodes_sum.arrive()
    bounds = matrix_bounds(width)
    for k in range(PAIR):
        stat_out[k] = new_statistics(m.gout_v[bounds[PAIR + k] : bounds[PAIR + k + 1], :], m.stat_v[k])
    start_out(5, m.gout_v.at[pl.ds(4 * width, 3 * width)], grad_ref.at[pl.ds(4 * width, 3 * width)])
    start_out(6, stat_out, stat_hbm)
    for k in range(PAIR):
        work_out[k, 0:width, :], work_out[k, width:, :] = prepare_bases(stat_out[k], m.bases_v[k], PAIR + k)
    start_out(7, work_out, work_hbm)
    for moment in moments:
        moment.finish()
    start_out(3, m.first_v.at[pl.ds(0, 4 * width)], first_ref)
    start_out(4, m.second_v.at[pl.ds(0, 4 * width)], second_ref)
    for k in range(PAIR):
        low, high = bounds[PAIR + k], bounds[PAIR + k + 1]
        half_out[low - 4 * width : high - 4 * width, :] = rounded_rows(
            m.gout_v[low:high, :], m.bases_v[k], weight_ref[low:high, :], m.first_v[low:high, :], m.second_v[low:high, :]
        )
    start_out(8, half_out, half_hbm)
    for s in range(samples):
        sample_copy(m.edge_out_v, egrad_ref, m.egrad_sem, s).wait()
    for copy in outs:
        copy.wait()
    reduce.forward()
    reduce.arrive()
    grad_out = pltpu.make_async_copy(m.gout_v.at[pl.ds(0, 4 * width)], grad_ref.at[pl.ds(0, 4 * width)], m.out_sem.at[9])
    grad_out.start()
    reduce.end()
    nodes_sum.end()
    vectors.end()
    grad_out.wait()


def round_call(z, count, edge, cot, node, ncot, five, senders, send_rows, kern, kfirst, ksecond, vectors, stat, bases):
    shard, width = kern.shape
    scratch = main_scratch(z)
    cube = Cube(count)
    spare = Reduce.scratch(cube, 4 * width, width) + Reduce.scratch(cube, 3 * width, width) + VectorSum.scratch(cube, (8, width))
    rows, per_node = z.samples * z.edges, z.samples * z.nodes
    whole = pl.BlockSpec(memory_space=pltpu.VMEM)
    anywhere = pl.BlockSpec(memory_space=pl.ANY)
    total = jax.ShapeDtypeStruct((7 * width, width), BF16)
    moments = jax.ShapeDtypeStruct((4 * width, width), BF16)
    return pl.pallas_call(
        partial(round_kernel, z, tuple(scratch), count),
        out_shape=(
            jax.ShapeDtypeStruct((rows, width), BF16),
            jax.ShapeDtypeStruct((rows, width), BF16),
            jax.ShapeDtypeStruct((per_node, width), BF16),
            jax.ShapeDtypeStruct((per_node, width), BF16),
            total,
            jax.ShapeDtypeStruct((8, width), F32),
            total, moments, moments,
            jax.ShapeDtypeStruct((PAIR, width, width), F32),
            jax.ShapeDtypeStruct((PAIR, 2 * width, width), F32),
            jax.ShapeDtypeStruct((3 * width, width), BF16),
        ),
        in_specs=[anywhere] * 4 + [whole] * 3 + [anywhere] * 3 + [whole] + [anywhere] * 2,
        out_specs=(anywhere,) * 5 + (whole,) + (anywhere,) * 6,
        scratch_shapes=list(scratch.values()) + spare,
        compiler_params=pltpu.CompilerParams(
            collective_id=0, has_side_effects=True, vmem_limit_bytes=VMEM_LIMIT
        ),
        name="edge_node_round",
    )(edge, cot, node, ncot, five, senders, send_rows, kern, kfirst, ksecond, vectors, stat, bases)


def update_kernel(
    grad_ref, stat_ref, bases_ref, kern_ref, kfirst_ref, ksecond_ref, rows_ref, first_ref, second_ref,
    gvec_ref, vec_ref, vfirst_ref, vsecond_ref, work_ref, eout_ref, egrad_ref, nout_ref, ngrad_ref, spair_ref, hpair_ref,
    eout_out, egrad_out, nout_out, ngrad_out, kern_out, kfirst_out, ksecond_out, vec_out, vfirst_out, vsecond_out,
    stat_out, bases_out, half_out,
    grad_v, stat_v, bases_v, kern_v, kfirst_v, ksecond_v, rows_v, first_v, second_v,
    work_v, kern_new, kfirst_new, ksecond_new, stat_new, bases_new, half_v, eout_v, egrad_v, nout_v, ngrad_v, spair_v, hpair_v, in_sem, out_sem, pass_sem,
):
    shard, width = kern_v.shape
    copies = [
        pltpu.make_async_copy(source, target, in_sem.at[i])
        for i, (source, target) in enumerate(
            [
                (bases_ref, bases_v), (stat_ref.at[pl.ds(0, PAIR)], stat_v), (grad_ref, grad_v),
                (work_ref, work_v.at[pl.ds(PAIR, PAIR)]), (kern_ref, kern_v), (kfirst_ref, kfirst_v),
                (ksecond_ref, ksecond_v), (rows_ref, rows_v), (first_ref, first_v), (second_ref, second_v),
            ]
        )
    ]
    passed = [
        (pltpu.make_async_copy(source, held, pass_sem.at[0, i]), pltpu.make_async_copy(held, target, pass_sem.at[1, i]))
        for i, (source, held, target) in enumerate(
            [
                (eout_ref, eout_v, eout_out), (egrad_ref, egrad_v, egrad_out),
                (nout_ref, nout_v, nout_out), (ngrad_ref, ngrad_v, ngrad_out),
                (spair_ref, spair_v, stat_out.at[pl.ds(PAIR, PAIR)]),
                (hpair_ref, hpair_v, half_out.at[pl.ds(4 * width, 3 * width)]),
            ]
        )
    ]
    outs = [
        pltpu.make_async_copy(source, target, out_sem.at[i])
        for i, (source, target) in enumerate(
            [
                (stat_new, stat_out.at[pl.ds(0, PAIR)]), (kern_new, kern_out), (kfirst_new, kfirst_out), (ksecond_new, ksecond_out),
                (half_v, half_out.at[pl.ds(0, 4 * width)]), (bases_new, bases_out),
            ]
        )
    ]
    for copy in copies:
        copy.start()
    bases_new[...] = jnp.zeros_like(bases_new)
    for copy in copies[:3]:
        copy.wait()
    bounds = matrix_bounds(width)
    for k in range(PAIR):
        stat_new[k] = new_statistics(grad_v[bounds[k] : bounds[k + 1], :], stat_v[k])
    outs[0].start()
    for copy in copies[3:]:
        copy.wait()
    for copy, _ in passed:
        copy.start()
    for k in range(PAIR):
        work_v[k, 0:width, :], work_v[k, width:, :] = prepare_bases(stat_new[k], bases_v[k], k)

    def own_rows():
        first_row = lax.axis_index("fs") * shard
        grad = grad_v[pl.ds(pl.multiple_of(first_row, 64), shard), :]
        one = matrix_of(first_row, width)
        two = matrix_of(first_row + shard - 1, width)
        in_two = matrix_of(first_row + iota((shard, width), 0), width) != one
        basis_one, basis_two = bases_v[one], bases_v[two]
        rotated = jnp.where(in_two, turn(grad, basis_two), turn(grad, basis_one))
        kfirst_new[...], ksecond_new[...], step = adam_step(kfirst_v[...], ksecond_v[...], rotated)
        turned = jnp.where(in_two, dot_three(step, basis_two), dot_three(step, basis_one))
        kern_new[...] = decayed(kern_v[...], turned)

    def all_rows(k):
        rows = slice(bounds[k], bounds[k + 1])
        half_v[rows, :] = rounded_rows(grad_v[rows, :], bases_v[k], rows_v[rows, :], first_v[rows, :], second_v[rows, :])

    def vector_rows():
        first, second, step = adam_step(vfirst_ref[...], vsecond_ref[...], gvec_ref[0:6, :])
        vfirst_out[...], vsecond_out[...] = first, second
        vec_out[...] = vec_ref[...] - RATE_VECTOR * step

    def beside(b):
        if b < PAIR:
            all_rows(b)
        elif b == PAIR:
            own_rows()
        elif b == PAIR + 2:
            vector_rows()
            for arrived, leaving in passed:
                arrived.wait()
                leaving.start()
            for copy in outs[1:5]:
                copy.start()

    orthogonalize(work_v, bases_new, width, beside)
    outs[5].start()
    for copy in outs + [leaving for _, leaving in passed]:
        copy.wait()


def update_call(grad, stat, bases, kern, kfirst, ksecond, rows, first, second, gvec, vec, vfirst, vsecond, work, *through):
    shard, width = kern.shape
    whole, anywhere = pl.BlockSpec(memory_space=pltpu.VMEM), pl.BlockSpec(memory_space=pl.ANY)

    def like(array):
        return jax.ShapeDtypeStruct(array.shape, array.dtype)

    def held(array):
        return pltpu.VMEM(array.shape, array.dtype)

    pair = jax.ShapeDtypeStruct((PAIR,) + stat.shape[1:], F32)
    four = jax.ShapeDtypeStruct((4 * width, width), BF16)
    loaded = (grad, stat, bases, kern, kfirst, ksecond, rows, first, second)
    return pl.pallas_call(
        update_kernel,
        out_shape=tuple(map(like, through[:4]))
        + (like(kern), like(kern), like(kern), like(vec), like(vec), like(vec), like(stat), like(stat), like(grad)),
        in_specs=[anywhere] * 9 + [whole] * 4 + [anywhere] * 7,
        out_specs=(anywhere,) * 7 + (whole,) * 3 + (anywhere,) * 3,
        scratch_shapes=[held(array) for array in (grad, pair, *loaded[2:])]
        + [pltpu.VMEM((COUNT, 2 * width, width), F32)]
        + [held(array) for array in (kern, kern, kern, pair, stat, four, *through)]
        + [pltpu.SemaphoreType.DMA((10,)), pltpu.SemaphoreType.DMA((6,)), pltpu.SemaphoreType.DMA((2, 6))],
        compiler_params=pltpu.CompilerParams(vmem_limit_bytes=VMEM_LIMIT),
        name="update",
    )(*loaded, gvec, vec, vfirst, vsecond, work, *through)


def on_device(
    edge_latent, node_latent, edge_cot, node_cot, five_flag, senders, send_rows, kernels, kernel_first, kernel_second,
    vectors, vector_first, vector_second, statistics, bases,
):
    samples, nodes, width = node_latent.shape
    slots = senders.shape[0] // nodes
    z = Sizes(samples, nodes, slots, send_rows.shape[1], width)
    edge_out, edge_grad, node_out, node_grad, grad, gvec, rows, first, second, stat_pair, work, half_pair = round_call(
        z,
        lax.axis_size("nodes"),
        edge_latent.reshape(-1, width),
        edge_cot.reshape(-1, width),
        node_latent.reshape(-1, width),
        node_cot.reshape(-1, width),
        five_flag.reshape(1, -1),
        senders.reshape(-1, LANES),
        send_rows,
        kernels,
        kernel_first,
        kernel_second,
        vectors,
        statistics,
        bases,
    )
    edge_out, edge_grad, node_out, node_grad, *rest = update_call(
        grad, statistics, bases, kernels, kernel_first, kernel_second, rows, first, second, gvec,
        vectors, vector_first, vector_second, work, edge_out, edge_grad, node_out, node_grad, stat_pair, half_pair,
    )
    return (
        edge_out.reshape(edge_latent.shape),
        node_out.reshape(node_latent.shape),
        edge_grad.reshape(edge_latent.shape),
        node_grad.reshape(node_latent.shape),
        *rest,
    )


def solution(mesh):
    in_specs = (
        P("fs", "nodes", None),
        P("fs", "nodes", None),
        P("fs", "nodes", None),
        P("fs", "nodes", None),
        P("nodes"),
        P("nodes"),
        P("nodes", None),
        P("fs", None),
        P("fs", None),
        P("fs", None),
        P(),
        P(),
        P(),
        P(),
        P(),
    )
    out_specs = (
        P("fs", "nodes", None),
        P("fs", "nodes", None),
        P("fs", "nodes", None),
        P("fs", "nodes", None),
        P("fs", None),
        P("fs", None),
        P("fs", None),
        P(),
        P(),
        P(),
        P(),
        P(),
        P(),
    )
    return jax.shard_map(
        on_device, mesh=mesh, in_specs=in_specs, out_specs=out_specs, check_vma=False
    )
```

```python
from functools import partial

import jax
import jax.numpy as jnp
from jax import lax
from jax.experimental import pallas as pl
from jax.experimental.pallas import tpu as pltpu
from jax.sharding import PartitionSpec as P

STEP = 5

NORM_EPS = 1e-05
BETA_ONE = 0.5
BETA_TWO = 0.5
RATE_MATRIX = 0.05
RATE_VECTOR = 0.2
DECAY_RATE = 0.01
ADAM_EPS = 1e-08
TINY = 1e-37
HIGH = lax.Precision.HIGHEST
F32 = jnp.float32
BF16 = jnp.bfloat16
LANES = 128
VMEM_LIMIT = 61 * 1024 * 1024


def dot_nn(left, right):
    return lax.dot_general(left, right, (((1,), (0,)), ((), ())), preferred_element_type=F32)


def dot_nt(left, right):
    return lax.dot_general(left, right, (((1,), (1,)), ((), ())), preferred_element_type=F32)


def dot_tn(left, right):
    return lax.dot_general(left, right, (((0,), (0,)), ((), ())), preferred_element_type=F32)


def split(value):
    high = value.astype(BF16)
    return high, (value - high.astype(F32)).astype(BF16)


def iota(shape, dim):
    return lax.broadcasted_iota(jnp.int32, shape, dim)


def ones_where(mask):
    return jnp.where(mask, 1.0, 0.0).astype(BF16)


def fold_rows(value):
    rows, width = value.shape
    return jnp.sum(value.reshape(rows // 8, 8, width), 0)


def aligned(index, step):
    return pl.ds(pl.multiple_of(index * step, step), step)


class Sizes:
    def __init__(self, samples, nodes, slots, halo, width):
        self.samples, self.nodes, self.slots = samples, nodes, slots
        self.halo, self.width = halo, width
        self.edges = nodes * slots
        self.fwd_nodes, self.bwd_nodes = 64, 128
        self.fwd_rows = self.fwd_nodes * slots
        self.bwd_rows = self.bwd_nodes * slots
        self.fwd_chunks = nodes // self.fwd_nodes
        self.bwd_chunks = nodes // self.bwd_nodes


def main_scratch(z):
    rows, width = z.samples * z.edges, z.width
    per_node = z.samples * z.nodes
    per_halo = z.samples * 2 * z.halo
    return dict(
        edge_v=pltpu.VMEM((rows, width), BF16),
        cot_v=pltpu.VMEM((rows, width), BF16),
        edge_out_v=pltpu.VMEM((rows, width), BF16),
        act_v=pltpu.VMEM((rows, width), BF16),
        slope_v=pltpu.VMEM((rows, width), F32),
        norm_v=pltpu.VMEM((rows, width), BF16),
        inv_v=pltpu.VMEM((rows, LANES), F32),
        own_v=pltpu.VMEM((z.edges, z.nodes), BF16),
        scat_v=pltpu.VMEM((z.bwd_chunks, z.nodes + 2 * z.halo + LANES, z.bwd_rows), BF16),
        sel_v=pltpu.VMEM((z.edges, 2 * LANES), BF16),
        rep_v=pltpu.VMEM((z.bwd_rows, 2 * LANES), BF16),
        live_v=pltpu.VMEM((z.edges, LANES), F32),
        half_v=pltpu.VMEM((7 * width, width), BF16),
        pown_v=pltpu.VMEM((per_node, width), BF16),
        psel_v=pltpu.VMEM((z.samples * z.fwd_chunks * 2 * LANES, width), BF16),
        gath_v=pltpu.VMEM((per_node, width), BF16),
        drep_v=pltpu.VMEM((z.samples * z.bwd_chunks * 2 * LANES, width), BF16),
        recv_v=pltpu.VMEM((per_node, width), F32),
        aown_v=pltpu.VMEM((per_node, width), F32),
        ahalo_v=pltpu.VMEM((per_halo, width), F32),
        table_v=pltpu.VMEM((per_halo, width), BF16),
        gmat_v=pltpu.VMEM((7 * width, width), F32),
        vsum_v=pltpu.VMEM((6 * 8, width), F32),
        pre_v=pltpu.VMEM((2, z.fwd_rows, width), F32),
        raw_v=pltpu.VMEM((2, z.fwd_rows, width), F32),
        upd_v=pltpu.VMEM((2, z.fwd_rows, width), BF16),
        dout_v=pltpu.VMEM((2, z.bwd_rows, width), BF16),
        dpre_v=pltpu.VMEM((2, z.bwd_rows, width), BF16),
        dall_v=pltpu.VMEM((rows, width), BF16),
        ncot_v=pltpu.VMEM((per_node, width), BF16),
        total_v=pltpu.VMEM((per_node, width), F32),
        rows_v=pltpu.VMEM((7 * width, width), BF16),
        first_v=pltpu.VMEM((7 * width, width), BF16),
        second_v=pltpu.VMEM((7 * width, width), BF16),
        list_v=pltpu.VMEM((2, z.samples * z.halo, width), BF16),
        halo_v=pltpu.VMEM((2, z.samples * z.halo, width), BF16),
        border_v=pltpu.VMEM((2, z.samples * z.halo, width), BF16),
        ret_v=pltpu.VMEM((2, z.samples * z.halo, width), BF16),
        gout_v=pltpu.VMEM((7 * width, width), BF16),
        edge_sem=pltpu.SemaphoreType.DMA((z.samples,)),
        cot_sem=pltpu.SemaphoreType.DMA((z.samples,)),
        eout_sem=pltpu.SemaphoreType.DMA((z.samples,)),
        egrad_sem=pltpu.SemaphoreType.DMA((z.samples,)),
        stat_v=pltpu.VMEM((PAIR, width, width), F32),
        bases_v=pltpu.VMEM((PAIR, width, width), F32),
        node_v=pltpu.VMEM((per_node, width), BF16),
        nout_v=pltpu.VMEM((per_node, width), BF16),
        ngrad_v=pltpu.VMEM((per_node, width), BF16),
        snew_v=pltpu.VMEM((PAIR, width, width), F32),
        work_v=pltpu.VMEM((PAIR, 2 * width, width), F32),
        hnew_v=pltpu.VMEM((3 * width, width), BF16),
        list_ids=pltpu.VMEM((2, z.halo), jnp.int32),
        five_v=pltpu.VMEM((1, z.nodes), jnp.int32),
        send_ids=pltpu.VMEM((z.edges // LANES, LANES), jnp.int32),
        vec_v=pltpu.VMEM((6, width), F32),
        gvec_v=pltpu.VMEM((8, width), F32),
        local_sem=pltpu.SemaphoreType.DMA((11,)),
        out_sem=pltpu.SemaphoreType.DMA((11,)),
        rows_sem=pltpu.SemaphoreType.DMA((2, 12)),
        first_sem=pltpu.SemaphoreType.DMA((2, 3)),
        second_sem=pltpu.SemaphoreType.DMA((2, 3)),
        halo_sem=pltpu.SemaphoreType.DMA((2, 2)),
        ret_sem=pltpu.SemaphoreType.DMA((2, 2)),
    )


def build_selectors(z, m, five_ref, send_ref):
    halo, nodes, slots = z.halo, z.nodes, z.slots
    lane = iota((LANES, LANES), 1)
    row = iota((LANES, LANES), 0)
    for g in range(z.edges // LANES):
        rows = slice(g * LANES, (g + 1) * LANES)
        line = jnp.broadcast_to(send_ref[g : g + 1, :].astype(F32), (LANES, LANES))
        column = line.T.astype(jnp.int32)
        for h in range(nodes // LANES):
            m.own_v[rows, h * LANES : (h + 1) * LANES] = ones_where(column == lane + (halo + h * LANES))
        place = jnp.where(column < halo, column, jnp.where(column >= halo + nodes, column - nodes, -1))
        in_halo = (place == (lane & (2 * halo - 1))) & (lane < 4 * halo)
        first = slots * (lane & (z.fwd_nodes - 1))
        local = row + (g * LANES) % z.fwd_rows
        m.sel_v[rows, 0:LANES] = ones_where((first <= local) & (local < first + slots))
        m.sel_v[rows, LANES : 2 * LANES] = ones_where(in_halo)
    place = iota((nodes + 2 * halo, z.bwd_rows), 0)
    place = jnp.where(place < nodes, place + halo, jnp.where(place < nodes + halo, place - nodes, place))
    first = slots * iota((LANES, z.bwd_rows), 0)
    local = iota((LANES, z.bwd_rows), 1)
    rep_t = ones_where((first <= local) & (local < first + slots))
    for c in range(z.bwd_chunks):
        lines = range(c * z.bwd_rows // LANES, (c + 1) * z.bwd_rows // LANES)
        senders = jnp.concatenate([send_ref[g : g + 1, :] for g in lines], 1)
        senders = jnp.broadcast_to(senders, place.shape)
        m.scat_v[c, 0 : nodes + 2 * halo, :] = ones_where(senders == place)
        m.scat_v[c, nodes + 2 * halo :, :] = rep_t
    first = slots * (iota((z.bwd_rows, 2 * LANES), 1) & (LANES - 1))
    local = iota((z.bwd_rows, 2 * LANES), 0)
    rep = ones_where((first <= local) & (local < first + slots))
    m.rep_v[...] = rep
    local = iota((z.bwd_rows, LANES), 0).astype(F32)
    slot = local - slots * jnp.floor((local + 0.5) * (1.0 / slots))
    for h in range(nodes // LANES):
        five = jnp.broadcast_to(five_ref[:, h * LANES : (h + 1) * LANES].astype(F32), (LANES, LANES)).T
        spread = dot_nn(rep[:, :LANES], five.astype(BF16))
        m.live_v[h * z.bwd_rows : (h + 1) * z.bwd_rows, :] = jnp.where(slot < slots - spread, 1.0, 0.0)


def both(column):
    return jnp.concatenate([column, column], 1)


def row_mean(value):
    return jnp.sum(value, -1, keepdims=True) * (1.0 / value.shape[-1])


def centred(value):
    centre = value - row_mean(value)
    return centre, lax.rsqrt(row_mean(centre * centre) + NORM_EPS)


def act_and_slope(half):
    turn = jnp.tanh(half)
    above = 1.0 + turn
    act = half * above
    return act, above + act * (1.0 - turn)


MESH = pl.DeviceIdType.MESH


def greet(partners):
    barrier = pltpu.get_barrier_semaphore()
    count = 0
    for device, exists in partners:
        if exists is None:
            pl.semaphore_signal(barrier, inc=1, device_id=device, device_id_type=MESH)
            count = count + 1
        else:
            pl.when(exists)(partial(pl.semaphore_signal, barrier, inc=1, device_id=device, device_id_type=MESH))
            count = count + exists.astype(jnp.int32)
    return lambda: pl.semaphore_wait(barrier, count)


def send(source, target, sems, slot, device):
    return pltpu.make_async_remote_copy(
        src_ref=source, dst_ref=target, send_sem=sems.at[0, slot], recv_sem=sems.at[1, slot],
        device_id=device, device_id_type=MESH,
    )


class Gather:
    def __init__(self, rows_v, sems, shard, fs, node):
        self.rows_v, self.sems, self.shard, self.fs = rows_v, sems, shard, fs
        self.parts = sems.shape[1] // 3
        self.next, self.far = (fs ^ 1, node), (fs ^ 2, node)

    def piece(self, owner, part):
        size = self.shard // self.parts
        return self.rows_v.at[pl.ds(pl.multiple_of(owner * self.shard + part * size, 16), size)]

    def copy(self, owner, part, slot, device):
        return send(self.piece(owner, part), self.piece(owner, part), self.sems, slot * self.parts + part, device)

    def start(self):
        for part in range(self.parts):
            self.copy(self.fs, part, 0, self.far).start()
        for part in range(self.parts):
            self.copy(self.fs, part, 1, self.next).start()

    def forward(self):
        for part in range(self.parts):
            self.copy(self.fs, part, 0, self.far).wait_recv()
            self.copy(self.fs ^ 2, part, 2, self.next).start()

    def finish(self):
        for part in range(self.parts):
            self.copy(self.fs, part, 0, self.far).wait_send()
            self.copy(self.fs, part, 1, self.next).wait()
            self.copy(self.fs ^ 2, part, 2, self.next).wait()


def list_matrix(send_ref, side, nodes):
    halo = send_ref.shape[1]
    listed = jnp.broadcast_to(send_ref[side : side + 1, :], (nodes, halo))
    return ones_where(listed == iota((nodes, halo), 0))


def sides(node, count):
    return ((node - 1, node > 0), (node + 1, node < count - 1))


class Cube:
    def __init__(self, count, fs=None, node=None):
        bits = count.bit_length() - 1
        self.node_bits = min(2, bits)
        self.size = 2 << self.node_bits
        self.extra = list(range(self.node_bits, bits))
        self.fs, self.node = fs, node
        if fs is not None:
            self.me = (fs >> 1) + 2 * (node & ((1 << self.node_bits) - 1))
        self.far_first = sorted(range(1, self.size), key=lambda r: (-r.bit_count(), -r))

    def device(self, r):
        return self.fs ^ (2 * (r & 1)), self.node ^ (r >> 1)

    def over(self, bit):
        return self.fs, self.node ^ (1 << bit)


def tree_sum(parts):
    while len(parts) > 1:
        parts = [left + right for left, right in zip(parts[::2], parts[1::2], strict=True)]
    return parts[0]


class Reduce:
    def __init__(self, cube, first, rows, sum_v, out_v, buffers):
        self.cube, self.sum_v, self.out_v = cube, sum_v, out_v
        self.give_v, self.land_v, self.near_v, self.cube_v, self.acc_v, self.extra_v, self.sems = buffers
        self.half = rows // 2
        self.size = self.half // cube.size
        core = cube.fs & 1
        self.keep, self.give = first + core * self.half, first + (1 - core) * self.half
        self.twin = (cube.fs ^ 1, cube.node)
        self.order = cube.far_first + [0]
        self.started = []

    @staticmethod
    def scratch(cube, rows, width):
        half, extra = rows // 2, max(2 * len(cube.extra), 1)
        size = half // cube.size
        return [
            pltpu.VMEM((half, width), BF16),
            pltpu.VMEM((half, width), BF16),
            pltpu.VMEM((half, width), BF16),
            pltpu.VMEM((cube.size, size, width), BF16),
            pltpu.VMEM((size, width), F32),
            pltpu.VMEM((extra, size, width), BF16),
            pltpu.SemaphoreType.DMA((2, 4 * cube.size + extra)),
        ]

    def rows(self, r, base=0):
        return pl.ds(pl.multiple_of(base + (self.cube.me ^ r) * self.size, 16), self.size)

    def launch(self, source, target, slot, device):
        copy = send(source, target, self.sems, slot, device)
        copy.start()
        self.started.append(copy)
        return copy

    def begin(self):
        self.core = {}
        for r in self.order:
            part = self.give_v.at[self.rows(r)]
            part[...] = self.sum_v[self.rows(r, self.give), :].astype(BF16)
            self.core[r] = self.launch(part, self.land_v.at[self.rows(r)], r, self.twin)

    def spread(self):
        self.near = {}
        for r in self.order:
            self.core[r].wait_recv()
            total = self.sum_v[self.rows(r, self.keep), :] + self.land_v[self.rows(r), :].astype(F32)
            if r:
                part = self.near_v.at[self.rows(r)]
                part[...] = total.astype(BF16)
                self.near[r] = self.launch(part, self.cube_v.at[r], self.cube.size + r, self.cube.device(r))
            else:
                self.acc_v[...] = total

    def meet(self):
        total = self.acc_v[...]
        for r in reversed(self.cube.far_first):
            self.near[r].wait_recv()
            total = total + self.cube_v[r].astype(F32)
        self.far = None
        if self.cube.extra:
            self.exchange(total, 0)
        else:
            self.acc_v[...] = total

    def exchange(self, total, e):
        self.extra_v[2 * e] = total.astype(BF16)
        self.far = self.launch(
            self.extra_v.at[2 * e], self.extra_v.at[2 * e + 1], 4 * self.cube.size + e, self.cube.over(self.cube.extra[e])
        )

    def settle(self):
        total = self.acc_v[...]
        for e in range(len(self.cube.extra)):
            self.far.wait_recv()
            total = self.extra_v[2 * e].astype(F32) + self.extra_v[2 * e + 1].astype(F32)
            if e + 1 < len(self.cube.extra):
                self.exchange(total, e + 1)
        own = self.out_v.at[self.rows(0, self.keep)]
        own[...] = total.astype(BF16)
        size = self.cube.size
        self.back = {r: self.launch(own, own, 2 * size + r, self.cube.device(r)) for r in self.cube.far_first}
        self.last = [self.launch(own, own, 3 * size, self.twin)]

    def forward(self):
        for r in reversed(self.cube.far_first):
            self.back[r].wait_recv()
            part = self.out_v.at[self.rows(r, self.keep)]
            self.last.append(self.launch(part, part, 3 * self.cube.size + r, self.twin))

    def arrive(self):
        for copy in self.last:
            copy.wait_recv()

    def end(self):
        for copy in self.started:
            copy.wait_send()


class VectorSum:
    def __init__(self, cube, send_v, land_v, sems):
        self.cube, self.send_v, self.land_v, self.sems = cube, send_v, land_v, sems
        self.started = []

    @staticmethod
    def scratch(cube, shape):
        extra = len(cube.extra)
        return [
            pltpu.VMEM((2 + extra,) + shape, F32),
            pltpu.VMEM((cube.size + extra,) + shape, F32),
            pltpu.SemaphoreType.DMA((2, cube.size + extra)),
        ]

    def launch(self, source, slot, device):
        copy = send(self.send_v.at[source], self.land_v.at[slot], self.sems, slot, device)
        copy.start()
        self.started.append(copy)
        return copy

    def begin(self, value):
        self.send_v[0] = value
        self.core = self.launch(0, 0, (self.cube.fs ^ 1, self.cube.node))

    def spread(self):
        self.core.wait_recv()
        self.send_v[1] = self.send_v[0] + self.land_v[0]
        self.near = [self.launch(1, r, self.cube.device(r)) for r in range(1, self.cube.size)]

    def meet(self):
        for copy in self.near:
            copy.wait_recv()
        self.total = tree_sum([self.send_v[1]] + [self.land_v[r] for r in range(1, self.cube.size)])
        self.far = self.exchange(0) if self.cube.extra else None

    def exchange(self, e):
        self.send_v[2 + e] = self.total
        return self.launch(2 + e, self.cube.size + e, self.cube.over(self.cube.extra[e]))

    def settle(self):
        for e in range(len(self.cube.extra)):
            self.far.wait_recv()
            self.total = self.total + self.land_v[self.cube.size + e]
            if e + 1 < len(self.cube.extra):
                self.far = self.exchange(e + 1)
        return self.total

    def end(self):
        for copy in self.started:
            copy.wait_send()


BLOCK = 32
COUNT = 4
PAIR = 2
AHEAD = 4
HALF = LANES // BLOCK


def wide_left(value):
    high, low = split(value)
    return jnp.concatenate([high, high, low], 1)


def wide_right(value):
    high, low = split(value)
    return jnp.concatenate([high, low, high], 1)


def dot_three(left, right):
    return dot_nt(wide_left(left), wide_right(right))


def factor_block(packed):
    sub = iota((8, LANES), 0)
    lane = iota((8, LANES), 1)
    tiles = BLOCK // 8
    group = lane & (LANES - BLOCK)
    plain = [packed[8 * r : 8 * r + 8, :] for r in range(tiles)]
    columns = {}

    def take_columns(panel):
        for l in range(8 * panel, 8 * panel + 8):
            columns[l] = [None] * panel + [jnp.take_along_axis(part, group + l, axis=1) for part in plain[panel:]]

    take_columns(0)
    inverse = [jnp.where((lane & (BLOCK - 1)) == sub + 8 * r, 1.0, 0.0) for r in range(tiles)]

    def line(tile, s):
        return jnp.broadcast_to(tile[s : s + 1, :], (8, LANES))

    for j in range(BLOCK):
        rj, sj = j // 8, j % 8
        scale = lax.rsqrt(line(columns[j][rj], sj))
        below = [None if r < rj else columns[j][r] * scale for r in range(tiles)]
        below[rj] = jnp.where(sub > sj, below[rj], 0.0)
        for l in [l for l in columns if l > j]:
            weight = line(below[l // 8], l % 8)
            for r in range(l // 8, tiles):
                columns[l][r] = columns[l][r] - below[r] * weight
        if j < BLOCK - 8 - AHEAD:
            row = line(plain[rj], sj) * scale
            for r in range(rj, tiles):
                plain[r] = plain[r] - below[r] * row
        if j % 8 == 7 - AHEAD and j < BLOCK - 8:
            take_columns(rj + 1)
        row = line(inverse[rj], sj) * scale
        inverse[rj] = jnp.where(sub == sj, row, inverse[rj] - below[rj] * row)
        for r in range(rj + 1, tiles):
            inverse[r] = inverse[r] - below[r] * row
    return jnp.concatenate(inverse, 0)


def turned_blocks(k, width):
    return [h * HALF + (g - k) % HALF for h in range(width // LANES) for g in range(HALF)]


def pick_rows(value, blocks):
    return jnp.concatenate([value[i * BLOCK : (i + 1) * BLOCK, :] for i in blocks], 0)


def orthogonalize(work_v, bases_out, width, beside):
    blocks = width // BLOCK
    group = iota((BLOCK, LANES), 1) // BLOCK
    square = iota((LANES, LANES), 0) // BLOCK == iota((LANES, LANES), 1) // BLOCK

    def placed(values, b):
        return [jnp.where(group == (b + k) % COUNT, values[k], jnp.zeros_like(values[k])) for k in range(COUNT)]

    def lanes_of(b):
        return slice(b // HALF * LANES, (b // HALF + 1) * LANES)

    def rows_of(b):
        return slice(b * BLOCK, (b + 1) * BLOCK)

    packed = sum(placed([work_v[k, rows_of(0), lanes_of(0)] for k in range(COUNT)], 0))
    for b in range(blocks):
        beside(b)
        lanes, after = lanes_of(b), (b + 1) * BLOCK
        high, low = split(factor_block(packed))
        whole_high = high.astype(F32)
        next_high, next_low = pltpu.roll(whole_high, BLOCK, 1), pltpu.roll(low.astype(F32), 2 * BLOCK, 1)
        high, low = placed([high] * COUNT, b), placed([low] * COUNT, b)
        if b < blocks - 1:
            spread_high, spread_low = jnp.concatenate(high, 0), jnp.concatenate(low, 0)
            spread = jnp.concatenate([spread_high, spread_low, spread_high], 1)
            ahead = jnp.concatenate([work_v[k, rows_of(b + 1), lanes] for k in range(COUNT)], 0)
            turned = jnp.where(square, dot_nt(wide_left(ahead), spread), 0.0)
            order = [(g - b - 1) % COUNT for g in range(COUNT)]
            update = dot_nt(wide_left(turned), pick_rows(wide_right(turned), order))
            current = placed([work_v[k, rows_of(b + 1), lanes_of(b + 1)] for k in range(COUNT)], b + 1)
            packed = sum(current) - sum(update[rows_of(k), :] for k in range(COUNT))
        start = after // LANES * LANES
        for k in range(COUNT):
            below = work_v[k, after:, lanes]
            place = (iota(below.shape, 1) // BLOCK - b - k) & (HALF - 1)
            below = jnp.where(
                place == 1, pltpu.roll(below, BLOCK, 1), jnp.where(place == 2, pltpu.roll(below, 2 * BLOCK, 1), below)
            )
            below_high, below_low = split(below)
            below = jnp.where(place == 1, below_low, below_high)
            place = (group - b - k) & (HALF - 1)
            factor = jnp.where(
                place == 0, whole_high, jnp.where(place == 1, next_high, jnp.where(place == 2, next_low, 0.0))
            ).astype(BF16)
            turned = dot_nt(below, jnp.concatenate([factor] * HALF, 0))
            mine = iota((width, LANES), 1) // BLOCK == b % HALF
            bases_out[k, :, lanes] = jnp.where(mine, turned[width - after :, :], bases_out[k, :, lanes])
            if b == blocks - 1:
                continue
            turned_high, turned_low = split(turned)
            part = iota(turned.shape, 1) // BLOCK
            zero = jnp.zeros_like(turned_high)
            left = jnp.where(part == 2, turned_low, jnp.where(part == 3, zero, turned_high))
            right = jnp.where(part == 1, turned_low, jnp.where(part == 3, zero, turned_high))
            right = jnp.concatenate(
                [
                    right[(i - b - 1) * BLOCK : (i - b) * BLOCK, :] if i > b else zero[0:BLOCK, :]
                    for i in turned_blocks(k, width)[start // BLOCK :]
                ],
                0,
            )
            work_v[k, after:, start:] -= dot_nt(left, right)


def matrix_bounds(width):
    return [0, 3 * width, 4 * width, 6 * width, 7 * width]


def new_statistics(rows, stat):
    return BETA_TWO * stat + (1.0 - BETA_TWO) * dot_tn(rows, rows)


def matrix_of(row, width):
    return sum((row >= bound).astype(jnp.int32) for bound in matrix_bounds(width)[1:-1])


def prepare_bases(stat, basis, k):
    width = stat.shape[-1]
    order = turned_blocks(k, width)
    flipped = basis.T
    proj_rows = dot_three(flipped, stat)
    gram = dot_three(proj_rows, pick_rows(proj_rows, order))
    return gram, dot_three(stat, pick_rows(flipped, order))


def adam_step(first, second, rotated):
    first = BETA_ONE * first + (1.0 - BETA_ONE) * rotated
    second = BETA_TWO * second + (1.0 - BETA_TWO) * rotated * rotated
    square = second * (1.0 / (1.0 - BETA_TWO**STEP))
    root = square * lax.rsqrt(jnp.maximum(square, TINY))
    return first, second, first * (1.0 / (1.0 - BETA_ONE**STEP)) * (1.0 / (root + ADAM_EPS))


def turn(rows, basis):
    high, low = split(basis)
    return dot_nn(rows, high) + dot_nn(rows, low)


def decayed(kern, turned):
    return kern - RATE_MATRIX * (turned + DECAY_RATE * kern)


def rounded_rows(grad, basis, kern, first, second):
    _, _, step = adam_step(first.astype(F32), second.astype(F32), turn(grad, basis))
    return decayed(kern.astype(F32), dot_nt(step.astype(BF16), basis.astype(BF16))).astype(BF16)


def round_kernel(
    z, names, count, edge_ref, cot_ref, node_hbm, ncot_ref, five_hbm, send_hbm, list_hbm, kern_ref, kfirst_ref, ksecond_ref,
    vec_hbm, stat_ref, bases_ref, eout_ref, egrad_ref, nout_hbm, ngrad_hbm, grad_ref, gvec_hbm, rows_ref, first_ref, second_ref,
    stat_hbm, work_hbm, half_hbm, *scratch,
):
    m = type("Held", (), {})()
    for name, ref in zip(names, scratch[: len(names)], strict=True):
        setattr(m, name, ref)
    spare = scratch[len(names) :]
    fs, node_id = lax.axis_index("fs"), lax.axis_index("nodes")
    cube = Cube(count, fs, node_id)
    around = sides(node_id, count)
    shard = kern_ref.shape[0]
    width, nodes, edges, samples, halo = z.width, z.nodes, z.edges, z.samples, z.halo
    two_halo = 2 * halo

    def sample_copy(source, target, sem, s):
        rows = aligned(s, edges)
        return pltpu.make_async_copy(source.at[rows], target.at[rows], sem.at[s])

    weight_ref = m.rows_v
    mine = pl.ds(pl.multiple_of(fs * shard, 16), shard)
    staged = [pl.ds(i * shard, shard) for i in range(3)]
    locals_in = [
        pltpu.make_async_copy(source, target, m.local_sem.at[i])
        for i, (source, target) in enumerate(
            [
                (kern_ref, m.slope_v.at[staged[0]]), (node_hbm, m.node_v), (list_hbm, m.list_ids), (five_hbm, m.five_v),
                (send_hbm, m.send_ids), (vec_hbm, m.vec_v), (kfirst_ref, m.slope_v.at[staged[1]]),
                (ksecond_ref, m.slope_v.at[staged[2]]), (ncot_ref, m.ncot_v),
                (stat_ref.at[pl.ds(PAIR, PAIR)], m.stat_v), (bases_ref.at[pl.ds(PAIR, PAIR)], m.bases_v),
            ]
        )
    ]
    node_ref, nout_ref, ngrad_ref = m.node_v, m.nout_v, m.ngrad_v
    list_ref, five_ref, send_ref, vec_ref = m.list_ids, m.five_v, m.send_ids, m.vec_v
    stat_out, work_out, half_out = m.snew_v, m.work_v, m.hnew_v

    def start_out(i, source, target):
        copy = pltpu.make_async_copy(source, target, m.out_sem.at[i])
        copy.start()
        outs.append(copy)

    outs = []
    gather = Gather(weight_ref, m.rows_sem, shard, fs, node_id)
    moments = [Gather(m.first_v, m.first_sem, shard, fs, node_id), Gather(m.second_v, m.second_sem, shard, fs, node_id)]
    for copy in locals_in[:6]:
        copy.start()
    m.halo_v[...] = jnp.zeros_like(m.halo_v)
    m.ret_v[...] = jnp.zeros_like(m.ret_v)
    all_in = greet(
        [(gather.next, None)]
        + [(cube.device(r), None) for r in range(1, cube.size)]
        + [(cube.over(bit), None) for bit in cube.extra]
        + [((fs, other), exists) for other, exists in around]
    )
    locals_in[0].wait()
    weight_ref[mine, :] = m.slope_v[staged[0], :].astype(BF16)
    all_in()
    gather.start()
    for copy in locals_in[6:]:
        copy.start()
    for s in range(samples):
        sample_copy(edge_ref, m.edge_v, m.edge_sem, s).start()
    for s in range(samples):
        sample_copy(cot_ref, m.cot_v, m.cot_sem, s).start()

    def to_side(source, target, sems, side, other):
        return send(source.at[side], target.at[1 - side], sems, side, (fs, other))

    def start_sides(source, target, sems):
        for side, (other, exists) in enumerate(around):
            pl.when(exists)(lambda side=side, other=other: to_side(source, target, sems, side, other).start())

    def finish_sides(source, target, sems):
        for side, (other, exists) in enumerate(around):
            def settle(side=side, other=other):
                to_side(source, target, sems, side, other).wait_send()
                to_side(source, target, sems, 1 - side, other).wait_recv()
            pl.when(exists)(settle)

    for copy in locals_in[1:6]:
        copy.wait()
    for side in range(2):
        chosen = list_matrix(list_ref, side, nodes)
        for s in range(samples):
            m.list_v[side, s * halo : (s + 1) * halo, :] = dot_tn(
                chosen, node_ref[s * nodes : (s + 1) * nodes, :]
            ).astype(BF16)
    start_sides(m.list_v, m.halo_v, m.halo_sem)
    build_selectors(z, m, five_ref, send_ref)
    gather.forward()
    gather.finish()
    finish_sides(m.list_v, m.halo_v, m.halo_sem)
    start_out(0, weight_ref, rows_ref)
    for copy in locals_in[6:]:
        copy.wait()
    for k, (moment, held) in enumerate(zip(moments, (m.first_v, m.second_v), strict=True)):
        held[mine, :] = m.slope_v[staged[k + 1], :].astype(BF16)
        moment.start()
    m.half_v[...] = weight_ref[...] * jnp.asarray(0.5, BF16)
    m.gmat_v[...] = jnp.zeros_like(m.gmat_v)
    m.vsum_v[...] = jnp.zeros_like(m.vsum_v)
    m.aown_v[...] = jnp.zeros_like(m.aown_v)
    m.ahalo_v[...] = jnp.zeros_like(m.ahalo_v)
    for s in range(samples):
        for side in range(2):
            m.table_v[s * two_halo + side * halo : s * two_halo + (side + 1) * halo, :] = m.halo_v[
                side, s * halo : (s + 1) * halo, :
            ]

    send_half = m.half_v[width : 2 * width, :]
    recv_half = m.half_v[2 * width : 3 * width, :]
    bias_edge, gain_edge, shift_edge = vec_ref[0:1, :] * 0.5, vec_ref[1:2, :], vec_ref[2:3, :]
    bias_node, gain_node, shift_node = vec_ref[3:4, :] * 0.5, vec_ref[4:5, :], vec_ref[5:6, :]

    for s in range(samples):
        node = node_ref[s * nodes : (s + 1) * nodes, :]
        m.pown_v[s * nodes : (s + 1) * nodes, :] = dot_nn(node, send_half).astype(BF16)
        high, low = split(dot_nn(node, recv_half) + bias_edge)
        out_high, out_low = split(dot_nn(m.table_v[s * two_halo : (s + 1) * two_halo, :], send_half))
        zero = jnp.zeros((2 * LANES - 2 * z.fwd_nodes - 2 * two_halo, width), BF16)
        for c in range(z.fwd_chunks):
            own = slice(c * z.fwd_nodes, (c + 1) * z.fwd_nodes)
            base = (s * z.fwd_chunks + c) * 2 * LANES
            m.psel_v[base : base + 2 * LANES, :] = jnp.concatenate(
                [high[own], low[own], out_high, out_low, zero], 0
            )

    per = z.fwd_chunks
    last = samples * per - 1

    def join_edges(i, slot):
        s, c = i // per, i % per
        local = aligned(c, z.fwd_rows)
        left = jnp.concatenate([m.edge_v[aligned(i, z.fwd_rows), :], m.own_v[local, :], m.sel_v[local, :]], 1)
        right = jnp.concatenate(
            [m.half_v[0:width, :], m.pown_v[aligned(s, nodes), :], m.psel_v[aligned(i, 2 * LANES), :]], 0
        )
        m.pre_v[slot] = dot_nn(left, right)

    def activate(i, slot):
        rows = aligned(i, z.fwd_rows)
        act, slope = act_and_slope(m.pre_v[slot])
        act = act.astype(BF16)
        m.act_v[rows, :] = act
        m.slope_v[rows, :] = slope
        m.raw_v[slot] = dot_nn(act, weight_ref[3 * width : 4 * width, :])

    def update_edges(i, slot):
        rows, local = aligned(i, z.fwd_rows), aligned(i % per, z.fwd_rows)
        centre, inv = centred(m.raw_v[slot])
        live = m.live_v[local, :]
        inv = inv * live
        m.inv_v[rows, :] = inv
        normed = centre * both(inv)
        m.norm_v[rows, :] = normed.astype(BF16)
        update = normed * gain_edge + both(live) * shift_edge
        m.edge_out_v[rows, :] = (m.edge_v[rows, :].astype(F32) + update).astype(BF16)
        m.upd_v[slot] = update.astype(BF16)

    def gather_updates(i, slot):
        take = slice(nodes + two_halo, nodes + two_halo + z.fwd_nodes)
        gathered = dot_nn(m.scat_v[0, take, 0 : z.fwd_rows], m.upd_v[slot])
        m.gath_v[aligned(i, z.fwd_nodes), :] = gathered.astype(BF16)

    def edge_in(s):
        return sample_copy(edge_ref, m.edge_v, m.edge_sem, s)

    edge_in(0).wait()
    join_edges(0, 0)

    def forward(s, carry):
        pl.when(s < samples - 1)(lambda: edge_in(s + 1).wait())
        for c in range(per):
            i = s * per + c
            join_edges(jnp.minimum(i + 1, last), (c + 1) % 2)
            gather_updates(jnp.maximum(i - 2, 0), c % 2)
            activate(i, c % 2)
            update_edges(jnp.maximum(i - 1, 0), (c + 1) % 2)
        pl.when(s > 0)(lambda: sample_copy(m.edge_out_v, eout_ref, m.eout_sem, s - 1).start())
        return carry

    lax.fori_loop(0, samples, forward, 0)
    gather_updates(last - 1, 0)
    update_edges(last, 1)
    gather_updates(last, 1)
    sample_copy(m.edge_out_v, eout_ref, m.eout_sem, samples - 1).start()

    def node_part(i, carry):
        rows = aligned(i, 2 * nodes)
        node, gath = node_ref[rows, :], m.gath_v[rows, :]
        joined = jnp.concatenate([node, gath], 1)
        act, slope = act_and_slope(dot_nn(joined, m.half_v[4 * width : 6 * width, :]) + bias_node)
        act = act.astype(BF16)
        centre, inv = centred(dot_nn(act, weight_ref[6 * width : 7 * width, :]))
        normed = centre * inv
        nout_ref[rows, :] = (node.astype(F32) + normed * gain_node + shift_node).astype(BF16)
        back = m.ncot_v[rows, :].astype(F32)
        back_normed = back * normed
        scaled, scaled_normed = back * gain_node, back_normed * gain_node
        d_out = (inv * (scaled - row_mean(scaled) - normed * row_mean(scaled_normed))).astype(BF16)
        m.gmat_v[6 * width : 7 * width, :] += dot_tn(act, d_out)
        m.vsum_v[32:40, :] += fold_rows(back_normed)
        m.vsum_v[40:48, :] += fold_rows(back)
        d_pre = dot_nt(d_out, m.half_v[6 * width : 7 * width, :]) * slope
        d_pre = d_pre.astype(BF16)
        m.vsum_v[24:32, :] += fold_rows(d_pre.astype(F32))
        m.gmat_v[4 * width : 6 * width, :] += dot_tn(joined, d_pre)
        d_joined = dot_nt(d_pre, weight_ref[4 * width : 6 * width, :])
        m.total_v[rows, :] = back + d_joined[:, :width]
        high, low = split(d_joined[:, width:])
        for k in range(2):
            for c in range(z.bwd_chunks):
                own = slice(k * nodes + c * z.bwd_nodes, k * nodes + (c + 1) * z.bwd_nodes)
                m.drep_v[aligned((i * 2 + k) * z.bwd_chunks + c, 2 * LANES), :] = jnp.concatenate(
                    [high[own], low[own]], 0
                )
        return carry

    lax.fori_loop(0, samples // 2, node_part, 0)

    halves = z.bwd_rows // z.fwd_rows
    pairs = samples * z.bwd_chunks

    def spread_back(i, slot):
        half = slice((slot % halves) * z.fwd_rows, (slot % halves + 1) * z.fwd_rows)
        m.pre_v[slot] = dot_nn(m.rep_v[half, :], m.drep_v[aligned(i // halves, 2 * LANES), :])

    def norm_back(i, slot, pair):
        rows, local = aligned(i, z.fwd_rows), aligned(i % per, z.fwd_rows)
        d_update = (m.cot_v[rows, :].astype(F32) + m.pre_v[slot]) * both(m.live_v[local, :])
        normed = m.norm_v[rows, :].astype(F32)
        d_normed = d_update * normed
        m.vsum_v[8:16, :] += fold_rows(d_normed)
        m.vsum_v[16:24, :] += fold_rows(d_update)
        scaled, scaled_normed = d_update * gain_edge, d_normed * gain_edge
        d_out = both(m.inv_v[rows, :]) * (scaled - row_mean(scaled) - normed * row_mean(scaled_normed))
        m.dout_v[pair, slot * z.fwd_rows : (slot + 1) * z.fwd_rows, :] = d_out.astype(BF16)

    def activate_back(i, slot, pair):
        part = slice(slot * z.fwd_rows, (slot + 1) * z.fwd_rows)
        d_act = dot_nt(m.dout_v[pair, part, :], m.half_v[3 * width : 4 * width, :])
        d_pre = (d_act * m.slope_v[aligned(i, z.fwd_rows), :]).astype(BF16)
        m.dpre_v[pair, part, :] = d_pre
        m.dall_v[aligned(i, z.fwd_rows), :] = d_pre

    def weights_back(p, pair):
        s, c = p // z.bwd_chunks, p % z.bwd_chunks
        rows = aligned(p, z.bwd_rows)
        d_out, d_pre = m.dout_v[pair], m.dpre_v[pair]
        m.gmat_v[3 * width : 4 * width, :] += dot_tn(m.act_v[rows, :], d_out)
        sums = dot_nn(jnp.concatenate([m.edge_v[rows, :].T, m.scat_v[c]], 0), d_pre)
        m.gmat_v[0:width, :] += sums[0:width, :]
        sums = sums[width:, :]
        m.aown_v[aligned(s, nodes), :] += sums[0:nodes, :]
        m.ahalo_v[aligned(s, two_halo), :] += sums[nodes : nodes + two_halo, :]
        m.recv_v[aligned(p, z.bwd_nodes), :] = sums[nodes + two_halo :, :]

    m.dout_v[1] = jnp.zeros_like(m.dout_v[1])
    m.dpre_v[1] = jnp.zeros_like(m.dpre_v[1])
    spread_back(0, 0)

    def backward(s, carry):
        sample_copy(cot_ref, m.cot_v, m.cot_sem, s).wait()
        for k in range(z.bwd_chunks):
            p = s * z.bwd_chunks + k
            i = p * halves
            spread_back(i + 1, 1)
            activate_back(jnp.maximum(i - 1, 0), 1, 1 - k)
            norm_back(i, 0, k)
            weights_back(jnp.maximum(p - 1, 0), 1 - k)
            spread_back(jnp.minimum(i + 2, last), 0)
            activate_back(i, 0, k)
            norm_back(i + 1, 1, k)
        return carry

    nodes_sum = Reduce(cube, 4 * width, 3 * width, m.gmat_v, m.gout_v, spare[7:14])
    nodes_sum.begin()
    start_out(1, nout_ref, nout_hbm)
    lax.fori_loop(0, 1, backward, 0)
    nodes_sum.spread()
    lax.fori_loop(1, samples, backward, 0)
    activate_back(last, 1, 1)
    weights_back(pairs - 1, 1)

    def edge_gradient(s, carry):
        for c in range(per):
            rows = aligned(s * per + c, z.fwd_rows)
            d_edge = dot_nt(m.dall_v[rows, :], weight_ref[0:width, :])
            m.edge_out_v[rows, :] = (m.cot_v[rows, :].astype(F32) + d_edge).astype(BF16)
        sample_copy(m.edge_out_v, egrad_ref, m.egrad_sem, s).start()
        return carry

    send_full = weight_ref[width : 2 * width, :]
    recv_full = weight_ref[2 * width : 3 * width, :]
    table = m.table_v[...]
    out_high, out_low = split(m.ahalo_v[...])
    nodes_all = node_ref[...]
    grad_send = dot_tn(table, out_high) + dot_tn(nodes_all, m.aown_v[...].astype(BF16))
    grad_recv = dot_tn(nodes_all, m.recv_v[...].astype(BF16))
    m.gmat_v[width : 2 * width, :] = grad_send
    m.gmat_v[2 * width : 3 * width, :] = grad_recv
    reduce = Reduce(cube, 0, 4 * width, m.gmat_v, m.gout_v, spare[:7])
    vectors = VectorSum(cube, *spare[14:])
    reduce.begin()
    nodes_sum.meet()
    border = (dot_nt(out_high, send_full) + dot_nt(out_low, send_full)).astype(BF16)
    for s in range(samples):
        for side in range(2):
            m.border_v[side, s * halo : (s + 1) * halo, :] = border[
                s * two_halo + side * halo : s * two_halo + (side + 1) * halo, :
            ]
    start_sides(m.border_v, m.ret_v, m.ret_sem)
    for s in range(samples):
        m.vsum_v[0:8, :] += fold_rows(m.recv_v[s * nodes : (s + 1) * nodes, :])
    vectors.begin(
        jnp.concatenate(
            [jnp.sum(m.vsum_v[k * 8 : (k + 1) * 8, :], 0, keepdims=True) for k in range(6)]
            + [jnp.zeros((2, width), F32)],
            0,
        )
    )
    reduce.spread()
    vectors.spread()
    for moment in moments:
        moment.forward()
    for s in range(samples):
        sample_copy(m.edge_out_v, eout_ref, m.eout_sem, s).wait()
    lax.fori_loop(0, samples, edge_gradient, 0)
    nodes_sum.settle()
    for s in range(samples):
        rows = slice(s * nodes, (s + 1) * nodes)
        recv_high, recv_low = split(m.recv_v[rows, :])
        own_high, own_low = split(m.aown_v[rows, :])
        m.total_v[rows, :] += (
            dot_nt(recv_high, recv_full) + dot_nt(recv_low, recv_full)
            + dot_nt(own_high, send_full) + dot_nt(own_low, send_full)
        )
    reduce.meet()
    vectors.meet()
    nodes_sum.forward()
    finish_sides(m.border_v, m.ret_v, m.ret_sem)
    low, high = (list_matrix(list_ref, side, nodes) for side in range(2))
    for s in range(samples):
        rows, part = slice(s * nodes, (s + 1) * nodes), slice(s * halo, (s + 1) * halo)
        ngrad_ref[rows, :] = (
            m.total_v[rows, :] + dot_nn(low, m.ret_v[0, part, :]) + dot_nn(high, m.ret_v[1, part, :])
        ).astype(BF16)
    start_out(2, ngrad_ref, ngrad_hbm)
    reduce.settle()
    m.gvec_v[...] = vectors.settle()
    start_out(10, m.gvec_v, gvec_hbm)
    nodes_sum.arrive()
    bounds = matrix_bounds(width)
    for k in range(PAIR):
        stat_out[k] = new_statistics(m.gout_v[bounds[PAIR + k] : bounds[PAIR + k + 1], :], m.stat_v[k])
    start_out(5, m.gout_v.at[pl.ds(4 * width, 3 * width)], grad_ref.at[pl.ds(4 * width, 3 * width)])
    start_out(6, stat_out, stat_hbm)
    for k in range(PAIR):
        work_out[k, 0:width, :], work_out[k, width:, :] = prepare_bases(stat_out[k], m.bases_v[k], PAIR + k)
    start_out(7, work_out, work_hbm)
    for moment in moments:
        moment.finish()
    start_out(3, m.first_v.at[pl.ds(0, 4 * width)], first_ref)
    start_out(4, m.second_v.at[pl.ds(0, 4 * width)], second_ref)
    for k in range(PAIR):
        low, high = bounds[PAIR + k], bounds[PAIR + k + 1]
        half_out[low - 4 * width : high - 4 * width, :] = rounded_rows(
            m.gout_v[low:high, :], m.bases_v[k], weight_ref[low:high, :], m.first_v[low:high, :], m.second_v[low:high, :]
        )
    start_out(8, half_out, half_hbm)
    for s in range(samples):
        sample_copy(m.edge_out_v, egrad_ref, m.egrad_sem, s).wait()
    for copy in outs:
        copy.wait()
    reduce.forward()
    reduce.arrive()
    grad_out = pltpu.make_async_copy(m.gout_v.at[pl.ds(0, 4 * width)], grad_ref.at[pl.ds(0, 4 * width)], m.out_sem.at[9])
    grad_out.start()
    reduce.end()
    nodes_sum.end()
    vectors.end()
    grad_out.wait()


def round_call(z, count, edge, cot, node, ncot, five, senders, send_rows, kern, kfirst, ksecond, vectors, stat, bases):
    shard, width = kern.shape
    scratch = main_scratch(z)
    cube = Cube(count)
    spare = Reduce.scratch(cube, 4 * width, width) + Reduce.scratch(cube, 3 * width, width) + VectorSum.scratch(cube, (8, width))
    rows, per_node = z.samples * z.edges, z.samples * z.nodes
    anywhere = pl.BlockSpec(memory_space=pl.ANY)
    total = jax.ShapeDtypeStruct((7 * width, width), BF16)
    moments = jax.ShapeDtypeStruct((4 * width, width), BF16)
    return pl.pallas_call(
        partial(round_kernel, z, tuple(scratch), count),
        out_shape=(
            jax.ShapeDtypeStruct((rows, width), BF16),
            jax.ShapeDtypeStruct((rows, width), BF16),
            jax.ShapeDtypeStruct((per_node, width), BF16),
            jax.ShapeDtypeStruct((per_node, width), BF16),
            total,
            jax.ShapeDtypeStruct((8, width), F32),
            total, moments, moments,
            jax.ShapeDtypeStruct((PAIR, width, width), F32),
            jax.ShapeDtypeStruct((PAIR, 2 * width, width), F32),
            jax.ShapeDtypeStruct((3 * width, width), BF16),
        ),
        in_specs=[anywhere] * 13,
        out_specs=(anywhere,) * 12,
        scratch_shapes=list(scratch.values()) + spare,
        compiler_params=pltpu.CompilerParams(
            collective_id=0, has_side_effects=True, vmem_limit_bytes=VMEM_LIMIT
        ),
        name="edge_node_round",
    )(edge, cot, node, ncot, five, senders, send_rows, kern, kfirst, ksecond, vectors, stat, bases)


def update_kernel(
    grad_ref, stat_ref, bases_ref, kern_ref, kfirst_ref, ksecond_ref, rows_ref, first_ref, second_ref,
    gvec_hbm, vec_hbm, vfirst_hbm, vsecond_hbm, work_ref, eout_ref, egrad_ref, nout_ref, ngrad_ref, spair_ref, hpair_ref,
    eout_out, egrad_out, nout_out, ngrad_out, kern_out, kfirst_out, ksecond_out, vec_hout, vfirst_hout, vsecond_hout,
    stat_out, bases_out, half_out,
    grad_v, stat_v, bases_v, kern_v, kfirst_v, ksecond_v, rows_v, first_v, second_v,
    work_v, kern_new, kfirst_new, ksecond_new, stat_new, bases_new, half_v, eout_v, egrad_v, nout_v, ngrad_v, spair_v, hpair_v, gvec_ref, vec_ref, vfirst_ref, vsecond_ref,
    vec_out, vfirst_out, vsecond_out, in_sem, out_sem, pass_sem,
):
    shard, width = kern_v.shape
    copies = [
        pltpu.make_async_copy(source, target, in_sem.at[i])
        for i, (source, target) in enumerate(
            [
                (bases_ref, bases_v), (stat_ref.at[pl.ds(0, PAIR)], stat_v), (grad_ref, grad_v),
                (work_ref, work_v.at[pl.ds(PAIR, PAIR)]), (kern_ref, kern_v), (kfirst_ref, kfirst_v),
                (ksecond_ref, ksecond_v), (rows_ref, rows_v), (first_ref, first_v), (second_ref, second_v),
                (gvec_hbm, gvec_ref), (vec_hbm, vec_ref), (vfirst_hbm, vfirst_ref), (vsecond_hbm, vsecond_ref),
            ]
        )
    ]
    passed = [
        (pltpu.make_async_copy(source, held, pass_sem.at[0, i]), pltpu.make_async_copy(held, target, pass_sem.at[1, i]))
        for i, (source, held, target) in enumerate(
            [
                (eout_ref, eout_v, eout_out), (egrad_ref, egrad_v, egrad_out),
                (nout_ref, nout_v, nout_out), (ngrad_ref, ngrad_v, ngrad_out),
                (spair_ref, spair_v, stat_out.at[pl.ds(PAIR, PAIR)]),
                (hpair_ref, hpair_v, half_out.at[pl.ds(4 * width, 3 * width)]),
            ]
        )
    ]
    outs = [
        pltpu.make_async_copy(source, target, out_sem.at[i])
        for i, (source, target) in enumerate(
            [
                (stat_new, stat_out.at[pl.ds(0, PAIR)]), (kern_new, kern_out), (kfirst_new, kfirst_out), (ksecond_new, ksecond_out),
                (half_v, half_out.at[pl.ds(0, 4 * width)]), (vec_out, vec_hout), (vfirst_out, vfirst_hout),
                (vsecond_out, vsecond_hout), (bases_new, bases_out),
            ]
        )
    ]
    for copy in copies:
        copy.start()
    bases_new[...] = jnp.zeros_like(bases_new)
    for copy in copies[:3]:
        copy.wait()
    bounds = matrix_bounds(width)
    for k in range(PAIR):
        stat_new[k] = new_statistics(grad_v[bounds[k] : bounds[k + 1], :], stat_v[k])
    outs[0].start()
    for copy in copies[3:]:
        copy.wait()
    for copy, _ in passed:
        copy.start()
    for k in range(PAIR):
        work_v[k, 0:width, :], work_v[k, width:, :] = prepare_bases(stat_new[k], bases_v[k], k)

    def own_rows():
        first_row = lax.axis_index("fs") * shard
        grad = grad_v[pl.ds(pl.multiple_of(first_row, 64), shard), :]
        one = matrix_of(first_row, width)
        two = matrix_of(first_row + shard - 1, width)
        in_two = matrix_of(first_row + iota((shard, width), 0), width) != one
        basis_one, basis_two = bases_v[one], bases_v[two]
        rotated = jnp.where(in_two, turn(grad, basis_two), turn(grad, basis_one))
        kfirst_new[...], ksecond_new[...], step = adam_step(kfirst_v[...], ksecond_v[...], rotated)
        turned = jnp.where(in_two, dot_three(step, basis_two), dot_three(step, basis_one))
        kern_new[...] = decayed(kern_v[...], turned)

    def all_rows(k):
        rows = slice(bounds[k], bounds[k + 1])
        half_v[rows, :] = rounded_rows(grad_v[rows, :], bases_v[k], rows_v[rows, :], first_v[rows, :], second_v[rows, :])

    def vector_rows():
        first, second, step = adam_step(vfirst_ref[...], vsecond_ref[...], gvec_ref[0:6, :])
        vfirst_out[...], vsecond_out[...] = first, second
        vec_out[...] = vec_ref[...] - RATE_VECTOR * step

    def beside(b):
        if b < PAIR:
            all_rows(b)
        elif b == PAIR:
            own_rows()
        elif b == PAIR + 2:
            vector_rows()
            for arrived, leaving in passed:
                arrived.wait()
                leaving.start()
            for copy in outs[1:8]:
                copy.start()

    orthogonalize(work_v, bases_new, width, beside)
    outs[8].start()
    for copy in outs + [leaving for _, leaving in passed]:
        copy.wait()


def update_call(grad, stat, bases, kern, kfirst, ksecond, rows, first, second, gvec, vec, vfirst, vsecond, work, *through):
    shard, width = kern.shape
    anywhere = pl.BlockSpec(memory_space=pl.ANY)

    def like(array):
        return jax.ShapeDtypeStruct(array.shape, array.dtype)

    def held(array):
        return pltpu.VMEM(array.shape, array.dtype)

    pair = jax.ShapeDtypeStruct((PAIR,) + stat.shape[1:], F32)
    four = jax.ShapeDtypeStruct((4 * width, width), BF16)
    loaded = (grad, stat, bases, kern, kfirst, ksecond, rows, first, second)
    return pl.pallas_call(
        update_kernel,
        out_shape=tuple(map(like, through[:4]))
        + (like(kern), like(kern), like(kern), like(vec), like(vec), like(vec), like(stat), like(stat), like(grad)),
        in_specs=[anywhere] * 20,
        out_specs=(anywhere,) * 13,
        scratch_shapes=[held(array) for array in (grad, pair, *loaded[2:])]
        + [pltpu.VMEM((COUNT, 2 * width, width), F32)]
        + [held(array) for array in (kern, kern, kern, pair, stat, four, *through, gvec, vec, vec, vec, vec, vec, vec)]
        + [pltpu.SemaphoreType.DMA((14,)), pltpu.SemaphoreType.DMA((9,)), pltpu.SemaphoreType.DMA((2, 6))],
        compiler_params=pltpu.CompilerParams(vmem_limit_bytes=VMEM_LIMIT),
        name="update",
    )(*loaded, gvec, vec, vfirst, vsecond, work, *through)


def on_device(
    edge_latent, node_latent, edge_cot, node_cot, five_flag, senders, send_rows, kernels, kernel_first, kernel_second,
    vectors, vector_first, vector_second, statistics, bases,
):
    samples, nodes, width = node_latent.shape
    slots = senders.shape[0] // nodes
    z = Sizes(samples, nodes, slots, send_rows.shape[1], width)
    edge_out, edge_grad, node_out, node_grad, grad, gvec, rows, first, second, stat_pair, work, half_pair = round_call(
        z,
        lax.axis_size("nodes"),
        edge_latent.reshape(-1, width),
        edge_cot.reshape(-1, width),
        node_latent.reshape(-1, width),
        node_cot.reshape(-1, width),
        five_flag.reshape(1, -1),
        senders.reshape(-1, LANES),
        send_rows,
        kernels,
        kernel_first,
        kernel_second,
        vectors,
        statistics,
        bases,
    )
    edge_out, edge_grad, node_out, node_grad, *rest = update_call(
        grad, statistics, bases, kernels, kernel_first, kernel_second, rows, first, second, gvec,
        vectors, vector_first, vector_second, work, edge_out, edge_grad, node_out, node_grad, stat_pair, half_pair,
    )
    return (
        edge_out.reshape(edge_latent.shape),
        node_out.reshape(node_latent.shape),
        edge_grad.reshape(edge_latent.shape),
        node_grad.reshape(node_latent.shape),
        *rest,
    )


def solution(mesh):
    in_specs = (
        P("fs", "nodes", None),
        P("fs", "nodes", None),
        P("fs", "nodes", None),
        P("fs", "nodes", None),
        P("nodes"),
        P("nodes"),
        P("nodes", None),
        P("fs", None),
        P("fs", None),
        P("fs", None),
        P(),
        P(),
        P(),
        P(),
        P(),
    )
    out_specs = (
        P("fs", "nodes", None),
        P("fs", "nodes", None),
        P("fs", "nodes", None),
        P("fs", "nodes", None),
        P("fs", None),
        P("fs", None),
        P("fs", None),
        P(),
        P(),
        P(),
        P(),
        P(),
        P(),
    )
    return jax.shard_map(
        on_device, mesh=mesh, in_specs=in_specs, out_specs=out_specs, check_vma=False
    )
```

```python
from functools import partial

import jax
import jax.numpy as jnp
from jax import lax
from jax.experimental import pallas as pl
from jax.experimental.pallas import tpu as pltpu
from jax.sharding import PartitionSpec as P

STEP = 5

NORM_EPS = 1e-05
BETA_ONE = 0.5
BETA_TWO = 0.5
RATE_MATRIX = 0.05
RATE_VECTOR = 0.2
DECAY_RATE = 0.01
ADAM_EPS = 1e-08
TINY = 1e-37
HIGH = lax.Precision.HIGHEST
F32 = jnp.float32
BF16 = jnp.bfloat16
LANES = 128
VMEM_LIMIT = 61 * 1024 * 1024


def dot_nn(left, right):
    return lax.dot_general(left, right, (((1,), (0,)), ((), ())), preferred_element_type=F32)


def dot_nt(left, right):
    return lax.dot_general(left, right, (((1,), (1,)), ((), ())), preferred_element_type=F32)


def dot_tn(left, right):
    return lax.dot_general(left, right, (((0,), (0,)), ((), ())), preferred_element_type=F32)


def split(value):
    high = value.astype(BF16)
    return high, (value - high.astype(F32)).astype(BF16)


def iota(shape, dim):
    return lax.broadcasted_iota(jnp.int32, shape, dim)


def ones_where(mask):
    return jnp.where(mask, 1.0, 0.0).astype(BF16)


def fold_rows(value):
    rows, width = value.shape
    return jnp.sum(value.reshape(rows // 8, 8, width), 0)


def aligned(index, step):
    return pl.ds(pl.multiple_of(index * step, step), step)


class Sizes:
    def __init__(self, samples, nodes, slots, halo, width):
        self.samples, self.nodes, self.slots = samples, nodes, slots
        self.halo, self.width = halo, width
        self.edges = nodes * slots
        self.fwd_nodes, self.bwd_nodes = 64, 128
        self.fwd_rows = self.fwd_nodes * slots
        self.bwd_rows = self.bwd_nodes * slots
        self.fwd_chunks = nodes // self.fwd_nodes
        self.bwd_chunks = nodes // self.bwd_nodes


def main_scratch(z):
    rows, width = z.samples * z.edges, z.width
    per_node = z.samples * z.nodes
    per_halo = z.samples * 2 * z.halo
    return dict(
        edge_v=pltpu.VMEM((rows, width), BF16),
        cot_v=pltpu.VMEM((rows, width), BF16),
        edge_out_v=pltpu.VMEM((rows, width), BF16),
        act_v=pltpu.VMEM((rows, width), BF16),
        slope_v=pltpu.VMEM((rows, width), F32),
        norm_v=pltpu.VMEM((rows, width), BF16),
        inv_v=pltpu.VMEM((rows, LANES), F32),
        own_v=pltpu.VMEM((z.edges, z.nodes), BF16),
        scat_v=pltpu.VMEM((z.bwd_chunks, z.nodes + 2 * z.halo + LANES, z.bwd_rows), BF16),
        sel_v=pltpu.VMEM((z.edges, 2 * LANES), BF16),
        rep_v=pltpu.VMEM((z.bwd_rows, 2 * LANES), BF16),
        live_v=pltpu.VMEM((z.edges, LANES), F32),
        half_v=pltpu.VMEM((7 * width, width), BF16),
        pown_v=pltpu.VMEM((per_node, width), BF16),
        psel_v=pltpu.VMEM((z.samples * z.fwd_chunks * 2 * LANES, width), BF16),
        gath_v=pltpu.VMEM((per_node, width), BF16),
        drep_v=pltpu.VMEM((z.samples * z.bwd_chunks * 2 * LANES, width), BF16),
        recv_v=pltpu.VMEM((per_node, width), F32),
        aown_v=pltpu.VMEM((per_node, width), F32),
        ahalo_v=pltpu.VMEM((per_halo, width), F32),
        table_v=pltpu.VMEM((per_halo, width), BF16),
        gmat_v=pltpu.VMEM((7 * width, width), F32),
        vsum_v=pltpu.VMEM((6 * 8, width), F32),
        pre_v=pltpu.VMEM((2, z.fwd_rows, width), F32),
        raw_v=pltpu.VMEM((2, z.fwd_rows, width), F32),
        upd_v=pltpu.VMEM((2, z.fwd_rows, width), BF16),
        dout_v=pltpu.VMEM((2, z.bwd_rows, width), BF16),
        dpre_v=pltpu.VMEM((2, z.bwd_rows, width), BF16),
        dall_v=pltpu.VMEM((rows, width), BF16),
        ncot_v=pltpu.VMEM((per_node, width), BF16),
        total_v=pltpu.VMEM((per_node, width), F32),
        rows_v=pltpu.VMEM((7 * width, width), BF16),
        first_v=pltpu.VMEM((7 * width, width), BF16),
        second_v=pltpu.VMEM((7 * width, width), BF16),
        list_v=pltpu.VMEM((2, z.samples * z.halo, width), BF16),
        halo_v=pltpu.VMEM((2, z.samples * z.halo, width), BF16),
        border_v=pltpu.VMEM((2, z.samples * z.halo, width), BF16),
        ret_v=pltpu.VMEM((2, z.samples * z.halo, width), BF16),
        gout_v=pltpu.VMEM((7 * width, width), BF16),
        edge_sem=pltpu.SemaphoreType.DMA((z.samples,)),
        cot_sem=pltpu.SemaphoreType.DMA((z.samples,)),
        eout_sem=pltpu.SemaphoreType.DMA((z.samples,)),
        egrad_sem=pltpu.SemaphoreType.DMA((z.samples,)),
        stat_v=pltpu.VMEM((PAIR, width, width), F32),
        bases_v=pltpu.VMEM((PAIR, width, width), F32),
        node_v=pltpu.VMEM((per_node, width), BF16),
        nout_v=pltpu.VMEM((per_node, width), BF16),
        ngrad_v=pltpu.VMEM((per_node, width), BF16),
        snew_v=pltpu.VMEM((PAIR, width, width), F32),
        work_v=pltpu.VMEM((PAIR, 2 * width, width), F32),
        hnew_v=pltpu.VMEM((3 * width, width), BF16),
        list_ids=pltpu.VMEM((2, z.halo), jnp.int32),
        five_v=pltpu.VMEM((1, z.nodes), jnp.int32),
        send_ids=pltpu.VMEM((z.edges // LANES, LANES), jnp.int32),
        vec_v=pltpu.VMEM((6, width), F32),
        gvec_v=pltpu.VMEM((8, width), F32),
        local_sem=pltpu.SemaphoreType.DMA((11,)),
        out_sem=pltpu.SemaphoreType.DMA((11,)),
        rows_sem=pltpu.SemaphoreType.DMA((2, 12)),
        first_sem=pltpu.SemaphoreType.DMA((2, 3)),
        second_sem=pltpu.SemaphoreType.DMA((2, 3)),
        halo_sem=pltpu.SemaphoreType.DMA((2, 2)),
        ret_sem=pltpu.SemaphoreType.DMA((2, 2)),
    )


def build_selectors(z, m, five_ref, send_ref):
    halo, nodes, slots = z.halo, z.nodes, z.slots
    lane = iota((LANES, LANES), 1)
    row = iota((LANES, LANES), 0)
    for g in range(z.edges // LANES):
        rows = slice(g * LANES, (g + 1) * LANES)
        line = jnp.broadcast_to(send_ref[g : g + 1, :].astype(F32), (LANES, LANES))
        column = line.T.astype(jnp.int32)
        for h in range(nodes // LANES):
            m.own_v[rows, h * LANES : (h + 1) * LANES] = ones_where(column == lane + (halo + h * LANES))
        place = jnp.where(column < halo, column, jnp.where(column >= halo + nodes, column - nodes, -1))
        in_halo = (place == (lane & (2 * halo - 1))) & (lane < 4 * halo)
        first = slots * (lane & (z.fwd_nodes - 1))
        local = row + (g * LANES) % z.fwd_rows
        m.sel_v[rows, 0:LANES] = ones_where((first <= local) & (local < first + slots))
        m.sel_v[rows, LANES : 2 * LANES] = ones_where(in_halo)
    place = iota((nodes + 2 * halo, z.bwd_rows), 0)
    place = jnp.where(place < nodes, place + halo, jnp.where(place < nodes + halo, place - nodes, place))
    first = slots * iota((LANES, z.bwd_rows), 0)
    local = iota((LANES, z.bwd_rows), 1)
    rep_t = ones_where((first <= local) & (local < first + slots))
    for c in range(z.bwd_chunks):
        lines = range(c * z.bwd_rows // LANES, (c + 1) * z.bwd_rows // LANES)
        senders = jnp.concatenate([send_ref[g : g + 1, :] for g in lines], 1)
        senders = jnp.broadcast_to(senders, place.shape)
        m.scat_v[c, 0 : nodes + 2 * halo, :] = ones_where(senders == place)
        m.scat_v[c, nodes + 2 * halo :, :] = rep_t
    first = slots * (iota((z.bwd_rows, 2 * LANES), 1) & (LANES - 1))
    local = iota((z.bwd_rows, 2 * LANES), 0)
    rep = ones_where((first <= local) & (local < first + slots))
    m.rep_v[...] = rep
    local = iota((z.bwd_rows, LANES), 0).astype(F32)
    slot = local - slots * jnp.floor((local + 0.5) * (1.0 / slots))
    for h in range(nodes // LANES):
        five = jnp.broadcast_to(five_ref[:, h * LANES : (h + 1) * LANES].astype(F32), (LANES, LANES)).T
        spread = dot_nn(rep[:, :LANES], five.astype(BF16))
        m.live_v[h * z.bwd_rows : (h + 1) * z.bwd_rows, :] = jnp.where(slot < slots - spread, 1.0, 0.0)


def both(column):
    return jnp.concatenate([column, column], 1)


def row_mean(value):
    return jnp.sum(value, -1, keepdims=True) * (1.0 / value.shape[-1])


def centred(value):
    centre = value - row_mean(value)
    return centre, lax.rsqrt(row_mean(centre * centre) + NORM_EPS)


def act_and_slope(half):
    turn = jnp.tanh(half)
    above = 1.0 + turn
    act = half * above
    return act, above + act * (1.0 - turn)


MESH = pl.DeviceIdType.MESH


def greet(partners):
    barrier = pltpu.get_barrier_semaphore()
    count = 0
    for device, exists in partners:
        if exists is None:
            pl.semaphore_signal(barrier, inc=1, device_id=device, device_id_type=MESH)
            count = count + 1
        else:
            pl.when(exists)(partial(pl.semaphore_signal, barrier, inc=1, device_id=device, device_id_type=MESH))
            count = count + exists.astype(jnp.int32)
    return lambda: pl.semaphore_wait(barrier, count)


def send(source, target, sems, slot, device):
    return pltpu.make_async_remote_copy(
        src_ref=source, dst_ref=target, send_sem=sems.at[0, slot], recv_sem=sems.at[1, slot],
        device_id=device, device_id_type=MESH,
    )


class Gather:
    def __init__(self, rows_v, sems, shard, fs, node):
        self.rows_v, self.sems, self.shard, self.fs = rows_v, sems, shard, fs
        self.parts = sems.shape[1] // 3
        self.next, self.far = (fs ^ 1, node), (fs ^ 2, node)

    def piece(self, owner, part):
        size = self.shard // self.parts
        return self.rows_v.at[pl.ds(pl.multiple_of(owner * self.shard + part * size, 16), size)]

    def copy(self, owner, part, slot, device):
        return send(self.piece(owner, part), self.piece(owner, part), self.sems, slot * self.parts + part, device)

    def start(self):
        for part in range(self.parts):
            self.copy(self.fs, part, 0, self.far).start()
        for part in range(self.parts):
            self.copy(self.fs, part, 1, self.next).start()

    def forward(self):
        for part in range(self.parts):
            self.copy(self.fs, part, 0, self.far).wait_recv()
            self.copy(self.fs ^ 2, part, 2, self.next).start()

    def finish(self):
        for part in range(self.parts):
            self.copy(self.fs, part, 0, self.far).wait_send()
            self.copy(self.fs, part, 1, self.next).wait()
            self.copy(self.fs ^ 2, part, 2, self.next).wait()


def list_matrix(send_ref, side, nodes):
    halo = send_ref.shape[1]
    listed = jnp.broadcast_to(send_ref[side : side + 1, :], (nodes, halo))
    return ones_where(listed == iota((nodes, halo), 0))


def sides(node, count):
    return ((node - 1, node > 0), (node + 1, node < count - 1))


class Cube:
    def __init__(self, count, fs=None, node=None):
        bits = count.bit_length() - 1
        self.node_bits = min(2, bits)
        self.size = 2 << self.node_bits
        self.extra = list(range(self.node_bits, bits))
        self.fs, self.node = fs, node
        if fs is not None:
            self.me = (fs >> 1) + 2 * (node & ((1 << self.node_bits) - 1))
        self.far_first = sorted(range(1, self.size), key=lambda r: (-r.bit_count(), -r))

    def device(self, r):
        return self.fs ^ (2 * (r & 1)), self.node ^ (r >> 1)

    def over(self, bit):
        return self.fs, self.node ^ (1 << bit)


def tree_sum(parts):
    while len(parts) > 1:
        parts = [left + right for left, right in zip(parts[::2], parts[1::2], strict=True)]
    return parts[0]


class Reduce:
    def __init__(self, cube, first, rows, sum_v, out_v, buffers):
        self.cube, self.sum_v, self.out_v = cube, sum_v, out_v
        self.give_v, self.land_v, self.near_v, self.cube_v, self.acc_v, self.extra_v, self.sems = buffers
        self.half = rows // 2
        self.size = self.half // cube.size
        core = cube.fs & 1
        self.keep, self.give = first + core * self.half, first + (1 - core) * self.half
        self.twin = (cube.fs ^ 1, cube.node)
        self.order = cube.far_first + [0]
        self.started = []

    @staticmethod
    def scratch(cube, rows, width):
        half, extra = rows // 2, max(2 * len(cube.extra), 1)
        size = half // cube.size
        return [
            pltpu.VMEM((half, width), BF16),
            pltpu.VMEM((half, width), BF16),
            pltpu.VMEM((half, width), BF16),
            pltpu.VMEM((cube.size, size, width), BF16),
            pltpu.VMEM((size, width), F32),
            pltpu.VMEM((extra, size, width), BF16),
            pltpu.SemaphoreType.DMA((2, 4 * cube.size + extra)),
        ]

    def rows(self, r, base=0):
        return pl.ds(pl.multiple_of(base + (self.cube.me ^ r) * self.size, 16), self.size)

    def launch(self, source, target, slot, device):
        copy = send(source, target, self.sems, slot, device)
        copy.start()
        self.started.append(copy)
        return copy

    def begin(self):
        self.core = {}
        for r in self.order:
            part = self.give_v.at[self.rows(r)]
            part[...] = self.sum_v[self.rows(r, self.give), :].astype(BF16)
            self.core[r] = self.launch(part, self.land_v.at[self.rows(r)], r, self.twin)

    def spread(self):
        self.near = {}
        for r in self.order:
            self.core[r].wait_recv()
            total = self.sum_v[self.rows(r, self.keep), :] + self.land_v[self.rows(r), :].astype(F32)
            if r:
                part = self.near_v.at[self.rows(r)]
                part[...] = total.astype(BF16)
                self.near[r] = self.launch(part, self.cube_v.at[r], self.cube.size + r, self.cube.device(r))
            else:
                self.acc_v[...] = total

    def meet(self):
        total = self.acc_v[...]
        for r in reversed(self.cube.far_first):
            self.near[r].wait_recv()
            total = total + self.cube_v[r].astype(F32)
        self.far = None
        if self.cube.extra:
            self.exchange(total, 0)
        else:
            self.acc_v[...] = total

    def exchange(self, total, e):
        self.extra_v[2 * e] = total.astype(BF16)
        self.far = self.launch(
            self.extra_v.at[2 * e], self.extra_v.at[2 * e + 1], 4 * self.cube.size + e, self.cube.over(self.cube.extra[e])
        )

    def settle(self):
        total = self.acc_v[...]
        for e in range(len(self.cube.extra)):
            self.far.wait_recv()
            total = self.extra_v[2 * e].astype(F32) + self.extra_v[2 * e + 1].astype(F32)
            if e + 1 < len(self.cube.extra):
                self.exchange(total, e + 1)
        own = self.out_v.at[self.rows(0, self.keep)]
        own[...] = total.astype(BF16)
        size = self.cube.size
        self.back = {r: self.launch(own, own, 2 * size + r, self.cube.device(r)) for r in self.cube.far_first}
        self.last = [self.launch(own, own, 3 * size, self.twin)]

    def forward(self):
        for r in reversed(self.cube.far_first):
            self.back[r].wait_recv()
            part = self.out_v.at[self.rows(r, self.keep)]
            self.last.append(self.launch(part, part, 3 * self.cube.size + r, self.twin))

    def arrive(self):
        for copy in self.last:
            copy.wait_recv()

    def end(self):
        for copy in self.started:
            copy.wait_send()


class VectorSum:
    def __init__(self, cube, send_v, land_v, sems):
        self.cube, self.send_v, self.land_v, self.sems = cube, send_v, land_v, sems
        self.started = []

    @staticmethod
    def scratch(cube, shape):
        extra = len(cube.extra)
        return [
            pltpu.VMEM((2 + extra,) + shape, F32),
            pltpu.VMEM((cube.size + extra,) + shape, F32),
            pltpu.SemaphoreType.DMA((2, cube.size + extra)),
        ]

    def launch(self, source, slot, device):
        copy = send(self.send_v.at[source], self.land_v.at[slot], self.sems, slot, device)
        copy.start()
        self.started.append(copy)
        return copy

    def begin(self, value):
        self.send_v[0] = value
        self.core = self.launch(0, 0, (self.cube.fs ^ 1, self.cube.node))

    def spread(self):
        self.core.wait_recv()
        self.send_v[1] = self.send_v[0] + self.land_v[0]
        self.near = [self.launch(1, r, self.cube.device(r)) for r in range(1, self.cube.size)]

    def meet(self):
        for copy in self.near:
            copy.wait_recv()
        self.total = tree_sum([self.send_v[1]] + [self.land_v[r] for r in range(1, self.cube.size)])
        self.far = self.exchange(0) if self.cube.extra else None

    def exchange(self, e):
        self.send_v[2 + e] = self.total
        return self.launch(2 + e, self.cube.size + e, self.cube.over(self.cube.extra[e]))

    def settle(self):
        for e in range(len(self.cube.extra)):
            self.far.wait_recv()
            self.total = self.total + self.land_v[self.cube.size + e]
            if e + 1 < len(self.cube.extra):
                self.far = self.exchange(e + 1)
        return self.total

    def end(self):
        for copy in self.started:
            copy.wait_send()


BLOCK = 32
COUNT = 4
PAIR = 2
AHEAD = 4
HALF = LANES // BLOCK


def wide_left(value):
    high, low = split(value)
    return jnp.concatenate([high, high, low], 1)


def wide_right(value):
    high, low = split(value)
    return jnp.concatenate([high, low, high], 1)


def dot_three(left, right):
    return dot_nt(wide_left(left), wide_right(right))


def factor_block(packed):
    sub = iota((8, LANES), 0)
    lane = iota((8, LANES), 1)
    tiles = BLOCK // 8
    group = lane & (LANES - BLOCK)
    plain = [packed[8 * r : 8 * r + 8, :] for r in range(tiles)]
    columns = {}

    def take_columns(panel):
        for l in range(8 * panel, 8 * panel + 8):
            columns[l] = [None] * panel + [jnp.take_along_axis(part, group + l, axis=1) for part in plain[panel:]]

    take_columns(0)
    inverse = [jnp.where((lane & (BLOCK - 1)) == sub + 8 * r, 1.0, 0.0) for r in range(tiles)]

    def line(tile, s):
        return jnp.broadcast_to(tile[s : s + 1, :], (8, LANES))

    for j in range(BLOCK):
        rj, sj = j // 8, j % 8
        scale = lax.rsqrt(line(columns[j][rj], sj))
        below = [None if r < rj else columns[j][r] * scale for r in range(tiles)]
        below[rj] = jnp.where(sub > sj, below[rj], 0.0)
        for l in [l for l in columns if l > j]:
            weight = line(below[l // 8], l % 8)
            for r in range(l // 8, tiles):
                columns[l][r] = columns[l][r] - below[r] * weight
        if j < BLOCK - 8 - AHEAD:
            row = line(plain[rj], sj) * scale
            for r in range(rj, tiles):
                plain[r] = plain[r] - below[r] * row
        if j % 8 == 7 - AHEAD and j < BLOCK - 8:
            take_columns(rj + 1)
        row = line(inverse[rj], sj) * scale
        inverse[rj] = jnp.where(sub == sj, row, inverse[rj] - below[rj] * row)
        for r in range(rj + 1, tiles):
            inverse[r] = inverse[r] - below[r] * row
    return jnp.concatenate(inverse, 0)


def turned_blocks(k, width):
    return [h * HALF + (g - k) % HALF for h in range(width // LANES) for g in range(HALF)]


def pick_rows(value, blocks):
    return jnp.concatenate([value[i * BLOCK : (i + 1) * BLOCK, :] for i in blocks], 0)


def orthogonalize(work_v, bases_out, width, beside):
    blocks = width // BLOCK
    group = iota((BLOCK, LANES), 1) // BLOCK
    square = iota((LANES, LANES), 0) // BLOCK == iota((LANES, LANES), 1) // BLOCK

    def placed(values, b):
        return [jnp.where(group == (b + k) % COUNT, values[k], jnp.zeros_like(values[k])) for k in range(COUNT)]

    def lanes_of(b):
        return slice(b // HALF * LANES, (b // HALF + 1) * LANES)

    def rows_of(b):
        return slice(b * BLOCK, (b + 1) * BLOCK)

    packed = sum(placed([work_v[k, rows_of(0), lanes_of(0)] for k in range(COUNT)], 0))
    for b in range(blocks):
        beside(b)
        lanes, after = lanes_of(b), (b + 1) * BLOCK
        high, low = split(factor_block(packed))
        whole_high = high.astype(F32)
        next_high, next_low = pltpu.roll(whole_high, BLOCK, 1), pltpu.roll(low.astype(F32), 2 * BLOCK, 1)
        high, low = placed([high] * COUNT, b), placed([low] * COUNT, b)
        if b < blocks - 1:
            spread_high, spread_low = jnp.concatenate(high, 0), jnp.concatenate(low, 0)
            spread = jnp.concatenate([spread_high, spread_low, spread_high], 1)
            ahead = jnp.concatenate([work_v[k, rows_of(b + 1), lanes] for k in range(COUNT)], 0)
            turned = jnp.where(square, dot_nt(wide_left(ahead), spread), 0.0)
            order = [(g - b - 1) % COUNT for g in range(COUNT)]
            update = dot_nt(wide_left(turned), pick_rows(wide_right(turned), order))
            current = placed([work_v[k, rows_of(b + 1), lanes_of(b + 1)] for k in range(COUNT)], b + 1)
            packed = sum(current) - sum(update[rows_of(k), :] for k in range(COUNT))
        start = after // LANES * LANES
        for k in range(COUNT):
            below = work_v[k, after:, lanes]
            place = (iota(below.shape, 1) // BLOCK - b - k) & (HALF - 1)
            below = jnp.where(
                place == 1, pltpu.roll(below, BLOCK, 1), jnp.where(place == 2, pltpu.roll(below, 2 * BLOCK, 1), below)
            )
            below_high, below_low = split(below)
            below = jnp.where(place == 1, below_low, below_high)
            place = (group - b - k) & (HALF - 1)
            factor = jnp.where(
                place == 0, whole_high, jnp.where(place == 1, next_high, jnp.where(place == 2, next_low, 0.0))
            ).astype(BF16)
            turned = dot_nt(below, jnp.concatenate([factor] * HALF, 0))
            mine = iota((width, LANES), 1) // BLOCK == b % HALF
            bases_out[k, :, lanes] = jnp.where(mine, turned[width - after :, :], bases_out[k, :, lanes])
            if b == blocks - 1:
                continue
            turned_high, turned_low = split(turned)
            part = iota(turned.shape, 1) // BLOCK
            zero = jnp.zeros_like(turned_high)
            left = jnp.where(part == 2, turned_low, jnp.where(part == 3, zero, turned_high))
            right = jnp.where(part == 1, turned_low, jnp.where(part == 3, zero, turned_high))
            right = jnp.concatenate(
                [
                    right[(i - b - 1) * BLOCK : (i - b) * BLOCK, :] if i > b else zero[0:BLOCK, :]
                    for i in turned_blocks(k, width)[start // BLOCK :]
                ],
                0,
            )
            work_v[k, after:, start:] -= dot_nt(left, right)


def matrix_bounds(width):
    return [0, 3 * width, 4 * width, 6 * width, 7 * width]


def new_statistics(rows, stat):
    return BETA_TWO * stat + (1.0 - BETA_TWO) * dot_tn(rows, rows)


def matrix_of(row, width):
    return sum((row >= bound).astype(jnp.int32) for bound in matrix_bounds(width)[1:-1])


def prepare_bases(stat, basis, k):
    width = stat.shape[-1]
    order = turned_blocks(k, width)
    flipped = basis.T
    proj_rows = dot_three(flipped, stat)
    gram = dot_three(proj_rows, pick_rows(proj_rows, order))
    return gram, dot_three(stat, pick_rows(flipped, order))


def adam_step(first, second, rotated):
    first = BETA_ONE * first + (1.0 - BETA_ONE) * rotated
    second = BETA_TWO * second + (1.0 - BETA_TWO) * rotated * rotated
    square = second * (1.0 / (1.0 - BETA_TWO**STEP))
    root = square * lax.rsqrt(jnp.maximum(square, TINY))
    return first, second, first * (1.0 / (1.0 - BETA_ONE**STEP)) * (1.0 / (root + ADAM_EPS))


def turn(rows, basis):
    high, low = split(basis)
    return dot_nn(rows, high) + dot_nn(rows, low)


def decayed(kern, turned):
    return kern - RATE_MATRIX * (turned + DECAY_RATE * kern)


def rounded_rows(grad, basis, kern, first, second):
    _, _, step = adam_step(first.astype(F32), second.astype(F32), turn(grad, basis))
    return decayed(kern.astype(F32), dot_nt(step.astype(BF16), basis.astype(BF16))).astype(BF16)


def round_kernel(
    z, names, count, edge_ref, cot_ref, node_hbm, ncot_ref, five_hbm, send_hbm, list_hbm, kern_ref, kfirst_ref, ksecond_ref,
    vec_hbm, stat_ref, bases_ref, eout_ref, egrad_ref, nout_hbm, ngrad_hbm, grad_ref, gvec_hbm, rows_ref, first_ref, second_ref,
    stat_hbm, work_hbm, half_hbm, *scratch,
):
    m = type("Held", (), {})()
    for name, ref in zip(names, scratch[: len(names)], strict=True):
        setattr(m, name, ref)
    spare = scratch[len(names) :]
    fs, node_id = lax.axis_index("fs"), lax.axis_index("nodes")
    cube = Cube(count, fs, node_id)
    around = sides(node_id, count)
    shard = kern_ref.shape[0]
    width, nodes, edges, samples, halo = z.width, z.nodes, z.edges, z.samples, z.halo
    two_halo = 2 * halo

    def sample_copy(source, target, sem, s):
        rows = aligned(s, edges)
        return pltpu.make_async_copy(source.at[rows], target.at[rows], sem.at[s])

    weight_ref = m.rows_v
    mine = pl.ds(pl.multiple_of(fs * shard, 16), shard)
    staged = [pl.ds(i * shard, shard) for i in range(3)]
    locals_in = [
        pltpu.make_async_copy(source, target, m.local_sem.at[i])
        for i, (source, target) in enumerate(
            [
                (kern_ref, m.slope_v.at[staged[0]]), (node_hbm, m.node_v), (list_hbm, m.list_ids), (five_hbm, m.five_v),
                (send_hbm, m.send_ids), (vec_hbm, m.vec_v), (kfirst_ref, m.slope_v.at[staged[1]]),
                (ksecond_ref, m.slope_v.at[staged[2]]), (ncot_ref, m.ncot_v),
                (stat_ref.at[pl.ds(PAIR, PAIR)], m.stat_v), (bases_ref.at[pl.ds(PAIR, PAIR)], m.bases_v),
            ]
        )
    ]
    node_ref, nout_ref, ngrad_ref = m.node_v, m.nout_v, m.ngrad_v
    list_ref, five_ref, send_ref, vec_ref = m.list_ids, m.five_v, m.send_ids, m.vec_v
    stat_out, work_out, half_out = m.snew_v, m.work_v, m.hnew_v

    def start_out(i, source, target):
        copy = pltpu.make_async_copy(source, target, m.out_sem.at[i])
        copy.start()
        outs.append(copy)

    outs = []
    gather = Gather(weight_ref, m.rows_sem, shard, fs, node_id)
    moments = [Gather(m.first_v, m.first_sem, shard, fs, node_id), Gather(m.second_v, m.second_sem, shard, fs, node_id)]
    for copy in locals_in[:6]:
        copy.start()
    m.halo_v[...] = jnp.zeros_like(m.halo_v)
    m.ret_v[...] = jnp.zeros_like(m.ret_v)
    all_in = greet(
        [(gather.next, None)]
        + [(cube.device(r), None) for r in range(1, cube.size)]
        + [(cube.over(bit), None) for bit in cube.extra]
        + [((fs, other), exists) for other, exists in around]
    )
    locals_in[0].wait()
    weight_ref[mine, :] = m.slope_v[staged[0], :].astype(BF16)
    all_in()
    gather.start()
    for copy in locals_in[6:]:
        copy.start()
    for s in range(samples):
        sample_copy(edge_ref, m.edge_v, m.edge_sem, s).start()
    for s in range(samples):
        sample_copy(cot_ref, m.cot_v, m.cot_sem, s).start()

    def to_side(source, target, sems, side, other):
        return send(source.at[side], target.at[1 - side], sems, side, (fs, other))

    def start_sides(source, target, sems):
        for side, (other, exists) in enumerate(around):
            pl.when(exists)(lambda side=side, other=other: to_side(source, target, sems, side, other).start())

    def finish_sides(source, target, sems):
        for side, (other, exists) in enumerate(around):
            def settle(side=side, other=other):
                to_side(source, target, sems, side, other).wait_send()
                to_side(source, target, sems, 1 - side, other).wait_recv()
            pl.when(exists)(settle)

    for copy in locals_in[1:6]:
        copy.wait()
    for side in range(2):
        chosen = list_matrix(list_ref, side, nodes)
        for s in range(samples):
            m.list_v[side, s * halo : (s + 1) * halo, :] = dot_tn(
                chosen, node_ref[s * nodes : (s + 1) * nodes, :]
            ).astype(BF16)
    start_sides(m.list_v, m.halo_v, m.halo_sem)
    build_selectors(z, m, five_ref, send_ref)
    gather.forward()
    gather.finish()
    finish_sides(m.list_v, m.halo_v, m.halo_sem)
    start_out(0, weight_ref, rows_ref)
    for copy in locals_in[6:]:
        copy.wait()
    for k, (moment, held) in enumerate(zip(moments, (m.first_v, m.second_v), strict=True)):
        held[mine, :] = m.slope_v[staged[k + 1], :].astype(BF16)
        moment.start()
    m.half_v[...] = weight_ref[...] * jnp.asarray(0.5, BF16)
    m.gmat_v[...] = jnp.zeros_like(m.gmat_v)
    m.vsum_v[...] = jnp.zeros_like(m.vsum_v)
    m.aown_v[...] = jnp.zeros_like(m.aown_v)
    m.ahalo_v[...] = jnp.zeros_like(m.ahalo_v)
    for s in range(samples):
        for side in range(2):
            m.table_v[s * two_halo + side * halo : s * two_halo + (side + 1) * halo, :] = m.halo_v[
                side, s * halo : (s + 1) * halo, :
            ]

    send_half = m.half_v[width : 2 * width, :]
    recv_half = m.half_v[2 * width : 3 * width, :]
    bias_edge, gain_edge, shift_edge = vec_ref[0:1, :] * 0.5, vec_ref[1:2, :], vec_ref[2:3, :]
    bias_node, gain_node, shift_node = vec_ref[3:4, :] * 0.5, vec_ref[4:5, :], vec_ref[5:6, :]

    for s in range(samples):
        node = node_ref[s * nodes : (s + 1) * nodes, :]
        m.pown_v[s * nodes : (s + 1) * nodes, :] = dot_nn(node, send_half).astype(BF16)
        high, low = split(dot_nn(node, recv_half) + bias_edge)
        out_high, out_low = split(dot_nn(m.table_v[s * two_halo : (s + 1) * two_halo, :], send_half))
        zero = jnp.zeros((2 * LANES - 2 * z.fwd_nodes - 2 * two_halo, width), BF16)
        for c in range(z.fwd_chunks):
            own = slice(c * z.fwd_nodes, (c + 1) * z.fwd_nodes)
            base = (s * z.fwd_chunks + c) * 2 * LANES
            m.psel_v[base : base + 2 * LANES, :] = jnp.concatenate(
                [high[own], low[own], out_high, out_low, zero], 0
            )

    per = z.fwd_chunks
    last = samples * per - 1

    def join_edges(i, slot):
        s, c = i // per, i % per
        local = aligned(c, z.fwd_rows)
        left = jnp.concatenate([m.edge_v[aligned(i, z.fwd_rows), :], m.own_v[local, :], m.sel_v[local, :]], 1)
        right = jnp.concatenate(
            [m.half_v[0:width, :], m.pown_v[aligned(s, nodes), :], m.psel_v[aligned(i, 2 * LANES), :]], 0
        )
        m.pre_v[slot] = dot_nn(left, right)

    def activate(i, slot):
        rows = aligned(i, z.fwd_rows)
        act, slope = act_and_slope(m.pre_v[slot])
        act = act.astype(BF16)
        m.act_v[rows, :] = act
        m.slope_v[rows, :] = slope
        m.raw_v[slot] = dot_nn(act, weight_ref[3 * width : 4 * width, :])

    def update_edges(i, slot):
        rows, local = aligned(i, z.fwd_rows), aligned(i % per, z.fwd_rows)
        centre, inv = centred(m.raw_v[slot])
        live = m.live_v[local, :]
        inv = inv * live
        m.inv_v[rows, :] = inv
        normed = centre * both(inv)
        m.norm_v[rows, :] = normed.astype(BF16)
        update = normed * gain_edge + both(live) * shift_edge
        m.edge_out_v[rows, :] = (m.edge_v[rows, :].astype(F32) + update).astype(BF16)
        m.upd_v[slot] = update.astype(BF16)

    def gather_updates(i, slot):
        take = slice(nodes + two_halo, nodes + two_halo + z.fwd_nodes)
        gathered = dot_nn(m.scat_v[0, take, 0 : z.fwd_rows], m.upd_v[slot])
        m.gath_v[aligned(i, z.fwd_nodes), :] = gathered.astype(BF16)

    def edge_in(s):
        return sample_copy(edge_ref, m.edge_v, m.edge_sem, s)

    edge_in(0).wait()
    join_edges(0, 0)

    def forward(s, carry):
        pl.when(s < samples - 1)(lambda: edge_in(s + 1).wait())
        for c in range(per):
            i = s * per + c
            join_edges(jnp.minimum(i + 1, last), (c + 1) % 2)
            gather_updates(jnp.maximum(i - 2, 0), c % 2)
            activate(i, c % 2)
            update_edges(jnp.maximum(i - 1, 0), (c + 1) % 2)
        pl.when(s > 0)(lambda: sample_copy(m.edge_out_v, eout_ref, m.eout_sem, s - 1).start())
        return carry

    lax.fori_loop(0, samples, forward, 0)
    gather_updates(last - 1, 0)
    update_edges(last, 1)
    gather_updates(last, 1)
    sample_copy(m.edge_out_v, eout_ref, m.eout_sem, samples - 1).start()

    def node_part(i, carry):
        rows = aligned(i, 2 * nodes)
        node, gath = node_ref[rows, :], m.gath_v[rows, :]
        joined = jnp.concatenate([node, gath], 1)
        act, slope = act_and_slope(dot_nn(joined, m.half_v[4 * width : 6 * width, :]) + bias_node)
        act = act.astype(BF16)
        centre, inv = centred(dot_nn(act, weight_ref[6 * width : 7 * width, :]))
        normed = centre * inv
        nout_ref[rows, :] = (node.astype(F32) + normed * gain_node + shift_node).astype(BF16)
        back = m.ncot_v[rows, :].astype(F32)
        back_normed = back * normed
        scaled, scaled_normed = back * gain_node, back_normed * gain_node
        d_out = (inv * (scaled - row_mean(scaled) - normed * row_mean(scaled_normed))).astype(BF16)
        m.gmat_v[6 * width : 7 * width, :] += dot_tn(act, d_out)
        m.vsum_v[32:40, :] += fold_rows(back_normed)
        m.vsum_v[40:48, :] += fold_rows(back)
        d_pre = dot_nt(d_out, m.half_v[6 * width : 7 * width, :]) * slope
        d_pre = d_pre.astype(BF16)
        m.vsum_v[24:32, :] += fold_rows(d_pre.astype(F32))
        m.gmat_v[4 * width : 6 * width, :] += dot_tn(joined, d_pre)
        d_joined = dot_nt(d_pre, weight_ref[4 * width : 6 * width, :])
        m.total_v[rows, :] = back + d_joined[:, :width]
        high, low = split(d_joined[:, width:])
        for k in range(2):
            for c in range(z.bwd_chunks):
                own = slice(k * nodes + c * z.bwd_nodes, k * nodes + (c + 1) * z.bwd_nodes)
                m.drep_v[aligned((i * 2 + k) * z.bwd_chunks + c, 2 * LANES), :] = jnp.concatenate(
                    [high[own], low[own]], 0
                )
        return carry

    lax.fori_loop(0, samples // 2, node_part, 0)

    halves = z.bwd_rows // z.fwd_rows
    pairs = samples * z.bwd_chunks

    def spread_back(i, slot):
        half = slice((slot % halves) * z.fwd_rows, (slot % halves + 1) * z.fwd_rows)
        m.pre_v[slot] = dot_nn(m.rep_v[half, :], m.drep_v[aligned(i // halves, 2 * LANES), :])

    def norm_back(i, slot, pair):
        rows, local = aligned(i, z.fwd_rows), aligned(i % per, z.fwd_rows)
        d_update = (m.cot_v[rows, :].astype(F32) + m.pre_v[slot]) * both(m.live_v[local, :])
        normed = m.norm_v[rows, :].astype(F32)
        d_normed = d_update * normed
        m.vsum_v[8:16, :] += fold_rows(d_normed)
        m.vsum_v[16:24, :] += fold_rows(d_update)
        scaled, scaled_normed = d_update * gain_edge, d_normed * gain_edge
        d_out = both(m.inv_v[rows, :]) * (scaled - row_mean(scaled) - normed * row_mean(scaled_normed))
        m.dout_v[pair, slot * z.fwd_rows : (slot + 1) * z.fwd_rows, :] = d_out.astype(BF16)

    def activate_back(i, slot, pair):
        part = slice(slot * z.fwd_rows, (slot + 1) * z.fwd_rows)
        d_act = dot_nt(m.dout_v[pair, part, :], m.half_v[3 * width : 4 * width, :])
        d_pre = (d_act * m.slope_v[aligned(i, z.fwd_rows), :]).astype(BF16)
        m.dpre_v[pair, part, :] = d_pre
        m.dall_v[aligned(i, z.fwd_rows), :] = d_pre

    def weights_back(p, pair):
        s, c = p // z.bwd_chunks, p % z.bwd_chunks
        rows = aligned(p, z.bwd_rows)
        d_out, d_pre = m.dout_v[pair], m.dpre_v[pair]
        m.gmat_v[3 * width : 4 * width, :] += dot_tn(m.act_v[rows, :], d_out)
        sums = dot_nn(jnp.concatenate([m.edge_v[rows, :].T, m.scat_v[c]], 0), d_pre)
        m.gmat_v[0:width, :] += sums[0:width, :]
        sums = sums[width:, :]
        m.aown_v[aligned(s, nodes), :] += sums[0:nodes, :]
        m.ahalo_v[aligned(s, two_halo), :] += sums[nodes : nodes + two_halo, :]
        m.recv_v[aligned(p, z.bwd_nodes), :] = sums[nodes + two_halo :, :]

    m.dout_v[1] = jnp.zeros_like(m.dout_v[1])
    m.dpre_v[1] = jnp.zeros_like(m.dpre_v[1])
    spread_back(0, 0)

    def backward(s, carry):
        sample_copy(cot_ref, m.cot_v, m.cot_sem, s).wait()
        for k in range(z.bwd_chunks):
            p = s * z.bwd_chunks + k
            i = p * halves
            spread_back(i + 1, 1)
            activate_back(jnp.maximum(i - 1, 0), 1, 1 - k)
            norm_back(i, 0, k)
            weights_back(jnp.maximum(p - 1, 0), 1 - k)
            spread_back(jnp.minimum(i + 2, last), 0)
            activate_back(i, 0, k)
            norm_back(i + 1, 1, k)
        return carry

    nodes_sum = Reduce(cube, 4 * width, 3 * width, m.gmat_v, m.gout_v, spare[7:14])
    nodes_sum.begin()
    start_out(1, nout_ref, nout_hbm)
    lax.fori_loop(0, 1, backward, 0)
    nodes_sum.spread()
    lax.fori_loop(1, samples, backward, 0)
    nodes_sum.meet()
    activate_back(last, 1, 1)
    weights_back(pairs - 1, 1)

    def edge_gradient(s, carry):
        for c in range(per):
            rows = aligned(s * per + c, z.fwd_rows)
            d_edge = dot_nt(m.dall_v[rows, :], weight_ref[0:width, :])
            m.edge_out_v[rows, :] = (m.cot_v[rows, :].astype(F32) + d_edge).astype(BF16)
        sample_copy(m.edge_out_v, egrad_ref, m.egrad_sem, s).start()
        return carry

    send_full = weight_ref[width : 2 * width, :]
    recv_full = weight_ref[2 * width : 3 * width, :]
    table = m.table_v[...]
    out_high, out_low = split(m.ahalo_v[...])
    nodes_all = node_ref[...]
    grad_send = dot_tn(table, out_high) + dot_tn(nodes_all, m.aown_v[...].astype(BF16))
    grad_recv = dot_tn(nodes_all, m.recv_v[...].astype(BF16))
    m.gmat_v[width : 2 * width, :] = grad_send
    m.gmat_v[2 * width : 3 * width, :] = grad_recv
    reduce = Reduce(cube, 0, 4 * width, m.gmat_v, m.gout_v, spare[:7])
    vectors = VectorSum(cube, *spare[14:])
    reduce.begin()
    border = (dot_nt(out_high, send_full) + dot_nt(out_low, send_full)).astype(BF16)
    for s in range(samples):
        for side in range(2):
            m.border_v[side, s * halo : (s + 1) * halo, :] = border[
                s * two_halo + side * halo : s * two_halo + (side + 1) * halo, :
            ]
    start_sides(m.border_v, m.ret_v, m.ret_sem)
    for s in range(samples):
        m.vsum_v[0:8, :] += fold_rows(m.recv_v[s * nodes : (s + 1) * nodes, :])
    vectors.begin(
        jnp.concatenate(
            [jnp.sum(m.vsum_v[k * 8 : (k + 1) * 8, :], 0, keepdims=True) for k in range(6)]
            + [jnp.zeros((2, width), F32)],
            0,
        )
    )
    reduce.spread()
    vectors.spread()
    for moment in moments:
        moment.forward()
    nodes_sum.settle()
    for s in range(samples):
        sample_copy(m.edge_out_v, eout_ref, m.eout_sem, s).wait()
    lax.fori_loop(0, samples, edge_gradient, 0)
    for s in range(samples):
        rows = slice(s * nodes, (s + 1) * nodes)
        recv_high, recv_low = split(m.recv_v[rows, :])
        own_high, own_low = split(m.aown_v[rows, :])
        m.total_v[rows, :] += (
            dot_nt(recv_high, recv_full) + dot_nt(recv_low, recv_full)
            + dot_nt(own_high, send_full) + dot_nt(own_low, send_full)
        )
    reduce.meet()
    vectors.meet()
    nodes_sum.forward()
    finish_sides(m.border_v, m.ret_v, m.ret_sem)
    low, high = (list_matrix(list_ref, side, nodes) for side in range(2))
    for s in range(samples):
        rows, part = slice(s * nodes, (s + 1) * nodes), slice(s * halo, (s + 1) * halo)
        ngrad_ref[rows, :] = (
            m.total_v[rows, :] + dot_nn(low, m.ret_v[0, part, :]) + dot_nn(high, m.ret_v[1, part, :])
        ).astype(BF16)
    start_out(2, ngrad_ref, ngrad_hbm)
    reduce.settle()
    m.gvec_v[...] = vectors.settle()
    start_out(10, m.gvec_v, gvec_hbm)
    nodes_sum.arrive()
    bounds = matrix_bounds(width)
    for k in range(PAIR):
        stat_out[k] = new_statistics(m.gout_v[bounds[PAIR + k] : bounds[PAIR + k + 1], :], m.stat_v[k])
    start_out(5, m.gout_v.at[pl.ds(4 * width, 3 * width)], grad_ref.at[pl.ds(4 * width, 3 * width)])
    start_out(6, stat_out, stat_hbm)
    for k in range(PAIR):
        work_out[k, 0:width, :], work_out[k, width:, :] = prepare_bases(stat_out[k], m.bases_v[k], PAIR + k)
    start_out(7, work_out, work_hbm)
    for moment in moments:
        moment.finish()
    start_out(3, m.first_v.at[pl.ds(0, 4 * width)], first_ref)
    start_out(4, m.second_v.at[pl.ds(0, 4 * width)], second_ref)
    for k in range(PAIR):
        low, high = bounds[PAIR + k], bounds[PAIR + k + 1]
        half_out[low - 4 * width : high - 4 * width, :] = rounded_rows(
            m.gout_v[low:high, :], m.bases_v[k], weight_ref[low:high, :], m.first_v[low:high, :], m.second_v[low:high, :]
        )
    start_out(8, half_out, half_hbm)
    for s in range(samples):
        sample_copy(m.edge_out_v, egrad_ref, m.egrad_sem, s).wait()
    for copy in outs:
        copy.wait()
    reduce.forward()
    reduce.arrive()
    grad_out = pltpu.make_async_copy(m.gout_v.at[pl.ds(0, 4 * width)], grad_ref.at[pl.ds(0, 4 * width)], m.out_sem.at[9])
    grad_out.start()
    reduce.end()
    nodes_sum.end()
    vectors.end()
    grad_out.wait()


def round_call(z, count, edge, cot, node, ncot, five, senders, send_rows, kern, kfirst, ksecond, vectors, stat, bases):
    shard, width = kern.shape
    scratch = main_scratch(z)
    cube = Cube(count)
    spare = Reduce.scratch(cube, 4 * width, width) + Reduce.scratch(cube, 3 * width, width) + VectorSum.scratch(cube, (8, width))
    rows, per_node = z.samples * z.edges, z.samples * z.nodes
    anywhere = pl.BlockSpec(memory_space=pl.ANY)
    total = jax.ShapeDtypeStruct((7 * width, width), BF16)
    moments = jax.ShapeDtypeStruct((4 * width, width), BF16)
    return pl.pallas_call(
        partial(round_kernel, z, tuple(scratch), count),
        out_shape=(
            jax.ShapeDtypeStruct((rows, width), BF16),
            jax.ShapeDtypeStruct((rows, width), BF16),
            jax.ShapeDtypeStruct((per_node, width), BF16),
            jax.ShapeDtypeStruct((per_node, width), BF16),
            total,
            jax.ShapeDtypeStruct((8, width), F32),
            total, moments, moments,
            jax.ShapeDtypeStruct((PAIR, width, width), F32),
            jax.ShapeDtypeStruct((PAIR, 2 * width, width), F32),
            jax.ShapeDtypeStruct((3 * width, width), BF16),
        ),
        in_specs=[anywhere] * 13,
        out_specs=(anywhere,) * 12,
        scratch_shapes=list(scratch.values()) + spare,
        compiler_params=pltpu.CompilerParams(
            collective_id=0, has_side_effects=True, vmem_limit_bytes=VMEM_LIMIT
        ),
        name="edge_node_round",
    )(edge, cot, node, ncot, five, senders, send_rows, kern, kfirst, ksecond, vectors, stat, bases)


def update_kernel(
    grad_ref, stat_ref, bases_ref, kern_ref, kfirst_ref, ksecond_ref, rows_ref, first_ref, second_ref,
    gvec_hbm, vec_hbm, vfirst_hbm, vsecond_hbm, work_ref, eout_ref, egrad_ref, nout_ref, ngrad_ref, spair_ref, hpair_ref,
    eout_out, egrad_out, nout_out, ngrad_out, kern_out, kfirst_out, ksecond_out, vec_hout, vfirst_hout, vsecond_hout,
    stat_out, bases_out, half_out,
    grad_v, stat_v, bases_v, kern_v, kfirst_v, ksecond_v, rows_v, first_v, second_v,
    work_v, kern_new, kfirst_new, ksecond_new, stat_new, bases_new, half_v, eout_v, egrad_v, nout_v, ngrad_v, spair_v, hpair_v, gvec_ref, vec_ref, vfirst_ref, vsecond_ref,
    vec_out, vfirst_out, vsecond_out, in_sem, out_sem, pass_sem,
):
    shard, width = kern_v.shape
    copies = [
        pltpu.make_async_copy(source, target, in_sem.at[i])
        for i, (source, target) in enumerate(
            [
                (bases_ref, bases_v), (stat_ref.at[pl.ds(0, PAIR)], stat_v), (grad_ref, grad_v),
                (work_ref, work_v.at[pl.ds(PAIR, PAIR)]), (kern_ref, kern_v), (kfirst_ref, kfirst_v),
                (ksecond_ref, ksecond_v), (rows_ref, rows_v), (first_ref, first_v), (second_ref, second_v),
                (gvec_hbm, gvec_ref), (vec_hbm, vec_ref), (vfirst_hbm, vfirst_ref), (vsecond_hbm, vsecond_ref),
            ]
        )
    ]
    passed = [
        (pltpu.make_async_copy(source, held, pass_sem.at[0, i]), pltpu.make_async_copy(held, target, pass_sem.at[1, i]))
        for i, (source, held, target) in enumerate(
            [
                (eout_ref, eout_v, eout_out), (egrad_ref, egrad_v, egrad_out),
                (nout_ref, nout_v, nout_out), (ngrad_ref, ngrad_v, ngrad_out),
                (spair_ref, spair_v, stat_out.at[pl.ds(PAIR, PAIR)]),
                (hpair_ref, hpair_v, half_out.at[pl.ds(4 * width, 3 * width)]),
            ]
        )
    ]
    outs = [
        pltpu.make_async_copy(source, target, out_sem.at[i])
        for i, (source, target) in enumerate(
            [
                (stat_new, stat_out.at[pl.ds(0, PAIR)]), (kern_new, kern_out), (kfirst_new, kfirst_out), (ksecond_new, ksecond_out),
                (half_v, half_out.at[pl.ds(0, 4 * width)]), (vec_out, vec_hout), (vfirst_out, vfirst_hout),
                (vsecond_out, vsecond_hout), (bases_new, bases_out),
            ]
        )
    ]
    for copy in copies:
        copy.start()
    bases_new[...] = jnp.zeros_like(bases_new)
    for copy in copies[:3]:
        copy.wait()
    bounds = matrix_bounds(width)
    for k in range(PAIR):
        stat_new[k] = new_statistics(grad_v[bounds[k] : bounds[k + 1], :], stat_v[k])
    outs[0].start()
    for k in range(PAIR):
        work_v[k, 0:width, :], work_v[k, width:, :] = prepare_bases(stat_new[k], bases_v[k], k)
    for copy in copies[3:]:
        copy.wait()
    for copy, _ in passed:
        copy.start()

    def own_rows():
        first_row = lax.axis_index("fs") * shard
        grad = grad_v[pl.ds(pl.multiple_of(first_row, 64), shard), :]
        one = matrix_of(first_row, width)
        two = matrix_of(first_row + shard - 1, width)
        in_two = matrix_of(first_row + iota((shard, width), 0), width) != one
        basis_one, basis_two = bases_v[one], bases_v[two]
        rotated = jnp.where(in_two, turn(grad, basis_two), turn(grad, basis_one))
        kfirst_new[...], ksecond_new[...], step = adam_step(kfirst_v[...], ksecond_v[...], rotated)
        turned = jnp.where(in_two, dot_three(step, basis_two), dot_three(step, basis_one))
        kern_new[...] = decayed(kern_v[...], turned)

    def all_rows(k):
        rows = slice(bounds[k], bounds[k + 1])
        half_v[rows, :] = rounded_rows(grad_v[rows, :], bases_v[k], rows_v[rows, :], first_v[rows, :], second_v[rows, :])

    def vector_rows():
        first, second, step = adam_step(vfirst_ref[...], vsecond_ref[...], gvec_ref[0:6, :])
        vfirst_out[...], vsecond_out[...] = first, second
        vec_out[...] = vec_ref[...] - RATE_VECTOR * step

    def beside(b):
        if b < PAIR:
            all_rows(b)
        elif b == PAIR:
            own_rows()
        elif b == PAIR + 2:
            vector_rows()
            for arrived, leaving in passed:
                arrived.wait()
                leaving.start()
            for copy in outs[1:8]:
                copy.start()

    orthogonalize(work_v, bases_new, width, beside)
    outs[8].start()
    for copy in outs + [leaving for _, leaving in passed]:
        copy.wait()


def update_call(grad, stat, bases, kern, kfirst, ksecond, rows, first, second, gvec, vec, vfirst, vsecond, work, *through):
    shard, width = kern.shape
    anywhere = pl.BlockSpec(memory_space=pl.ANY)

    def like(array):
        return jax.ShapeDtypeStruct(array.shape, array.dtype)

    def held(array):
        return pltpu.VMEM(array.shape, array.dtype)

    pair = jax.ShapeDtypeStruct((PAIR,) + stat.shape[1:], F32)
    four = jax.ShapeDtypeStruct((4 * width, width), BF16)
    loaded = (grad, stat, bases, kern, kfirst, ksecond, rows, first, second)
    return pl.pallas_call(
        update_kernel,
        out_shape=tuple(map(like, through[:4]))
        + (like(kern), like(kern), like(kern), like(vec), like(vec), like(vec), like(stat), like(stat), like(grad)),
        in_specs=[anywhere] * 20,
        out_specs=(anywhere,) * 13,
        scratch_shapes=[held(array) for array in (grad, pair, *loaded[2:])]
        + [pltpu.VMEM((COUNT, 2 * width, width), F32)]
        + [held(array) for array in (kern, kern, kern, pair, stat, four, *through, gvec, vec, vec, vec, vec, vec, vec)]
        + [pltpu.SemaphoreType.DMA((14,)), pltpu.SemaphoreType.DMA((9,)), pltpu.SemaphoreType.DMA((2, 6))],
        compiler_params=pltpu.CompilerParams(vmem_limit_bytes=VMEM_LIMIT),
        name="update",
    )(*loaded, gvec, vec, vfirst, vsecond, work, *through)


def on_device(
    edge_latent, node_latent, edge_cot, node_cot, five_flag, senders, send_rows, kernels, kernel_first, kernel_second,
    vectors, vector_first, vector_second, statistics, bases,
):
    samples, nodes, width = node_latent.shape
    slots = senders.shape[0] // nodes
    z = Sizes(samples, nodes, slots, send_rows.shape[1], width)
    edge_out, edge_grad, node_out, node_grad, grad, gvec, rows, first, second, stat_pair, work, half_pair = round_call(
        z,
        lax.axis_size("nodes"),
        edge_latent.reshape(-1, width),
        edge_cot.reshape(-1, width),
        node_latent.reshape(-1, width),
        node_cot.reshape(-1, width),
        five_flag.reshape(1, -1),
        senders.reshape(-1, LANES),
        send_rows,
        kernels,
        kernel_first,
        kernel_second,
        vectors,
        statistics,
        bases,
    )
    edge_out, edge_grad, node_out, node_grad, *rest = update_call(
        grad, statistics, bases, kernels, kernel_first, kernel_second, rows, first, second, gvec,
        vectors, vector_first, vector_second, work, edge_out, edge_grad, node_out, node_grad, stat_pair, half_pair,
    )
    return (
        edge_out.reshape(edge_latent.shape),
        node_out.reshape(node_latent.shape),
        edge_grad.reshape(edge_latent.shape),
        node_grad.reshape(node_latent.shape),
        *rest,
    )


def solution(mesh):
    in_specs = (
        P("fs", "nodes", None),
        P("fs", "nodes", None),
        P("fs", "nodes", None),
        P("fs", "nodes", None),
        P("nodes"),
        P("nodes"),
        P("nodes", None),
        P("fs", None),
        P("fs", None),
        P("fs", None),
        P(),
        P(),
        P(),
        P(),
        P(),
    )
    out_specs = (
        P("fs", "nodes", None),
        P("fs", "nodes", None),
        P("fs", "nodes", None),
        P("fs", "nodes", None),
        P("fs", None),
        P("fs", None),
        P("fs", None),
        P(),
        P(),
        P(),
        P(),
        P(),
        P(),
    )
    return jax.shard_map(
        on_device, mesh=mesh, in_specs=in_specs, out_specs=out_specs, check_vma=False
    )
```

```python
from functools import partial

import jax
import jax.numpy as jnp
from jax import lax
from jax.experimental import pallas as pl
from jax.experimental.pallas import tpu as pltpu
from jax.sharding import PartitionSpec as P

STEP = 5

NORM_EPS = 1e-05
BETA_ONE = 0.5
BETA_TWO = 0.5
RATE_MATRIX = 0.05
RATE_VECTOR = 0.2
DECAY_RATE = 0.01
ADAM_EPS = 1e-08
TINY = 1e-37
HIGH = lax.Precision.HIGHEST
F32 = jnp.float32
BF16 = jnp.bfloat16
LANES = 128
VMEM_LIMIT = 61 * 1024 * 1024


def dot_nn(left, right):
    return lax.dot_general(left, right, (((1,), (0,)), ((), ())), preferred_element_type=F32)


def dot_nt(left, right):
    return lax.dot_general(left, right, (((1,), (1,)), ((), ())), preferred_element_type=F32)


def dot_tn(left, right):
    return lax.dot_general(left, right, (((0,), (0,)), ((), ())), preferred_element_type=F32)


def split(value):
    high = value.astype(BF16)
    return high, (value - high.astype(F32)).astype(BF16)


def iota(shape, dim):
    return lax.broadcasted_iota(jnp.int32, shape, dim)


def ones_where(mask):
    return jnp.where(mask, 1.0, 0.0).astype(BF16)


def fold_rows(value):
    rows, width = value.shape
    return jnp.sum(value.reshape(rows // 8, 8, width), 0)


def aligned(index, step):
    return pl.ds(pl.multiple_of(index * step, step), step)


class Sizes:
    def __init__(self, samples, nodes, slots, halo, width):
        self.samples, self.nodes, self.slots = samples, nodes, slots
        self.halo, self.width = halo, width
        self.edges = nodes * slots
        self.fwd_nodes, self.bwd_nodes = 64, 128
        self.fwd_rows = self.fwd_nodes * slots
        self.bwd_rows = self.bwd_nodes * slots
        self.fwd_chunks = nodes // self.fwd_nodes
        self.bwd_chunks = nodes // self.bwd_nodes


def main_scratch(z):
    rows, width = z.samples * z.edges, z.width
    per_node = z.samples * z.nodes
    per_halo = z.samples * 2 * z.halo
    return dict(
        edge_v=pltpu.VMEM((rows, width), BF16),
        cot_v=pltpu.VMEM((rows, width), BF16),
        edge_out_v=pltpu.VMEM((rows, width), BF16),
        act_v=pltpu.VMEM((rows, width), BF16),
        slope_v=pltpu.VMEM((rows, width), F32),
        norm_v=pltpu.VMEM((rows, width), BF16),
        inv_v=pltpu.VMEM((rows, LANES), F32),
        own_v=pltpu.VMEM((z.edges, z.nodes), BF16),
        scat_v=pltpu.VMEM((z.bwd_chunks, z.nodes + 2 * z.halo + LANES, z.bwd_rows), BF16),
        sel_v=pltpu.VMEM((z.edges, 2 * LANES), BF16),
        rep_v=pltpu.VMEM((z.bwd_rows, 2 * LANES), BF16),
        live_v=pltpu.VMEM((z.edges, LANES), F32),
        half_v=pltpu.VMEM((7 * width, width), BF16),
        pown_v=pltpu.VMEM((per_node, width), BF16),
        psel_v=pltpu.VMEM((z.samples * z.fwd_chunks * 2 * LANES, width), BF16),
        gath_v=pltpu.VMEM((per_node, width), BF16),
        drep_v=pltpu.VMEM((z.samples * z.bwd_chunks * 2 * LANES, width), BF16),
        recv_v=pltpu.VMEM((per_node, width), F32),
        aown_v=pltpu.VMEM((per_node, width), F32),
        ahalo_v=pltpu.VMEM((per_halo, width), F32),
        table_v=pltpu.VMEM((per_halo, width), BF16),
        gmat_v=pltpu.VMEM((7 * width, width), F32),
        vsum_v=pltpu.VMEM((6 * 8, width), F32),
        pre_v=pltpu.VMEM((2, z.fwd_rows, width), F32),
        raw_v=pltpu.VMEM((2, z.fwd_rows, width), F32),
        upd_v=pltpu.VMEM((2, z.fwd_rows, width), BF16),
        dout_v=pltpu.VMEM((2, z.bwd_rows, width), BF16),
        dpre_v=pltpu.VMEM((2, z.bwd_rows, width), BF16),
        dall_v=pltpu.VMEM((rows, width), BF16),
        ncot_v=pltpu.VMEM((per_node, width), BF16),
        total_v=pltpu.VMEM((per_node, width), F32),
        rows_v=pltpu.VMEM((7 * width, width), BF16),
        first_v=pltpu.VMEM((7 * width, width), BF16),
        second_v=pltpu.VMEM((7 * width, width), BF16),
        list_v=pltpu.VMEM((2, z.samples * z.halo, width), BF16),
        halo_v=pltpu.VMEM((2, z.samples * z.halo, width), BF16),
        border_v=pltpu.VMEM((2, z.samples * z.halo, width), BF16),
        ret_v=pltpu.VMEM((2, z.samples * z.halo, width), BF16),
        gout_v=pltpu.VMEM((7 * width, width), BF16),
        edge_sem=pltpu.SemaphoreType.DMA((z.samples,)),
        cot_sem=pltpu.SemaphoreType.DMA((z.samples,)),
        eout_sem=pltpu.SemaphoreType.DMA((z.samples,)),
        egrad_sem=pltpu.SemaphoreType.DMA((z.samples,)),
        stat_v=pltpu.VMEM((PAIR, width, width), F32),
        bases_v=pltpu.VMEM((PAIR, width, width), F32),
        node_v=pltpu.VMEM((per_node, width), BF16),
        nout_v=pltpu.VMEM((per_node, width), BF16),
        ngrad_v=pltpu.VMEM((per_node, width), BF16),
        snew_v=pltpu.VMEM((PAIR, width, width), F32),
        work_v=pltpu.VMEM((PAIR, 2 * width, width), F32),
        hnew_v=pltpu.VMEM((3 * width, width), BF16),
        list_ids=pltpu.VMEM((2, z.halo), jnp.int32),
        five_v=pltpu.VMEM((1, z.nodes), jnp.int32),
        send_ids=pltpu.VMEM((z.edges // LANES, LANES), jnp.int32),
        vec_v=pltpu.VMEM((6, width), F32),
        gvec_v=pltpu.VMEM((8, width), F32),
        local_sem=pltpu.SemaphoreType.DMA((11,)),
        out_sem=pltpu.SemaphoreType.DMA((11,)),
        rows_sem=pltpu.SemaphoreType.DMA((2, 12)),
        first_sem=pltpu.SemaphoreType.DMA((2, 3)),
        second_sem=pltpu.SemaphoreType.DMA((2, 3)),
        halo_sem=pltpu.SemaphoreType.DMA((2, 2)),
        ret_sem=pltpu.SemaphoreType.DMA((2, 2)),
    )


def build_selectors(z, m, five_ref, send_ref):
    halo, nodes, slots = z.halo, z.nodes, z.slots
    lane = iota((LANES, LANES), 1)
    row = iota((LANES, LANES), 0)
    for g in range(z.edges // LANES):
        rows = slice(g * LANES, (g + 1) * LANES)
        line = jnp.broadcast_to(send_ref[g : g + 1, :].astype(F32), (LANES, LANES))
        column = line.T.astype(jnp.int32)
        for h in range(nodes // LANES):
            m.own_v[rows, h * LANES : (h + 1) * LANES] = ones_where(column == lane + (halo + h * LANES))
        place = jnp.where(column < halo, column, jnp.where(column >= halo + nodes, column - nodes, -1))
        in_halo = (place == (lane & (2 * halo - 1))) & (lane < 4 * halo)
        first = slots * (lane & (z.fwd_nodes - 1))
        local = row + (g * LANES) % z.fwd_rows
        m.sel_v[rows, 0:LANES] = ones_where((first <= local) & (local < first + slots))
        m.sel_v[rows, LANES : 2 * LANES] = ones_where(in_halo)
    place = iota((nodes + 2 * halo, z.bwd_rows), 0)
    place = jnp.where(place < nodes, place + halo, jnp.where(place < nodes + halo, place - nodes, place))
    first = slots * iota((LANES, z.bwd_rows), 0)
    local = iota((LANES, z.bwd_rows), 1)
    rep_t = ones_where((first <= local) & (local < first + slots))
    for c in range(z.bwd_chunks):
        lines = range(c * z.bwd_rows // LANES, (c + 1) * z.bwd_rows // LANES)
        senders = jnp.concatenate([send_ref[g : g + 1, :] for g in lines], 1)
        senders = jnp.broadcast_to(senders, place.shape)
        m.scat_v[c, 0 : nodes + 2 * halo, :] = ones_where(senders == place)
        m.scat_v[c, nodes + 2 * halo :, :] = rep_t
    first = slots * (iota((z.bwd_rows, 2 * LANES), 1) & (LANES - 1))
    local = iota((z.bwd_rows, 2 * LANES), 0)
    rep = ones_where((first <= local) & (local < first + slots))
    m.rep_v[...] = rep
    local = iota((z.bwd_rows, LANES), 0).astype(F32)
    slot = local - slots * jnp.floor((local + 0.5) * (1.0 / slots))
    for h in range(nodes // LANES):
        five = jnp.broadcast_to(five_ref[:, h * LANES : (h + 1) * LANES].astype(F32), (LANES, LANES)).T
        spread = dot_nn(rep[:, :LANES], five.astype(BF16))
        m.live_v[h * z.bwd_rows : (h + 1) * z.bwd_rows, :] = jnp.where(slot < slots - spread, 1.0, 0.0)


def both(column):
    return jnp.concatenate([column, column], 1)


def row_mean(value):
    return jnp.sum(value, -1, keepdims=True) * (1.0 / value.shape[-1])


def centred(value):
    centre = value - row_mean(value)
    return centre, lax.rsqrt(row_mean(centre * centre) + NORM_EPS)


def act_and_slope(half):
    turn = jnp.tanh(half)
    above = 1.0 + turn
    act = half * above
    return act, above + act * (1.0 - turn)


MESH = pl.DeviceIdType.MESH


def greet(partners):
    barrier = pltpu.get_barrier_semaphore()
    count = 0
    for device, exists in partners:
        if exists is None:
            pl.semaphore_signal(barrier, inc=1, device_id=device, device_id_type=MESH)
            count = count + 1
        else:
            pl.when(exists)(partial(pl.semaphore_signal, barrier, inc=1, device_id=device, device_id_type=MESH))
            count = count + exists.astype(jnp.int32)
    return lambda: pl.semaphore_wait(barrier, count)


def send(source, target, sems, slot, device):
    return pltpu.make_async_remote_copy(
        src_ref=source, dst_ref=target, send_sem=sems.at[0, slot], recv_sem=sems.at[1, slot],
        device_id=device, device_id_type=MESH,
    )


class Gather:
    def __init__(self, rows_v, sems, shard, fs, node):
        self.rows_v, self.sems, self.shard, self.fs = rows_v, sems, shard, fs
        self.parts = sems.shape[1] // 3
        self.next, self.far = (fs ^ 1, node), (fs ^ 2, node)

    def piece(self, owner, part):
        size = self.shard // self.parts
        return self.rows_v.at[pl.ds(pl.multiple_of(owner * self.shard + part * size, 16), size)]

    def copy(self, owner, part, slot, device):
        return send(self.piece(owner, part), self.piece(owner, part), self.sems, slot * self.parts + part, device)

    def start(self):
        for part in range(self.parts):
            self.copy(self.fs, part, 0, self.far).start()
        for part in range(self.parts):
            self.copy(self.fs, part, 1, self.next).start()

    def forward(self):
        for part in range(self.parts):
            self.copy(self.fs, part, 0, self.far).wait_recv()
            self.copy(self.fs ^ 2, part, 2, self.next).start()

    def finish(self):
        for part in range(self.parts):
            self.copy(self.fs, part, 0, self.far).wait_send()
            self.copy(self.fs, part, 1, self.next).wait()
            self.copy(self.fs ^ 2, part, 2, self.next).wait()


def list_matrix(send_ref, side, nodes):
    halo = send_ref.shape[1]
    listed = jnp.broadcast_to(send_ref[side : side + 1, :], (nodes, halo))
    return ones_where(listed == iota((nodes, halo), 0))


def sides(node, count):
    return ((node - 1, node > 0), (node + 1, node < count - 1))


class Cube:
    def __init__(self, count, fs=None, node=None):
        bits = count.bit_length() - 1
        self.node_bits = min(2, bits)
        self.size = 2 << self.node_bits
        self.extra = list(range(self.node_bits, bits))
        self.fs, self.node = fs, node
        if fs is not None:
            self.me = (fs >> 1) + 2 * (node & ((1 << self.node_bits) - 1))
        self.far_first = sorted(range(1, self.size), key=lambda r: (-r.bit_count(), -r))

    def device(self, r):
        return self.fs ^ (2 * (r & 1)), self.node ^ (r >> 1)

    def over(self, bit):
        return self.fs, self.node ^ (1 << bit)


def tree_sum(parts):
    while len(parts) > 1:
        parts = [left + right for left, right in zip(parts[::2], parts[1::2], strict=True)]
    return parts[0]


class Reduce:
    def __init__(self, cube, first, rows, sum_v, out_v, buffers):
        self.cube, self.sum_v, self.out_v = cube, sum_v, out_v
        self.give_v, self.land_v, self.near_v, self.cube_v, self.acc_v, self.extra_v, self.sems = buffers
        self.half = rows // 2
        self.size = self.half // cube.size
        core = cube.fs & 1
        self.keep, self.give = first + core * self.half, first + (1 - core) * self.half
        self.twin = (cube.fs ^ 1, cube.node)
        self.order = cube.far_first + [0]
        self.started = []

    @staticmethod
    def scratch(cube, rows, width):
        half, extra = rows // 2, max(2 * len(cube.extra), 1)
        size = half // cube.size
        return [
            pltpu.VMEM((half, width), BF16),
            pltpu.VMEM((half, width), BF16),
            pltpu.VMEM((half, width), BF16),
            pltpu.VMEM((cube.size, size, width), BF16),
            pltpu.VMEM((size, width), F32),
            pltpu.VMEM((extra, size, width), BF16),
            pltpu.SemaphoreType.DMA((2, 4 * cube.size + extra)),
        ]

    def rows(self, r, base=0):
        return pl.ds(pl.multiple_of(base + (self.cube.me ^ r) * self.size, 16), self.size)

    def launch(self, source, target, slot, device):
        copy = send(source, target, self.sems, slot, device)
        copy.start()
        self.started.append(copy)
        return copy

    def begin(self):
        self.core = {}
        for r in self.order:
            part = self.give_v.at[self.rows(r)]
            part[...] = self.sum_v[self.rows(r, self.give), :].astype(BF16)
            self.core[r] = self.launch(part, self.land_v.at[self.rows(r)], r, self.twin)

    def spread(self):
        self.near = {}
        for r in self.order:
            self.core[r].wait_recv()
            total = self.sum_v[self.rows(r, self.keep), :] + self.land_v[self.rows(r), :].astype(F32)
            if r:
                part = self.near_v.at[self.rows(r)]
                part[...] = total.astype(BF16)
                self.near[r] = self.launch(part, self.cube_v.at[r], self.cube.size + r, self.cube.device(r))
            else:
                self.acc_v[...] = total

    def meet(self):
        total = self.acc_v[...]
        for r in reversed(self.cube.far_first):
            self.near[r].wait_recv()
            total = total + self.cube_v[r].astype(F32)
        self.far = None
        if self.cube.extra:
            self.exchange(total, 0)
        else:
            self.acc_v[...] = total

    def exchange(self, total, e):
        self.extra_v[2 * e] = total.astype(BF16)
        self.far = self.launch(
            self.extra_v.at[2 * e], self.extra_v.at[2 * e + 1], 4 * self.cube.size + e, self.cube.over(self.cube.extra[e])
        )

    def settle(self):
        total = self.acc_v[...]
        for e in range(len(self.cube.extra)):
            self.far.wait_recv()
            total = self.extra_v[2 * e].astype(F32) + self.extra_v[2 * e + 1].astype(F32)
            if e + 1 < len(self.cube.extra):
                self.exchange(total, e + 1)
        own = self.out_v.at[self.rows(0, self.keep)]
        own[...] = total.astype(BF16)
        size = self.cube.size
        self.back = {r: self.launch(own, own, 2 * size + r, self.cube.device(r)) for r in self.cube.far_first}
        self.last = [self.launch(own, own, 3 * size, self.twin)]

    def forward(self):
        for r in reversed(self.cube.far_first):
            self.back[r].wait_recv()
            part = self.out_v.at[self.rows(r, self.keep)]
            self.last.append(self.launch(part, part, 3 * self.cube.size + r, self.twin))

    def arrive(self):
        for copy in self.last:
            copy.wait_recv()

    def end(self):
        for copy in self.started:
            copy.wait_send()


class VectorSum:
    def __init__(self, cube, send_v, land_v, sems):
        self.cube, self.send_v, self.land_v, self.sems = cube, send_v, land_v, sems
        self.started = []

    @staticmethod
    def scratch(cube, shape):
        extra = len(cube.extra)
        return [
            pltpu.VMEM((2 + extra,) + shape, F32),
            pltpu.VMEM((cube.size + extra,) + shape, F32),
            pltpu.SemaphoreType.DMA((2, cube.size + extra)),
        ]

    def launch(self, source, slot, device):
        copy = send(self.send_v.at[source], self.land_v.at[slot], self.sems, slot, device)
        copy.start()
        self.started.append(copy)
        return copy

    def begin(self, value):
        self.send_v[0] = value
        self.core = self.launch(0, 0, (self.cube.fs ^ 1, self.cube.node))

    def spread(self):
        self.core.wait_recv()
        self.send_v[1] = self.send_v[0] + self.land_v[0]
        self.near = [self.launch(1, r, self.cube.device(r)) for r in range(1, self.cube.size)]

    def meet(self):
        for copy in self.near:
            copy.wait_recv()
        self.total = tree_sum([self.send_v[1]] + [self.land_v[r] for r in range(1, self.cube.size)])
        self.far = self.exchange(0) if self.cube.extra else None

    def exchange(self, e):
        self.send_v[2 + e] = self.total
        return self.launch(2 + e, self.cube.size + e, self.cube.over(self.cube.extra[e]))

    def settle(self):
        for e in range(len(self.cube.extra)):
            self.far.wait_recv()
            self.total = self.total + self.land_v[self.cube.size + e]
            if e + 1 < len(self.cube.extra):
                self.far = self.exchange(e + 1)
        return self.total

    def end(self):
        for copy in self.started:
            copy.wait_send()


BLOCK = 32
COUNT = 4
PAIR = 2
AHEAD = 4
HALF = LANES // BLOCK


def wide_left(value):
    high, low = split(value)
    return jnp.concatenate([high, high, low], 1)


def wide_right(value):
    high, low = split(value)
    return jnp.concatenate([high, low, high], 1)


def dot_three(left, right):
    return dot_nt(wide_left(left), wide_right(right))


def factor_block(packed):
    sub = iota((8, LANES), 0)
    lane = iota((8, LANES), 1)
    tiles = BLOCK // 8
    group = lane & (LANES - BLOCK)
    plain = [packed[8 * r : 8 * r + 8, :] for r in range(tiles)]
    columns = {}

    def take_columns(panel):
        for l in range(8 * panel, 8 * panel + 8):
            columns[l] = [None] * panel + [jnp.take_along_axis(part, group + l, axis=1) for part in plain[panel:]]

    take_columns(0)
    inverse = [jnp.where((lane & (BLOCK - 1)) == sub + 8 * r, 1.0, 0.0) for r in range(tiles)]

    def line(tile, s):
        return jnp.broadcast_to(tile[s : s + 1, :], (8, LANES))

    for j in range(BLOCK):
        rj, sj = j // 8, j % 8
        scale = lax.rsqrt(line(columns[j][rj], sj))
        below = [None if r < rj else columns[j][r] * scale for r in range(tiles)]
        below[rj] = jnp.where(sub > sj, below[rj], 0.0)
        for l in [l for l in columns if l > j]:
            weight = line(below[l // 8], l % 8)
            for r in range(l // 8, tiles):
                columns[l][r] = columns[l][r] - below[r] * weight
        if j < BLOCK - 8 - AHEAD:
            row = line(plain[rj], sj) * scale
            for r in range(rj, tiles):
                plain[r] = plain[r] - below[r] * row
        if j % 8 == 7 - AHEAD and j < BLOCK - 8:
            take_columns(rj + 1)
        row = line(inverse[rj], sj) * scale
        inverse[rj] = jnp.where(sub == sj, row, inverse[rj] - below[rj] * row)
        for r in range(rj + 1, tiles):
            inverse[r] = inverse[r] - below[r] * row
    return jnp.concatenate(inverse, 0)


def turned_blocks(k, width):
    return [h * HALF + (g - k) % HALF for h in range(width // LANES) for g in range(HALF)]


def pick_rows(value, blocks):
    return jnp.concatenate([value[i * BLOCK : (i + 1) * BLOCK, :] for i in blocks], 0)


def orthogonalize(work_v, bases_out, width, beside):
    blocks = width // BLOCK
    group = iota((BLOCK, LANES), 1) // BLOCK
    square = iota((LANES, LANES), 0) // BLOCK == iota((LANES, LANES), 1) // BLOCK

    def placed(values, b):
        return [jnp.where(group == (b + k) % COUNT, values[k], jnp.zeros_like(values[k])) for k in range(COUNT)]

    def lanes_of(b):
        return slice(b // HALF * LANES, (b // HALF + 1) * LANES)

    def rows_of(b):
        return slice(b * BLOCK, (b + 1) * BLOCK)

    packed = sum(placed([work_v[k, rows_of(0), lanes_of(0)] for k in range(COUNT)], 0))
    for b in range(blocks):
        beside(b)
        lanes, after = lanes_of(b), (b + 1) * BLOCK
        high, low = split(factor_block(packed))
        whole_high = high.astype(F32)
        next_high, next_low = pltpu.roll(whole_high, BLOCK, 1), pltpu.roll(low.astype(F32), 2 * BLOCK, 1)
        high, low = placed([high] * COUNT, b), placed([low] * COUNT, b)
        if b < blocks - 1:
            spread_high, spread_low = jnp.concatenate(high, 0), jnp.concatenate(low, 0)
            spread = jnp.concatenate([spread_high, spread_low, spread_high], 1)
            ahead = jnp.concatenate([work_v[k, rows_of(b + 1), lanes] for k in range(COUNT)], 0)
            turned = jnp.where(square, dot_nt(wide_left(ahead), spread), 0.0)
            order = [(g - b - 1) % COUNT for g in range(COUNT)]
            update = dot_nt(wide_left(turned), pick_rows(wide_right(turned), order))
            current = placed([work_v[k, rows_of(b + 1), lanes_of(b + 1)] for k in range(COUNT)], b + 1)
            packed = sum(current) - sum(update[rows_of(k), :] for k in range(COUNT))
        start = after // LANES * LANES
        for k in range(COUNT):
            below = work_v[k, after:, lanes]
            place = (iota(below.shape, 1) // BLOCK - b - k) & (HALF - 1)
            below = jnp.where(
                place == 1, pltpu.roll(below, BLOCK, 1), jnp.where(place == 2, pltpu.roll(below, 2 * BLOCK, 1), below)
            )
            below_high, below_low = split(below)
            below = jnp.where(place == 1, below_low, below_high)
            place = (group - b - k) & (HALF - 1)
            factor = jnp.where(
                place == 0, whole_high, jnp.where(place == 1, next_high, jnp.where(place == 2, next_low, 0.0))
            ).astype(BF16)
            turned = dot_nt(below, jnp.concatenate([factor] * HALF, 0))
            mine = iota((width, LANES), 1) // BLOCK == b % HALF
            bases_out[k, :, lanes] = jnp.where(mine, turned[width - after :, :], bases_out[k, :, lanes])
            if b == blocks - 1:
                continue
            turned_high, turned_low = split(turned)
            part = iota(turned.shape, 1) // BLOCK
            zero = jnp.zeros_like(turned_high)
            left = jnp.where(part == 2, turned_low, turned_high)
            rest = width - after
            right = jnp.where(
                part[0:rest] == 1, turned_low[0:rest], jnp.where(part[0:rest] == 3, zero[0:rest], turned_high[0:rest])
            )
            right = jnp.concatenate(
                [
                    right[(i - b - 1) * BLOCK : (i - b) * BLOCK, :] if i > b else zero[0:BLOCK, :]
                    for i in turned_blocks(k, width)[start // BLOCK :]
                ],
                0,
            )
            work_v[k, after:, start:] -= dot_nt(left, right)


def matrix_bounds(width):
    return [0, 3 * width, 4 * width, 6 * width, 7 * width]


def new_statistics(rows, stat):
    return BETA_TWO * stat + (1.0 - BETA_TWO) * dot_tn(rows, rows)


def matrix_of(row, width):
    return sum((row >= bound).astype(jnp.int32) for bound in matrix_bounds(width)[1:-1])


def prepare_bases(stat, flipped, k):
    width = stat.shape[-1]
    order = turned_blocks(k, width)
    proj_rows = dot_three(flipped, stat)
    gram = dot_three(proj_rows, pick_rows(proj_rows, order))
    return gram, dot_three(stat, pick_rows(flipped, order))


def adam_step(first, second, rotated):
    first = BETA_ONE * first + (1.0 - BETA_ONE) * rotated
    second = BETA_TWO * second + (1.0 - BETA_TWO) * rotated * rotated
    square = second * (1.0 / (1.0 - BETA_TWO**STEP))
    root = square * lax.rsqrt(jnp.maximum(square, TINY))
    return first, second, first * (1.0 / (1.0 - BETA_ONE**STEP)) * (1.0 / (root + ADAM_EPS))


def turn(rows, basis):
    high, low = split(basis)
    return dot_nn(rows, high) + dot_nn(rows, low)


def decayed(kern, turned):
    return kern - RATE_MATRIX * (turned + DECAY_RATE * kern)


def rounded_rows(grad, basis, kern, first, second):
    _, _, step = adam_step(first.astype(F32), second.astype(F32), turn(grad, basis))
    return decayed(kern.astype(F32), dot_nt(step.astype(BF16), basis.astype(BF16))).astype(BF16)


def round_kernel(
    z, names, count, edge_ref, cot_ref, node_hbm, ncot_ref, five_hbm, send_hbm, list_hbm, kern_ref, kfirst_ref, ksecond_ref,
    vec_hbm, stat_ref, bases_ref, eout_ref, egrad_ref, nout_hbm, ngrad_hbm, grad_ref, gvec_hbm, rows_ref, first_ref, second_ref,
    stat_hbm, work_hbm, half_hbm, *scratch,
):
    m = type("Held", (), {})()
    for name, ref in zip(names, scratch[: len(names)], strict=True):
        setattr(m, name, ref)
    spare = scratch[len(names) :]
    fs, node_id = lax.axis_index("fs"), lax.axis_index("nodes")
    cube = Cube(count, fs, node_id)
    around = sides(node_id, count)
    shard = kern_ref.shape[0]
    width, nodes, edges, samples, halo = z.width, z.nodes, z.edges, z.samples, z.halo
    two_halo = 2 * halo

    def sample_copy(source, target, sem, s):
        rows = aligned(s, edges)
        return pltpu.make_async_copy(source.at[rows], target.at[rows], sem.at[s])

    weight_ref = m.rows_v
    mine = pl.ds(pl.multiple_of(fs * shard, 16), shard)
    staged = [pl.ds(i * shard, shard) for i in range(3)]
    locals_in = [
        pltpu.make_async_copy(source, target, m.local_sem.at[i])
        for i, (source, target) in enumerate(
            [
                (kern_ref, m.slope_v.at[staged[0]]), (node_hbm, m.node_v), (list_hbm, m.list_ids), (five_hbm, m.five_v),
                (send_hbm, m.send_ids), (vec_hbm, m.vec_v), (kfirst_ref, m.slope_v.at[staged[1]]),
                (ksecond_ref, m.slope_v.at[staged[2]]), (ncot_ref, m.ncot_v),
                (stat_ref.at[pl.ds(PAIR, PAIR)], m.stat_v), (bases_ref.at[pl.ds(PAIR, PAIR)], m.bases_v),
            ]
        )
    ]
    node_ref, nout_ref, ngrad_ref = m.node_v, m.nout_v, m.ngrad_v
    list_ref, five_ref, send_ref, vec_ref = m.list_ids, m.five_v, m.send_ids, m.vec_v
    stat_out, work_out, half_out = m.snew_v, m.work_v, m.hnew_v

    def start_out(i, source, target):
        copy = pltpu.make_async_copy(source, target, m.out_sem.at[i])
        copy.start()
        outs.append(copy)

    outs = []
    gather = Gather(weight_ref, m.rows_sem, shard, fs, node_id)
    moments = [Gather(m.first_v, m.first_sem, shard, fs, node_id), Gather(m.second_v, m.second_sem, shard, fs, node_id)]
    for copy in locals_in[:6]:
        copy.start()
    m.halo_v[...] = jnp.zeros_like(m.halo_v)
    m.ret_v[...] = jnp.zeros_like(m.ret_v)
    all_in = greet(
        [(gather.next, None)]
        + [(cube.device(r), None) for r in range(1, cube.size)]
        + [(cube.over(bit), None) for bit in cube.extra]
        + [((fs, other), exists) for other, exists in around]
    )
    locals_in[0].wait()
    weight_ref[mine, :] = m.slope_v[staged[0], :].astype(BF16)
    all_in()
    gather.start()
    for copy in locals_in[6:]:
        copy.start()
    for s in range(samples):
        sample_copy(edge_ref, m.edge_v, m.edge_sem, s).start()
    for s in range(samples):
        sample_copy(cot_ref, m.cot_v, m.cot_sem, s).start()

    def to_side(source, target, sems, side, other):
        return send(source.at[side], target.at[1 - side], sems, side, (fs, other))

    def start_sides(source, target, sems):
        for side, (other, exists) in enumerate(around):
            pl.when(exists)(lambda side=side, other=other: to_side(source, target, sems, side, other).start())

    def finish_sides(source, target, sems):
        for side, (other, exists) in enumerate(around):
            def settle(side=side, other=other):
                to_side(source, target, sems, side, other).wait_send()
                to_side(source, target, sems, 1 - side, other).wait_recv()
            pl.when(exists)(settle)

    for copy in locals_in[1:6]:
        copy.wait()
    for side in range(2):
        chosen = list_matrix(list_ref, side, nodes)
        for s in range(samples):
            m.list_v[side, s * halo : (s + 1) * halo, :] = dot_tn(
                chosen, node_ref[s * nodes : (s + 1) * nodes, :]
            ).astype(BF16)
    start_sides(m.list_v, m.halo_v, m.halo_sem)
    build_selectors(z, m, five_ref, send_ref)
    m.gmat_v[...] = jnp.zeros_like(m.gmat_v)
    m.vsum_v[...] = jnp.zeros_like(m.vsum_v)
    m.aown_v[...] = jnp.zeros_like(m.aown_v)
    m.ahalo_v[...] = jnp.zeros_like(m.ahalo_v)
    m.dout_v[1] = jnp.zeros_like(m.dout_v[1])
    m.dpre_v[1] = jnp.zeros_like(m.dpre_v[1])
    gather.forward()
    gather.finish()
    finish_sides(m.list_v, m.halo_v, m.halo_sem)
    start_out(0, weight_ref, rows_ref)
    for copy in locals_in[6:]:
        copy.wait()
    for k, (moment, held) in enumerate(zip(moments, (m.first_v, m.second_v), strict=True)):
        held[mine, :] = m.slope_v[staged[k + 1], :].astype(BF16)
        moment.start()
    m.half_v[...] = weight_ref[...] * jnp.asarray(0.5, BF16)
    for s in range(samples):
        for side in range(2):
            m.table_v[s * two_halo + side * halo : s * two_halo + (side + 1) * halo, :] = m.halo_v[
                side, s * halo : (s + 1) * halo, :
            ]

    send_half = m.half_v[width : 2 * width, :]
    recv_half = m.half_v[2 * width : 3 * width, :]
    bias_edge, gain_edge, shift_edge = vec_ref[0:1, :] * 0.5, vec_ref[1:2, :], vec_ref[2:3, :]
    bias_node, gain_node, shift_node = vec_ref[3:4, :] * 0.5, vec_ref[4:5, :], vec_ref[5:6, :]

    for s in range(samples):
        node = node_ref[s * nodes : (s + 1) * nodes, :]
        m.pown_v[s * nodes : (s + 1) * nodes, :] = dot_nn(node, send_half).astype(BF16)
        high, low = split(dot_nn(node, recv_half) + bias_edge)
        out_high, out_low = split(dot_nn(m.table_v[s * two_halo : (s + 1) * two_halo, :], send_half))
        zero = jnp.zeros((2 * LANES - 2 * z.fwd_nodes - 2 * two_halo, width), BF16)
        for c in range(z.fwd_chunks):
            own = slice(c * z.fwd_nodes, (c + 1) * z.fwd_nodes)
            base = (s * z.fwd_chunks + c) * 2 * LANES
            m.psel_v[base : base + 2 * LANES, :] = jnp.concatenate(
                [high[own], low[own], out_high, out_low, zero], 0
            )

    per = z.fwd_chunks
    last = samples * per - 1

    def join_edges(i, slot):
        s, c = i // per, i % per
        local = aligned(c, z.fwd_rows)
        left = jnp.concatenate([m.edge_v[aligned(i, z.fwd_rows), :], m.own_v[local, :], m.sel_v[local, :]], 1)
        right = jnp.concatenate(
            [m.half_v[0:width, :], m.pown_v[aligned(s, nodes), :], m.psel_v[aligned(i, 2 * LANES), :]], 0
        )
        m.pre_v[slot] = dot_nn(left, right)

    def activate(i, slot):
        rows = aligned(i, z.fwd_rows)
        act, slope = act_and_slope(m.pre_v[slot])
        act = act.astype(BF16)
        m.act_v[rows, :] = act
        m.slope_v[rows, :] = slope
        m.raw_v[slot] = dot_nn(act, weight_ref[3 * width : 4 * width, :])

    def update_edges(i, slot):
        rows, local = aligned(i, z.fwd_rows), aligned(i % per, z.fwd_rows)
        centre, inv = centred(m.raw_v[slot])
        live = m.live_v[local, :]
        inv = inv * live
        m.inv_v[rows, :] = inv
        normed = centre * both(inv)
        m.norm_v[rows, :] = normed.astype(BF16)
        update = normed * gain_edge + both(live) * shift_edge
        m.edge_out_v[rows, :] = (m.edge_v[rows, :].astype(F32) + update).astype(BF16)
        m.upd_v[slot] = update.astype(BF16)

    def gather_updates(i, slot):
        take = slice(nodes + two_halo, nodes + two_halo + z.fwd_nodes)
        gathered = dot_nn(m.scat_v[0, take, 0 : z.fwd_rows], m.upd_v[slot])
        m.gath_v[aligned(i, z.fwd_nodes), :] = gathered.astype(BF16)

    def edge_in(s):
        return sample_copy(edge_ref, m.edge_v, m.edge_sem, s)

    edge_in(0).wait()
    join_edges(0, 0)

    def forward(s, carry):
        pl.when(s < samples - 1)(lambda: edge_in(s + 1).wait())
        for c in range(per):
            i = s * per + c
            join_edges(jnp.minimum(i + 1, last), (c + 1) % 2)
            gather_updates(jnp.maximum(i - 2, 0), c % 2)
            activate(i, c % 2)
            update_edges(jnp.maximum(i - 1, 0), (c + 1) % 2)
        pl.when(s > 0)(lambda: sample_copy(m.edge_out_v, eout_ref, m.eout_sem, s - 1).start())
        return carry

    lax.fori_loop(0, samples, forward, 0)
    gather_updates(last - 1, 0)
    update_edges(last, 1)
    gather_updates(last, 1)
    sample_copy(m.edge_out_v, eout_ref, m.eout_sem, samples - 1).start()

    def node_part(i, carry):
        rows = aligned(i, 2 * nodes)
        node, gath = node_ref[rows, :], m.gath_v[rows, :]
        joined = jnp.concatenate([node, gath], 1)
        act, slope = act_and_slope(dot_nn(joined, m.half_v[4 * width : 6 * width, :]) + bias_node)
        act = act.astype(BF16)
        centre, inv = centred(dot_nn(act, weight_ref[6 * width : 7 * width, :]))
        normed = centre * inv
        nout_ref[rows, :] = (node.astype(F32) + normed * gain_node + shift_node).astype(BF16)
        back = m.ncot_v[rows, :].astype(F32)
        back_normed = back * normed
        scaled, scaled_normed = back * gain_node, back_normed * gain_node
        d_out = (inv * (scaled - row_mean(scaled) - normed * row_mean(scaled_normed))).astype(BF16)
        m.gmat_v[6 * width : 7 * width, :] += dot_tn(act, d_out)
        m.vsum_v[32:40, :] += fold_rows(back_normed)
        m.vsum_v[40:48, :] += fold_rows(back)
        d_pre = dot_nt(d_out, m.half_v[6 * width : 7 * width, :]) * slope
        d_pre = d_pre.astype(BF16)
        m.vsum_v[24:32, :] += fold_rows(d_pre.astype(F32))
        m.gmat_v[4 * width : 6 * width, :] += dot_tn(joined, d_pre)
        d_joined = dot_nt(d_pre, weight_ref[4 * width : 6 * width, :])
        m.total_v[rows, :] = back + d_joined[:, :width]
        high, low = split(d_joined[:, width:])
        for k in range(2):
            for c in range(z.bwd_chunks):
                own = slice(k * nodes + c * z.bwd_nodes, k * nodes + (c + 1) * z.bwd_nodes)
                m.drep_v[aligned((i * 2 + k) * z.bwd_chunks + c, 2 * LANES), :] = jnp.concatenate(
                    [high[own], low[own]], 0
                )
        return carry

    lax.fori_loop(0, samples // 2, node_part, 0)

    halves = z.bwd_rows // z.fwd_rows
    pairs = samples * z.bwd_chunks

    def spread_back(i, slot):
        half = slice((slot % halves) * z.fwd_rows, (slot % halves + 1) * z.fwd_rows)
        m.pre_v[slot] = dot_nn(m.rep_v[half, :], m.drep_v[aligned(i // halves, 2 * LANES), :])

    def norm_back(i, slot, pair):
        rows, local = aligned(i, z.fwd_rows), aligned(i % per, z.fwd_rows)
        d_update = (m.cot_v[rows, :].astype(F32) + m.pre_v[slot]) * both(m.live_v[local, :])
        normed = m.norm_v[rows, :].astype(F32)
        d_normed = d_update * normed
        m.vsum_v[8:16, :] += fold_rows(d_normed)
        m.vsum_v[16:24, :] += fold_rows(d_update)
        scaled, scaled_normed = d_update * gain_edge, d_normed * gain_edge
        d_out = both(m.inv_v[rows, :]) * (scaled - row_mean(scaled) - normed * row_mean(scaled_normed))
        m.dout_v[pair, slot * z.fwd_rows : (slot + 1) * z.fwd_rows, :] = d_out.astype(BF16)

    def activate_back(i, slot, pair):
        part = slice(slot * z.fwd_rows, (slot + 1) * z.fwd_rows)
        d_act = dot_nt(m.dout_v[pair, part, :], m.half_v[3 * width : 4 * width, :])
        d_pre = (d_act * m.slope_v[aligned(i, z.fwd_rows), :]).astype(BF16)
        m.dpre_v[pair, part, :] = d_pre
        m.dall_v[aligned(i, z.fwd_rows), :] = d_pre

    def weights_back(p, pair):
        s, c = p // z.bwd_chunks, p % z.bwd_chunks
        rows = aligned(p, z.bwd_rows)
        d_out, d_pre = m.dout_v[pair], m.dpre_v[pair]
        m.gmat_v[3 * width : 4 * width, :] += dot_tn(m.act_v[rows, :], d_out)
        sums = dot_nn(jnp.concatenate([m.edge_v[rows, :].T, m.scat_v[c]], 0), d_pre)
        m.gmat_v[0:width, :] += sums[0:width, :]
        sums = sums[width:, :]
        m.aown_v[aligned(s, nodes), :] += sums[0:nodes, :]
        m.ahalo_v[aligned(s, two_halo), :] += sums[nodes : nodes + two_halo, :]
        m.recv_v[aligned(p, z.bwd_nodes), :] = sums[nodes + two_halo :, :]

    spread_back(0, 0)

    def backward(s, carry):
        sample_copy(cot_ref, m.cot_v, m.cot_sem, s).wait()
        for k in range(z.bwd_chunks):
            p = s * z.bwd_chunks + k
            i = p * halves
            spread_back(i + 1, 1)
            activate_back(jnp.maximum(i - 1, 0), 1, 1 - k)
            norm_back(i, 0, k)
            weights_back(jnp.maximum(p - 1, 0), 1 - k)
            spread_back(jnp.minimum(i + 2, last), 0)
            activate_back(i, 0, k)
            norm_back(i + 1, 1, k)
        return carry

    nodes_sum = Reduce(cube, 4 * width, 3 * width, m.gmat_v, m.gout_v, spare[7:14])
    nodes_sum.begin()
    start_out(1, nout_ref, nout_hbm)
    lax.fori_loop(0, 1, backward, 0)
    nodes_sum.spread()
    lax.fori_loop(1, samples, backward, 0)
    nodes_sum.meet()
    activate_back(last, 1, 1)
    weights_back(pairs - 1, 1)

    def edge_gradient(s, carry):
        for c in range(per):
            rows = aligned(s * per + c, z.fwd_rows)
            d_edge = dot_nt(m.dall_v[rows, :], weight_ref[0:width, :])
            m.edge_out_v[rows, :] = (m.cot_v[rows, :].astype(F32) + d_edge).astype(BF16)
        sample_copy(m.edge_out_v, egrad_ref, m.egrad_sem, s).start()
        return carry

    send_full = weight_ref[width : 2 * width, :]
    recv_full = weight_ref[2 * width : 3 * width, :]
    table = m.table_v[...]
    out_high, out_low = split(m.ahalo_v[...])
    nodes_all = node_ref[...]
    grad_send = dot_tn(table, out_high) + dot_tn(nodes_all, m.aown_v[...].astype(BF16))
    grad_recv = dot_tn(nodes_all, m.recv_v[...].astype(BF16))
    m.gmat_v[width : 2 * width, :] = grad_send
    m.gmat_v[2 * width : 3 * width, :] = grad_recv
    reduce = Reduce(cube, 0, 4 * width, m.gmat_v, m.gout_v, spare[:7])
    vectors = VectorSum(cube, *spare[14:])
    reduce.begin()
    border = (dot_nt(out_high, send_full) + dot_nt(out_low, send_full)).astype(BF16)
    for s in range(samples):
        for side in range(2):
            m.border_v[side, s * halo : (s + 1) * halo, :] = border[
                s * two_halo + side * halo : s * two_halo + (side + 1) * halo, :
            ]
    start_sides(m.border_v, m.ret_v, m.ret_sem)
    for s in range(samples):
        m.vsum_v[0:8, :] += fold_rows(m.recv_v[s * nodes : (s + 1) * nodes, :])
    vectors.begin(
        jnp.concatenate(
            [jnp.sum(m.vsum_v[k * 8 : (k + 1) * 8, :], 0, keepdims=True) for k in range(6)]
            + [jnp.zeros((2, width), F32)],
            0,
        )
    )
    reduce.spread()
    vectors.spread()
    for moment in moments:
        moment.forward()
    nodes_sum.settle()
    for s in range(samples):
        sample_copy(m.edge_out_v, eout_ref, m.eout_sem, s).wait()
    lax.fori_loop(0, samples, edge_gradient, 0)
    for s in range(samples):
        rows = slice(s * nodes, (s + 1) * nodes)
        recv_high, recv_low = split(m.recv_v[rows, :])
        own_high, own_low = split(m.aown_v[rows, :])
        m.total_v[rows, :] += (
            dot_nt(recv_high, recv_full) + dot_nt(recv_low, recv_full)
            + dot_nt(own_high, send_full) + dot_nt(own_low, send_full)
        )
    reduce.meet()
    vectors.meet()
    nodes_sum.forward()
    finish_sides(m.border_v, m.ret_v, m.ret_sem)
    low, high = (list_matrix(list_ref, side, nodes) for side in range(2))
    for s in range(samples):
        rows, part = slice(s * nodes, (s + 1) * nodes), slice(s * halo, (s + 1) * halo)
        ngrad_ref[rows, :] = (
            m.total_v[rows, :] + dot_nn(low, m.ret_v[0, part, :]) + dot_nn(high, m.ret_v[1, part, :])
        ).astype(BF16)
    start_out(2, ngrad_ref, ngrad_hbm)
    reduce.settle()
    m.gvec_v[...] = vectors.settle()
    start_out(10, m.gvec_v, gvec_hbm)
    nodes_sum.arrive()
    bounds = matrix_bounds(width)
    for k in range(PAIR):
        stat_out[k] = new_statistics(m.gout_v[bounds[PAIR + k] : bounds[PAIR + k + 1], :], m.stat_v[k])
    start_out(5, m.gout_v.at[pl.ds(4 * width, 3 * width)], grad_ref.at[pl.ds(4 * width, 3 * width)])
    start_out(6, stat_out, stat_hbm)
    for k in range(PAIR):
        work_out[k, 0:width, :], work_out[k, width:, :] = prepare_bases(stat_out[k], m.bases_v[k].T, PAIR + k)
    start_out(7, work_out, work_hbm)
    for moment in moments:
        moment.finish()
    start_out(3, m.first_v.at[pl.ds(0, 4 * width)], first_ref)
    start_out(4, m.second_v.at[pl.ds(0, 4 * width)], second_ref)
    for k in range(PAIR):
        low, high = bounds[PAIR + k], bounds[PAIR + k + 1]
        half_out[low - 4 * width : high - 4 * width, :] = rounded_rows(
            m.gout_v[low:high, :], m.bases_v[k], weight_ref[low:high, :], m.first_v[low:high, :], m.second_v[low:high, :]
        )
    start_out(8, half_out, half_hbm)
    for s in range(samples):
        sample_copy(m.edge_out_v, egrad_ref, m.egrad_sem, s).wait()
    for copy in outs:
        copy.wait()
    reduce.forward()
    reduce.arrive()
    grad_out = pltpu.make_async_copy(m.gout_v.at[pl.ds(0, 4 * width)], grad_ref.at[pl.ds(0, 4 * width)], m.out_sem.at[9])
    grad_out.start()
    reduce.end()
    nodes_sum.end()
    vectors.end()
    grad_out.wait()


def round_call(z, count, edge, cot, node, ncot, five, senders, send_rows, kern, kfirst, ksecond, vectors, stat, bases):
    shard, width = kern.shape
    scratch = main_scratch(z)
    cube = Cube(count)
    spare = Reduce.scratch(cube, 4 * width, width) + Reduce.scratch(cube, 3 * width, width) + VectorSum.scratch(cube, (8, width))
    rows, per_node = z.samples * z.edges, z.samples * z.nodes
    anywhere = pl.BlockSpec(memory_space=pl.ANY)
    total = jax.ShapeDtypeStruct((7 * width, width), BF16)
    moments = jax.ShapeDtypeStruct((4 * width, width), BF16)
    return pl.pallas_call(
        partial(round_kernel, z, tuple(scratch), count),
        out_shape=(
            jax.ShapeDtypeStruct((rows, width), BF16),
            jax.ShapeDtypeStruct((rows, width), BF16),
            jax.ShapeDtypeStruct((per_node, width), BF16),
            jax.ShapeDtypeStruct((per_node, width), BF16),
            total,
            jax.ShapeDtypeStruct((8, width), F32),
            total, moments, moments,
            jax.ShapeDtypeStruct((PAIR, width, width), F32),
            jax.ShapeDtypeStruct((PAIR, 2 * width, width), F32),
            jax.ShapeDtypeStruct((3 * width, width), BF16),
        ),
        in_specs=[anywhere] * 13,
        out_specs=(anywhere,) * 12,
        scratch_shapes=list(scratch.values()) + spare,
        compiler_params=pltpu.CompilerParams(
            collective_id=0, has_side_effects=True, vmem_limit_bytes=VMEM_LIMIT
        ),
        name="edge_node_round",
    )(edge, cot, node, ncot, five, senders, send_rows, kern, kfirst, ksecond, vectors, stat, bases)


def update_kernel(
    grad_ref, stat_ref, bases_ref, kern_ref, kfirst_ref, ksecond_ref, rows_ref, first_ref, second_ref,
    gvec_hbm, vec_hbm, vfirst_hbm, vsecond_hbm, work_ref, eout_ref, egrad_ref, nout_ref, ngrad_ref, spair_ref, hpair_ref,
    eout_out, egrad_out, nout_out, ngrad_out, kern_out, kfirst_out, ksecond_out, vec_hout, vfirst_hout, vsecond_hout,
    stat_out, bases_out, half_out,
    grad_v, stat_v, bases_v, kern_v, kfirst_v, ksecond_v, rows_v, first_v, second_v,
    work_v, kern_new, kfirst_new, ksecond_new, stat_new, bases_new, half_v, eout_v, egrad_v, nout_v, ngrad_v, spair_v, hpair_v, gvec_ref, vec_ref, vfirst_ref, vsecond_ref,
    vec_out, vfirst_out, vsecond_out, in_sem, out_sem, pass_sem,
):
    shard, width = kern_v.shape
    copies = [
        pltpu.make_async_copy(source, target, in_sem.at[i])
        for i, (source, target) in enumerate(
            [
                (bases_ref, bases_v), (stat_ref.at[pl.ds(0, PAIR)], stat_v), (grad_ref, grad_v),
                (work_ref, work_v.at[pl.ds(PAIR, PAIR)]), (kern_ref, kern_v), (kfirst_ref, kfirst_v),
                (ksecond_ref, ksecond_v), (rows_ref, rows_v), (first_ref, first_v), (second_ref, second_v),
                (gvec_hbm, gvec_ref), (vec_hbm, vec_ref), (vfirst_hbm, vfirst_ref), (vsecond_hbm, vsecond_ref),
            ]
        )
    ]
    passed = [
        (pltpu.make_async_copy(source, held, pass_sem.at[0, i]), pltpu.make_async_copy(held, target, pass_sem.at[1, i]))
        for i, (source, held, target) in enumerate(
            [
                (eout_ref, eout_v, eout_out), (egrad_ref, egrad_v, egrad_out),
                (nout_ref, nout_v, nout_out), (ngrad_ref, ngrad_v, ngrad_out),
                (spair_ref, spair_v, stat_out.at[pl.ds(PAIR, PAIR)]),
                (hpair_ref, hpair_v, half_out.at[pl.ds(4 * width, 3 * width)]),
            ]
        )
    ]
    outs = [
        pltpu.make_async_copy(source, target, out_sem.at[i])
        for i, (source, target) in enumerate(
            [
                (stat_new, stat_out.at[pl.ds(0, PAIR)]), (kern_new, kern_out), (kfirst_new, kfirst_out), (ksecond_new, ksecond_out),
                (half_v, half_out.at[pl.ds(0, 4 * width)]), (vec_out, vec_hout), (vfirst_out, vfirst_hout),
                (vsecond_out, vsecond_hout), (bases_new.at[:, :, pl.ds(0, LANES)], bases_out.at[:, :, pl.ds(0, LANES)]),
                (bases_new.at[:, :, pl.ds(LANES, width - LANES)], bases_out.at[:, :, pl.ds(LANES, width - LANES)]),
            ]
        )
    ]
    for copy in copies:
        copy.start()
    bases_new[...] = jnp.zeros_like(bases_new)
    copies[0].wait()
    flipped = [bases_v[k].T for k in range(PAIR)]
    for copy in copies[1:3]:
        copy.wait()
    bounds = matrix_bounds(width)
    for k in range(PAIR):
        stat_new[k] = new_statistics(grad_v[bounds[k] : bounds[k + 1], :], stat_v[k])
    outs[0].start()
    for k in range(PAIR):
        work_v[k, 0:width, :], work_v[k, width:, :] = prepare_bases(stat_new[k], flipped[k], k)
    for copy in copies[3:]:
        copy.wait()
    for copy, _ in passed:
        copy.start()

    def own_rows():
        first_row = lax.axis_index("fs") * shard
        grad = grad_v[pl.ds(pl.multiple_of(first_row, 64), shard), :]
        one = matrix_of(first_row, width)
        two = matrix_of(first_row + shard - 1, width)
        in_two = matrix_of(first_row + iota((shard, width), 0), width) != one
        basis_one, basis_two = bases_v[one], bases_v[two]
        rotated = jnp.where(in_two, turn(grad, basis_two), turn(grad, basis_one))
        kfirst_new[...], ksecond_new[...], step = adam_step(kfirst_v[...], ksecond_v[...], rotated)
        turned = jnp.where(in_two, dot_three(step, basis_two), dot_three(step, basis_one))
        kern_new[...] = decayed(kern_v[...], turned)

    def all_rows(k):
        rows = slice(bounds[k], bounds[k + 1])
        half_v[rows, :] = rounded_rows(grad_v[rows, :], bases_v[k], rows_v[rows, :], first_v[rows, :], second_v[rows, :])

    def vector_rows():
        first, second, step = adam_step(vfirst_ref[...], vsecond_ref[...], gvec_ref[0:6, :])
        vfirst_out[...], vsecond_out[...] = first, second
        vec_out[...] = vec_ref[...] - RATE_VECTOR * step

    def beside(b):
        if b == 0:
            all_rows(0)
        if b == 1:
            all_rows(1)
        if b == 4:
            own_rows()
        if b == 3:
            vector_rows()
            for arrived, leaving in passed:
                arrived.wait()
                leaving.start()
        if b == 5:
            for copy in outs[1:9]:
                copy.start()

    orthogonalize(work_v, bases_new, width, beside)
    outs[9].start()
    for copy in outs + [leaving for _, leaving in passed]:
        copy.wait()


def update_call(grad, stat, bases, kern, kfirst, ksecond, rows, first, second, gvec, vec, vfirst, vsecond, work, *through):
    shard, width = kern.shape
    anywhere = pl.BlockSpec(memory_space=pl.ANY)

    def like(array):
        return jax.ShapeDtypeStruct(array.shape, array.dtype)

    def held(array):
        return pltpu.VMEM(array.shape, array.dtype)

    pair = jax.ShapeDtypeStruct((PAIR,) + stat.shape[1:], F32)
    four = jax.ShapeDtypeStruct((4 * width, width), BF16)
    loaded = (grad, stat, bases, kern, kfirst, ksecond, rows, first, second)
    return pl.pallas_call(
        update_kernel,
        out_shape=tuple(map(like, through[:4]))
        + (like(kern), like(kern), like(kern), like(vec), like(vec), like(vec), like(stat), like(stat), like(grad)),
        in_specs=[anywhere] * 20,
        out_specs=(anywhere,) * 13,
        scratch_shapes=[held(array) for array in (grad, pair, *loaded[2:])]
        + [pltpu.VMEM((COUNT, 2 * width, width), F32)]
        + [held(array) for array in (kern, kern, kern, pair, stat, four, *through, gvec, vec, vec, vec, vec, vec, vec)]
        + [pltpu.SemaphoreType.DMA((14,)), pltpu.SemaphoreType.DMA((10,)), pltpu.SemaphoreType.DMA((2, 6))],
        compiler_params=pltpu.CompilerParams(vmem_limit_bytes=VMEM_LIMIT),
        name="update",
    )(*loaded, gvec, vec, vfirst, vsecond, work, *through)


def on_device(
    edge_latent, node_latent, edge_cot, node_cot, five_flag, senders, send_rows, kernels, kernel_first, kernel_second,
    vectors, vector_first, vector_second, statistics, bases,
):
    samples, nodes, width = node_latent.shape
    slots = senders.shape[0] // nodes
    z = Sizes(samples, nodes, slots, send_rows.shape[1], width)
    edge_out, edge_grad, node_out, node_grad, grad, gvec, rows, first, second, stat_pair, work, half_pair = round_call(
        z,
        lax.axis_size("nodes"),
        edge_latent.reshape(-1, width),
        edge_cot.reshape(-1, width),
        node_latent.reshape(-1, width),
        node_cot.reshape(-1, width),
        five_flag.reshape(1, -1),
        senders.reshape(-1, LANES),
        send_rows,
        kernels,
        kernel_first,
        kernel_second,
        vectors,
        statistics,
        bases,
    )
    edge_out, edge_grad, node_out, node_grad, *rest = update_call(
        grad, statistics, bases, kernels, kernel_first, kernel_second, rows, first, second, gvec,
        vectors, vector_first, vector_second, work, edge_out, edge_grad, node_out, node_grad, stat_pair, half_pair,
    )
    return (
        edge_out.reshape(edge_latent.shape),
        node_out.reshape(node_latent.shape),
        edge_grad.reshape(edge_latent.shape),
        node_grad.reshape(node_latent.shape),
        *rest,
    )


def solution(mesh):
    in_specs = (
        P("fs", "nodes", None),
        P("fs", "nodes", None),
        P("fs", "nodes", None),
        P("fs", "nodes", None),
        P("nodes"),
        P("nodes"),
        P("nodes", None),
        P("fs", None),
        P("fs", None),
        P("fs", None),
        P(),
        P(),
        P(),
        P(),
        P(),
    )
    out_specs = (
        P("fs", "nodes", None),
        P("fs", "nodes", None),
        P("fs", "nodes", None),
        P("fs", "nodes", None),
        P("fs", None),
        P("fs", None),
        P("fs", None),
        P(),
        P(),
        P(),
        P(),
        P(),
        P(),
    )
    return jax.shard_map(
        on_device, mesh=mesh, in_specs=in_specs, out_specs=out_specs, check_vma=False
    )
```
